32 devices in a mesh: dp: 4 (over y, x), wide: 8 (over z, core).
Axes of the slice: x: 2, y: 2, z: 4, core: 2. Of those that a mesh axis runs over, the one named last changes fastest.
Arguments:
- chars: bfloat16 [32, 8, 64, 16, 256], P(('dp', 'wide')), may hold values from -6 to 6
- char_counts: int32 [32, 8, 64], P(('dp', 'wide')), may hold values from 1 to 16
- buckets: int32 [32, 256, 1], P(('dp', 'wide')), may hold values from 0 to 7; in each aligned block of 256 rows (0 to 255, 256 to 511, ..., all dimensions but the last counted through in order) at most 64 rows name the same one
- assign: int32 [8], replicated, may hold values from 0 to 7, each once
- segments: int32 [32, 256], P(('dp', 'wide')), may hold values from 0 to 15, never falling along the last dimension, each value on 1 to 128 neighbouring positions
- char_gain: bfloat16 [256], P('wide'), may hold values from 0.5 to 1.5
- char_shift: bfloat16 [256], P('wide'), may hold values from -1 to 1
- char_inproj: bfloat16 [256, 768], P('wide'), may hold values from -0.375 to 0.375
- char_outproj: bfloat16 [256, 256], P('wide'), may hold values from -0.75 to 0.75
- char_gain_mid: bfloat16 [256], P('wide'), may hold values from 0.5 to 1.5
- char_shift_mid: bfloat16 [256], P('wide'), may hold values from -1 to 1
- char_up: bfloat16 [256, 1024], P('wide'), may hold values from -0.375 to 0.375
- char_up_bias: bfloat16 [1024], P('wide'), may hold values from -1.5 to 1.5
- char_down: bfloat16 [1024, 256], P('wide'), may hold values from -0.1875 to 0.1875
- char_down_bias: bfloat16 [256], P('wide'), may hold values from -1.5 to 1.5
- pool_query: bfloat16 [256], P('wide'), may hold values from -4 to 4
- char_proj: bfloat16 [256, 512], P('wide'), may hold values from -0.375 to 0.375
- char_proj_bias: bfloat16 [512], P('wide'), may hold values from -1.5 to 1.5
- word_gain: bfloat16 [512], P('wide'), may hold values from 0.5 to 1.5
- word_shift: bfloat16 [512], P('wide'), may hold values from -1 to 1
- word_inproj: bfloat16 [512, 1536], P('wide'), may hold values from -0.25 to 0.25
- word_outproj: bfloat16 [512, 512], P('wide'), may hold values from -0.75 to 0.75
- word_gain_mid: bfloat16 [512], P('wide'), may hold values from 0.5 to 1.5
- word_shift_mid: bfloat16 [512], P('wide'), may hold values from -1 to 1
- word_up: bfloat16 [512, 2048], P('wide'), may hold values from -0.25 to 0.25
- word_up_bias: bfloat16 [2048], P('wide'), may hold values from -1.5 to 1.5
- word_down: bfloat16 [2048, 512], P('wide'), may hold values from -0.125 to 0.125
- word_down_bias: bfloat16 [512], P('wide'), may hold values from -1.5 to 1.5
- out_grad: bfloat16 [32, 256, 512], P(('dp', 'wide')), may hold values from -6 to 6
Outputs:
- word_output: float32 [32, 256, 512], P(('dp', 'wide'))
- grad_chars: float32 [32, 8, 64, 16, 256], P(('dp', 'wide'))
- grad_char_gain: float32 [256], P('wide')
- grad_char_shift: float32 [256], P('wide')
- grad_char_inproj: float32 [256, 768], P('wide')
- grad_char_outproj: float32 [256, 256], P('wide')
- grad_char_gain_mid: float32 [256], P('wide')
- grad_char_shift_mid: float32 [256], P('wide')
- grad_char_up: float32 [256, 1024], P('wide')
- grad_char_up_bias: float32 [1024], P('wide')
- grad_char_down: float32 [1024, 256], P('wide')
- grad_char_down_bias: float32 [256], P('wide')
- grad_pool_query: float32 [256], P('wide')
- grad_char_proj: float32 [256, 512], P('wide')
- grad_char_proj_bias: float32 [512], P('wide')
- grad_word_gain: float32 [512], P('wide')
- grad_word_shift: float32 [512], P('wide')
- grad_word_inproj: float32 [512, 1536], P('wide')
- grad_word_outproj: float32 [512, 512], P('wide')
- grad_word_gain_mid: float32 [512], P('wide')
- grad_word_shift_mid: float32 [512], P('wide')
- grad_word_up: float32 [512, 2048], P('wide')
- grad_word_up_bias: float32 [2048], P('wide')
- grad_word_down: float32 [2048, 512], P('wide')
- grad_word_down_bias: float32 [512], P('wide')
The draws below stay inside these ranges and needn't reach their ends.
Inputs may be any that keep to these rules, and one draw needn't show every extreme that they name: `buckets`: within one sequence at most 64 words name the same bucket, and in some sequence one bucket is named by exactly 64. `assign`: A permutation of the buckets over the wide indices. `segments`: never falling along a sequence; each document has 1 to 128 words, and one has exactly that many.
All inputs are finite; a program needn't handle non-finite values.
Results may differ from the reference program's by a relative error of at most 0.023.
Values may be sent and summed in bfloat16 or wider, within the bound.
A program may use at most 192 MiB of HBM per device.

```python
import math
import jax
import jax.numpy as jnp
import numpy as np
from jax import lax

D = 512
HEADS = 8
HD = 64
FFN = 2048
CW = 256
CHEADS = 4
CHD = 64
CFF = 1024
NCHAR = 16
LEN = 256
SEQS = 32
MOST = 64
N_WIDE = 8


def place_ends(array, stream_key, low, largest):
    dims = array.shape
    spot = [jax.random.randint(jax.random.fold_in(stream_key, axis), (), 0, dims[axis]) for axis in range(len(dims))]
    array = array.at[tuple(spot)].set(low)
    longest = dims.index(max(dims))
    spot[longest] = (spot[longest] + 1) % dims[longest]
    return array.at[tuple(spot)].set(largest)


def shard_levels(stream_key, extent, cuts, smallest, top_value):
    def one(dim, blocks):
        draws = jax.random.uniform(jax.random.fold_in(jax.random.fold_in(stream_key, 6), dim), (blocks,), jnp.float32, smallest / len(cuts), top_value / len(cuts))
        return jnp.repeat(jnp.exp(draws), extent[dim] // blocks).reshape((-1,) + (1,) * (len(extent) - dim - 1))

    loudness = one(*cuts[0])
    for cut in cuts[1:]:
        loudness = loudness * one(*cut)
    return loudness


def profile(amount, total, reach, slope):
    portions = [(1 << 20) // math.isqrt(standing ** slope) + 1 for standing in range(2, amount + 1)]
    rest, given = total - reach - (amount - 1), [1] * (amount - 1)
    while rest > 0:
        free = [i for i in range(amount - 1) if given[i] < reach]
        pool, budget = sum([portions[i] for i in free]), rest
        for i in free:
            addition = min(reach - given[i], max(1, budget * portions[i] // pool), rest)
            given[i] = given[i] + addition
            rest = rest - addition
    return np.array([reach] + given)


def uneven_parts(rng, number_of, total, limit, lean):
    if number_of == 2:
        one = jax.random.randint(rng, (), max(1, total - limit), min(limit, total - 1) + 1)
        return jnp.stack([one, total - one])
    sizes = jnp.asarray(profile(number_of, total, limit, lean), jnp.int32)
    twos = (number_of - 1) // 2
    donor, sink = sizes[1:1 + 2 * twos:2], sizes[2:2 + 2 * twos:2]
    room = jnp.minimum(donor - 1, limit - sink)
    moved = jax.random.randint(jax.random.fold_in(rng, 1), (twos,), 0, 1 << 20) % (room + 1)
    sizes = sizes.at[1:1 + 2 * twos:2].set(donor - moved).at[2:2 + 2 * twos:2].set(sink + moved)
    return sizes[jax.random.permutation(jax.random.fold_in(rng, 2), number_of)]


def shared_out(key, own, number, rows, count, top, most, slope):
    ranking = jax.random.permutation(key, count)
    crowded, common = portions_of(count, rows * top, most, slope, True), portions_of(count, rows * top, most, slope, False)
    places = jnp.arange(count)

    def named(tallies, offset_by):
        used = int((tallies > 0).sum())
        fixed = max(1, used // 4)
        moved = fixed + (places - fixed + offset_by * (used - fixed)) % max(1, count - fixed)
        return jnp.zeros((count,), jnp.int32).at[ranking[jnp.where(places < fixed, places, moved)]].set(jnp.asarray(tallies, jnp.int32))

    tallies = jnp.where(number % 4 == 0, named(crowded, number // 4), named(common, number - number // 4 - 1))
    mixed = jax.random.permutation(jax.random.fold_in(own, 3), count)
    donor, sink = mixed[0:count // 2 * 2:2], mixed[1:count // 2 * 2:2]
    room = jnp.minimum(tallies[donor] - 1, most - tallies[sink]) // 2
    room = jnp.where((donor == ranking[0]) | (sink == ranking[0]) | (tallies[sink] == 0), 0, jnp.maximum(room, 0))
    moved = jax.random.randint(jax.random.fold_in(own, 4), (count // 2,), 0, 1 << 20) % (room + 1)
    tallies = tallies.at[donor].add(-moved).at[sink].add(moved)
    members = jnp.searchsorted(jnp.cumsum(tallies), jnp.arange(rows * top), side="right").astype(jnp.int32)
    grid = members.reshape(top, rows).T
    grid = grid[jax.random.permutation(jax.random.fold_in(own, 1), rows)]
    offset_by = jax.random.randint(jax.random.fold_in(own, 2), (rows, 1), 0, top)
    return jnp.take_along_axis(grid, (jnp.arange(top)[None, :] + offset_by) % top, axis=1)


def portions_of(count, total, most, slope, full):
    portions = [(1 << 20) // math.isqrt(standing ** slope) + 1 for standing in range(1, count + 1)]
    largest = most if full else min(most, max(-(-total // count), total * portions[0] // sum(portions)))
    least = 1 if total - largest >= count - 1 else 0
    given, spare = [largest] + [least] * (count - 1), total - largest - least * (count - 1)
    while spare > 0:
        movable = [i for i in range(1, count) if given[i] < largest] or [i for i in range(1, count) if given[i] < most]
        pool, left = sum([portions[i] for i in movable]), spare
        for i in movable:
            addition = min(most - given[i], max(1, left * portions[i] // pool), spare)
            given[i] = given[i] + addition
            spare = spare - addition
    return np.array(given)


def normal_values(own_key, extent, width, reach, split=(), kind=jnp.bfloat16):
    entries = jax.random.normal(own_key, extent, jnp.float32) * width
    if len(split) > 0:
        entries = shard_levels(own_key, extent, split, -0.22, 0.18) * entries
    return jnp.clip(entries, min=-reach, max=reach).astype(kind)


def setup_inputs(seed: int = 0) -> dict:
    streams_of = jax.random.split(jax.random.key(seed), 30)
    chars = normal_values(streams_of[0], (SEQS, N_WIDE, MOST, NCHAR, CW), 1.0, 6.0, ((0, 32),))
    char_counts = place_ends(jax.random.randint(streams_of[1], (SEQS, N_WIDE, MOST), 1, NCHAR + 1), jax.random.fold_in(streams_of[1], 1), 1, NCHAR).astype(jnp.int32)
    buckets_keys = jax.random.split(jax.random.fold_in(streams_of[2], 1), SEQS * LEN // LEN)
    buckets_turns = jax.random.permutation(jax.random.fold_in(streams_of[2], 3), SEQS * LEN // LEN)
    buckets = jax.vmap(lambda own, number: shared_out(jax.random.fold_in(streams_of[2], 2), own, number, LEN, N_WIDE, 1, MOST, 2))(buckets_keys, buckets_turns).reshape((SEQS, LEN, 1))
    assign = jax.random.permutation(streams_of[3], N_WIDE).astype(jnp.int32)
    segments = jax.vmap(lambda own: jnp.searchsorted(jnp.cumsum(uneven_parts(own, LEN // 16, LEN, LEN // 2, 2)), jnp.arange(LEN), side="right"))(jax.random.split(streams_of[4], SEQS)).reshape((SEQS, LEN)).astype(jnp.int32)
    char_gain = jnp.clip(1.0 + 0.1 * jax.random.normal(streams_of[5], (CW,), jnp.float32), 0.5, 1.5).astype(jnp.bfloat16)
    char_shift = normal_values(streams_of[6], (CW,), 0.2, 1.0, ((0, 8),))
    char_inproj = normal_values(streams_of[7], (CW, 3 * CW), CW ** -0.5, 0.375, ((0, 8),))
    char_outproj = normal_values(streams_of[8], (CW, CW), (CW // 4) ** -0.5, 0.75, ((0, 8),))
    char_gain_mid = jnp.clip(1.0 + 0.1 * jax.random.normal(streams_of[9], (CW,), jnp.float32), 0.5, 1.5).astype(jnp.bfloat16)
    char_shift_mid = normal_values(streams_of[10], (CW,), 0.2, 1.0, ((0, 8),))
    char_up = normal_values(streams_of[11], (CW, CFF), CW ** -0.5, 0.375, ((0, 8),))
    char_up_bias = normal_values(streams_of[12], (CFF,), 0.3, 1.5, ((0, 8),))
    char_down = normal_values(streams_of[13], (CFF, CW), CFF ** -0.5, 0.1875, ((0, 8),))
    char_down_bias = normal_values(streams_of[14], (CW,), 0.3, 1.5, ((0, 8),))
    pool_query = normal_values(streams_of[15], (CW,), 1.0, 4.0, ((0, 8),))
    char_proj = normal_values(streams_of[16], (CW, D), CW ** -0.5, 0.375, ((0, 8),))
    char_proj_bias = normal_values(streams_of[17], (D,), 0.3, 1.5, ((0, 8),))
    word_gain = jnp.clip(1.0 + 0.1 * jax.random.normal(streams_of[18], (D,), jnp.float32), 0.5, 1.5).astype(jnp.bfloat16)
    word_shift = normal_values(streams_of[19], (D,), 0.2, 1.0, ((0, 8),))
    word_inproj = normal_values(streams_of[20], (D, 3 * D), D ** -0.5, 0.25, ((0, 8),))
    word_outproj = normal_values(streams_of[21], (D, D), (D // 8) ** -0.5, 0.75, ((0, 8),))
    word_gain_mid = jnp.clip(1.0 + 0.1 * jax.random.normal(streams_of[22], (D,), jnp.float32), 0.5, 1.5).astype(jnp.bfloat16)
    word_shift_mid = normal_values(streams_of[23], (D,), 0.2, 1.0, ((0, 8),))
    word_up = normal_values(streams_of[24], (D, FFN), D ** -0.5, 0.25, ((0, 8),))
    word_up_bias = normal_values(streams_of[25], (FFN,), 0.3, 1.5, ((0, 8),))
    word_down = normal_values(streams_of[26], (FFN, D), FFN ** -0.5, 0.125, ((0, 8),))
    word_down_bias = normal_values(streams_of[27], (D,), 0.3, 1.5, ((0, 8),))
    out_grad = normal_values(streams_of[28], (SEQS, LEN, D), 1.0, 6.0, ((0, 32),))
    return dict(chars=chars, char_counts=char_counts, buckets=buckets, assign=assign, segments=segments, char_gain=char_gain, char_shift=char_shift, char_inproj=char_inproj, char_outproj=char_outproj, char_gain_mid=char_gain_mid, char_shift_mid=char_shift_mid, char_up=char_up, char_up_bias=char_up_bias, char_down=char_down, char_down_bias=char_down_bias, pool_query=pool_query, char_proj=char_proj, char_proj_bias=char_proj_bias, word_gain=word_gain, word_shift=word_shift, word_inproj=word_inproj, word_outproj=word_outproj, word_gain_mid=word_gain_mid, word_shift_mid=word_shift_mid, word_up=word_up, word_up_bias=word_up_bias, word_down=word_down, word_down_bias=word_down_bias, out_grad=out_grad)


EPS = 1e-05
NEG = -1e+30
ROOT_HALF = 0.7071067811865476
HIGHEST = lax.Precision.HIGHEST

@jax.custom_vjp
def low(v):
    return lax.optimization_barrier(v.astype(jnp.bfloat16)).astype(jnp.float32)

@jax.custom_vjp
def low_back(v):
    return v

def low_keep(v):
    return (low(v), None)

def low_pass(kept, grad):
    return (grad,)

def back_keep(v):
    return (v, None)

def back_low(kept, grad):
    return (low(grad),)
low.defvjp(low_keep, low_pass)
low_back.defvjp(back_keep, back_low)

def round_both(value):
    return low_back(low(value))

def matmul_high(left, right):
    return jnp.dot(left, right, precision=HIGHEST)

def gelu_exact(value):
    return 0.5 * value * (1.0 + lax.erf(value * ROOT_HALF))

def layer_norm(values, gain, shift):
    center = values - lax.optimization_barrier(jnp.mean(values, -1, keepdims=True))
    return center * lax.rsqrt(lax.optimization_barrier(jnp.mean(center * center, -1, keepdims=True)) + EPS) * gain + shift

def char_unit(params, char_grid, counts):
    gain_a, shift_a, inproj, outproj, gain_b, shift_b, up_weight, up_bias, down_weight, down_bias, query_vec, proj_weight, proj_bias = params
    word_count = char_grid.shape[0]
    valid_mask = jnp.arange(NCHAR, dtype=jnp.int32)[None, :] < counts[:, None]
    normed = low(layer_norm(char_grid, gain_a, shift_a))
    triple = round_both(jnp.einsum('wic,cf->wif', normed, inproj, precision=HIGHEST)).reshape(word_count, NCHAR, 3, CHEADS, CHD)
    scores = jnp.einsum('wihd,wjhd->whij', triple[:, :, 0], triple[:, :, 1], precision=HIGHEST) * CHD ** (-0.5)
    scores = low_back(jnp.where(valid_mask[:, None, None, :], scores, NEG))
    soft_weights = low(jax.nn.softmax(scores, -1))
    mixed = round_both(jnp.einsum('whij,wjhd->wihd', soft_weights, triple[:, :, 2], precision=HIGHEST)).reshape(word_count, NCHAR, CW)
    inner_sum = char_grid + low_back(jnp.einsum('wic,cf->wif', mixed, outproj, precision=HIGHEST))
    spread = low(layer_norm(inner_sum, gain_b, shift_b))
    before = low_back(jnp.einsum('wic,cf->wif', spread, up_weight, precision=HIGHEST) + up_bias)
    active = low(gelu_exact(before))
    outer_sum = inner_sum + low_back(jnp.einsum('wif,fc->wic', active, down_weight, precision=HIGHEST) + down_bias)
    attend = lax.optimization_barrier(jnp.sum(outer_sum * query_vec, -1)) * CW ** (-0.5)
    pool_weights = jax.nn.softmax(jnp.where(valid_mask, attend, NEG), -1)
    pooled = round_both(lax.optimization_barrier(jnp.sum(pool_weights[:, :, None] * outer_sum, 1)))
    return round_both(matmul_high(pooled, proj_weight) + proj_bias)

def word_unit(params, word_rows, segment_row):
    gain_a, shift_a, inproj, outproj, gain_b, shift_b, up_weight, up_bias, down_weight, down_bias = params
    length = word_rows.shape[0]
    normed = low(layer_norm(word_rows, gain_a, shift_a))
    triple = round_both(matmul_high(normed, inproj)).reshape(length, 3, HEADS, HD)
    scores = jnp.einsum('ihd,jhd->hij', triple[:, 0], triple[:, 1], precision=HIGHEST) * HD ** (-0.5)
    position = jnp.arange(length, dtype=jnp.int32)
    allowed = (segment_row[:, None] == segment_row[None, :]) & (position[None, :] <= position[:, None])
    scores = low_back(jnp.where(allowed[None], scores, NEG))
    soft_weights = low(jax.nn.softmax(scores, -1))
    mixed = round_both(jnp.einsum('hij,jhd->ihd', soft_weights, triple[:, 2], precision=HIGHEST)).reshape(length, D)
    inner_sum = word_rows + low_back(matmul_high(mixed, outproj))
    spread = low(layer_norm(inner_sum, gain_b, shift_b))
    before = low_back(matmul_high(spread, up_weight) + up_bias)
    active = low(gelu_exact(before))
    return inner_sum + low_back(matmul_high(active, down_weight) + down_bias)

def reference(chars, char_counts, buckets, assign, segments, char_gain, char_shift, char_inproj, char_outproj, char_gain_mid, char_shift_mid, char_up, char_up_bias, char_down, char_down_bias, pool_query, char_proj, char_proj_bias, word_gain, word_shift, word_inproj, word_outproj, word_gain_mid, word_shift_mid, word_up, word_up_bias, word_down, word_down_bias, out_grad):
    char_params = tuple((item.astype(jnp.float32) for item in (char_gain, char_shift, char_inproj, char_outproj, char_gain_mid, char_shift_mid, char_up, char_up_bias, char_down, char_down_bias, pool_query, char_proj, char_proj_bias)))
    word_params = tuple((item.astype(jnp.float32) for item in (word_gain, word_shift, word_inproj, word_outproj, word_gain_mid, word_shift_mid, word_up, word_up_bias, word_down, word_down_bias)))
    char_data = chars.astype(jnp.float32)
    bucket_rows = buckets[:, :, 0]
    onehot = bucket_rows[:, :, None] == jnp.arange(N_WIDE, dtype=jnp.int32)[None, None, :]
    target = lax.optimization_barrier(jnp.sum(jnp.where(onehot, assign[None, None, :], 0), -1)).astype(jnp.int32)
    rank = lax.optimization_barrier(jnp.sum(jnp.where(onehot, jnp.cumsum(onehot.astype(jnp.int32), 1) - 1, 0), -1)).astype(jnp.int32)
    seq_index = jnp.arange(SEQS, dtype=jnp.int32)[:, None]
    device = seq_index // N_WIDE * N_WIDE + target
    flat_index = ((device * N_WIDE + seq_index % N_WIDE) * MOST + rank).astype(jnp.int32)

    def forward(char_set, word_set, char_input):

        def char_device(block_pair):
            return char_unit(char_set, block_pair[0], block_pair[1])
        vectors = lax.map(jax.checkpoint(char_device), (char_input.reshape(SEQS, N_WIDE * MOST, NCHAR, CW), char_counts.reshape(SEQS, N_WIDE * MOST)))
        word_in = vectors.reshape(SEQS * N_WIDE * MOST, D)[flat_index]

        def word_seq(block_pair):
            return word_unit(word_set, block_pair[0], block_pair[1])
        return lax.map(jax.checkpoint(word_seq), (word_in, segments))
    outputs, pullback = jax.vjp(forward, char_params, word_params, char_data)
    char_grads, word_grads, input_grad = pullback(out_grad.astype(jnp.float32))
    return (outputs, input_grad, char_grads[0], char_grads[1], char_grads[2], char_grads[3], char_grads[4], char_grads[5], char_grads[6], char_grads[7], char_grads[8], char_grads[9], char_grads[10], char_grads[11], char_grads[12], word_grads[0], word_grads[1], word_grads[2], word_grads[3], word_grads[4], word_grads[5], word_grads[6], word_grads[7], word_grads[8], word_grads[9])
```

```python
import functools

import jax
import jax.numpy as jnp
from jax import lax
from jax.experimental import pallas as pl
from jax.experimental.pallas import tpu as pltpu
from jax.sharding import PartitionSpec as P

HEADS = 8
HD = 64
CHEADS = 4
CHD = 64


def split_up(shard, dim, size):
    before, after = (shard.shape[:dim], shard.shape[dim + 1 :])
    return jnp.moveaxis(shard.reshape(*before, size, -1, *after), dim, 0)


def sum_at_owner(shard, axis, dim):
    parts = split_up(shard, dim, lax.axis_size(axis))
    arrived = lax.all_to_all(parts, axis, split_axis=0, concat_axis=0, tiled=True)
    return arrived.astype(jnp.float32).sum(axis=0)


def sent_together(arrays, axis, dim, along):
    columns = [a.reshape(*a.shape[:along], -1) for a in arrays]
    both = jnp.concatenate(columns, axis=along)
    filled, at, outs = (sum_at_owner(both, axis, dim), 0, [])
    for a, column in zip(arrays, columns):
        slab = filled[..., at : at + column.shape[along]]
        outs.append(slab.reshape(*slab.shape[:along], *a.shape[along:]))
        at += column.shape[along]
    return tuple(outs)


def dense(left, right):
    return jnp.dot(left, right, preferred_element_type=jnp.float32)


def dense_left(left, right):
    return lax.dot_general(
        left, right, (((0,), (0,)), ((), ())), preferred_element_type=jnp.float32
    )


def dense_right(left, right):
    return lax.dot_general(
        left, right, (((1,), (1,)), ((), ())), preferred_element_type=jnp.float32
    )


def rounded(value):
    return lax.optimization_barrier(value.astype(jnp.bfloat16)).astype(jnp.float32)


def gelu_exact(value):
    return 0.5 * value * (1.0 + lax.erf(value * ROOT_HALF))


def gelu_slope(value):
    return (
        0.5 * (1.0 + lax.erf(value * ROOT_HALF))
        + value * jnp.exp(-0.5 * value * value) * INV_ROOT_TWO_PI
    )


def softmax_rows(scores):
    row_max = jnp.max(scores, -1, keepdims=True)
    exponent = jnp.exp(scores - row_max)
    return exponent / jnp.sum(exponent, -1, keepdims=True)


def norm_forward(values, gain, shift):
    center = values - jnp.mean(values, -1, keepdims=True)
    inv_scale = lax.rsqrt(jnp.mean(center * center, -1, keepdims=True) + EPS)
    normal = center * inv_scale
    return (normal * gain.astype(jnp.float32) + shift.astype(jnp.float32), normal, inv_scale)


def norm_backward(upstream, normal, inv_scale, gain):
    weighted = upstream * gain.astype(jnp.float32)
    inner = (
        weighted
        - jnp.mean(weighted, -1, keepdims=True)
        - normal * jnp.mean(weighted * normal, -1, keepdims=True)
    )
    return (inv_scale * inner, jnp.sum(upstream * normal, 0), jnp.sum(upstream, 0))


EPS = 1e-05
NEG = -1e30
ROOT_HALF = 0.7071067811865476
INV_ROOT_TWO_PI = 0.3989422804014327
CHD = 64
GROUP = 128
F32 = jnp.float32
BF = jnp.bfloat16


def nn(a, b):
    return lax.dot_general(a, b, (((1,), (0,)), ((), ())), preferred_element_type=F32)


def nt(a, b):
    return lax.dot_general(a, b, (((1,), (1,)), ((), ())), preferred_element_type=F32)


def tn(a, b):
    return lax.dot_general(a, b, (((0,), (0,)), ((), ())), preferred_element_type=F32)


def normal_of(x):
    c = x - jnp.mean(x, -1, keepdims=True)
    r = lax.rsqrt(jnp.mean(c * c, -1, keepdims=True) + EPS)
    return c * r, r


def norm_back(d, n, r, g):
    dg = d * g
    return r * (dg - jnp.mean(dg, -1, keepdims=True) - n * jnp.mean(dg * n, -1, keepdims=True))


def two_heads(t):
    left = lax.broadcasted_iota(jnp.int32, t.shape, 1) < CHD
    zero = jnp.zeros_like(t)
    return jnp.concatenate([jnp.where(left, t, zero), jnp.where(left, zero, t)], 0)


def pool_weights(h2, query, counts, chars_per):
    rows = h2.shape[0]
    words = rows // chars_per
    e = jnp.sum(h2 * query, -1, keepdims=True) * (h2.shape[1] ** -0.5)
    e = e.reshape(words, chars_per, 1)
    place = lax.broadcasted_iota(jnp.int32, (words, chars_per, 1), 1)
    e = jnp.where(place < counts.reshape(words, 1, 1), e, NEG)
    top = jnp.max(e, 1, keepdims=True)
    ex = jnp.exp(e - top)
    return ex / jnp.sum(ex, 1, keepdims=True)


def char_forward(chars_per, c_ref, vb_ref, cnt_ref, win, wout, wup, wdn, wpj, ga, sa, gb, sb, ub, db, qv, pb,
                 x_ref, pooled_ref, qkv_ref, p_ref, o_ref, h1_ref, h2_ref, m_ref, s_ref):
    rows, width = c_ref.shape
    x = c_ref[...].astype(F32)
    n, _ = normal_of(x)
    a = (n * ga[...] + sa[...]).astype(BF)
    qkv = nn(a, win[...])
    qkv_ref[:, :width] = (qkv[:, :width] * CHD ** -0.5).astype(BF)
    qkv_ref[:, width:] = qkv[:, width:].astype(BF)
    ri = lax.broadcasted_iota(jnp.int32, (GROUP, GROUP), 0) // chars_per
    ci = lax.broadcasted_iota(jnp.int32, (GROUP, GROUP), 1) // chars_per
    same = ri == ci
    for g in range(rows // GROUP):
        at = slice(g * GROUP, (g + 1) * GROUP)
        bias = jnp.where(same, jnp.broadcast_to(vb_ref[g:g + 1, :], (GROUP, GROUP)), NEG)
        for p in range(width // GROUP):
            lanes = slice(p * GROUP, (p + 1) * GROUP)
            q = qkv_ref[at, p * GROUP:(p + 1) * GROUP]
            k = qkv_ref[at, width + p * GROUP:width + (p + 1) * GROUP]
            v = qkv_ref[at, 2 * width + p * GROUP:2 * width + (p + 1) * GROUP]
            s = nt(q, two_heads(k))
            parts = []
            for h in range(2):
                sh = s[:, h * GROUP:(h + 1) * GROUP] + bias
                ex = jnp.exp(sh - jnp.max(sh, -1, keepdims=True))
                parts.append((ex * (1.0 / jnp.sum(ex, -1, keepdims=True))).astype(BF))
            soft = jnp.concatenate(parts, 1)
            p_ref[at, p * 2 * GROUP:(p + 1) * 2 * GROUP] = soft
            o_ref[at, lanes] = nn(soft, two_heads(v)).astype(BF)
    chunk = min(rows, 256)
    for t in range(rows // chunk):
        at = slice(t * chunk, (t + 1) * chunk)
        h1 = c_ref[at, :].astype(F32) + nn(o_ref[at, :], wout[...])
        h1_ref[at, :] = h1
        n, _ = normal_of(h1)
        u = (n * gb[...] + sb[...]).astype(BF)
        z = nn(u, wup[...]) + ub[...]
        cdf = 0.5 * (1.0 + lax.erf(z * ROOT_HALF))
        m = (z * cdf).astype(BF)
        m_ref[at, :] = m
        s_ref[at, :] = (cdf + z * jnp.exp(-0.5 * z * z) * INV_ROOT_TWO_PI).astype(BF)
        h2 = h1 + (nn(m, wdn[...]) + db[...])
        h2_ref[at, :] = h2
        words = chunk // chars_per
        wat = slice(t * words, (t + 1) * words)
        om = pool_weights(h2, qv[...], cnt_ref[wat, :], chars_per)
        pooled = jnp.sum(om * h2.reshape(words, chars_per, width), 1).astype(BF)
        pooled_ref[wat, :] = pooled
    x_ref[...] = (nn(pooled_ref[...], wpj[...]) + pb[...]).astype(BF)


def char_backward(chars_per, gx_ref, c_ref, cnt_ref, qkv_ref, p_ref, o_ref, h1_ref, h2_ref, m_ref, s_ref,
                  pooled_all, gx_all, win, wout, wup, wdn, wpj, ga, sa, gb, sb, qv,
                  gc_ref, dga, dsa, dwin, dwout, dgb, dsb, dwup, dub, dwdn, ddb, dqv, dwpj, dpb, gq_ref, gh1_ref, gm_ref, gz_ref):
    rows, width = c_ref.shape
    words = rows // chars_per
    accs = (dga, dsa, dwin, dwout, dgb, dsb, dwup, dub, dwdn, ddb, dqv)

    @pl.when(pl.program_id(0) == 0)
    def _():
        for acc in accs:
            acc[...] = jnp.zeros_like(acc)
        dwpj[...] = tn(pooled_all[...], gx_all[...])
        dpb[...] = jnp.sum(gx_all[...].astype(F32), 0, keepdims=True)

    gp = nt(gx_ref[...], wpj[...]).astype(BF).astype(F32)
    factor = width ** -0.5
    chunk = min(rows, 256)
    cw = chunk // chars_per
    for t in range(rows // chunk):
        at = slice(t * chunk, (t + 1) * chunk)
        wat = slice(t * cw, (t + 1) * cw)
        h2 = h2_ref[at, :]
        om = pool_weights(h2, qv[...], cnt_ref[wat, :], chars_per)
        gpb = jnp.broadcast_to(gp[wat, :].reshape(cw, 1, width), (cw, chars_per, width)).reshape(chunk, width)
        w = jnp.sum(h2 * gpb, -1, keepdims=True).reshape(cw, chars_per, 1)
        de = om * (w - jnp.sum(om * w, 1, keepdims=True))
        de = de.reshape(chunk, 1) * factor
        gh2 = om.reshape(chunk, 1) * gpb + de * qv[...]
        dqv[...] += jnp.sum(de * h2, 0, keepdims=True)
        gy = gh2.astype(BF)
        ddb[...] += jnp.sum(gy.astype(F32), 0, keepdims=True)
        gm_ref[at, :] = gy
        gz = (nt(gy, wdn[...]) * s_ref[at, :].astype(F32)).astype(BF)
        gz_ref[at, :] = gz
        dub[...] += jnp.sum(gz.astype(F32), 0, keepdims=True)
        du = nt(gz, wup[...])
        n, r = normal_of(h1_ref[at, :])
        dgb[...] += jnp.sum(du * n, 0, keepdims=True)
        dsb[...] += jnp.sum(du, 0, keepdims=True)
        gh1_ref[at, :] = gh2 + norm_back(du, n, r, gb[...])
        o_u = (n * gb[...] + sb[...]).astype(BF)
        dwup[...] += tn(o_u, gz)
    dwdn[...] += tn(gm_ref[...], m_ref[...])
    gh1 = gh1_ref[...]
    g1 = gh1.astype(BF)
    dwout[...] += tn(o_ref[...], g1)
    gm_ref[...] = nt(g1, wout[...]).astype(BF)
    for g in range(rows // GROUP):
        at = slice(g * GROUP, (g + 1) * GROUP)
        for p in range(width // GROUP):
            q = qkv_ref[at, p * GROUP:(p + 1) * GROUP]
            k = qkv_ref[at, width + p * GROUP:width + (p + 1) * GROUP]
            v = qkv_ref[at, 2 * width + p * GROUP:2 * width + (p + 1) * GROUP]
            soft = p_ref[at, p * 2 * GROUP:(p + 1) * 2 * GROUP]
            gm = gm_ref[at, p * GROUP:(p + 1) * GROUP]
            dp = nt(gm, two_heads(v))
            parts = []
            for h in range(2):
                ph = soft[:, h * GROUP:(h + 1) * GROUP].astype(F32)
                dh = dp[:, h * GROUP:(h + 1) * GROUP]
                parts.append((ph * (dh - jnp.sum(dh * ph, -1, keepdims=True))).astype(BF))
            gs = jnp.concatenate(parts, 1)
            left = lax.broadcasted_iota(jnp.int32, (GROUP, GROUP), 1) < CHD
            gv = tn(soft, gm)
            gk = tn(gs, q)
            gq = nn(gs, two_heads(k)) * CHD ** -0.5
            gq_ref[at, p * GROUP:(p + 1) * GROUP] = gq.astype(BF)
            gq_ref[at, width + p * GROUP:width + (p + 1) * GROUP] = jnp.where(left, gk[:GROUP], gk[GROUP:]).astype(BF)
            gq_ref[at, 2 * width + p * GROUP:2 * width + (p + 1) * GROUP] = jnp.where(left, gv[:GROUP], gv[GROUP:]).astype(BF)
    for t in range(rows // chunk):
        at = slice(t * chunk, (t + 1) * chunk)
        n, r = normal_of(c_ref[at, :].astype(F32))
        a = (n * ga[...] + sa[...]).astype(BF)
        gqkv = gq_ref[at, :]
        dwin[...] += tn(a, gqkv)
        da = nt(gqkv, win[...])
        dga[...] += jnp.sum(da * n, 0, keepdims=True)
        dsa[...] += jnp.sum(da, 0, keepdims=True)
        gc_ref[at, :] = gh1_ref[at, :] + norm_back(da, n, r, ga[...])


def full(shape):
    return pl.BlockSpec(shape, lambda i: (0,) * len(shape))


def by_row(rows, width):
    return pl.BlockSpec((rows, width), lambda i: (i, 0))


def run_forward(chars, vb, cnt, weights, chars_per, rows):
    total, width = chars.shape
    win, wout, wup, wdn, wpj, ga, sa, gb, sb, ub, db, qv, pb = weights
    words, cw = total // chars_per, rows // chars_per
    ff, out = wup.shape[1], wpj.shape[1]
    outs = [((words, out), BF, cw), ((words, width), BF, cw), ((total, 3 * width), BF, rows), ((total, 2 * width), BF, rows),
            ((total, width), BF, rows), ((total, width), F32, rows), ((total, width), F32, rows),
            ((total, ff), BF, rows), ((total, ff), BF, rows)]
    return pl.pallas_call(
        functools.partial(char_forward, chars_per),
        grid=(total // rows,),
        in_specs=[by_row(rows, width), by_row(rows // GROUP, GROUP), by_row(cw, 1)] + [full(w.shape) for w in weights],
        out_specs=[by_row(b, s[1]) for s, _, b in outs],
        out_shape=[jax.ShapeDtypeStruct(s, d) for s, d, _ in outs],
        compiler_params=pltpu.CompilerParams(vmem_limit_bytes=60 << 20),
    )(chars, vb, cnt, *weights)


def run_backward(gx, chars, cnt, saved, weights, chars_per, rows):
    total, width = chars.shape
    win, wout, wup, wdn, wpj, ga, sa, gb, sb, ub, db, qv, pb = weights
    pooled, qkv, soft, mixed, h1, h2, m, s = saved
    words, cw = total // chars_per, rows // chars_per
    ff, out = wup.shape[1], wpj.shape[1]
    ws = (win, wout, wup, wdn, wpj, ga, sa, gb, sb, qv)
    row = [((total, width), F32)]
    accs = [(1, width), (1, width), (width, 3 * width), (width, width), (1, width), (1, width), (width, ff), (1, ff),
            (width, ff), (1, width), (1, width), (width, out), (1, out)]
    return pl.pallas_call(
        functools.partial(char_backward, chars_per),
        grid=(total // rows,),
        in_specs=[by_row(cw, out), by_row(rows, width), by_row(cw, 1), by_row(rows, 3 * width), by_row(rows, 2 * width),
                  by_row(rows, width), by_row(rows, width), by_row(rows, width), by_row(rows, ff), by_row(rows, ff),
                  full(pooled.shape), full(gx.shape)] + [full(w.shape) for w in ws],
        out_specs=[by_row(rows, width)] + [full(a) for a in accs],
        out_shape=[jax.ShapeDtypeStruct((total, width), F32)] + [jax.ShapeDtypeStruct(a, F32) for a in accs],
        scratch_shapes=[pltpu.VMEM((rows, 3 * width), BF), pltpu.VMEM((rows, width), F32), pltpu.VMEM((rows, width), BF),
                        pltpu.VMEM((rows, ff), BF)],
        compiler_params=pltpu.CompilerParams(vmem_limit_bytes=60 << 20),
    )(gx, chars, cnt, qkv, soft, mixed, h1, h2, m, s, pooled, gx, *ws)


def word_forward(params, word_in, segment_row):
    (
        gain_a,
        shift_a,
        inproj,
        outproj,
        gain_b,
        shift_b,
        up_weight,
        up_bias,
        down_weight,
        down_bias,
    ) = params
    length, feature_width = word_in.shape
    input_rows = word_in.astype(jnp.float32)
    normed, normal_a, scale_a = norm_forward(input_rows, gain_a, shift_a)
    normed_low = normed.astype(jnp.bfloat16)
    triple = dense(normed_low, inproj).astype(jnp.bfloat16).reshape(length, 3, HEADS, HD)
    query_rows = triple[:, 0]
    key_rows = triple[:, 1]
    value_rows = triple[:, 2]
    row_place = lax.broadcasted_iota(jnp.int32, (length, length), 0)
    col_place = lax.broadcasted_iota(jnp.int32, (length, length), 1)
    allowed = (segment_row[:, None] == segment_row[None, :]) & (col_place <= row_place)
    scores = jnp.einsum(
        "ihd,jhd->hij", query_rows, key_rows, preferred_element_type=jnp.float32
    ) * HD ** (-0.5)
    scores = jnp.where(allowed[None], scores, NEG)
    row_max = jnp.max(scores, -1, keepdims=True)
    exponent = jnp.exp(scores - row_max)
    total = jnp.sum(exponent, -1, keepdims=True)
    log_total = row_max + jnp.log(total)
    soft_low = (exponent / total).astype(jnp.bfloat16)
    mixed = (
        jnp.einsum("hij,jhd->ihd", soft_low, value_rows, preferred_element_type=jnp.float32)
        .astype(jnp.bfloat16)
        .reshape(length, feature_width)
    )
    inner_sum = input_rows + dense(mixed, outproj)
    spread, normal_b, scale_b = norm_forward(inner_sum, gain_b, shift_b)
    spread_low = spread.astype(jnp.bfloat16)
    before = dense(spread_low, up_weight) + up_bias.astype(jnp.float32)
    active = gelu_exact(before).astype(jnp.bfloat16)
    result = inner_sum + dense(active, down_weight) + down_bias.astype(jnp.float32)
    kept = (
        normed_low,
        normal_a,
        scale_a,
        query_rows,
        key_rows,
        value_rows,
        allowed,
        log_total,
        mixed,
        normal_b,
        scale_b,
        spread_low,
        before,
        active,
    )
    return (result, kept)


def word_back(params, kept, upstream):
    (
        gain_a,
        shift_a,
        inproj,
        outproj,
        gain_b,
        shift_b,
        up_weight,
        up_bias,
        down_weight,
        down_bias,
    ) = params
    (
        normed_low,
        normal_a,
        scale_a,
        query_rows,
        key_rows,
        value_rows,
        allowed,
        log_total,
        mixed,
        normal_b,
        scale_b,
        spread_low,
        before,
        active,
    ) = kept
    length, feature_width = upstream.shape
    outer_low = upstream.astype(jnp.bfloat16)
    down_grad = dense_left(active, outer_low)
    down_bias_grad = jnp.sum(outer_low.astype(jnp.float32), 0)
    before_low = (dense_right(outer_low, down_weight) * gelu_slope(before)).astype(jnp.bfloat16)
    up_grad = dense_left(spread_low, before_low)
    up_bias_grad = jnp.sum(before_low.astype(jnp.float32), 0)
    inner_part, gain_b_grad, shift_b_grad = norm_backward(
        dense_right(before_low, up_weight), normal_b, scale_b, gain_b
    )
    inner_grad = upstream + inner_part
    inner_low = inner_grad.astype(jnp.bfloat16)
    outproj_grad = dense_left(mixed, inner_low)
    mixed_grad = dense_right(inner_low, outproj).astype(jnp.bfloat16).reshape(length, HEADS, HD)
    scores = jnp.einsum(
        "ihd,jhd->hij", query_rows, key_rows, preferred_element_type=jnp.float32
    ) * HD ** (-0.5)
    soft_weights = jnp.exp(jnp.where(allowed[None], scores, NEG) - log_total)
    soft_grad = jnp.einsum(
        "ihd,jhd->hij", mixed_grad, value_rows, preferred_element_type=jnp.float32
    )
    value_grad = jnp.einsum(
        "hij,ihd->jhd",
        soft_weights.astype(jnp.bfloat16),
        mixed_grad,
        preferred_element_type=jnp.float32,
    )
    score_grad = (
        soft_weights * (soft_grad - jnp.sum(soft_grad * soft_weights, -1, keepdims=True))
    ).astype(jnp.bfloat16)
    query_part = jnp.einsum(
        "hij,jhd->ihd", score_grad, key_rows, preferred_element_type=jnp.float32
    ) * HD ** (-0.5)
    key_part = jnp.einsum(
        "hij,ihd->jhd", score_grad, query_rows, preferred_element_type=jnp.float32
    ) * HD ** (-0.5)
    triple_grad = (
        jnp.stack((query_part, key_part, value_grad), 1)
        .reshape(length, 3 * feature_width)
        .astype(jnp.bfloat16)
    )
    inproj_grad = dense_left(normed_low, triple_grad)
    input_part, gain_a_grad, shift_a_grad = norm_backward(
        dense_right(triple_grad, inproj), normal_a, scale_a, gain_a
    )
    return (
        inner_grad + input_part,
        (
            gain_a_grad,
            shift_a_grad,
            inproj_grad,
            outproj_grad,
            gain_b_grad,
            shift_b_grad,
            up_grad,
            up_bias_grad,
            down_grad,
            down_bias_grad,
        ),
    )


def shards(
    chars,
    char_counts,
    buckets,
    assign,
    segments,
    char_gain,
    char_shift,
    char_inproj,
    char_outproj,
    char_gain_mid,
    char_shift_mid,
    char_up,
    char_up_bias,
    char_down,
    char_down_bias,
    pool_query,
    char_proj,
    char_proj_bias,
    word_gain,
    word_shift,
    word_inproj,
    word_outproj,
    word_gain_mid,
    word_shift_mid,
    word_up,
    word_up_bias,
    word_down,
    word_down_bias,
    out_grad,
):
    owners = lax.axis_size("wide")
    slot_cap = chars.shape[2]
    char_slots = chars.shape[3]
    feature_width = chars.shape[4]
    slot_total = chars.shape[1] * slot_cap
    char_params = (
        lax.all_gather(char_gain, "wide", axis=0, tiled=True),
        lax.all_gather(char_shift, "wide", axis=0, tiled=True),
        lax.all_gather(char_inproj, "wide", axis=0, tiled=True),
        lax.all_gather(char_outproj, "wide", axis=0, tiled=True),
        lax.all_gather(char_gain_mid, "wide", axis=0, tiled=True),
        lax.all_gather(char_shift_mid, "wide", axis=0, tiled=True),
        lax.all_gather(char_up, "wide", axis=0, tiled=True),
        lax.all_gather(char_up_bias, "wide", axis=0, tiled=True),
        lax.all_gather(char_down, "wide", axis=0, tiled=True),
        lax.all_gather(char_down_bias, "wide", axis=0, tiled=True),
        lax.all_gather(pool_query, "wide", axis=0, tiled=True),
        lax.all_gather(char_proj, "wide", axis=0, tiled=True),
        lax.all_gather(char_proj_bias, "wide", axis=0, tiled=True),
    )
    word_params = (
        lax.all_gather(word_gain, "wide", axis=0, tiled=True),
        lax.all_gather(word_shift, "wide", axis=0, tiled=True),
        lax.all_gather(word_inproj, "wide", axis=0, tiled=True),
        lax.all_gather(word_outproj, "wide", axis=0, tiled=True),
        lax.all_gather(word_gain_mid, "wide", axis=0, tiled=True),
        lax.all_gather(word_shift_mid, "wide", axis=0, tiled=True),
        lax.all_gather(word_up, "wide", axis=0, tiled=True),
        lax.all_gather(word_up_bias, "wide", axis=0, tiled=True),
        lax.all_gather(word_down, "wide", axis=0, tiled=True),
        lax.all_gather(word_down_bias, "wide", axis=0, tiled=True),
    )
    rows = chars.reshape(-1, feature_width)
    counts = char_counts.reshape(slot_total, 1)
    places = lax.broadcasted_iota(jnp.int32, (slot_total, char_slots), 1)
    key_bias = jnp.where(places < counts, 0.0, NEG).reshape(-1, GROUP)
    as_row = lambda v: v.astype(F32)[None]
    weights = (
        char_params[2],
        char_params[3],
        char_params[6],
        char_params[8],
        char_params[11],
        *(as_row(char_params[i]) for i in (0, 1, 4, 5, 7, 9, 10, 12)),
    )
    outgoing, *saved = run_forward(rows, key_bias, counts, weights, char_slots, 1024)
    outgoing = outgoing.reshape(owners, slot_cap, outgoing.shape[-1])
    bucket_row = buckets[0, :, 0]
    length = bucket_row.shape[0]
    onehot = bucket_row[:, None] == lax.broadcasted_iota(jnp.int32, (length, owners), 1)
    target = jnp.sum(jnp.where(onehot, assign[None, :], 0), 1)
    rank = jnp.sum(jnp.where(onehot, jnp.cumsum(onehot.astype(jnp.int32), 0) - 1, 0), 1)
    slot_index = target * slot_cap + rank
    arrived = lax.all_to_all(outgoing, "wide", split_axis=0, concat_axis=0, tiled=True)
    word_in = arrived.reshape(owners * slot_cap, arrived.shape[-1])[slot_index]
    result, kept = word_forward(word_params, word_in, segments[0])
    input_grad, word_grads = word_back(word_params, kept, out_grad[0].astype(jnp.float32))
    input_low = input_grad.astype(jnp.bfloat16)
    word_parts = (
        lax.psum_scatter(word_grads[0], "wide", scatter_dimension=0, tiled=True),
        lax.psum_scatter(word_grads[1], "wide", scatter_dimension=0, tiled=True),
        lax.psum_scatter(word_grads[2], "wide", scatter_dimension=0, tiled=True),
        lax.psum_scatter(word_grads[3], "wide", scatter_dimension=0, tiled=True),
        lax.psum_scatter(word_grads[4], "wide", scatter_dimension=0, tiled=True),
        lax.psum_scatter(word_grads[5], "wide", scatter_dimension=0, tiled=True),
        lax.psum_scatter(word_grads[6], "wide", scatter_dimension=0, tiled=True),
        lax.psum_scatter(word_grads[7], "wide", scatter_dimension=0, tiled=True),
        lax.psum_scatter(word_grads[8], "wide", scatter_dimension=0, tiled=True),
        lax.psum_scatter(word_grads[9], "wide", scatter_dimension=0, tiled=True),
    )
    word_total = (
        lax.psum(word_parts[0].astype(jnp.bfloat16), "dp").astype(jnp.float32),
        lax.psum(word_parts[1].astype(jnp.bfloat16), "dp").astype(jnp.float32),
        lax.psum(word_parts[2].astype(jnp.bfloat16), "dp").astype(jnp.float32),
        lax.psum(word_parts[3].astype(jnp.bfloat16), "dp").astype(jnp.float32),
        lax.psum(word_parts[4].astype(jnp.bfloat16), "dp").astype(jnp.float32),
        lax.psum(word_parts[5].astype(jnp.bfloat16), "dp").astype(jnp.float32),
        lax.psum(word_parts[6].astype(jnp.bfloat16), "dp").astype(jnp.float32),
        lax.psum(word_parts[7].astype(jnp.bfloat16), "dp").astype(jnp.float32),
        lax.psum(word_parts[8].astype(jnp.bfloat16), "dp").astype(jnp.float32),
        lax.psum(word_parts[9].astype(jnp.bfloat16), "dp").astype(jnp.float32),
    )
    back_rows = (
        jnp.zeros((owners * slot_cap, input_low.shape[1]), jnp.bfloat16)
        .at[slot_index]
        .set(input_low)
    )
    returned = lax.all_to_all(
        back_rows.reshape(owners, slot_cap, input_low.shape[1]),
        "wide",
        split_axis=0,
        concat_axis=0,
        tiled=True,
    )
    incoming = returned.reshape(slot_total, returned.shape[-1])
    char_grads, *pieces = run_backward(incoming, rows, counts, saved, weights, char_slots, 1024)
    dga, dsa, dwin, dwout, dgb, dsb, dwup, dub, dwdn, ddb, dqv, dwpj, dpb = pieces
    totals = (dga[0], dsa[0], dwin, dwout, dgb[0], dsb[0], dwup, dub[0], dwdn.T, ddb[0], dqv[0], dwpj, dpb[0])
    char_parts = (
        sum_at_owner(totals[0].astype(jnp.bfloat16), "wide", 0),
        *sent_together(
            (
                totals[1].astype(jnp.bfloat16),
                totals[2].astype(jnp.bfloat16),
                totals[3].astype(jnp.bfloat16),
                totals[4].astype(jnp.bfloat16),
                totals[5].astype(jnp.bfloat16),
                totals[6].astype(jnp.bfloat16),
            ),
            "wide",
            0,
            1,
        ),
        *sent_together(
            (totals[7].astype(jnp.bfloat16), totals[8].astype(jnp.bfloat16)), "wide", 0, 1
        ),
        sum_at_owner(totals[9].astype(jnp.bfloat16), "wide", 0),
        *sent_together(
            (totals[10].astype(jnp.bfloat16), (totals[11]).astype(jnp.bfloat16)),
            "wide",
            0,
            1,
        ),
        sum_at_owner((totals[12]).astype(jnp.bfloat16), "wide", 0),
    )
    char_total = (
        lax.psum(char_parts[0].astype(jnp.bfloat16), "dp").astype(jnp.float32),
        lax.psum(char_parts[1].astype(jnp.bfloat16), "dp").astype(jnp.float32),
        lax.psum(char_parts[2].astype(jnp.bfloat16), "dp").astype(jnp.float32),
        lax.psum(char_parts[3].astype(jnp.bfloat16), "dp").astype(jnp.float32),
        lax.psum(char_parts[4].astype(jnp.bfloat16), "dp").astype(jnp.float32),
        lax.psum(char_parts[5].astype(jnp.bfloat16), "dp").astype(jnp.float32),
        lax.psum(char_parts[6].astype(jnp.bfloat16), "dp").astype(jnp.float32),
        lax.psum(char_parts[7].astype(jnp.bfloat16), "dp").astype(jnp.float32),
        lax.psum(char_parts[8].astype(jnp.bfloat16), "dp").astype(jnp.float32),
        lax.psum(char_parts[9].astype(jnp.bfloat16), "dp").astype(jnp.float32),
        lax.psum(char_parts[10].astype(jnp.bfloat16), "dp").astype(jnp.float32),
        lax.psum(char_parts[11].astype(jnp.bfloat16), "dp").astype(jnp.float32),
        lax.psum(char_parts[12].astype(jnp.bfloat16), "dp").astype(jnp.float32),
    )
    return (
        result[None],
        char_grads.reshape(chars.shape),
        char_total[0],
        char_total[1],
        char_total[2],
        char_total[3],
        char_total[4],
        char_total[5],
        char_total[6],
        char_total[7],
        char_total[8],
        char_total[9],
        char_total[10],
        char_total[11],
        char_total[12],
        word_total[0],
        word_total[1],
        word_total[2],
        word_total[3],
        word_total[4],
        word_total[5],
        word_total[6],
        word_total[7],
        word_total[8],
        word_total[9],
    )


def solution(mesh):
    placed = (
        P(("dp", "wide"), None, None, None, None),
        P(("dp", "wide"), None, None),
        P(("dp", "wide"), None, None),
        P(),
        P(("dp", "wide"), None),
        P("wide"),
        P("wide"),
        P("wide", None),
        P("wide", None),
        P("wide"),
        P("wide"),
        P("wide", None),
        P("wide"),
        P("wide", None),
        P("wide"),
        P("wide"),
        P("wide", None),
        P("wide"),
        P("wide"),
        P("wide"),
        P("wide", None),
        P("wide", None),
        P("wide"),
        P("wide"),
        P("wide", None),
        P("wide"),
        P("wide", None),
        P("wide"),
        P(("dp", "wide"), None, None),
    )
    return jax.shard_map(
        shards,
        mesh=mesh,
        in_specs=placed,
        out_specs=(
            P(("dp", "wide"), None, None),
            P(("dp", "wide"), None, None, None, None),
            P("wide"),
            P("wide"),
            P("wide", None),
            P("wide", None),
            P("wide"),
            P("wide"),
            P("wide", None),
            P("wide"),
            P("wide", None),
            P("wide"),
            P("wide"),
            P("wide", None),
            P("wide"),
            P("wide"),
            P("wide"),
            P("wide", None),
            P("wide", None),
            P("wide"),
            P("wide"),
            P("wide", None),
            P("wide"),
            P("wide", None),
            P("wide"),
        ),
        check_vma=False,
    )
```

```python
import functools

import jax
import jax.numpy as jnp
from jax import lax
from jax.experimental import pallas as pl
from jax.experimental.pallas import tpu as pltpu
from jax.sharding import PartitionSpec as P

EPS = 1e-05
NEG = -1e30
ROOT_HALF = 0.7071067811865476
INV_ROOT_TWO_PI = 0.3989422804014327
HD = 64
GROUP = 128
F32 = jnp.float32
BF = jnp.bfloat16
MESH = pl.DeviceIdType.MESH
VMEM_LIMIT = 60 << 20


def nn(a, b):
    return lax.dot_general(a, b, (((1,), (0,)), ((), ())), preferred_element_type=F32)


def nt(a, b):
    return lax.dot_general(a, b, (((1,), (1,)), ((), ())), preferred_element_type=F32)


def tn(a, b):
    return lax.dot_general(a, b, (((0,), (0,)), ((), ())), preferred_element_type=F32)


def column_sum(x):
    return jnp.sum(x, 0, keepdims=True)


def normal_of(x):
    c = x - jnp.mean(x, -1, keepdims=True)
    r = lax.rsqrt(jnp.mean(c * c, -1, keepdims=True) + EPS)
    return c * r, r


def norm_back(d, n, r, g):
    dg = d * g
    return r * (dg - jnp.mean(dg, -1, keepdims=True) - n * jnp.mean(dg * n, -1, keepdims=True))


def gelu_and_slope(z):
    cdf = 0.5 * (1.0 + lax.erf(z * ROOT_HALF))
    return z * cdf, cdf + z * jnp.exp(-0.5 * z * z) * INV_ROOT_TWO_PI


def softmax_low(s):
    ex = jnp.exp(s - jnp.max(s, -1, keepdims=True))
    return (ex * (1.0 / jnp.sum(ex, -1, keepdims=True))).astype(BF)


def softmax_back(soft, d):
    soft = soft.astype(F32)
    return (soft * (d - jnp.sum(d * soft, -1, keepdims=True))).astype(BF)


def two_heads(t):
    left = lax.broadcasted_iota(jnp.int32, t.shape, 1) < HD
    zero = jnp.zeros_like(t)
    return jnp.concatenate([jnp.where(left, t, zero), jnp.where(left, zero, t)], 0)


def one_of_two(t):
    half = t.shape[0] // 2
    left = lax.broadcasted_iota(jnp.int32, (half, t.shape[1]), 1) < HD
    return jnp.where(left, t[:half], t[half:])


def pool_weights(h2, query, counts, chars_per):
    rows = h2.shape[0]
    words = rows // chars_per
    e = jnp.sum(h2 * query, -1, keepdims=True) * (h2.shape[1] ** -0.5)
    e = e.reshape(words, chars_per, 1)
    place = lax.broadcasted_iota(jnp.int32, (words, chars_per, 1), 1)
    e = jnp.where(place < counts.reshape(words, 1, 1), e, NEG)
    ex = jnp.exp(e - jnp.max(e, 1, keepdims=True))
    return ex / jnp.sum(ex, 1, keepdims=True)


class Net:
    def __init__(self, n_dp, n_wide):
        self.n_dp, self.n_wide, self.n_z = n_dp, n_wide, n_wide // 2
        self.dp, self.wide = lax.axis_index("dp"), lax.axis_index("wide")
        self.z, self.core = self.wide // 2, lax.rem(self.wide, 2)
        self.sibling = (self.dp, self.wide + 1 - 2 * self.core)

    def z_peer(self, j):
        z = lax.rem(self.z + j, self.n_z)
        return z, (self.dp, 2 * z + self.core)

    def dp_peer(self, j):
        q = lax.rem(self.dp + j, self.n_dp)
        return q, (q, self.wide)

    def wide_peer(self, j):
        w = lax.rem(self.wide + j, self.n_wide)
        return w, (self.dp, w)

    def greet(self, peers):
        barrier = pltpu.get_barrier_semaphore()
        for peer in peers:
            pl.semaphore_signal(barrier, inc=1, device_id=peer, device_id_type=MESH)

    def met(self, peers):
        pl.semaphore_wait(pltpu.get_barrier_semaphore(), len(peers))


def remote(src, dst, send, recv, peer):
    return pltpu.make_async_remote_copy(src_ref=src, dst_ref=dst, send_sem=send, recv_sem=recv, device_id=peer, device_id_type=MESH)


class Reduce:
    def __init__(self, net, grads, kept, from_core, part, from_dp, from_z, done, sems):
        self.net, self.grads = net, grads
        self.kept, self.from_core, self.part = kept, from_core, part
        self.from_dp, self.from_z, self.done = from_dp, from_z, done
        self.send, self.recv = sems
        self.span = part.shape[-1]

    @staticmethod
    def scratch(n_dp, n_z, rows, width):
        span = width // n_dp
        count = 2 + 2 * n_dp + n_z
        return [
            pltpu.VMEM((n_z, rows, width), BF),
            pltpu.VMEM((n_z, rows, width), BF),
            pltpu.VMEM((n_z, rows, span), BF),
            pltpu.VMEM((n_dp - 1, n_z, rows, span), BF),
            pltpu.VMEM((n_z - 1, rows, span), BF),
            pltpu.VMEM((n_dp, rows, span), BF),
            pltpu.SemaphoreType.DMA((count,)),
            pltpu.SemaphoreType.DMA((count,)),
        ]

    def lanes(self, q):
        return pl.ds(pl.multiple_of(q * self.span, GROUP), self.span)

    def to_core(self):
        net = self.net
        return remote(self.grads.at[:, 1 - net.core], self.from_core, self.send.at[0], self.recv.at[0], net.sibling)

    def own(self):
        return pltpu.make_async_copy(self.grads.at[:, self.net.core], self.kept, self.recv.at[1])

    def to_dp(self, j):
        q, peer = self.net.dp_peer(j)
        return remote(self.kept.at[:, :, self.lanes(q)], self.from_dp.at[j - 1], self.send.at[1 + j], self.recv.at[1 + j], peer)

    def to_z(self, j):
        z, peer = self.net.z_peer(j)
        at = 1 + self.net.n_dp + j
        return remote(self.part.at[z], self.from_z.at[j - 1], self.send.at[at], self.recv.at[at], peer)

    def to_all(self, j):
        net = self.net
        _, peer = net.dp_peer(j)
        at = 1 + net.n_dp + net.n_z + j
        mine = self.done.at[net.dp]
        return remote(mine, mine, self.send.at[at], self.recv.at[at], peer)

    def start(self):
        self.to_core().start()
        self.own().start()

    def over_dp(self):
        net = self.net
        self.own().wait()
        self.to_core().wait()

        @pl.loop(0, net.n_z)
        def _(z):
            self.kept[z] = (self.kept[z].astype(F32) + self.from_core[z].astype(F32)).astype(BF)

        for j in range(1, net.n_dp):
            self.to_dp(j).start()

    def over_z(self):
        net = self.net
        for j in range(1, net.n_dp):
            self.to_dp(j).wait()

        @pl.loop(0, net.n_z)
        def _(z):
            total = self.kept[z, :, self.lanes(net.dp)].astype(F32)
            for j in range(net.n_dp - 1):
                total = total + self.from_dp[j, z].astype(F32)
            self.part[z] = total.astype(BF)

        for j in range(1, net.n_z):
            self.to_z(j).start()

    def back_over_dp(self):
        net = self.net
        for j in range(1, net.n_z):
            self.to_z(j).wait()
        total = self.part[net.z].astype(F32)
        for j in range(net.n_z - 1):
            total = total + self.from_z[j].astype(F32)
        self.done[net.dp] = total.astype(BF)
        for j in range(1, net.n_dp):
            self.to_all(j).start()

    def finish(self, outs):
        net = self.net
        for j in range(1, net.n_dp):
            self.to_all(j).wait()
        rows = self.part.shape[1]
        for ref, first, columns, side in outs:
            for k in range(side):
                for at in range(0, columns, GROUP):
                    column = first + k * columns + at
                    q, lane = column // self.span, column % self.span
                    ref[k * rows : (k + 1) * rows, at : at + GROUP] = self.done[q, :, lane : lane + GROUP].astype(F32)


class ReduceRows:
    def __init__(self, net, row, from_core, of_dp, of_z, sems):
        self.net, self.row, self.from_core, self.of_dp, self.of_z = net, row, from_core, of_dp, of_z
        self.send, self.recv = sems

    @staticmethod
    def scratch(n_dp, n_z, width):
        count = 1 + n_dp + n_z
        return [
            pltpu.VMEM((1, width), F32),
            pltpu.VMEM((1, width), F32),
            pltpu.VMEM((n_dp, 1, width), F32),
            pltpu.VMEM((n_z, 1, width), F32),
            pltpu.SemaphoreType.DMA((count,)),
            pltpu.SemaphoreType.DMA((count,)),
        ]

    def to_core(self):
        return remote(self.row, self.from_core, self.send.at[0], self.recv.at[0], self.net.sibling)

    def to_dp(self, j):
        mine = self.of_dp.at[self.net.dp]
        return remote(mine, mine, self.send.at[j], self.recv.at[j], self.net.dp_peer(j)[1])

    def to_z(self, j):
        mine = self.of_z.at[self.net.z]
        at = self.net.n_dp + j
        return remote(mine, mine, self.send.at[at], self.recv.at[at], self.net.z_peer(j)[1])

    def start(self):
        self.to_core().start()

    def over_dp(self):
        self.to_core().wait()
        self.of_dp[self.net.dp] = self.row[...] + self.from_core[...]
        for j in range(1, self.net.n_dp):
            self.to_dp(j).start()

    def over_z(self):
        net = self.net
        for j in range(1, net.n_dp):
            self.to_dp(j).wait()
        total = self.of_dp[0]
        for q in range(1, net.n_dp):
            total = total + self.of_dp[q]
        self.of_z[net.z] = total
        for j in range(1, net.n_z):
            self.to_z(j).start()

    def finish(self, outs):
        net = self.net
        for j in range(1, net.n_z):
            self.to_z(j).wait()
        total = self.of_z[0]
        for z in range(1, net.n_z):
            total = total + self.of_z[z]
        for ref, first, length in outs:
            piece = ref.shape[1]
            vector = jnp.broadcast_to(total[:, first : first + length], (8, length))
            turned = pltpu.roll(vector, lax.rem(length - net.wide * piece, length), 1)
            ref[...] = turned[:1, :piece]


class Gather:
    def __init__(self, net, shards, wholes, send, recv, near):
        self.net, self.shards, self.wholes = net, shards, wholes
        self.send, self.recv, self.near = send, recv, near

    @staticmethod
    def scratch(count, n_z):
        return [
            pltpu.SemaphoreType.DMA((count, 2 * n_z)),
            pltpu.SemaphoreType.DMA((count, 2 * n_z)),
            pltpu.SemaphoreType.DMA((count,)),
        ]

    def block(self, a, owner):
        rows = self.shards[a].shape[0]
        return self.wholes[a].at[pl.ds(pl.multiple_of(owner * rows, rows), rows)]

    def along_z(self, a, j):
        net = self.net
        return remote(self.shards[a], self.block(a, net.wide), self.send.at[a, j], self.recv.at[a, net.wide], net.z_peer(j)[1])

    def across(self, a):
        net = self.net
        return remote(self.shards[a], self.block(a, net.wide), self.send.at[a, 0], self.recv.at[a, net.wide], net.sibling)

    def relayed(self, a, j):
        net = self.net
        owner = 2 * net.z_peer(j)[0] + net.core
        here = self.block(a, owner)
        return remote(here, here, self.send.at[a, net.n_z + j], self.recv.at[a, owner], net.sibling)

    def own(self, a):
        return pltpu.make_async_copy(self.shards[a], self.block(a, self.net.wide), self.near.at[a])

    def arrival(self, a, owner):
        here = self.block(a, owner)
        return remote(here, here, self.send.at[a, 0], self.recv.at[a, owner], self.net.sibling)

    def start(self, a):
        for j in range(1, self.net.n_z):
            self.along_z(a, j).start()
        self.across(a).start()
        self.own(a).start()

    def relay(self, a):
        net = self.net
        for j in range(1, net.n_z):
            self.arrival(a, 2 * net.z_peer(j)[0] + net.core).wait_recv()
            self.relayed(a, j).start()

    def finish(self, a):
        net = self.net
        self.own(a).wait()
        self.across(a).wait_send()
        for j in range(1, net.n_z):
            self.along_z(a, j).wait_send()
            self.relayed(a, j).wait_send()
        for z in range(net.n_z):
            self.arrival(a, 2 * z + 1 - net.core).wait_recv()


class SharedGather:
    def __init__(self, net, shards, wholes, send_z, send_dp, send_core, recv_z, recv_dp, recv_core, near):
        self.net, self.shards, self.wholes = net, shards, wholes
        self.send_z, self.send_dp, self.send_core = send_z, send_dp, send_core
        self.recv_z, self.recv_dp, self.recv_core, self.near = recv_z, recv_dp, recv_core, near

    @staticmethod
    def scratch(count, n_dp, n_z):
        sem = pltpu.SemaphoreType.DMA
        return [
            sem((count, n_z)), sem((count, n_z, n_dp)), sem((count, n_z)),
            sem((count, n_z)), sem((count, n_z, n_dp)), sem((count, n_z)), sem((count,)),
        ]

    def block(self, a, owner):
        rows = self.shards[a].shape[0]
        return self.wholes[a].at[pl.ds(pl.multiple_of(owner * rows, rows), rows)]

    def piece(self, a, owner, q):
        rows = self.shards[a].shape[0]
        some = rows // self.net.n_dp
        return self.wholes[a].at[pl.ds(pl.multiple_of(owner * rows + q * some, some), some)]

    def along_z(self, a, j):
        net = self.net
        some = self.shards[a].shape[0] // net.n_dp
        mine = self.shards[a].at[pl.ds(pl.multiple_of(net.dp * some, some), some)]
        return remote(mine, self.piece(a, net.wide, net.dp), self.send_z.at[a, j], self.recv_z.at[a, net.z], net.z_peer(j)[1])

    def from_z(self, a, j):
        net = self.net
        z, peer = net.z_peer(j)
        here = self.piece(a, 2 * z + net.core, net.dp)
        return remote(here, here, self.send_z.at[a, j], self.recv_z.at[a, z], peer)

    def over_dp(self, a, j, i):
        net = self.net
        z = net.z_peer(j)[0]
        here = self.piece(a, 2 * z + net.core, net.dp)
        return remote(here, here, self.send_dp.at[a, j, i], self.recv_dp.at[a, j, net.dp], net.dp_peer(i)[1])

    def from_dp(self, a, j, i):
        net = self.net
        z = net.z_peer(j)[0]
        q, peer = net.dp_peer(i)
        here = self.piece(a, 2 * z + net.core, q)
        return remote(here, here, self.send_dp.at[a, j, i], self.recv_dp.at[a, j, q], peer)

    def across(self, a, j):
        net = self.net
        z = net.z_peer(j)[0]
        here = self.block(a, 2 * z + net.core)
        source = self.shards[a] if j == 0 else here
        return remote(source, here, self.send_core.at[a, j], self.recv_core.at[a, z], net.sibling)

    def from_core(self, a, z):
        net = self.net
        here = self.block(a, 2 * z + 1 - net.core)
        return remote(here, here, self.send_core.at[a, 0], self.recv_core.at[a, z], net.sibling)

    def own(self, a):
        return pltpu.make_async_copy(self.shards[a], self.block(a, self.net.wide), self.near.at[a])

    def start(self):
        for a in range(len(self.shards)):
            for j in range(1, self.net.n_z):
                self.along_z(a, j).start()
        for a in range(len(self.shards)):
            self.across(a, 0).start()
            self.own(a).start()

    def relay(self, a):
        net = self.net
        for j in range(1, net.n_z):
            self.from_z(a, j).wait_recv()
            for i in range(1, net.n_dp):
                self.over_dp(a, j, i).start()

    def pass_on(self, a):
        net = self.net
        for j in range(1, net.n_z):
            for i in range(1, net.n_dp):
                self.from_dp(a, j, i).wait_recv()
            self.across(a, j).start()

    def finish(self, a):
        net = self.net
        self.own(a).wait()
        for j in range(1, net.n_z):
            self.along_z(a, j).wait_send()
            for i in range(1, net.n_dp):
                self.over_dp(a, j, i).wait_send()
        for j in range(net.n_z):
            self.across(a, j).wait_send()
            self.from_core(a, j).wait_recv()


class Exchange:
    def __init__(self, net, out, inbox, send, recv, near):
        self.net, self.out, self.inbox = net, out, inbox
        self.send, self.recv, self.near = send, recv, near

    @staticmethod
    def scratch(n_wide):
        return [pltpu.SemaphoreType.DMA((n_wide,)), pltpu.SemaphoreType.DMA((n_wide,)), pltpu.SemaphoreType.DMA(())]

    def to(self, w):
        net = self.net
        return remote(self.out.at[w], self.inbox.at[net.wide], self.send.at[w], self.recv.at[net.wide], (net.dp, w))

    def arrival(self, w):
        here = self.inbox.at[w]
        return remote(here, here, self.send.at[w], self.recv.at[w], (self.net.dp, w))

    def own(self):
        me = self.net.wide
        return pltpu.make_async_copy(self.out.at[me], self.inbox.at[me], self.near)

    def send_block(self, w):
        @pl.when(w != self.net.wide)
        def _():
            self.to(w).start()

        @pl.when(w == self.net.wide)
        def _():
            self.own().start()

    def send_all(self):
        for j in range(1, self.net.n_wide):
            self.to(self.net.wide_peer(j)[0]).start()
        self.own().start()

    def finish(self):
        for j in range(1, self.net.n_wide):
            w = self.net.wide_peer(j)[0]
            self.to(w).wait_send()
            self.arrival(w).wait_recv()
        self.own().wait()


def slices_of(ref, first, lengths):
    views = []
    for length in lengths:
        views.append(ref.at[:, first : first + length])
        first += length
    return views


def char_vectors(row, width, ff, out):
    return slices_of(row, 0, [width] * 6 + [ff, out])


def word_vectors(row, width, ff):
    return slices_of(row, row.shape[1] - 5 * width - ff, [width] * 5 + [ff])


def char_back_kernel(chars_per, steps, net_sizes, *refs):
    (
        gx_ref, c_ref, cnt_ref, qkv_ref, p_ref, o_ref, h1_ref, h2_ref, m_ref, s_ref, pooled_all, gx_all,
        win, wout, wup, wdn, wpj, vec, *refs
    ) = refs
    if net_sizes:
        word_grads, word_row, *refs = refs
    gc_ref, *refs = refs
    if net_sizes:
        outs, refs = refs[:23], refs[23:]
        accs, refs = refs[:13], refs[13:]
    else:
        accs, refs = refs[:13], refs[13:]
    dga, dsa, dwin, dwout, dgb, dsb, dwup, dub, dwdn, ddb, dqv, dwpj, dpb = accs
    gh1_ref, gm_ref, u_ref, gz_ref, gq_ref, *refs = refs
    rows, width = c_ref.shape
    ga, sa, gb, sb, _, qv, _, _ = char_vectors(vec, width, wup.shape[1], wpj.shape[1])
    phase, step = pl.program_id(0), pl.program_id(1)
    now = phase * steps + step
    factor = width**-0.5
    chunk = min(rows, 256)
    cw = chunk // chars_per

    if net_sizes:
        net = Net(*net_sizes)
        ff_grads, at_grads, row, *refs = refs
        word = Reduce(net, word_grads, *refs[:6], refs[6:8])
        ff = Reduce(net, ff_grads, *refs[8:14], refs[14:16])
        att = Reduce(net, at_grads, *refs[16:22], refs[22:24])
        rowsum = ReduceRows(net, row, *refs[24:27], refs[27:29])

        @pl.when(now == 0)
        def _():
            peers = [net.sibling] + [net.dp_peer(j)[1] for j in range(1, net.n_dp)] + [net.z_peer(j)[1] for j in range(1, net.n_z)]
            net.greet(peers)
            net.met(peers)
            word.start()

        schedule = {
            steps // 4: word.over_dp,
            steps - steps // 8: word.over_z,
            steps: ff.start,
            steps + steps // 8: ff.over_dp,
            steps + steps // 4: word.back_over_dp,
            steps + 3 * steps // 8: ff.over_z,
            steps + 5 * steps // 8: ff.back_over_dp,
        }
        for when, act in schedule.items():
            pl.when(now == when)(act)

    @pl.when(now == 0)
    def _():
        for acc in accs:
            acc[...] = jnp.zeros_like(acc)
        dwpj[...] = tn(pooled_all[...], gx_all[...])
        dpb[...] = column_sum(gx_all[...].astype(F32))

    here = pl.ds(pl.multiple_of(step * rows, rows), rows)

    @pl.when(phase == 0)
    def _():
        gp = nt(gx_ref[...], wpj[...]).astype(BF).astype(F32)
        for t in range(rows // chunk):
            at = slice(t * chunk, (t + 1) * chunk)
            wat = slice(t * cw, (t + 1) * cw)
            h2 = h2_ref[at, :]
            om = pool_weights(h2, qv[...], cnt_ref[wat, :], chars_per)
            gpb = jnp.broadcast_to(gp[wat, :].reshape(cw, 1, width), (cw, chars_per, width)).reshape(chunk, width)
            w = jnp.sum(h2 * gpb, -1, keepdims=True).reshape(cw, chars_per, 1)
            de = om * (w - jnp.sum(om * w, 1, keepdims=True))
            de = de.reshape(chunk, 1) * factor
            gh2 = om.reshape(chunk, 1) * gpb + de * qv[...]
            dqv[...] += column_sum(de * h2)
            gy = gh2.astype(BF)
            ddb[...] += column_sum(gy.astype(F32))
            gm_ref[at, :] = gy
            gz = (nt(gy, wdn[...]) * s_ref[at, :].astype(F32)).astype(BF)
            gz_ref[at, :] = gz
            dub[...] += column_sum(gz.astype(F32))
            du = nt(gz, wup[...])
            n, r = normal_of(h1_ref[at, :])
            dgb[...] += column_sum(du * n)
            dsb[...] += column_sum(du)
            u_ref[at, :] = (n * gb[...] + sb[...]).astype(BF)
            gh1_ref[pl.ds(pl.multiple_of(step * rows + t * chunk, chunk), chunk), :] = gh2 + norm_back(du, n, r, gb[...])
        dwup[...] += tn(u_ref[...], gz_ref[...])
        dwdn[...] += tn(gm_ref[...], m_ref[...])

    if net_sizes:
        n_z, n_wide = net.n_z, net.n_wide

        @pl.when(now == steps - 1)
        def _():
            up, proj = dwup.shape[1], dwpj.shape[1]
            down = dwdn[...].T
            some = width // n_wide
            side = down.shape[0] // n_wide // some
            for owner in range(n_wide):
                z, core = owner // 2, owner % 2
                mine = slice(owner * some, (owner + 1) * some)
                ff_grads[z, core, :, :up] = dwup[mine, :].astype(BF)
                ff_grads[z, core, :, up : up + proj] = dwpj[mine, :].astype(BF)
                for k in range(side):
                    first = (owner * side + k) * some
                    ff_grads[z, core, :, up + proj + k * width : up + proj + (k + 1) * width] = down[first : first + some].astype(BF)

    @pl.when(phase == 1)
    def _():
        g1 = gh1_ref[here, :].astype(BF)
        dwout[...] += tn(o_ref[...], g1)
        gm_ref[...] = nt(g1, wout[...]).astype(BF)
        for g in range(rows // GROUP):
            at = slice(g * GROUP, (g + 1) * GROUP)
            for p in range(width // GROUP):
                q = qkv_ref[at, p * GROUP : (p + 1) * GROUP]
                k = qkv_ref[at, width + p * GROUP : width + (p + 1) * GROUP]
                v = qkv_ref[at, 2 * width + p * GROUP : 2 * width + (p + 1) * GROUP]
                soft = p_ref[at, p * 2 * GROUP : (p + 1) * 2 * GROUP]
                gm = gm_ref[at, p * GROUP : (p + 1) * GROUP]
                dp = nt(gm, two_heads(v))
                gs = jnp.concatenate([softmax_back(soft[:, h * GROUP : (h + 1) * GROUP], dp[:, h * GROUP : (h + 1) * GROUP]) for h in range(2)], 1)
                gq_ref[at, p * GROUP : (p + 1) * GROUP] = (nn(gs, two_heads(k)) * HD**-0.5).astype(BF)
                gq_ref[at, width + p * GROUP : width + (p + 1) * GROUP] = one_of_two(tn(gs, q)).astype(BF)
                gq_ref[at, 2 * width + p * GROUP : 2 * width + (p + 1) * GROUP] = one_of_two(tn(soft, gm)).astype(BF)
        for t in range(rows // chunk):
            at = slice(t * chunk, (t + 1) * chunk)
            n, r = normal_of(c_ref[at, :].astype(F32))
            u_ref[at, :] = (n * ga[...] + sa[...]).astype(BF)
            da = nt(gq_ref[at, :], win[...])
            dga[...] += column_sum(da * n)
            dsa[...] += column_sum(da)
            gc_ref[at, :] = gh1_ref[pl.ds(pl.multiple_of(step * rows + t * chunk, chunk), chunk), :] + norm_back(da, n, r, ga[...])
        dwin[...] += tn(u_ref[...], gq_ref[...])

    if net_sizes:

        @pl.when(now == 2 * steps - 1)
        def _():
            some = width // n_wide
            for owner in range(n_wide):
                z, core = owner // 2, owner % 2
                mine = slice(owner * some, (owner + 1) * some)
                at_grads[z, core, :, : 3 * width] = dwin[mine, :].astype(BF)
                at_grads[z, core, :, 3 * width :] = dwout[mine, :].astype(BF)
            column, places = 0, []
            for acc in (dga, dsa, dgb, dsb, ddb, dqv, dub, dpb):
                row[:, column : column + acc.shape[1]] = acc[...]
                places.append((column, acc.shape[1]))
                column += acc.shape[1]
            row[:, column:] = word_row[...]
            (
                oga, osa, owin, owout, ogb, osb, oup, oub, odn, odb, oqv, opj, opb,
                xga, xsa, xwin, xwout, xgb, xsb, xup, xub, xdn, xdb,
            ) = outs
            for ref in (xga, xsa, xgb, xsb, xdb, xub):
                length = ref.shape[1] * n_wide
                places.append((column, length))
                column += length
            att.start()
            rowsum.start()
            word.finish(columns_of((xwin, xwout, xup), xdn))
            ff.finish(columns_of((oup, opj), odn))
            att.over_dp()
            rowsum.over_dp()
            att.over_z()
            rowsum.over_z()
            att.back_over_dp()
            ordered = (oga, osa, ogb, osb, odb, oqv, oub, opb, xga, xsa, xgb, xsb, xdb, xub)
            rowsum.finish([(ref, *place) for ref, place in zip(ordered, places)])
            att.finish(columns_of((owin, owout), None))


def columns_of(across, down):
    outs, column = [], 0
    for ref in across:
        outs.append((ref, column, ref.shape[1], 1))
        column += ref.shape[1]
    if down is not None:
        outs.append((down, column, down.shape[1], down.shape[0] // across[0].shape[0]))
    return outs


def whole_block(shape):
    return pl.BlockSpec(shape, lambda p, i: (0,) * len(shape))


def char_backward(gx, chars, counts, saved, weights, chars_per, rows, net_sizes=None, word_grads=None, word_row=None):
    total, width = chars.shape
    win, wout, wup, wdn, wpj, vec = weights
    pooled, qkv, soft, mixed, h1, h2, m, s = saved
    words, cw = total // chars_per, rows // chars_per
    ff, out = wup.shape[1], wpj.shape[1]
    steps = total // rows

    def early(count, columns):
        return pl.BlockSpec((count, columns), lambda p, i: (i + p * (steps - 1 - i), 0))

    def late(count, columns):
        return pl.BlockSpec((count, columns), lambda p, i: (i * p, 0))

    accs = [(1, width), (1, width), (width, 3 * width), (width, width), (1, width), (1, width), (width, ff), (1, ff),
            (width, ff), (1, width), (1, width), (width, out), (1, out)]
    in_specs = [early(cw, out), late(rows, width), early(cw, 1), late(rows, 3 * width), late(rows, 2 * width),
                late(rows, width), early(rows, width), early(rows, width), early(rows, ff), early(rows, ff),
                whole_block(pooled.shape), whole_block(gx.shape)] + [whole_block(w.shape) for w in weights]
    operands = [gx, chars, counts, qkv, soft, mixed, h1, h2, m, s, pooled, gx, *weights]
    scratch = [pltpu.VMEM((total, width), F32), pltpu.VMEM((rows, width), BF), pltpu.VMEM((rows, width), BF),
               pltpu.VMEM((rows, ff), BF), pltpu.VMEM((rows, 3 * width), BF)]
    out_shapes = [(total, width)]
    if net_sizes:
        n_dp, n_wide = net_sizes
        n_z, some = n_wide // 2, width // n_wide
        word_rows, word_width = word_grads.shape[2:]
        wide_d = n_wide * word_rows
        word_ff = word_row.shape[1] - 5 * wide_d
        operands += [word_grads, word_row]
        in_specs += [pl.BlockSpec(memory_space=pl.ANY), whole_block(word_row.shape)]
        part = lambda a: (1, a[1] // n_wide) if a[0] == 1 else (a[0] // n_wide, a[1])
        words_accs = [(1, wide_d), (1, wide_d), (wide_d, 3 * wide_d), (wide_d, wide_d), (1, wide_d), (1, wide_d), (wide_d, word_ff),
                      (1, word_ff), (word_ff, wide_d), (1, wide_d)]
        out_shapes += [part(a) for a in accs[:8] + [(ff, width)] + accs[9:] + words_accs]
        ff_width, at_width = ff + out + ff, 4 * width
        row_width = 6 * width + ff + out + word_row.shape[1]
        scratch = (
            [pltpu.VMEM(a, F32) for a in accs]
            + scratch
            + [pltpu.VMEM((n_z, 2, some, ff_width), BF), pltpu.VMEM((n_z, 2, some, at_width), BF), pltpu.VMEM((1, row_width), F32)]
            + Reduce.scratch(n_dp, n_z, word_rows, word_width)
            + Reduce.scratch(n_dp, n_z, some, ff_width)
            + Reduce.scratch(n_dp, n_z, some, at_width)
            + ReduceRows.scratch(n_dp, n_z, row_width)[1:]
        )
        params = pltpu.CompilerParams(vmem_limit_bytes=VMEM_LIMIT, collective_id=3, has_side_effects=True)
    else:
        out_shapes += accs
        params = pltpu.CompilerParams(vmem_limit_bytes=VMEM_LIMIT)
    return pl.pallas_call(
        functools.partial(char_back_kernel, chars_per, steps, net_sizes),
        grid=(2, steps),
        in_specs=in_specs,
        out_specs=[late(rows, width)] + [whole_block(a) for a in out_shapes[1:]],
        out_shape=[jax.ShapeDtypeStruct(a, F32) for a in out_shapes],
        scratch_shapes=scratch,
        compiler_params=params,
        name="char_backward",
    )(*operands)


def char_forward_kernel(chars_per, steps, net_sizes, lengths, *refs):
    c_ref, bias_ref, cnt_ref, *refs = refs
    if net_sizes:
        net = Net(*net_sizes)
        shards, word_shards, refs = refs[:6], refs[6:10], refs[10:]
        inbox, vec, *refs = refs
        char_out, word_out, refs = refs[:5], refs[5:9], refs[9:]
    else:
        win, wout, wup, wdn, wpj, vec, *refs = refs
        x_ref, *refs = refs
    pooled_ref, qkv_ref, p_ref, o_ref, h1_ref, h2_ref, m_ref, s_ref, *refs = refs
    h1_all, *refs = refs
    rows, width = c_ref.shape
    phase, step = pl.program_id(0), pl.program_id(1)
    now = phase * steps + step
    chunk = min(rows, 256)
    cw = chunk // chars_per

    if net_sizes:
        x_out, win, wout, wup, wdn, wpj, pieces, *refs = refs
        gather = Gather(net, shards, [win, wout, wup, wdn, wpj, pieces], *refs[:3])
        shared = SharedGather(net, word_shards, word_out, *refs[3:10])
        exchange = Exchange(net, x_out, inbox, *refs[10:13])
        keep = refs[13]
        first, later = (5, 0, 1), (2, 3, 4)

        @pl.when(now == 0)
        def _():
            peers = [net.wide_peer(j)[1] for j in range(1, net.n_wide)] + [net.dp_peer(j)[1] for j in range(1, net.n_dp)]
            net.greet(peers)
            net.met(peers)
            for a in first + later:
                gather.start(a)
            for a in first:
                gather.relay(a)
            shared.start()
            for a in first:
                gather.finish(a)
            column = 0
            for at, length in lengths:
                some = length // net.n_wide
                row = jnp.concatenate([pieces[w, :, at : at + some] for w in range(net.n_wide)], 1)
                vec[:, column : column + length] = row
                column += length

        @pl.when(now == 3 * steps // 8)
        def _():
            for a in later:
                gather.relay(a)

        @pl.when(now == steps)
        def _():
            for a in later:
                gather.finish(a)
            for a in range(5):
                pltpu.make_async_copy(gather.wholes[a], char_out[a], keep.at[a]).start()

        for a in range(4):

            @pl.when(now == steps - steps // 4 + a * steps // 8)
            def _(a=a):
                shared.relay(a)

            @pl.when(now == 2 * steps - 5 * steps // 8 + a * steps // 8)
            def _(a=a):
                shared.pass_on(a)

    ga, sa, gb, sb, db, qv, ub, pb = char_vectors(vec, width, wup.shape[1], wpj.shape[1])

    def block(t):
        return pl.ds(pl.multiple_of(step * rows + t * chunk, chunk), chunk)

    @pl.when(phase == 0)
    def _():
        n, _ = normal_of(c_ref[...].astype(F32))
        a = (n * ga[...] + sa[...]).astype(BF)
        qkv = nn(a, win[...])
        qkv_ref[:, :width] = (qkv[:, :width] * HD**-0.5).astype(BF)
        qkv_ref[:, width:] = qkv[:, width:].astype(BF)
        ri = lax.broadcasted_iota(jnp.int32, (GROUP, GROUP), 0) // chars_per
        ci = lax.broadcasted_iota(jnp.int32, (GROUP, GROUP), 1) // chars_per
        same = ri == ci
        for g in range(rows // GROUP):
            at = slice(g * GROUP, (g + 1) * GROUP)
            bias = jnp.where(same, jnp.broadcast_to(bias_ref[0, g : g + 1, :], (GROUP, GROUP)), NEG)
            for p in range(width // GROUP):
                q = qkv_ref[at, p * GROUP : (p + 1) * GROUP]
                k = qkv_ref[at, width + p * GROUP : width + (p + 1) * GROUP]
                v = qkv_ref[at, 2 * width + p * GROUP : 2 * width + (p + 1) * GROUP]
                s = nt(q, two_heads(k))
                soft = jnp.concatenate([softmax_low(s[:, h * GROUP : (h + 1) * GROUP] + bias) for h in range(2)], 1)
                p_ref[at, p * 2 * GROUP : (p + 1) * 2 * GROUP] = soft
                o_ref[at, p * GROUP : (p + 1) * GROUP] = nn(soft, two_heads(v)).astype(BF)
        for t in range(rows // chunk):
            at = slice(t * chunk, (t + 1) * chunk)
            h1 = c_ref[at, :].astype(F32) + nn(o_ref[at, :], wout[...])
            h1_ref[at, :] = h1
            h1_all[block(t), :] = h1

    @pl.when(phase == 1)
    def _():
        for t in range(rows // chunk):
            at = slice(t * chunk, (t + 1) * chunk)
            wat = slice(t * cw, (t + 1) * cw)
            h1 = h1_all[block(t), :]
            n, _ = normal_of(h1)
            u = (n * gb[...] + sb[...]).astype(BF)
            m, s = gelu_and_slope(nn(u, wup[...]) + ub[...])
            m_ref[at, :] = m.astype(BF)
            s_ref[at, :] = s.astype(BF)
            h2 = h1 + (nn(m_ref[at, :], wdn[...]) + db[...])
            h2_ref[at, :] = h2
            om = pool_weights(h2, qv[...], cnt_ref[wat, :], chars_per)
            pooled_ref[wat, :] = jnp.sum(om * h2.reshape(cw, chars_per, width), 1).astype(BF)
        x = (nn(pooled_ref[...], wpj[...]) + pb[...]).astype(BF)
        if net_sizes:
            cap = x_out.shape[1]
            words = rows // chars_per
            first_word = step * words
            target = first_word // cap
            x_out[target, pl.ds(pl.multiple_of(lax.rem(first_word, cap), words), words)] = x
            pl.when(lax.rem(first_word + words, cap) == 0)(lambda: exchange.send_block(target))
        else:
            x_ref[...] = x

    if net_sizes:

        @pl.when(now == 2 * steps - 1)
        def _():
            for a in range(4):
                shared.finish(a)
            exchange.finish()
            for a in range(5):
                pltpu.make_async_copy(gather.wholes[a], char_out[a], keep.at[a]).wait()


def char_forward(chars, key_bias, counts, weights, chars_per, rows, net_sizes=None, word_shards=None, lengths=None, cap=None):
    total, width = chars.shape
    words, cw = total // chars_per, rows // chars_per
    ff, out = weights[2].shape[1], weights[4].shape[1]
    steps = total // rows

    def early(count, columns):
        return pl.BlockSpec((count, columns), lambda p, i: (i + p * (steps - 1 - i), 0))

    def late(count, columns):
        return pl.BlockSpec((count, columns), lambda p, i: (i * p, 0))

    saved = [((words, width), BF, cw, late), ((total, 3 * width), BF, rows, early), ((total, 2 * width), BF, rows, early),
             ((total, width), BF, rows, early), ((total, width), F32, rows, early), ((total, width), F32, rows, late),
             ((total, ff), BF, rows, late), ((total, ff), BF, rows, late)]
    saved_specs = [where(count, s[1]) for s, _, count, where in saved]
    saved_shapes = [jax.ShapeDtypeStruct(s, d) for s, d, _, _ in saved]
    groups = rows // GROUP
    bias_spec = pl.BlockSpec((1, groups, GROUP), lambda p, i: (i + p * (steps - 1 - i), 0, 0))
    in_specs = [early(rows, width), bias_spec, late(cw, 1)]
    operands = [chars, key_bias.reshape(steps, groups, GROUP), counts]
    scratch = [pltpu.VMEM((total, width), F32)]
    anywhere = pl.BlockSpec(memory_space=pl.ANY)
    if net_sizes:
        n_dp, n_wide = net_sizes
        n_z = n_wide // 2
        in_specs += [anywhere] * 10
        operands += [*weights, *word_shards]
        vec_shape = jax.ShapeDtypeStruct((1, sum(length for _, length in lengths)), F32)
        grown = lambda a: jax.ShapeDtypeStruct((a.shape[0] * n_wide, a.shape[1]), a.dtype)
        fulls = [grown(a) for a in weights[:5]]
        out_specs = [anywhere, whole_block(vec_shape.shape)] + [anywhere] * 9 + saved_specs
        out_shapes = [jax.ShapeDtypeStruct((n_wide, cap, out), BF), vec_shape, *fulls, *(grown(a) for a in word_shards), *saved_shapes]
        scratch += (
            [pltpu.VMEM((n_wide, cap, out), BF)]
            + [pltpu.VMEM(a.shape, a.dtype) for a in fulls]
            + [pltpu.VMEM((n_wide, *weights[5].shape[1:]), F32)]
            + Gather.scratch(6, n_z)
            + SharedGather.scratch(4, n_dp, n_z)
            + Exchange.scratch(n_wide)
            + [pltpu.SemaphoreType.DMA((5,))]
        )
        params = pltpu.CompilerParams(vmem_limit_bytes=VMEM_LIMIT, collective_id=1, has_side_effects=True)
    else:
        in_specs += [whole_block(w.shape) for w in weights]
        operands += [*weights]
        out_specs = [late(cw, out)] + saved_specs
        out_shapes = [jax.ShapeDtypeStruct((words, out), BF), *saved_shapes]
        params = pltpu.CompilerParams(vmem_limit_bytes=VMEM_LIMIT)
    return pl.pallas_call(
        functools.partial(char_forward_kernel, chars_per, steps, net_sizes, lengths),
        grid=(2, steps),
        in_specs=in_specs,
        out_specs=out_specs,
        out_shape=out_shapes,
        scratch_shapes=scratch,
        compiler_params=params,
        name="char_forward",
    )(*operands)


def word_kernel(slot_cap, net_sizes, *refs):
    arrived, bucket, assign, seg_row, seg_col, grad_ref, win, wout, wup, wdn, vec, out_ref, back_out, *refs = refs
    length, width = grad_ref.shape
    ff = wup.shape[1]
    if net_sizes:
        net = Net(*net_sizes)
        word_grads, word_row, *refs = refs
        dga, dsa, dgb, dsb, ddb, dub = word_vectors(word_row, width, ff)
    else:
        dga, dsa, dwin, dwout, dgb, dsb, dwup, dub, dwdn, ddb, *refs = refs
    qkv_ref, p_ref, mix_ref, h_ref, s_ref, gq_ref, *refs = refs
    ga, sa, gb, sb, db, ub = word_vectors(vec, width, ff)
    owners = assign.shape[1]
    slots = owners * slot_cap
    if net_sizes:
        back_ref, *sems = refs
        exchange = Exchange(net, back_ref, back_out, *sems)
        peers = [net.wide_peer(j)[1] for j in range(1, net.n_wide)]
        net.greet(peers)
    named = jnp.where(bucket[...] == lax.broadcasted_iota(jnp.int32, (length, owners), 1), 1.0, 0.0)
    ri = lax.broadcasted_iota(jnp.int32, (length, length), 0)
    ci = lax.broadcasted_iota(jnp.int32, (length, length), 1)
    earlier = nn(jnp.where(ci < ri, 1.0, 0.0).astype(BF), named.astype(BF))
    slot = jnp.sum(named * (assign[...].astype(F32) * slot_cap + earlier), -1, keepdims=True).astype(jnp.int32)
    hot = jnp.where(lax.broadcasted_iota(jnp.int32, (length, slots), 1) == slot, 1.0, 0.0).astype(BF)
    x = nn(hot, arrived[...].reshape(slots, width))
    n1, r1 = normal_of(x)
    a = (n1 * ga[...] + sa[...]).astype(BF)
    qkv = nn(a, win[...])
    qkv_ref[:, :width] = (qkv[:, :width] * HD**-0.5).astype(BF)
    qkv_ref[:, width:] = qkv[:, width:].astype(BF)
    bias = jnp.where((seg_row[...] == seg_col[...]) & (ci <= ri), 0.0, NEG)

    def pair(p):
        return [qkv_ref[:, i * width + p * GROUP : i * width + (p + 1) * GROUP] for i in range(3)]

    for p in range(width // GROUP):
        q, k, v = pair(p)
        s = nt(q, two_heads(k))
        soft = jnp.concatenate([softmax_low(s[:, h * length : (h + 1) * length] + bias) for h in range(2)], 1)
        p_ref[:, 2 * p * length : (2 * p + 2) * length] = soft
        mix_ref[:, p * GROUP : (p + 1) * GROUP] = nn(soft, two_heads(v)).astype(BF)
    inner = x + nn(mix_ref[...], wout[...])
    n2, r2 = normal_of(inner)
    u = (n2 * gb[...] + sb[...]).astype(BF)
    h, slope = gelu_and_slope(nn(u, wup[...]) + ub[...])
    h_ref[...] = h.astype(BF)
    s_ref[...] = slope
    out_ref[...] = inner + (nn(h_ref[...], wdn[...]) + db[...])
    g = grad_ref[...]
    gz = (nt(g, wdn[...]) * s_ref[...]).astype(BF)
    du = nt(gz, wup[...])
    g1 = g.astype(F32) + norm_back(du, n2, r2, gb[...])
    g1_low = g1.astype(BF)
    gm = nt(g1_low, wout[...]).astype(BF)
    for p in range(width // GROUP):
        q, k, v = pair(p)
        gmp = gm[:, p * GROUP : (p + 1) * GROUP]
        soft = p_ref[:, 2 * p * length : (2 * p + 2) * length]
        dp = nt(gmp, two_heads(v))
        gs = jnp.concatenate([softmax_back(soft[:, h * length : (h + 1) * length], dp[:, h * length : (h + 1) * length]) for h in range(2)], 1)
        gq_ref[:, p * GROUP : (p + 1) * GROUP] = (nn(gs, two_heads(k)) * HD**-0.5).astype(BF)
        gq_ref[:, width + p * GROUP : width + (p + 1) * GROUP] = one_of_two(tn(gs, q)).astype(BF)
        gq_ref[:, 2 * width + p * GROUP : 2 * width + (p + 1) * GROUP] = one_of_two(tn(soft, gmp)).astype(BF)
    da = nt(gq_ref[...], win[...])
    gx = (g1 + norm_back(da, n1, r1, ga[...])).astype(BF)
    back = tn(hot, gx).astype(BF).reshape(owners, slot_cap, width)
    if net_sizes:
        back_ref[...] = back
        net.met(peers)
        exchange.send_all()
        some = width // net.n_wide
        side = ff // width

        def put(value, column):
            value = value.astype(BF)
            for w in range(net.n_wide):
                word_grads[w // 2, w % 2, :, column : column + value.shape[1]] = value[w * some : (w + 1) * some]

        put(tn(a, gq_ref[...]), 0)
        put(tn(mix_ref[...], g1_low), 3 * width)
        put(tn(u, gz), 4 * width)
        down = tn(h_ref[...], g).astype(BF)
        for w in range(net.n_wide):
            for k in range(side):
                first = (w * side + k) * some
                column = 4 * width + ff + k * width
                word_grads[w // 2, w % 2, :, column : column + width] = down[first : first + some]
    else:
        back_out[...] = back
        dwin[...] = tn(a, gq_ref[...])
        dwout[...] = tn(mix_ref[...], g1_low)
        dwup[...] = tn(u, gz)
        dwdn[...] = tn(h_ref[...], g)
    dga[...] = column_sum(da * n1)
    dsa[...] = column_sum(da)
    dgb[...] = column_sum(du * n2)
    dsb[...] = column_sum(du)
    dub[...] = column_sum(gz.astype(F32))
    ddb[...] = column_sum(g.astype(F32))
    if net_sizes:
        exchange.finish()


def word_block(arrived, bucket, assign, segments, grad, weights, slot_cap, net_sizes=None):
    length, width = grad.shape
    ff = weights[2].shape[1]
    owners = assign.shape[1]
    low = lambda *s: jax.ShapeDtypeStruct(s, BF)
    full = lambda *s: jax.ShapeDtypeStruct(s, F32)
    vmem = pl.BlockSpec(memory_space=pltpu.VMEM)
    out_shapes, out_specs = [full(length, width), low(owners, slot_cap, width)], [vmem, vmem]
    scratch = [pltpu.VMEM((length, 3 * width), BF), pltpu.VMEM((length, width // HD * length), BF), pltpu.VMEM((length, width), BF),
               pltpu.VMEM((length, ff), BF), pltpu.VMEM((length, ff), F32), pltpu.VMEM((length, 3 * width), BF)]
    if net_sizes:
        n_dp, n_wide = net_sizes
        out_shapes += [low(n_wide // 2, 2, width // n_wide, 4 * width + 2 * ff), full(1, 5 * width + ff)]
        out_specs = [vmem, pl.BlockSpec(memory_space=pl.ANY), vmem, vmem]
        scratch += [pltpu.VMEM((owners, slot_cap, width), BF)] + Exchange.scratch(n_wide)
        params = pltpu.CompilerParams(vmem_limit_bytes=VMEM_LIMIT, collective_id=2, has_side_effects=True)
    else:
        row = full(1, width)
        out_shapes += [row, row, full(width, 3 * width), full(width, width), row, row, full(width, ff), full(1, ff), full(ff, width), row]
        out_specs += [vmem] * 10
        params = pltpu.CompilerParams(vmem_limit_bytes=VMEM_LIMIT)
    return pl.pallas_call(
        functools.partial(word_kernel, slot_cap, net_sizes),
        in_specs=[vmem] * 11,
        out_specs=out_specs,
        out_shape=out_shapes,
        scratch_shapes=scratch,
        compiler_params=params,
        name="word_block",
    )(arrived, bucket, assign, segments, segments.reshape(length, 1), grad, *weights)


def gathered(shard):
    return lax.all_gather(shard, "wide", axis=0, tiled=True)


def exchanged(blocks):
    return lax.all_to_all(blocks, "wide", split_axis=0, concat_axis=0, tiled=True)


def summed(grad):
    part = lax.psum_scatter(grad.astype(BF), "wide", scatter_dimension=0, tiled=True)
    return lax.psum(part, "dp").astype(F32)


def shards(
    chars, char_counts, buckets, assign, segments,
    char_gain, char_shift, char_inproj, char_outproj, char_gain_mid, char_shift_mid, char_up, char_up_bias, char_down, char_down_bias,
    pool_query, char_proj, char_proj_bias,
    word_gain, word_shift, word_inproj, word_outproj, word_gain_mid, word_shift_mid, word_up, word_up_bias, word_down, word_down_bias,
    out_grad,
):
    n_dp, n_wide = lax.axis_size("dp"), lax.axis_size("wide")
    cap, chars_per, width = chars.shape[2:]
    slots = n_wide * cap
    rows = chars.reshape(slots * chars_per, width)
    counts = char_counts.reshape(slots, 1)
    key_bias = jnp.where(lax.broadcasted_iota(jnp.int32, (slots, chars_per), 1) < counts, 0.0, NEG)
    block = min(512, rows.shape[0])
    char_shards = (char_inproj, char_outproj, char_up, char_down, char_proj)
    word_shards = (word_inproj, word_outproj, word_up, word_down)
    vectors = (char_gain, char_shift, char_gain_mid, char_shift_mid, char_down_bias, pool_query, char_up_bias, char_proj_bias,
               word_gain, word_shift, word_gain_mid, word_shift_mid, word_down_bias, word_up_bias)
    matrices = char_shards + word_shards
    fast = (
        all(m.shape[0] % 16 == 0 for m in char_shards)
        and all(m.shape[0] % (16 * n_dp) == 0 for m in word_shards)
        and cap % (block // chars_per) == 0
        and (4 * width) % (GROUP * n_dp) == 0
        and n_wide % 2 == 0
    )
    bucket, names, seg, upstream = buckets[0], assign[None], segments, out_grad[0]
    if fast:
        sizes = (n_dp, n_wide)
        padded, lengths, at = [], [], 0
        for v in vectors:
            room = -(-v.shape[0] // GROUP) * GROUP
            padded.append(jnp.pad(v.astype(F32), (0, room - v.shape[0])))
            lengths.append((at, v.shape[0] * n_wide))
            at += room
        pieces = jnp.concatenate(padded).reshape(1, 1, at)
        arrived, vec, *rest = char_forward(rows, key_bias, counts, (*char_shards, pieces), chars_per, block, sizes, word_shards, tuple(lengths), cap)
        char_full, word_full, saved = rest[:5], rest[5:9], rest[9:]
        result, returned, word_grads, word_row = word_block(arrived, bucket, names, seg, upstream, (*word_full, vec), cap, sizes)
        incoming = returned.reshape(slots, -1)
        outs = char_backward(incoming, rows, counts, saved, (*char_full, vec), chars_per, block, sizes, word_grads, word_row)
        char_grads, *grads = outs
        grads = [g[0] if g.shape[0] == 1 else g for g in grads]
    else:
        vec = jnp.concatenate([gathered(v) for v in vectors]).astype(F32)[None]
        char_full, word_full = [gathered(m) for m in char_shards], [gathered(m) for m in word_shards]
        outgoing, *saved = char_forward(rows, key_bias, counts, (*char_full, vec), chars_per, block)
        arrived = exchanged(outgoing.reshape(n_wide, cap, -1))
        result, back, *word_grads = word_block(arrived, bucket, names, seg, upstream, (*word_full, vec), cap)
        incoming = exchanged(back).reshape(slots, -1)
        char_grads, *grads = char_backward(incoming, rows, counts, saved, (*char_full, vec), chars_per, block)
        grads[8] = grads[8].T
        grads = [summed(g[0] if g.shape[0] == 1 else g) for g in grads + word_grads]
    return (result[None], char_grads.reshape(chars.shape), *grads)


def solution(mesh):
    whole, split = ("dp", "wide"), "wide"
    row, flat = P(split, None), P(split)
    word = [flat, flat, row, row, flat, flat, row, flat, row, flat]
    char = word + [flat, row, flat]
    chars = P(whole, None, None, None, None)
    three = P(whole, None, None)
    return jax.shard_map(
        shards,
        mesh=mesh,
        in_specs=(chars, three, three, P(), P(whole, None), *char, *word, three),
        out_specs=(three, chars, *char, *word),
        check_vma=False,
    )
```

```python
import functools

import jax
import jax.numpy as jnp
from jax import lax
from jax.experimental import pallas as pl
from jax.experimental.pallas import tpu as pltpu
from jax.sharding import PartitionSpec as P

EPS = 1e-05
NEG = -1e30
ROOT_HALF = 0.7071067811865476
INV_ROOT_TWO_PI = 0.3989422804014327
HD = 64
GROUP = 128
F32 = jnp.float32
BF = jnp.bfloat16
MESH = pl.DeviceIdType.MESH
VMEM_LIMIT = 60 << 20


def nn(a, b):
    return lax.dot_general(a, b, (((1,), (0,)), ((), ())), preferred_element_type=F32)


def nt(a, b):
    return lax.dot_general(a, b, (((1,), (1,)), ((), ())), preferred_element_type=F32)


def tn(a, b):
    return lax.dot_general(a, b, (((0,), (0,)), ((), ())), preferred_element_type=F32)


def padded(lanes):
    return -(-lanes // GROUP) * GROUP


def column_sum(x):
    return jnp.sum(x, 0, keepdims=True)


def normal_of(x):
    c = x - jnp.mean(x, -1, keepdims=True)
    r = lax.rsqrt(jnp.mean(c * c, -1, keepdims=True) + EPS)
    return c * r, r


def norm_back(d, n, r, g):
    dg = d * g
    return r * (dg - jnp.mean(dg, -1, keepdims=True) - n * jnp.mean(dg * n, -1, keepdims=True))


def gelu_and_slope(z):
    cdf = 0.5 * (1.0 + lax.erf(z * ROOT_HALF))
    return z * cdf, cdf + z * jnp.exp(-0.5 * z * z) * INV_ROOT_TWO_PI


def softmax_low(s):
    ex = jnp.exp(s - jnp.max(s, -1, keepdims=True))
    return (ex * (1.0 / jnp.sum(ex, -1, keepdims=True))).astype(BF)


def softmax_back(soft, d):
    soft = soft.astype(F32)
    return (soft * (d - jnp.sum(d * soft, -1, keepdims=True))).astype(BF)


def two_heads(t):
    left = lax.broadcasted_iota(jnp.int32, t.shape, 1) < HD
    zero = jnp.zeros_like(t)
    return jnp.concatenate([jnp.where(left, t, zero), jnp.where(left, zero, t)], 0)


def one_of_two(t):
    half = t.shape[0] // 2
    left = lax.broadcasted_iota(jnp.int32, (half, t.shape[1]), 1) < HD
    return jnp.where(left, t[:half], t[half:])


def as_column(row):
    n = row.shape[1]
    same = lax.broadcasted_iota(jnp.int32, (n, n), 0) == lax.broadcasted_iota(jnp.int32, (n, n), 1)
    return jnp.sum(jnp.where(same, jnp.broadcast_to(row, (n, n)), 0.0), -1, keepdims=True)


def key_bias(row, chars_per):
    n = row.shape[1]
    lanes = n * chars_per
    of_word = lax.broadcasted_iota(jnp.int32, (n, lanes), 1) // chars_per == lax.broadcasted_iota(jnp.int32, (n, lanes), 0)
    counts = nn(jnp.broadcast_to(row, (8, n)).astype(BF), jnp.where(of_word, 1.0, 0.0).astype(BF))
    place = lax.rem(lax.broadcasted_iota(jnp.int32, (8, lanes), 1), chars_per)
    return jnp.where(place.astype(F32) < counts, 0.0, NEG)


def pool_weights(h2, query, counts, chars_per):
    rows = h2.shape[0]
    words = rows // chars_per
    e = jnp.sum(h2 * query, -1, keepdims=True) * (h2.shape[1] ** -0.5)
    e = e.reshape(words, chars_per, 1)
    place = lax.broadcasted_iota(jnp.int32, (words, chars_per, 1), 1).astype(F32)
    e = jnp.where(place < counts.reshape(words, 1, 1), e, NEG)
    ex = jnp.exp(e - jnp.max(e, 1, keepdims=True))
    return ex / jnp.sum(ex, 1, keepdims=True)


class Net:
    def __init__(self, n_dp, n_wide):
        self.n_dp, self.n_wide, self.n_z = n_dp, n_wide, n_wide // 2
        self.dp, self.wide = lax.axis_index("dp"), lax.axis_index("wide")
        self.z, self.core = self.wide // 2, lax.rem(self.wide, 2)
        self.sibling = (self.dp, self.wide + 1 - 2 * self.core)

    def z_peer(self, j):
        z = lax.rem(self.z + j, self.n_z)
        return z, (self.dp, 2 * z + self.core)

    def dp_peer(self, j):
        q = lax.rem(self.dp + j, self.n_dp)
        return q, (q, self.wide)

    def wide_peer(self, j):
        w = lax.rem(self.wide + j, self.n_wide)
        return w, (self.dp, w)

    def greet(self, peers):
        barrier = pltpu.get_barrier_semaphore()
        for peer in peers:
            pl.semaphore_signal(barrier, inc=1, device_id=peer, device_id_type=MESH)

    def met(self, peers):
        pl.semaphore_wait(pltpu.get_barrier_semaphore(), len(peers))


def remote(src, dst, send, recv, peer):
    return pltpu.make_async_remote_copy(src_ref=src, dst_ref=dst, send_sem=send, recv_sem=recv, device_id=peer, device_id_type=MESH)


class Reduce:
    def __init__(self, net, grads, kept, from_core, part, from_dp, from_z, done, sems):
        self.net, self.grads = net, grads
        self.kept, self.from_core, self.part = kept, from_core, part
        self.from_dp, self.from_z, self.done = from_dp, from_z, done
        self.send, self.recv = sems
        self.span = part.shape[-1]

    @staticmethod
    def scratch(n_dp, n_z, rows, width):
        span = width // n_dp
        count = 2 + 2 * n_dp + n_z
        return [
            pltpu.VMEM((n_z, rows, width), BF),
            pltpu.VMEM((n_z, rows, width), BF),
            pltpu.VMEM((n_z, rows, span), BF),
            pltpu.VMEM((n_dp - 1, n_z, rows, span), BF),
            pltpu.VMEM((n_z - 1, rows, span), BF),
            pltpu.VMEM((n_dp, rows, span), BF),
            pltpu.SemaphoreType.DMA((count,)),
            pltpu.SemaphoreType.DMA((count,)),
        ]

    def lanes(self, q):
        return pl.ds(pl.multiple_of(q * self.span, GROUP), self.span)

    def to_core(self):
        net = self.net
        return remote(self.grads.at[:, 1 - net.core], self.from_core, self.send.at[0], self.recv.at[0], net.sibling)

    def own(self):
        return pltpu.make_async_copy(self.grads.at[:, self.net.core], self.kept, self.recv.at[1])

    def to_dp(self, j):
        q, peer = self.net.dp_peer(j)
        return remote(self.kept.at[:, :, self.lanes(q)], self.from_dp.at[j - 1], self.send.at[1 + j], self.recv.at[1 + j], peer)

    def to_z(self, j):
        z, peer = self.net.z_peer(j)
        at = 1 + self.net.n_dp + j
        return remote(self.part.at[z], self.from_z.at[j - 1], self.send.at[at], self.recv.at[at], peer)

    def to_all(self, j):
        net = self.net
        _, peer = net.dp_peer(j)
        at = 1 + net.n_dp + net.n_z + j
        mine = self.done.at[net.dp]
        return remote(mine, mine, self.send.at[at], self.recv.at[at], peer)

    def start(self):
        self.to_core().start()
        self.own().start()

    def over_dp(self):
        net = self.net
        self.own().wait()
        self.to_core().wait()

        @pl.loop(0, net.n_z)
        def _(z):
            self.kept[z] = (self.kept[z].astype(F32) + self.from_core[z].astype(F32)).astype(BF)

        for j in range(1, net.n_dp):
            self.to_dp(j).start()

    def over_z(self):
        net = self.net
        for j in range(1, net.n_dp):
            self.to_dp(j).wait()

        @pl.loop(0, net.n_z)
        def _(z):
            total = self.kept[z, :, self.lanes(net.dp)].astype(F32)
            for j in range(net.n_dp - 1):
                total = total + self.from_dp[j, z].astype(F32)
            self.part[z] = total.astype(BF)

        for j in range(1, net.n_z):
            self.to_z(j).start()

    def back_over_dp(self):
        net = self.net
        for j in range(1, net.n_z):
            self.to_z(j).wait()
        total = self.part[net.z].astype(F32)
        for j in range(net.n_z - 1):
            total = total + self.from_z[j].astype(F32)
        self.done[net.dp] = total.astype(BF)
        for j in range(1, net.n_dp):
            self.to_all(j).start()

    def finish(self):
        for j in range(1, self.net.n_dp):
            self.to_all(j).wait()


class ReduceRows:
    def __init__(self, net, row, from_core, of_dp, of_z, sems):
        self.net, self.row, self.from_core, self.of_dp, self.of_z = net, row, from_core, of_dp, of_z
        self.send, self.recv = sems

    @staticmethod
    def scratch(n_dp, n_z, width):
        count = 1 + n_dp + n_z
        return [
            pltpu.VMEM((1, width), F32),
            pltpu.VMEM((1, width), F32),
            pltpu.VMEM((n_dp, 1, width), F32),
            pltpu.VMEM((n_z, 1, width), F32),
            pltpu.SemaphoreType.DMA((count,)),
            pltpu.SemaphoreType.DMA((count,)),
        ]

    def to_core(self):
        return remote(self.row, self.from_core, self.send.at[0], self.recv.at[0], self.net.sibling)

    def to_dp(self, j):
        mine = self.of_dp.at[self.net.dp]
        return remote(mine, mine, self.send.at[j], self.recv.at[j], self.net.dp_peer(j)[1])

    def to_z(self, j):
        mine = self.of_z.at[self.net.z]
        at = self.net.n_dp + j
        return remote(mine, mine, self.send.at[at], self.recv.at[at], self.net.z_peer(j)[1])

    def start(self):
        self.to_core().start()

    def over_dp(self):
        self.to_core().wait()
        self.of_dp[self.net.dp] = self.row[...] + self.from_core[...]
        for j in range(1, self.net.n_dp):
            self.to_dp(j).start()

    def over_z(self):
        net = self.net
        for j in range(1, net.n_dp):
            self.to_dp(j).wait()
        total = self.of_dp[0]
        for q in range(1, net.n_dp):
            total = total + self.of_dp[q]
        self.of_z[net.z] = total
        for j in range(1, net.n_z):
            self.to_z(j).start()

    def finish(self, out, places):
        net = self.net
        for j in range(1, net.n_z):
            self.to_z(j).wait()
        total = self.of_z[0]
        for z in range(1, net.n_z):
            total = total + self.of_z[z]
        at = 0
        for first, length in places:
            piece = length // net.n_wide
            vector = jnp.broadcast_to(total[:, first : first + length], (8, length))
            turned = pltpu.roll(vector, lax.rem(length - net.wide * piece, length), 1)
            out[:, at : at + piece] = turned[:1, :piece]
            at += padded(piece)


class Gather:
    def __init__(self, net, shards, wholes, send, recv, near):
        self.net, self.shards, self.wholes = net, shards, wholes
        self.send, self.recv, self.near = send, recv, near

    @staticmethod
    def scratch(count, n_z):
        return [
            pltpu.SemaphoreType.DMA((count, 2 * n_z)),
            pltpu.SemaphoreType.DMA((count, 2 * n_z)),
            pltpu.SemaphoreType.DMA((count,)),
        ]

    def block(self, a, owner):
        rows = self.shards[a].shape[0]
        return self.wholes[a].at[pl.ds(pl.multiple_of(owner * rows, rows), rows)]

    def along_z(self, a, j):
        net = self.net
        return remote(self.shards[a], self.block(a, net.wide), self.send.at[a, j], self.recv.at[a, net.wide], net.z_peer(j)[1])

    def across(self, a):
        net = self.net
        return remote(self.shards[a], self.block(a, net.wide), self.send.at[a, 0], self.recv.at[a, net.wide], net.sibling)

    def relayed(self, a, j):
        net = self.net
        owner = 2 * net.z_peer(j)[0] + net.core
        here = self.block(a, owner)
        return remote(here, here, self.send.at[a, net.n_z + j], self.recv.at[a, owner], net.sibling)

    def own(self, a):
        return pltpu.make_async_copy(self.shards[a], self.block(a, self.net.wide), self.near.at[a])

    def arrival(self, a, owner):
        here = self.block(a, owner)
        return remote(here, here, self.send.at[a, 0], self.recv.at[a, owner], self.net.sibling)

    def start(self, a):
        for j in range(1, self.net.n_z):
            self.along_z(a, j).start()
        self.across(a).start()
        self.own(a).start()

    def relay(self, a):
        net = self.net
        for j in range(1, net.n_z):
            self.arrival(a, 2 * net.z_peer(j)[0] + net.core).wait_recv()
            self.relayed(a, j).start()

    def finish(self, a):
        net = self.net
        self.own(a).wait()
        self.across(a).wait_send()
        for j in range(1, net.n_z):
            self.along_z(a, j).wait_send()
            self.relayed(a, j).wait_send()
        for z in range(net.n_z):
            self.arrival(a, 2 * z + 1 - net.core).wait_recv()


class SharedGather:
    def __init__(self, net, shards, wholes, send_z, send_dp, send_core, recv_z, recv_dp, recv_core, near):
        self.net, self.shards, self.wholes = net, shards, wholes
        self.send_z, self.send_dp, self.send_core = send_z, send_dp, send_core
        self.recv_z, self.recv_dp, self.recv_core, self.near = recv_z, recv_dp, recv_core, near

    @staticmethod
    def scratch(count, n_dp, n_z):
        sem = pltpu.SemaphoreType.DMA
        return [
            sem((count, n_z)), sem((count, n_z, n_dp)), sem((count, n_z)),
            sem((count, n_z)), sem((count, n_z, n_dp)), sem((count, n_z)), sem((count,)),
        ]

    def block(self, a, owner):
        rows = self.shards[a].shape[0]
        return self.wholes[a].at[pl.ds(pl.multiple_of(owner * rows, rows), rows)]

    def piece(self, a, owner, q):
        rows = self.shards[a].shape[0]
        some = rows // self.net.n_dp
        return self.wholes[a].at[pl.ds(pl.multiple_of(owner * rows + q * some, some), some)]

    def along_z(self, a, j):
        net = self.net
        some = self.shards[a].shape[0] // net.n_dp
        mine = self.shards[a].at[pl.ds(pl.multiple_of(net.dp * some, some), some)]
        return remote(mine, self.piece(a, net.wide, net.dp), self.send_z.at[a, j], self.recv_z.at[a, net.z], net.z_peer(j)[1])

    def from_z(self, a, j):
        net = self.net
        z, peer = net.z_peer(j)
        here = self.piece(a, 2 * z + net.core, net.dp)
        return remote(here, here, self.send_z.at[a, j], self.recv_z.at[a, z], peer)

    def over_dp(self, a, j, i):
        net = self.net
        z = net.z_peer(j)[0]
        here = self.piece(a, 2 * z + net.core, net.dp)
        return remote(here, here, self.send_dp.at[a, j, i], self.recv_dp.at[a, j, net.dp], net.dp_peer(i)[1])

    def from_dp(self, a, j, i):
        net = self.net
        z = net.z_peer(j)[0]
        q, peer = net.dp_peer(i)
        here = self.piece(a, 2 * z + net.core, q)
        return remote(here, here, self.send_dp.at[a, j, i], self.recv_dp.at[a, j, q], peer)

    def across(self, a, j):
        net = self.net
        z = net.z_peer(j)[0]
        here = self.block(a, 2 * z + net.core)
        source = self.shards[a] if j == 0 else here
        return remote(source, here, self.send_core.at[a, j], self.recv_core.at[a, z], net.sibling)

    def from_core(self, a, z):
        net = self.net
        here = self.block(a, 2 * z + 1 - net.core)
        return remote(here, here, self.send_core.at[a, 0], self.recv_core.at[a, z], net.sibling)

    def own(self, a):
        return pltpu.make_async_copy(self.shards[a], self.block(a, self.net.wide), self.near.at[a])

    def start(self):
        for a in range(len(self.shards)):
            for j in range(1, self.net.n_z):
                self.along_z(a, j).start()
        for a in range(len(self.shards)):
            self.across(a, 0).start()
            self.own(a).start()

    def relay(self, a):
        net = self.net
        for j in range(1, net.n_z):
            self.from_z(a, j).wait_recv()
            for i in range(1, net.n_dp):
                self.over_dp(a, j, i).start()

    def pass_on(self, a):
        net = self.net
        for j in range(1, net.n_z):
            for i in range(1, net.n_dp):
                self.from_dp(a, j, i).wait_recv()
            self.across(a, j).start()

    def finish(self, a):
        net = self.net
        self.own(a).wait()
        for j in range(1, net.n_z):
            self.along_z(a, j).wait_send()
            for i in range(1, net.n_dp):
                self.over_dp(a, j, i).wait_send()
        for j in range(net.n_z):
            self.across(a, j).wait_send()
            self.from_core(a, j).wait_recv()


class Exchange:
    def __init__(self, net, out, inbox, send, recv, near):
        self.net, self.out, self.inbox = net, out, inbox
        self.send, self.recv, self.near = send, recv, near

    @staticmethod
    def scratch(n_wide):
        return [pltpu.SemaphoreType.DMA((n_wide,)), pltpu.SemaphoreType.DMA((n_wide,)), pltpu.SemaphoreType.DMA(())]

    def to(self, w):
        net = self.net
        return remote(self.out.at[w], self.inbox.at[net.wide], self.send.at[w], self.recv.at[net.wide], (net.dp, w))

    def arrival(self, w):
        here = self.inbox.at[w]
        return remote(here, here, self.send.at[w], self.recv.at[w], (self.net.dp, w))

    def own(self):
        me = self.net.wide
        return pltpu.make_async_copy(self.out.at[me], self.inbox.at[me], self.near)

    def send_block(self, w):
        @pl.when(w != self.net.wide)
        def _():
            self.to(w).start()

        @pl.when(w == self.net.wide)
        def _():
            self.own().start()

    def send_all(self):
        for j in range(1, self.net.n_wide):
            self.to(self.net.wide_peer(j)[0]).start()
        self.own().start()

    def finish(self):
        for j in range(1, self.net.n_wide):
            w = self.net.wide_peer(j)[0]
            self.to(w).wait_send()
            self.arrival(w).wait_recv()
        self.own().wait()


def slices_of(ref, first, lengths):
    views = []
    for length in lengths:
        views.append(ref.at[:, first : first + length])
        first += length
    return views


def char_vectors(row, width, ff, out):
    return slices_of(row, 0, [width] * 6 + [ff, out])


def word_vectors(row, width, ff):
    return slices_of(row, row.shape[1] - 5 * width - ff, [width] * 5 + [ff])


def char_back_kernel(chars_per, steps, net_sizes, word_sizes, *refs):
    (
        gx_ref, c_ref, cnt_ref, qkv_ref, p_ref, o_ref, h1_ref, h2_ref, m_ref, s_ref, pooled_all, gx_all,
        win, wout, wup, wdn, wpj, vec, *refs
    ) = refs
    if net_sizes:
        word_grads, word_row, *refs = refs
    gc_ref, *refs = refs
    if net_sizes:
        outs, refs = refs[:4], refs[4:]
    accs, refs = refs[:13], refs[13:]
    dga, dsa, dwin, dwout, dgb, dsb, dwup, dub, dwdn, ddb, dqv, dwpj, dpb = accs
    gh1_ref, gm_ref, u_ref, gz_ref, gq_ref, gs_ref, *refs = refs
    rows, width = c_ref.shape
    ga, sa, gb, sb, _, qv, _, _ = char_vectors(vec, width, wup.shape[1], wpj.shape[1])
    phase, step = pl.program_id(0), pl.program_id(1)
    now = phase * steps + step
    factor = width**-0.5
    chunk = min(rows, 512)
    cw = chunk // chars_per
    words = rows // chars_per

    if net_sizes:
        net = Net(*net_sizes)
        ff_grads, at_grads, row, *refs = refs
        word = Reduce(net, word_grads, *refs[:6], refs[6:8])
        ff = Reduce(net, ff_grads, *refs[8:14], refs[14:16])
        att = Reduce(net, at_grads, *refs[16:22], refs[22:24])
        rowsum = ReduceRows(net, row, *refs[24:27], refs[27:29])
        keep = refs[29]

        @pl.when(now == 0)
        def _():
            peers = [net.sibling] + [net.dp_peer(j)[1] for j in range(1, net.n_dp)] + [net.z_peer(j)[1] for j in range(1, net.n_z)]
            net.greet(peers)
            net.met(peers)
            word.start()

        schedule = {
            steps // 4: word.over_dp,
            steps - steps // 8: word.over_z,
            steps: ff.start,
            steps + steps // 8: ff.over_dp,
            steps + steps // 4: word.back_over_dp,
            steps + 3 * steps // 8: ff.over_z,
            steps + 5 * steps // 8: ff.back_over_dp,
        }
        for when, act in schedule.items():
            pl.when(now == when)(act)

    @pl.when(now == 0)
    def _():
        for acc in accs:
            acc[...] = jnp.zeros_like(acc)
        dwpj[...] = tn(pooled_all[...], gx_all[...])
        dpb[...] = column_sum(gx_all[...].astype(F32))

    here = pl.ds(pl.multiple_of(step * rows, rows), rows)

    @pl.when(phase == 0)
    def _():
        gp = nt(gx_ref[...], wpj[...]).astype(BF).astype(F32)
        counts = as_column(cnt_ref[pl.ds(step, 1), :].astype(F32))
        for t in range(rows // chunk):
            at = slice(t * chunk, (t + 1) * chunk)
            wat = slice(t * cw, (t + 1) * cw)
            h2 = h2_ref[at, :].astype(F32)
            om = pool_weights(h2, qv[...], counts[wat, :], chars_per)
            gpb = jnp.broadcast_to(gp[wat, :].reshape(cw, 1, width), (cw, chars_per, width)).reshape(chunk, width)
            w = jnp.sum(h2 * gpb, -1, keepdims=True).reshape(cw, chars_per, 1)
            de = om * (w - jnp.sum(om * w, 1, keepdims=True))
            de = de.reshape(chunk, 1) * factor
            gh2 = om.reshape(chunk, 1) * gpb + de * qv[...]
            dqv[...] += column_sum(de * h2)
            gy = gh2.astype(BF)
            ddb[...] += column_sum(gy.astype(F32))
            gm_ref[at, :] = gy
            gz = (nt(gy, wdn[...]) * s_ref[at, :].astype(F32)).astype(BF)
            gz_ref[at, :] = gz
            dub[...] += column_sum(gz.astype(F32))
            du = nt(gz, wup[...])
            n, r = normal_of(h1_ref[at, :].astype(F32))
            dgb[...] += column_sum(du * n)
            dsb[...] += column_sum(du)
            u_ref[at, :] = (n * gb[...] + sb[...]).astype(BF)
            gh1_ref[pl.ds(pl.multiple_of(step * rows + t * chunk, chunk), chunk), :] = (gh2 + norm_back(du, n, r, gb[...])).astype(BF)
        dwup[...] += tn(u_ref[...], gz_ref[...])
        dwdn[...] += tn(gm_ref[...], m_ref[...])

    if net_sizes:
        n_z, n_wide = net.n_z, net.n_wide

        @pl.when(now == steps - 1)
        def _():
            up, proj = dwup.shape[1], dwpj.shape[1]
            down = dwdn[...].T
            some = width // n_wide
            side = down.shape[0] // n_wide // some
            for owner in range(n_wide):
                z, core = owner // 2, owner % 2
                mine = slice(owner * some, (owner + 1) * some)
                ff_grads[z, core, :, :up] = dwup[mine, :].astype(BF)
                ff_grads[z, core, :, up : up + proj] = dwpj[mine, :].astype(BF)
                for k in range(side):
                    first = (owner * side + k) * some
                    ff_grads[z, core, :, up + proj + k * width : up + proj + (k + 1) * width] = down[first : first + some].astype(BF)

    @pl.when(phase == 1)
    def _():
        g1 = gh1_ref[here, :]
        dwout[...] += tn(o_ref[...], g1)
        gm_ref[...] = nt(g1, wout[...]).astype(BF)
        units = [(slice(g * GROUP, (g + 1) * GROUP), p) for g in range(rows // GROUP) for p in range(width // GROUP)]

        def head_pair(at, p, i):
            return qkv_ref[at, i * width + p * GROUP : i * width + (p + 1) * GROUP]

        for at, p in units:
            dp = nt(gm_ref[at, p * GROUP : (p + 1) * GROUP], two_heads(head_pair(at, p, 2)))
            for h in range(2):
                lanes = slice((2 * p + h) * GROUP, (2 * p + h + 1) * GROUP)
                gs_ref[at, lanes] = softmax_back(p_ref[at, lanes], dp[:, h * GROUP : (h + 1) * GROUP])
        for at, p in units:
            gs = gs_ref[at, 2 * p * GROUP : 2 * (p + 1) * GROUP]
            gq_ref[at, p * GROUP : (p + 1) * GROUP] = (nn(gs, two_heads(head_pair(at, p, 1))) * HD**-0.5).astype(BF)
            gq_ref[at, width + p * GROUP : width + (p + 1) * GROUP] = one_of_two(tn(gs, head_pair(at, p, 0))).astype(BF)
            soft = p_ref[at, p * 2 * GROUP : (p + 1) * 2 * GROUP]
            gm = gm_ref[at, p * GROUP : (p + 1) * GROUP]
            gq_ref[at, 2 * width + p * GROUP : 2 * width + (p + 1) * GROUP] = one_of_two(tn(soft, gm)).astype(BF)
        for t in range(rows // chunk):
            at = slice(t * chunk, (t + 1) * chunk)
            n, r = normal_of(c_ref[at, :].astype(F32))
            u_ref[at, :] = (n * ga[...] + sa[...]).astype(BF)
            da = nt(gq_ref[at, :], win[...])
            dga[...] += column_sum(da * n)
            dsa[...] += column_sum(da)
            grad = gh1_ref[pl.ds(pl.multiple_of(step * rows + t * chunk, chunk), chunk), :].astype(F32) + norm_back(da, n, r, ga[...])
            gc_ref[at, :] = grad.astype(gc_ref.dtype)
        dwin[...] += tn(u_ref[...], gq_ref[...])

    if net_sizes:

        @pl.when(now == 2 * steps - 1)
        def _():
            some = width // n_wide
            for owner in range(n_wide):
                z, core = owner // 2, owner % 2
                mine = slice(owner * some, (owner + 1) * some)
                at_grads[z, core, :, : 3 * width] = dwin[mine, :].astype(BF)
                at_grads[z, core, :, 3 * width :] = dwout[mine, :].astype(BF)
            column, places = 0, []
            for acc in (dga, dsa, dgb, dsb, ddb, dqv, dub, dpb):
                row[:, column : column + acc.shape[1]] = acc[...]
                places.append((column, acc.shape[1]))
                column += acc.shape[1]
            row[:, column:] = word_row[...]
            for ref in word_vectors(row, *word_sizes):
                places.append((column, ref.shape[1]))
                column += ref.shape[1]
            att.start()
            rowsum.start()
            word.finish()
            ff.finish()
            att.over_dp()
            rowsum.over_dp()
            att.over_z()
            rowsum.over_z()
            att.back_over_dp()
            rowsum.finish(outs[3], places)
            att.finish()
            copies = [pltpu.make_async_copy(piece.done, out, keep.at[i]) for i, (piece, out) in enumerate(zip((word, ff, att), outs))]
            for copy in copies:
                copy.start()
            for copy in copies:
                copy.wait()


def whole_block(shape):
    return pl.BlockSpec(shape, lambda *_: (0,) * len(shape), pipeline_mode=pl.Buffered(1))


def whole_out(shape):
    return pl.BlockSpec(shape, lambda *_: (0,) * len(shape))


def char_backward(gx, chars, counts, saved, weights, chars_per, rows, net_sizes=None, word_grads=None, word_row=None):
    total, width = chars.shape
    win, wout, wup, wdn, wpj, vec = weights
    pooled, qkv, soft, mixed, h1, h2, m, s = saved
    words, cw = total // chars_per, rows // chars_per
    ff, out = wup.shape[1], wpj.shape[1]
    steps = total // rows

    def early(count, columns):
        return pl.BlockSpec((count, columns), lambda p, i: (i + p * (steps - 1 - i), 0))

    def late(count, columns):
        return pl.BlockSpec((count, columns), lambda p, i: (i * p, 0))

    accs = [(1, width), (1, width), (width, 3 * width), (width, width), (1, width), (1, width), (width, ff), (1, ff),
            (width, ff), (1, width), (1, width), (width, out), (1, out)]
    in_specs = [early(cw, out), late(rows, width), whole_block(counts.shape), late(rows, 3 * width), late(rows, 2 * width),
                late(rows, width), early(rows, width), early(rows, width), early(rows, ff), early(rows, ff),
                whole_block(pooled.shape), whole_block(gx.shape)] + [whole_block(w.shape) for w in weights]
    operands = [gx, chars, counts, qkv, soft, mixed, h1, h2, m, s, pooled, gx, *weights]
    scratch = [pltpu.VMEM((total, width), BF), pltpu.VMEM((rows, width), BF), pltpu.VMEM((rows, width), BF),
               pltpu.VMEM((rows, ff), BF), pltpu.VMEM((rows, 3 * width), BF), pltpu.VMEM((rows, 2 * width), BF)]
    if net_sizes:
        n_dp, n_wide = net_sizes
        n_z, some = n_wide // 2, width // n_wide
        word_rows, word_width = word_grads.shape[2:]
        wide_d = n_wide * word_rows
        word_ff = word_row.shape[1] - 5 * wide_d
        operands += [word_grads, word_row]
        in_specs += [pl.BlockSpec(memory_space=pl.ANY), whole_block(word_row.shape)]
        ff_width, at_width = ff + out + ff, 4 * width
        row_width = 6 * width + ff + out + word_row.shape[1]
        word_sizes = (wide_d, word_ff)
        sums = [(n_dp, word_rows, word_width // n_dp), (n_dp, some, ff_width // n_dp), (n_dp, some, at_width // n_dp)]
        pieces = sum(padded(n // n_wide) for n in [width] * 6 + [ff, out] + [wide_d] * 5 + [word_ff])
        out_shapes = [jax.ShapeDtypeStruct((total, width), BF)] + [jax.ShapeDtypeStruct(a, BF) for a in sums] + [jax.ShapeDtypeStruct((1, pieces), F32)]
        out_specs = [late(rows, width)] + [pl.BlockSpec(memory_space=pl.ANY)] * 3 + [whole_out((1, pieces))]
        scratch = (
            [pltpu.VMEM(a, F32) for a in accs]
            + scratch
            + [pltpu.VMEM((n_z, 2, some, ff_width), BF), pltpu.VMEM((n_z, 2, some, at_width), BF), pltpu.VMEM((1, row_width), F32)]
            + Reduce.scratch(n_dp, n_z, word_rows, word_width)
            + Reduce.scratch(n_dp, n_z, some, ff_width)
            + Reduce.scratch(n_dp, n_z, some, at_width)
            + ReduceRows.scratch(n_dp, n_z, row_width)[1:]
            + [pltpu.SemaphoreType.DMA((3,))]
        )
        params = pltpu.CompilerParams(vmem_limit_bytes=VMEM_LIMIT, collective_id=3, has_side_effects=True)
    else:
        word_sizes = None
        out_shapes = [jax.ShapeDtypeStruct(a, F32) for a in [(total, width)] + accs]
        out_specs = [late(rows, width)] + [whole_out(a) for a in accs]
        params = pltpu.CompilerParams(vmem_limit_bytes=VMEM_LIMIT)
    return pl.pallas_call(
        functools.partial(char_back_kernel, chars_per, steps, net_sizes, word_sizes),
        grid=(2, steps),
        in_specs=in_specs,
        out_specs=out_specs,
        out_shape=out_shapes,
        scratch_shapes=scratch,
        compiler_params=params,
        name="char_backward",
    )(*operands)


def unpack(done, outs):
    rows, span = done.shape[1:]
    for ref, first, columns, side in outs:
        for k in range(side):
            for at in range(0, columns, GROUP):
                column = first + k * columns + at
                q, lane = column // span, column % span
                ref[k * rows : (k + 1) * rows, at : at + GROUP] = done[q, :, lane : lane + GROUP].astype(F32)


def output_kernel(gc_low, word_done, ff_done, at_done, row, gc_ref, *outs):
    gc_ref[...] = gc_low[...].astype(F32)

    @pl.when(pl.program_id(0) == 0)
    def _():
        (
            oga, osa, owin, owout, ogb, osb, oup, oub, odn, odb, oqv, opj, opb,
            xga, xsa, xwin, xwout, xgb, xsb, xup, xub, xdn, xdb,
        ) = outs
        for done, across, down in ((word_done, (xwin, xwout, xup), xdn), (ff_done, (oup, opj), odn), (at_done, (owin, owout), None)):
            places, column = [], 0
            for ref in across:
                places.append((ref, column, ref.shape[1], 1))
                column += ref.shape[1]
            if down is not None:
                places.append((down, column, down.shape[1], down.shape[0] // done.shape[1]))
            unpack(done, places)
        at = 0
        for ref in (oga, osa, ogb, osb, odb, oqv, oub, opb, xga, xsa, xgb, xsb, xdb, xub):
            ref[...] = row[:, at : at + ref.shape[1]]
            at += padded(ref.shape[1])


def outputs_of(gc_low, word_done, ff_done, at_done, row, shapes, rows):
    total, width = gc_low.shape
    by_row = pl.BlockSpec((rows, width), lambda i: (i, 0))
    wholes = [word_done, ff_done, at_done, row]
    return pl.pallas_call(
        output_kernel,
        grid=(total // rows,),
        in_specs=[by_row] + [whole_block(a.shape) for a in wholes],
        out_specs=[by_row] + [whole_out(a) for a in shapes],
        out_shape=[jax.ShapeDtypeStruct(a, F32) for a in [(total, width), *shapes]],
        compiler_params=pltpu.CompilerParams(vmem_limit_bytes=VMEM_LIMIT),
        name="outputs",
    )(gc_low, *wholes)


def char_forward_kernel(chars_per, steps, net_sizes, lengths, *refs):
    c_ref, cnt_ref, *refs = refs
    if net_sizes:
        net = Net(*net_sizes)
        shards, word_shards, vectors, refs = refs[:5], refs[5:9], refs[9:23], refs[23:]
        inbox, vec, *refs = refs
        char_out, word_out, refs = refs[:5], refs[5:9], refs[9:]
    else:
        win, wout, wup, wdn, wpj, vec, *refs = refs
        x_ref, *refs = refs
    pooled_ref, qkv_ref, p_ref, o_ref, h1_ref, h2_ref, m_ref, s_ref, *refs = refs
    h1_all, *refs = refs
    rows, width = c_ref.shape
    phase, step = pl.program_id(0), pl.program_id(1)
    now = phase * steps + step
    chunk = min(rows, 512)
    cw = chunk // chars_per
    words = rows // chars_per

    if net_sizes:
        x_out, win, wout, wup, wdn, wpj, pieces, piece, *refs = refs
        gather = Gather(net, (*shards, piece), [win, wout, wup, wdn, wpj, pieces], *refs[:3])
        shared = SharedGather(net, word_shards, word_out, *refs[3:10])
        exchange = Exchange(net, x_out, inbox, *refs[10:13])
        keep = refs[13]
        first, later = (5, 0, 1), (2, 3, 4)

        @pl.when(now == 0)
        def _():
            peers = [net.wide_peer(j)[1] for j in range(1, net.n_wide)] + [net.dp_peer(j)[1] for j in range(1, net.n_dp)]
            net.greet(peers)
            net.met(peers)
            for ref, (at, length) in zip(vectors, lengths):
                some = length // net.n_wide
                piece[0, :, at : at + some] = ref[...].astype(F32).reshape(1, some)
            for a in first + later:
                gather.start(a)
            for a in first:
                gather.relay(a)
            shared.start()
            for a in first:
                gather.finish(a)
            column = 0
            for at, length in lengths:
                some = length // net.n_wide
                row = jnp.concatenate([pieces[w, :, at : at + some] for w in range(net.n_wide)], 1)
                vec[:, column : column + length] = row
                column += length

        @pl.when(now == 3 * steps // 8)
        def _():
            for a in later:
                gather.relay(a)

        @pl.when(now == steps)
        def _():
            for a in later:
                gather.finish(a)
            for a in range(5):
                pltpu.make_async_copy(gather.wholes[a], char_out[a], keep.at[a]).start()

        for a in range(4):

            @pl.when(now == steps - steps // 4 + a * steps // 8)
            def _(a=a):
                shared.relay(a)

            @pl.when(now == 2 * steps - 5 * steps // 8 + a * steps // 8)
            def _(a=a):
                shared.pass_on(a)

    ga, sa, gb, sb, db, qv, ub, pb = char_vectors(vec, width, wup.shape[1], wpj.shape[1])

    def block(t):
        return pl.ds(pl.multiple_of(step * rows + t * chunk, chunk), chunk)

    @pl.when(phase == 0)
    def _():
        n, _ = normal_of(c_ref[...].astype(F32))
        a = (n * ga[...] + sa[...]).astype(BF)
        qkv = nn(a, win[...])
        qkv_ref[:, :width] = (qkv[:, :width] * HD**-0.5).astype(BF)
        qkv_ref[:, width:] = qkv[:, width:].astype(BF)
        ri = lax.broadcasted_iota(jnp.int32, (GROUP, GROUP), 0) // chars_per
        ci = lax.broadcasted_iota(jnp.int32, (GROUP, GROUP), 1) // chars_per
        same = ri == ci
        units = [(g, slice(g * GROUP, (g + 1) * GROUP), p) for g in range(rows // GROUP) for p in range(width // GROUP)]

        def head_pair(at, p, i):
            return qkv_ref[at, i * width + p * GROUP : i * width + (p + 1) * GROUP]

        valid = key_bias(cnt_ref[pl.ds(step, 1), :].astype(F32), chars_per)
        for g, at, p in units:
            bias = jnp.where(same, jnp.broadcast_to(valid[:1, g * GROUP : (g + 1) * GROUP], (GROUP, GROUP)), NEG)
            s = nt(head_pair(at, p, 0), two_heads(head_pair(at, p, 1)))
            for h in range(2):
                p_ref[at, (2 * p + h) * GROUP : (2 * p + h + 1) * GROUP] = softmax_low(s[:, h * GROUP : (h + 1) * GROUP] + bias)
        for _, at, p in units:
            o_ref[at, p * GROUP : (p + 1) * GROUP] = nn(p_ref[at, 2 * p * GROUP : 2 * (p + 1) * GROUP], two_heads(head_pair(at, p, 2))).astype(BF)
        for t in range(rows // chunk):
            at = slice(t * chunk, (t + 1) * chunk)
            h1 = c_ref[at, :].astype(F32) + nn(o_ref[at, :], wout[...])
            h1_ref[at, :] = h1.astype(BF)
            h1_all[block(t), :] = h1

    @pl.when(phase == 1)
    def _():
        counts = as_column(cnt_ref[pl.ds(step, 1), :].astype(F32))
        for t in range(rows // chunk):
            at = slice(t * chunk, (t + 1) * chunk)
            wat = slice(t * cw, (t + 1) * cw)
            h1 = h1_all[block(t), :]
            n, _ = normal_of(h1)
            u = (n * gb[...] + sb[...]).astype(BF)
            m, s = gelu_and_slope(nn(u, wup[...]) + ub[...])
            m_ref[at, :] = m.astype(BF)
            s_ref[at, :] = s.astype(BF)
            h2 = h1 + (nn(m_ref[at, :], wdn[...]) + db[...])
            h2_ref[at, :] = h2.astype(BF)
            om = pool_weights(h2, qv[...], counts[wat, :], chars_per)
            pooled_ref[wat, :] = jnp.sum(om * h2.reshape(cw, chars_per, width), 1).astype(BF)
        x = (nn(pooled_ref[...], wpj[...]) + pb[...]).astype(BF)
        if net_sizes:
            cap = x_out.shape[1]
            first_word = step * words
            target = first_word // cap
            x_out[target, pl.ds(pl.multiple_of(lax.rem(first_word, cap), words), words)] = x
            pl.when(lax.rem(first_word + words, cap) == 0)(lambda: exchange.send_block(target))
        else:
            x_ref[...] = x

    if net_sizes:

        @pl.when(now == 2 * steps - 1)
        def _():
            for a in range(4):
                shared.finish(a)
            exchange.finish()
            for a in range(5):
                pltpu.make_async_copy(gather.wholes[a], char_out[a], keep.at[a]).wait()


def char_forward(chars, counts, weights, chars_per, rows, net_sizes=None, word_shards=None, vectors=None, cap=None):
    total, width = chars.shape
    words, cw = total // chars_per, rows // chars_per
    ff, out = weights[2].shape[1], weights[4].shape[1]
    steps = total // rows

    def early(count, columns):
        return pl.BlockSpec((count, columns), lambda p, i: (i + p * (steps - 1 - i), 0))

    def late(count, columns):
        return pl.BlockSpec((count, columns), lambda p, i: (i * p, 0))

    saved = [((words, width), BF, cw, late), ((total, 3 * width), BF, rows, early), ((total, 2 * width), BF, rows, early),
             ((total, width), BF, rows, early), ((total, width), BF, rows, early), ((total, width), BF, rows, late),
             ((total, ff), BF, rows, late), ((total, ff), BF, rows, late)]
    saved_specs = [where(count, s[1]) for s, _, count, where in saved]
    saved_shapes = [jax.ShapeDtypeStruct(s, d) for s, d, _, _ in saved]
    in_specs = [early(rows, width), whole_block(counts.shape)]
    operands = [chars, counts]
    scratch = [pltpu.VMEM((total, width), F32)]
    anywhere = pl.BlockSpec(memory_space=pl.ANY)
    if net_sizes:
        n_dp, n_wide = net_sizes
        n_z = n_wide // 2
        lengths, room = [], 0
        for v in vectors:
            lengths.append((room, v.shape[0] * n_wide))
            room += padded(v.shape[0])
        in_specs += [anywhere] * 9 + [whole_block(v.shape) for v in vectors]
        operands += [*weights, *word_shards, *vectors]
        vec_shape = jax.ShapeDtypeStruct((1, sum(length for _, length in lengths)), F32)
        grown = lambda a: jax.ShapeDtypeStruct((a.shape[0] * n_wide, a.shape[1]), a.dtype)
        fulls = [grown(a) for a in weights]
        out_specs = [anywhere, whole_out(vec_shape.shape)] + [anywhere] * 9 + saved_specs
        out_shapes = [jax.ShapeDtypeStruct((n_wide, cap, out), BF), vec_shape, *fulls, *(grown(a) for a in word_shards), *saved_shapes]
        scratch += (
            [pltpu.VMEM((n_wide, cap, out), BF)]
            + [pltpu.VMEM(a.shape, a.dtype) for a in fulls]
            + [pltpu.VMEM((n_wide, 1, room), F32), pltpu.VMEM((1, 1, room), F32)]
            + Gather.scratch(6, n_z)
            + SharedGather.scratch(4, n_dp, n_z)
            + Exchange.scratch(n_wide)
            + [pltpu.SemaphoreType.DMA((5,))]
        )
        params = pltpu.CompilerParams(vmem_limit_bytes=VMEM_LIMIT, collective_id=1, has_side_effects=True)
    else:
        lengths = None
        in_specs += [whole_block(w.shape) for w in weights]
        operands += [*weights]
        out_specs = [late(cw, out)] + saved_specs
        out_shapes = [jax.ShapeDtypeStruct((words, out), BF), *saved_shapes]
        params = pltpu.CompilerParams(vmem_limit_bytes=VMEM_LIMIT)
    return pl.pallas_call(
        functools.partial(char_forward_kernel, chars_per, steps, net_sizes, lengths),
        grid=(2, steps),
        in_specs=in_specs,
        out_specs=out_specs,
        out_shape=out_shapes,
        scratch_shapes=scratch,
        compiler_params=params,
        name="char_forward",
    )(*operands)


def word_kernel(slot_cap, net_sizes, *refs):
    arrived, bucket, assign, segment, grad_ref, win, wout, wup, wdn, vec, out_ref, back_out, *refs = refs
    length, width = grad_ref.shape
    ff = wup.shape[1]
    if net_sizes:
        net = Net(*net_sizes)
        word_grads, word_row, *refs = refs
        dga, dsa, dgb, dsb, ddb, dub = word_vectors(word_row, width, ff)
    else:
        dga, dsa, dwin, dwout, dgb, dsb, dwup, dub, dwdn, ddb, *refs = refs
    qkv_ref, p_ref, mix_ref, h_ref, s_ref, gq_ref, *refs = refs
    ga, sa, gb, sb, db, ub = word_vectors(vec, width, ff)
    owners = assign.shape[1]
    slots = owners * slot_cap
    if net_sizes:
        back_ref, *sems = refs
        exchange = Exchange(net, back_ref, back_out, *sems)
        peers = [net.wide_peer(j)[1] for j in range(1, net.n_wide)]
        net.greet(peers)
    named = jnp.where(bucket[...] == lax.broadcasted_iota(jnp.int32, (owners, length), 0), 1.0, 0.0)
    ri = lax.broadcasted_iota(jnp.int32, (length, length), 0)
    ci = lax.broadcasted_iota(jnp.int32, (length, length), 1)
    earlier = nn(named.astype(BF), jnp.where(ri < ci, 1.0, 0.0).astype(BF))
    served = as_column(assign[...].astype(F32)) * slot_cap
    slot = jnp.sum(named * (served + earlier), 0, keepdims=True).astype(jnp.int32)
    hot = jnp.where(lax.broadcasted_iota(jnp.int32, (slots, length), 0) == slot, 1.0, 0.0).astype(BF)
    x = tn(hot, arrived[...].reshape(slots, width))
    n1, r1 = normal_of(x)
    a = (n1 * ga[...] + sa[...]).astype(BF)
    qkv = nn(a, win[...])
    qkv_ref[:, :width] = (qkv[:, :width] * HD**-0.5).astype(BF)
    qkv_ref[:, width:] = qkv[:, width:].astype(BF)
    seg = segment[...].astype(F32)
    bias = jnp.where((seg == as_column(seg)) & (ci <= ri), 0.0, NEG)

    def pair(p):
        return [qkv_ref[:, i * width + p * GROUP : i * width + (p + 1) * GROUP] for i in range(3)]

    for p in range(width // GROUP):
        q, k, v = pair(p)
        s = nt(q, two_heads(k))
        soft = jnp.concatenate([softmax_low(s[:, h * length : (h + 1) * length] + bias) for h in range(2)], 1)
        p_ref[:, 2 * p * length : (2 * p + 2) * length] = soft
        mix_ref[:, p * GROUP : (p + 1) * GROUP] = nn(soft, two_heads(v)).astype(BF)
    inner = x + nn(mix_ref[...], wout[...])
    n2, r2 = normal_of(inner)
    u = (n2 * gb[...] + sb[...]).astype(BF)
    h, slope = gelu_and_slope(nn(u, wup[...]) + ub[...])
    h_ref[...] = h.astype(BF)
    s_ref[...] = slope
    out_ref[...] = inner + (nn(h_ref[...], wdn[...]) + db[...])
    g = grad_ref[...]
    gz = (nt(g, wdn[...]) * s_ref[...]).astype(BF)
    du = nt(gz, wup[...])
    g1 = g.astype(F32) + norm_back(du, n2, r2, gb[...])
    g1_low = g1.astype(BF)
    gm = nt(g1_low, wout[...]).astype(BF)
    for p in range(width // GROUP):
        q, k, v = pair(p)
        gmp = gm[:, p * GROUP : (p + 1) * GROUP]
        soft = p_ref[:, 2 * p * length : (2 * p + 2) * length]
        dp = nt(gmp, two_heads(v))
        gs = jnp.concatenate([softmax_back(soft[:, h * length : (h + 1) * length], dp[:, h * length : (h + 1) * length]) for h in range(2)], 1)
        gq_ref[:, p * GROUP : (p + 1) * GROUP] = (nn(gs, two_heads(k)) * HD**-0.5).astype(BF)
        gq_ref[:, width + p * GROUP : width + (p + 1) * GROUP] = one_of_two(tn(gs, q)).astype(BF)
        gq_ref[:, 2 * width + p * GROUP : 2 * width + (p + 1) * GROUP] = one_of_two(tn(soft, gmp)).astype(BF)
    da = nt(gq_ref[...], win[...])
    gx = (g1 + norm_back(da, n1, r1, ga[...])).astype(BF)
    back = nn(hot, gx).astype(BF).reshape(owners, slot_cap, width)
    if net_sizes:
        back_ref[...] = back
        net.met(peers)
        exchange.send_all()
        some = width // net.n_wide
        side = ff // width

        def put(value, column):
            value = value.astype(BF)
            for w in range(net.n_wide):
                word_grads[w // 2, w % 2, :, column : column + value.shape[1]] = value[w * some : (w + 1) * some]

        put(tn(a, gq_ref[...]), 0)
        put(tn(mix_ref[...], g1_low), 3 * width)
        put(tn(u, gz), 4 * width)
        down = tn(h_ref[...], g).astype(BF)
        for w in range(net.n_wide):
            for k in range(side):
                first = (w * side + k) * some
                column = 4 * width + ff + k * width
                word_grads[w // 2, w % 2, :, column : column + width] = down[first : first + some]
    else:
        back_out[...] = back
        dwin[...] = tn(a, gq_ref[...])
        dwout[...] = tn(mix_ref[...], g1_low)
        dwup[...] = tn(u, gz)
        dwdn[...] = tn(h_ref[...], g)
    dga[...] = column_sum(da * n1)
    dsa[...] = column_sum(da)
    dgb[...] = column_sum(du * n2)
    dsb[...] = column_sum(du)
    dub[...] = column_sum(gz.astype(F32))
    ddb[...] = column_sum(g.astype(F32))
    if net_sizes:
        exchange.finish()


def word_block(arrived, bucket, assign, segments, grad, weights, slot_cap, net_sizes=None):
    length, width = grad.shape
    ff = weights[2].shape[1]
    owners = assign.shape[1]
    low = lambda *s: jax.ShapeDtypeStruct(s, BF)
    full = lambda *s: jax.ShapeDtypeStruct(s, F32)
    vmem = pl.BlockSpec(memory_space=pltpu.VMEM)
    out_shapes, out_specs = [full(length, width), low(owners, slot_cap, width)], [vmem, vmem]
    scratch = [pltpu.VMEM((length, 3 * width), BF), pltpu.VMEM((length, width // HD * length), BF), pltpu.VMEM((length, width), BF),
               pltpu.VMEM((length, ff), BF), pltpu.VMEM((length, ff), F32), pltpu.VMEM((length, 3 * width), BF)]
    if net_sizes:
        n_dp, n_wide = net_sizes
        out_shapes += [low(n_wide // 2, 2, width // n_wide, 4 * width + 2 * ff), full(1, 5 * width + ff)]
        out_specs = [vmem, pl.BlockSpec(memory_space=pl.ANY), vmem, vmem]
        scratch += [pltpu.VMEM((owners, slot_cap, width), BF)] + Exchange.scratch(n_wide)
        params = pltpu.CompilerParams(vmem_limit_bytes=VMEM_LIMIT, collective_id=2, has_side_effects=True)
    else:
        row = full(1, width)
        out_shapes += [row, row, full(width, 3 * width), full(width, width), row, row, full(width, ff), full(1, ff), full(ff, width), row]
        out_specs += [vmem] * 10
        params = pltpu.CompilerParams(vmem_limit_bytes=VMEM_LIMIT)
    return pl.pallas_call(
        functools.partial(word_kernel, slot_cap, net_sizes),
        in_specs=[vmem] * 10,
        out_specs=out_specs,
        out_shape=out_shapes,
        scratch_shapes=scratch,
        compiler_params=params,
        name="word_block",
    )(arrived, bucket, assign, segments, grad, *weights)


def gathered(shard):
    return lax.all_gather(shard, "wide", axis=0, tiled=True)


def exchanged(blocks):
    return lax.all_to_all(blocks, "wide", split_axis=0, concat_axis=0, tiled=True)


def summed(grad):
    part = lax.psum_scatter(grad.astype(BF), "wide", scatter_dimension=0, tiled=True)
    return lax.psum(part, "dp").astype(F32)


def shards(
    chars, char_counts, buckets, assign, segments,
    char_gain, char_shift, char_inproj, char_outproj, char_gain_mid, char_shift_mid, char_up, char_up_bias, char_down, char_down_bias,
    pool_query, char_proj, char_proj_bias,
    word_gain, word_shift, word_inproj, word_outproj, word_gain_mid, word_shift_mid, word_up, word_up_bias, word_down, word_down_bias,
    out_grad,
):
    n_dp, n_wide = lax.axis_size("dp"), lax.axis_size("wide")
    cap, chars_per, width = chars.shape[2:]
    slots = n_wide * cap
    rows = chars.reshape(slots * chars_per, width)
    block = min(1024, rows.shape[0])
    counts = char_counts.reshape(-1, block // chars_per)
    char_shards = (char_inproj, char_outproj, char_up, char_down, char_proj)
    word_shards = (word_inproj, word_outproj, word_up, word_down)
    vectors = (char_gain, char_shift, char_gain_mid, char_shift_mid, char_down_bias, pool_query, char_up_bias, char_proj_bias,
               word_gain, word_shift, word_gain_mid, word_shift_mid, word_down_bias, word_up_bias)
    fast = (
        all(m.shape[0] % 16 == 0 for m in char_shards)
        and all(m.shape[0] % (16 * n_dp) == 0 for m in word_shards)
        and cap % (block // chars_per) == 0
        and (4 * width) % (GROUP * n_dp) == 0
        and n_wide % 2 == 0
    )
    bucket, names, upstream = buckets.reshape(1, -1), assign[None], out_grad[0]
    if fast:
        sizes = (n_dp, n_wide)
        arrived, vec, *rest = char_forward(rows, counts, char_shards, chars_per, block, sizes, word_shards, vectors, cap)
        char_full, word_full, saved = rest[:5], rest[5:9], rest[9:]
        result, returned, word_grads, word_row = word_block(arrived, bucket, names, segments, upstream, (*word_full, vec), cap, sizes)
        incoming = returned.reshape(slots, -1)
        sums = char_backward(incoming, rows, counts, saved, (*char_full, vec), chars_per, block, sizes, word_grads, word_row)
        params = (char_gain, char_shift, char_inproj, char_outproj, char_gain_mid, char_shift_mid, char_up, char_up_bias, char_down,
                  char_down_bias, pool_query, char_proj, char_proj_bias, word_gain, word_shift, word_inproj, word_outproj, word_gain_mid,
                  word_shift_mid, word_up, word_up_bias, word_down, word_down_bias)
        shapes = [p.shape if p.ndim == 2 else (1, *p.shape) for p in params]
        char_grads, *grads = outputs_of(*sums, shapes, block)
        grads = [g[0] if g.shape[0] == 1 else g for g in grads]
    else:
        vec = jnp.concatenate([gathered(v) for v in vectors]).astype(F32)[None]
        char_full, word_full = [gathered(m) for m in char_shards], [gathered(m) for m in word_shards]
        outgoing, *saved = char_forward(rows, counts, (*char_full, vec), chars_per, block)
        arrived = exchanged(outgoing.reshape(n_wide, cap, -1))
        result, back, *word_grads = word_block(arrived, bucket, names, segments, upstream, (*word_full, vec), cap)
        incoming = exchanged(back).reshape(slots, -1)
        char_grads, *grads = char_backward(incoming, rows, counts, saved, (*char_full, vec), chars_per, block)
        grads[8] = grads[8].T
        grads = [summed(g[0] if g.shape[0] == 1 else g) for g in grads + word_grads]
    return (result[None], char_grads.reshape(chars.shape), *grads)


def solution(mesh):
    whole, split = ("dp", "wide"), "wide"
    row, flat = P(split, None), P(split)
    word = [flat, flat, row, row, flat, flat, row, flat, row, flat]
    char = word + [flat, row, flat]
    chars = P(whole, None, None, None, None)
    three = P(whole, None, None)
    return jax.shard_map(
        shards,
        mesh=mesh,
        in_specs=(chars, three, three, P(), P(whole, None), *char, *word, three),
        out_specs=(three, chars, *char, *word),
        check_vma=False,
    )
```

```python
import functools

import jax
import jax.numpy as jnp
from jax import lax
from jax.experimental import pallas as pl
from jax.experimental.pallas import tpu as pltpu
from jax.sharding import PartitionSpec as P

EPS = 1e-05
NEG = -1e30
ROOT_HALF = 0.7071067811865476
INV_ROOT_TWO_PI = 0.3989422804014327
HD = 64
GROUP = 128
F32 = jnp.float32
BF = jnp.bfloat16
MESH = pl.DeviceIdType.MESH
VMEM_LIMIT = 60 << 20
WORD_PARTS = 3


def nn(a, b):
    return lax.dot_general(a, b, (((1,), (0,)), ((), ())), preferred_element_type=F32)


def nt(a, b):
    return lax.dot_general(a, b, (((1,), (1,)), ((), ())), preferred_element_type=F32)


def tn(a, b):
    return lax.dot_general(a, b, (((0,), (0,)), ((), ())), preferred_element_type=F32)


def padded(lanes):
    return -(-lanes // GROUP) * GROUP


def column_sum(x):
    return jnp.sum(x, 0, keepdims=True)


def normal_of(x):
    c = x - jnp.mean(x, -1, keepdims=True)
    r = lax.rsqrt(jnp.mean(c * c, -1, keepdims=True) + EPS)
    return c * r, r


def norm_back(d, n, r, g):
    dg = d * g
    return r * (dg - jnp.mean(dg, -1, keepdims=True) - n * jnp.mean(dg * n, -1, keepdims=True))


def gelu_and_slope(z):
    cdf = 0.5 * (1.0 + lax.erf(z * ROOT_HALF))
    return z * cdf, cdf + z * jnp.exp(-0.5 * z * z) * INV_ROOT_TWO_PI


def softmax_low(s):
    ex = jnp.exp(s - jnp.max(s, -1, keepdims=True))
    return (ex * (1.0 / jnp.sum(ex, -1, keepdims=True))).astype(BF)


def softmax_back(soft, d):
    soft = soft.astype(F32)
    return (soft * (d - jnp.sum(d * soft, -1, keepdims=True))).astype(BF)


def two_heads(t):
    left = lax.broadcasted_iota(jnp.int32, t.shape, 1) < HD
    zero = jnp.zeros_like(t)
    return jnp.concatenate([jnp.where(left, t, zero), jnp.where(left, zero, t)], 0)


def one_of_two(t):
    half = t.shape[0] // 2
    left = lax.broadcasted_iota(jnp.int32, (half, t.shape[1]), 1) < HD
    return jnp.where(left, t[:half], t[half:])


def as_column(row):
    n = row.shape[1]
    same = lax.broadcasted_iota(jnp.int32, (n, n), 0) == lax.broadcasted_iota(jnp.int32, (n, n), 1)
    return jnp.sum(jnp.where(same, jnp.broadcast_to(row, (n, n)), 0.0), -1, keepdims=True)


def key_bias(row, chars_per):
    n = row.shape[1]
    lanes = n * chars_per
    of_word = lax.broadcasted_iota(jnp.int32, (n, lanes), 1) // chars_per == lax.broadcasted_iota(jnp.int32, (n, lanes), 0)
    counts = nn(jnp.broadcast_to(row, (8, n)).astype(BF), jnp.where(of_word, 1.0, 0.0).astype(BF))
    place = lax.rem(lax.broadcasted_iota(jnp.int32, (8, lanes), 1), chars_per)
    return jnp.where(place.astype(F32) < counts, 0.0, NEG)


def pool_weights(h2, query, counts, chars_per):
    rows = h2.shape[0]
    words = rows // chars_per
    e = jnp.sum(h2 * query, -1, keepdims=True) * (h2.shape[1] ** -0.5)
    e = e.reshape(words, chars_per, 1)
    place = lax.broadcasted_iota(jnp.int32, (words, chars_per, 1), 1).astype(F32)
    e = jnp.where(place < counts.reshape(words, 1, 1), e, NEG)
    ex = jnp.exp(e - jnp.max(e, 1, keepdims=True))
    return ex / jnp.sum(ex, 1, keepdims=True)


class Net:
    def __init__(self, n_dp, n_wide):
        self.n_dp, self.n_wide, self.n_z = n_dp, n_wide, n_wide // 2
        self.dp, self.wide = lax.axis_index("dp"), lax.axis_index("wide")
        self.z, self.core = self.wide // 2, lax.rem(self.wide, 2)
        self.sibling = (self.dp, self.wide + 1 - 2 * self.core)

    def z_peer(self, j):
        z = lax.rem(self.z + j, self.n_z)
        return z, (self.dp, 2 * z + self.core)

    def dp_peer(self, j):
        q = lax.rem(self.dp + j, self.n_dp)
        return q, (q, self.wide)

    def wide_peer(self, j):
        w = lax.rem(self.wide + j, self.n_wide)
        return w, (self.dp, w)

    def greet(self, peers):
        barrier = pltpu.get_barrier_semaphore()
        for peer in peers:
            pl.semaphore_signal(barrier, inc=1, device_id=peer, device_id_type=MESH)

    def met(self, peers):
        pl.semaphore_wait(pltpu.get_barrier_semaphore(), len(peers))


def remote(src, dst, send, recv, peer):
    return pltpu.make_async_remote_copy(src_ref=src, dst_ref=dst, send_sem=send, recv_sem=recv, device_id=peer, device_id_type=MESH)


class Reduce:
    def __init__(self, net, grads, first, kept, from_core, part, from_dp, from_z, done, sems):
        self.net, self.grads = net, grads
        self.columns = pl.ds(first, kept.shape[-1])
        self.kept, self.from_core, self.part = kept, from_core, part
        self.from_dp, self.from_z, self.done = from_dp, from_z, done
        self.send, self.recv = sems
        self.span = part.shape[-1]

    @staticmethod
    def scratch(n_dp, n_z, rows, width):
        span = width // n_dp
        count = 2 + 2 * n_dp + n_z
        return [
            pltpu.VMEM((n_z, rows, width), BF),
            pltpu.VMEM((n_z, rows, width), BF),
            pltpu.VMEM((n_z, rows, span), BF),
            pltpu.VMEM((n_dp - 1, n_z, rows, span), BF),
            pltpu.VMEM((n_z - 1, rows, span), BF),
            pltpu.VMEM((n_dp, rows, span), BF),
            pltpu.SemaphoreType.DMA((count,)),
            pltpu.SemaphoreType.DMA((count,)),
        ]

    def lanes(self, q):
        return pl.ds(pl.multiple_of(q * self.span, GROUP), self.span)

    def to_core(self):
        net = self.net
        return remote(self.grads.at[:, 1 - net.core, :, self.columns], self.from_core, self.send.at[0], self.recv.at[0], net.sibling)

    def own(self):
        return pltpu.make_async_copy(self.grads.at[:, self.net.core, :, self.columns], self.kept, self.recv.at[1])

    def to_dp(self, j):
        q, peer = self.net.dp_peer(j)
        return remote(self.kept.at[:, :, self.lanes(q)], self.from_dp.at[j - 1], self.send.at[1 + j], self.recv.at[1 + j], peer)

    def to_z(self, j):
        z, peer = self.net.z_peer(j)
        at = 1 + self.net.n_dp + j
        return remote(self.part.at[z], self.from_z.at[j - 1], self.send.at[at], self.recv.at[at], peer)

    def to_all(self, j):
        net = self.net
        _, peer = net.dp_peer(j)
        at = 1 + net.n_dp + net.n_z + j
        mine = self.done.at[net.dp]
        return remote(mine, mine, self.send.at[at], self.recv.at[at], peer)

    def start(self):
        self.to_core().start()
        self.own().start()

    def over_dp(self):
        net = self.net
        self.own().wait()
        self.to_core().wait()

        @pl.loop(0, net.n_z)
        def _(z):
            self.kept[z] = (self.kept[z].astype(F32) + self.from_core[z].astype(F32)).astype(BF)

        for j in range(1, net.n_dp):
            self.to_dp(j).start()

    def over_z(self):
        net = self.net
        for j in range(1, net.n_dp):
            self.to_dp(j).wait()

        @pl.loop(0, net.n_z)
        def _(z):
            total = self.kept[z, :, self.lanes(net.dp)].astype(F32)
            for j in range(net.n_dp - 1):
                total = total + self.from_dp[j, z].astype(F32)
            self.part[z] = total.astype(BF)

        for j in range(1, net.n_z):
            self.to_z(j).start()

    def back_over_dp(self):
        net = self.net
        for j in range(1, net.n_z):
            self.to_z(j).wait()
        total = self.part[net.z].astype(F32)
        for j in range(net.n_z - 1):
            total = total + self.from_z[j].astype(F32)
        self.done[net.dp] = total.astype(BF)
        for j in range(1, net.n_dp):
            self.to_all(j).start()

    def finish(self):
        for j in range(1, self.net.n_dp):
            self.to_all(j).wait()


class TwoWayReduce(Reduce):
    @staticmethod
    def scratch(n_dp, n_z, rows, width):
        count = 2 + 2 * n_dp + n_z
        return [
            pltpu.VMEM((n_z, rows, width), BF),
            pltpu.VMEM((n_z, rows, width), BF),
            pltpu.VMEM((n_z, rows, width // n_dp), BF),
            pltpu.VMEM((2, n_z, rows, width // 4), BF),
            pltpu.VMEM((2, n_z, rows, width // 8), BF),
            pltpu.VMEM((n_z - 1, rows, width // n_dp), BF),
            pltpu.VMEM((n_dp, rows, width // n_dp), BF),
            pltpu.SemaphoreType.DMA((count,)),
            pltpu.SemaphoreType.DMA((count,)),
        ]

    def __init__(self, net, grads, first, kept, from_core, part, half, quarter, from_z, done, sems):
        super().__init__(net, grads, first, kept, from_core, part, None, from_z, done, sems)
        self.half, self.quarter = half, quarter
        x, y = lax.rem(net.dp, 2), net.dp // 2
        along_x, along_y = (net.dp + 1 - 2 * x, net.wide), (lax.rem(net.dp + 2, 4), net.wide)
        self.order = ((x, y, along_x, along_y), (y, x, along_y, along_x))

    def window(self, h, a, b=None):
        eighth = self.span // 2
        at = h * 4 * eighth + a * 2 * eighth
        if b is None:
            return pl.ds(pl.multiple_of(at, GROUP), 2 * eighth)
        return pl.ds(pl.multiple_of(at + b * eighth, GROUP), eighth)

    def first_step(self, h):
        a, _, peer, _ = self.order[h]
        return remote(self.kept.at[:, :, self.window(h, 1 - a)], self.half.at[h], self.send.at[2 + h], self.recv.at[2 + h], peer)

    def second_step(self, h):
        a, b, _, peer = self.order[h]
        return remote(self.kept.at[:, :, self.window(h, a, 1 - b)], self.quarter.at[h], self.send.at[4 + h], self.recv.at[4 + h], peer)

    def over_dp(self):
        self.own().wait()
        self.to_core().wait()

        @pl.loop(0, self.net.n_z)
        def _(z):
            self.kept[z] = (self.kept[z].astype(F32) + self.from_core[z].astype(F32)).astype(BF)

        for h in range(2):
            self.first_step(h).start()

    def over_dp_again(self):
        for h in range(2):
            self.first_step(h).wait()
        for h in range(2):
            mine = self.window(h, self.order[h][0])

            @pl.loop(0, self.net.n_z)
            def _(z):
                self.kept[z, :, mine] = (self.kept[z, :, mine].astype(F32) + self.half[h, z].astype(F32)).astype(BF)

        for h in range(2):
            self.second_step(h).start()

    def over_z(self):
        net = self.net
        for h in range(2):
            self.second_step(h).wait()
        eighth = self.span // 2
        for h in range(2):
            a, b, _, _ = self.order[h]
            mine = self.window(h, a, b)

            @pl.loop(0, net.n_z)
            def _(z):
                total = self.kept[z, :, mine].astype(F32) + self.quarter[h, z].astype(F32)
                self.part[z, :, h * eighth : (h + 1) * eighth] = total.astype(BF)

        for j in range(1, net.n_z):
            self.to_z(j).start()


class ReduceRows:
    def __init__(self, net, row, from_core, of_dp, of_z, sems):
        self.net, self.row, self.from_core, self.of_dp, self.of_z = net, row, from_core, of_dp, of_z
        self.send, self.recv = sems

    @staticmethod
    def scratch(n_dp, n_z, width):
        count = 1 + n_dp + n_z
        return [
            pltpu.VMEM((1, width), F32),
            pltpu.VMEM((1, width), F32),
            pltpu.VMEM((n_dp, 1, width), F32),
            pltpu.VMEM((n_z, 1, width), F32),
            pltpu.SemaphoreType.DMA((count,)),
            pltpu.SemaphoreType.DMA((count,)),
        ]

    def to_core(self):
        return remote(self.row, self.from_core, self.send.at[0], self.recv.at[0], self.net.sibling)

    def to_dp(self, j):
        mine = self.of_dp.at[self.net.dp]
        return remote(mine, mine, self.send.at[j], self.recv.at[j], self.net.dp_peer(j)[1])

    def to_z(self, j):
        mine = self.of_z.at[self.net.z]
        at = self.net.n_dp + j
        return remote(mine, mine, self.send.at[at], self.recv.at[at], self.net.z_peer(j)[1])

    def start(self):
        self.to_core().start()

    def over_dp(self):
        self.to_core().wait()
        self.of_dp[self.net.dp] = self.row[...] + self.from_core[...]
        for j in range(1, self.net.n_dp):
            self.to_dp(j).start()

    def over_z(self):
        net = self.net
        for j in range(1, net.n_dp):
            self.to_dp(j).wait()
        total = self.of_dp[0]
        for q in range(1, net.n_dp):
            total = total + self.of_dp[q]
        self.of_z[net.z] = total
        for j in range(1, net.n_z):
            self.to_z(j).start()

    def finish(self, out, places):
        net = self.net
        for j in range(1, net.n_z):
            self.to_z(j).wait()
        total = self.of_z[0]
        for z in range(1, net.n_z):
            total = total + self.of_z[z]
        at = 0
        for first, length in places:
            piece = length // net.n_wide
            vector = jnp.broadcast_to(total[:, first : first + length], (8, length))
            turned = pltpu.roll(vector, lax.rem(length - net.wide * piece, length), 1)
            out[:, at : at + piece] = turned[:1, :piece]
            at += padded(piece)


class Gather:
    def __init__(self, net, shards, wholes, send, recv, near):
        self.net, self.shards, self.wholes = net, shards, wholes
        self.send, self.recv, self.near = send, recv, near

    @staticmethod
    def scratch(count, n_z):
        return [
            pltpu.SemaphoreType.DMA((count, 2 * n_z)),
            pltpu.SemaphoreType.DMA((count, 2 * n_z)),
            pltpu.SemaphoreType.DMA((count,)),
        ]

    def block(self, a, owner):
        rows = self.shards[a].shape[0]
        return self.wholes[a].at[pl.ds(pl.multiple_of(owner * rows, rows), rows)]

    def along_z(self, a, j):
        net = self.net
        return remote(self.shards[a], self.block(a, net.wide), self.send.at[a, j], self.recv.at[a, net.wide], net.z_peer(j)[1])

    def across(self, a):
        net = self.net
        return remote(self.shards[a], self.block(a, net.wide), self.send.at[a, 0], self.recv.at[a, net.wide], net.sibling)

    def relayed(self, a, j):
        net = self.net
        owner = 2 * net.z_peer(j)[0] + net.core
        here = self.block(a, owner)
        return remote(here, here, self.send.at[a, net.n_z + j], self.recv.at[a, owner], net.sibling)

    def own(self, a):
        return pltpu.make_async_copy(self.shards[a], self.block(a, self.net.wide), self.near.at[a])

    def arrival(self, a, owner):
        here = self.block(a, owner)
        return remote(here, here, self.send.at[a, 0], self.recv.at[a, owner], self.net.sibling)

    def start(self, a):
        for j in range(1, self.net.n_z):
            self.along_z(a, j).start()
        self.across(a).start()
        self.own(a).start()

    def relay(self, a):
        net = self.net
        for j in range(1, net.n_z):
            self.arrival(a, 2 * net.z_peer(j)[0] + net.core).wait_recv()
            self.relayed(a, j).start()

    def finish(self, a):
        net = self.net
        self.own(a).wait()
        self.across(a).wait_send()
        for j in range(1, net.n_z):
            self.along_z(a, j).wait_send()
            self.relayed(a, j).wait_send()
        for z in range(net.n_z):
            self.arrival(a, 2 * z + 1 - net.core).wait_recv()


class SharedGather:
    def __init__(self, net, shards, wholes, send_z, send_dp, send_core, recv_z, recv_dp, recv_core, near):
        self.net, self.shards, self.wholes = net, shards, wholes
        self.send_z, self.send_dp, self.send_core = send_z, send_dp, send_core
        self.recv_z, self.recv_dp, self.recv_core, self.near = recv_z, recv_dp, recv_core, near

    @staticmethod
    def scratch(count, n_dp, n_z):
        sem = pltpu.SemaphoreType.DMA
        return [
            sem((count, n_z)), sem((count, n_z, n_dp)), sem((count, n_z)),
            sem((count, n_z)), sem((count, n_z, n_dp)), sem((count, n_z)), sem((count,)),
        ]

    def block(self, a, owner):
        rows = self.shards[a].shape[0]
        return self.wholes[a].at[pl.ds(pl.multiple_of(owner * rows, rows), rows)]

    def part(self, a, q):
        rows, columns = self.shards[a].shape
        n_dp = self.net.n_dp
        if rows % (16 * n_dp) == 0:
            some = rows // n_dp
            return pl.multiple_of(q * some, some), some, 0, columns
        some = columns // n_dp
        return 0, rows, pl.multiple_of(q * some, some), some

    def piece(self, a, owner, q):
        rows = self.shards[a].shape[0]
        row, height, column, width = self.part(a, q)
        return self.wholes[a].at[pl.ds(pl.multiple_of(owner * rows + row, height), height), pl.ds(column, width)]

    def along_z(self, a, j):
        net = self.net
        row, height, column, width = self.part(a, net.dp)
        mine = self.shards[a].at[pl.ds(row, height), pl.ds(column, width)]
        return remote(mine, self.piece(a, net.wide, net.dp), self.send_z.at[a, j], self.recv_z.at[a, net.z], net.z_peer(j)[1])

    def from_z(self, a, j):
        net = self.net
        z, peer = net.z_peer(j)
        here = self.piece(a, 2 * z + net.core, net.dp)
        return remote(here, here, self.send_z.at[a, j], self.recv_z.at[a, z], peer)

    def over_dp(self, a, j, i):
        net = self.net
        z = net.z_peer(j)[0]
        here = self.piece(a, 2 * z + net.core, net.dp)
        return remote(here, here, self.send_dp.at[a, j, i], self.recv_dp.at[a, j, net.dp], net.dp_peer(i)[1])

    def from_dp(self, a, j, i):
        net = self.net
        z = net.z_peer(j)[0]
        q, peer = net.dp_peer(i)
        here = self.piece(a, 2 * z + net.core, q)
        return remote(here, here, self.send_dp.at[a, j, i], self.recv_dp.at[a, j, q], peer)

    def across(self, a, j):
        net = self.net
        z = net.z_peer(j)[0]
        here = self.block(a, 2 * z + net.core)
        source = self.shards[a] if j == 0 else here
        return remote(source, here, self.send_core.at[a, j], self.recv_core.at[a, z], net.sibling)

    def from_core(self, a, z):
        net = self.net
        here = self.block(a, 2 * z + 1 - net.core)
        return remote(here, here, self.send_core.at[a, 0], self.recv_core.at[a, z], net.sibling)

    def own(self, a):
        return pltpu.make_async_copy(self.shards[a], self.block(a, self.net.wide), self.near.at[a])

    def start(self, a):
        for j in range(1, self.net.n_z):
            self.along_z(a, j).start()
        self.across(a, 0).start()
        self.own(a).start()

    def relay(self, a):
        net = self.net
        for j in range(1, net.n_z):
            self.from_z(a, j).wait_recv()
            for i in range(1, net.n_dp):
                self.over_dp(a, j, i).start()

    def pass_on(self, a):
        net = self.net
        for j in range(1, net.n_z):
            for i in range(1, net.n_dp):
                self.from_dp(a, j, i).wait_recv()
            self.across(a, j).start()

    def finish(self, a):
        net = self.net
        self.own(a).wait()
        for j in range(1, net.n_z):
            self.along_z(a, j).wait_send()
            for i in range(1, net.n_dp):
                self.over_dp(a, j, i).wait_send()
        for j in range(net.n_z):
            self.across(a, j).wait_send()
            self.from_core(a, j).wait_recv()


class Exchange:
    def __init__(self, net, out, inbox, send, recv, near):
        self.net, self.out, self.inbox = net, out, inbox
        self.send, self.recv, self.near = send, recv, near

    @staticmethod
    def scratch(n_wide):
        return [pltpu.SemaphoreType.DMA((n_wide,)), pltpu.SemaphoreType.DMA((n_wide,)), pltpu.SemaphoreType.DMA(())]

    def to(self, w):
        net = self.net
        return remote(self.out.at[w], self.inbox.at[net.wide], self.send.at[w], self.recv.at[net.wide], (net.dp, w))

    def arrival(self, w):
        here = self.inbox.at[w]
        return remote(here, here, self.send.at[w], self.recv.at[w], (self.net.dp, w))

    def own(self):
        me = self.net.wide
        return pltpu.make_async_copy(self.out.at[me], self.inbox.at[me], self.near)

    def send_block(self, w):
        @pl.when(w != self.net.wide)
        def _():
            self.to(w).start()

        @pl.when(w == self.net.wide)
        def _():
            self.own().start()

    def send_all(self):
        for j in range(1, self.net.n_wide):
            self.to(self.net.wide_peer(j)[0]).start()
        self.own().start()

    def finish(self):
        for j in range(1, self.net.n_wide):
            w = self.net.wide_peer(j)[0]
            self.to(w).wait_send()
            self.arrival(w).wait_recv()
        self.own().wait()


def slices_of(ref, first, lengths):
    views = []
    for length in lengths:
        views.append(ref.at[:, first : first + length])
        first += length
    return views


def char_vectors(row, width, ff, out):
    return slices_of(row, 0, [width] * 6 + [ff, out])


def word_vectors(row, width, ff):
    return slices_of(row, row.shape[1] - 5 * width - ff, [width] * 5 + [ff])


def char_back_kernel(chars_per, steps, net_sizes, word_sizes, *refs):
    (
        gx_ref, c_ref, cnt_ref, qkv_ref, p_ref, o_ref, h1_ref, h2_ref, m_ref, s_ref, pooled_all, gx_all,
        win, wout, wup, wdn, wpj, vec, *refs
    ) = refs
    if net_sizes:
        word_grads, word_row, *refs = refs
    gc_ref, *refs = refs
    if net_sizes:
        outs, refs = refs[: WORD_PARTS + 3], refs[WORD_PARTS + 3 :]
    accs, refs = refs[:13], refs[13:]
    dga, dsa, dwin, dwout, dgb, dsb, dwup, dub, dwdn, ddb, dqv, dwpj, dpb = accs
    gh1_ref, gm_ref, u_ref, gz_ref, gq_ref, gs_ref, *refs = refs
    rows, width = c_ref.shape
    ga, sa, gb, sb, _, qv, _, _ = char_vectors(vec, width, wup.shape[1], wpj.shape[1])
    phase, step = pl.program_id(0), pl.program_id(1)
    now = phase * steps + step
    factor = width**-0.5
    chunk = min(rows, 512)
    cw = chunk // chars_per
    words = rows // chars_per

    if net_sizes:
        net = Net(*net_sizes)
        ff_grads, at_grads, row, *refs = refs
        each = word_grads.shape[-1] // WORD_PARTS
        words_of = []
        for part in range(WORD_PARTS):
            words_of.append(TwoWayReduce(net, word_grads, part * each, *refs[:7], refs[7:9]))
            refs = refs[9:]
        ff = Reduce(net, ff_grads, 0, *refs[:6], refs[6:8])
        att = Reduce(net, at_grads, 0, *refs[8:14], refs[14:16])
        rowsum = ReduceRows(net, row, *refs[16:19], refs[19:21])
        keep = refs[21]

        @pl.when(now == 0)
        def _():
            peers = [net.sibling] + [net.dp_peer(j)[1] for j in range(1, net.n_dp)] + [net.z_peer(j)[1] for j in range(1, net.n_z)]
            net.greet(peers)
            net.met(peers)
            for part in words_of:
                part.start()

        one, two, three = words_of
        schedule = (
            (2, one.over_dp),
            (4, one.over_dp_again),
            (4, two.over_dp),
            (6, one.over_z),
            (6, two.over_dp_again),
            (6, three.over_dp),
            (8, one.back_over_dp),
            (8, two.over_z),
            (8, three.over_dp_again),
            (8, ff.start),
            (9, ff.over_dp),
            (10, two.back_over_dp),
            (10, three.over_z),
            (12, three.back_over_dp),
            (12, ff.over_z),
            (14, ff.back_over_dp),
        )
        for when, act in schedule:
            pl.when(now == when * steps // 8)(act)

    @pl.when(now == 0)
    def _():
        for acc in accs:
            acc[...] = jnp.zeros_like(acc)
        dwpj[...] = tn(pooled_all[...], gx_all[...])
        dpb[...] = column_sum(gx_all[...].astype(F32))

    here = pl.ds(pl.multiple_of(step * rows, rows), rows)

    @pl.when(phase == 0)
    def _():
        gp = nt(gx_ref[...], wpj[...]).astype(BF).astype(F32)
        counts = as_column(cnt_ref[pl.ds(step, 1), :].astype(F32))
        for t in range(rows // chunk):
            at = slice(t * chunk, (t + 1) * chunk)
            wat = slice(t * cw, (t + 1) * cw)
            h2 = h2_ref[at, :].astype(F32)
            om = pool_weights(h2, qv[...], counts[wat, :], chars_per)
            gpb = jnp.broadcast_to(gp[wat, :].reshape(cw, 1, width), (cw, chars_per, width)).reshape(chunk, width)
            w = jnp.sum(h2 * gpb, -1, keepdims=True).reshape(cw, chars_per, 1)
            de = om * (w - jnp.sum(om * w, 1, keepdims=True))
            de = de.reshape(chunk, 1) * factor
            gh2 = om.reshape(chunk, 1) * gpb + de * qv[...]
            dqv[...] += column_sum(de * h2)
            gy = gh2.astype(BF)
            ddb[...] += column_sum(gy.astype(F32))
            gm_ref[at, :] = gy
            gz = (nt(gy, wdn[...]) * s_ref[at, :].astype(F32)).astype(BF)
            gz_ref[at, :] = gz
            dub[...] += column_sum(gz.astype(F32))
            du = nt(gz, wup[...])
            n, r = normal_of(h1_ref[at, :].astype(F32))
            dgb[...] += column_sum(du * n)
            dsb[...] += column_sum(du)
            u_ref[at, :] = (n * gb[...] + sb[...]).astype(BF)
            gh1_ref[pl.ds(pl.multiple_of(step * rows + t * chunk, chunk), chunk), :] = (gh2 + norm_back(du, n, r, gb[...])).astype(BF)
        dwup[...] += tn(u_ref[...], gz_ref[...])
        dwdn[...] += tn(gm_ref[...], m_ref[...])

    if net_sizes:
        n_z, n_wide = net.n_z, net.n_wide

        @pl.when(now == steps - 1)
        def _():
            up, proj = dwup.shape[1], dwpj.shape[1]
            down = dwdn[...].T
            some = width // n_wide
            side = down.shape[0] // n_wide // some
            for owner in range(n_wide):
                z, core = owner // 2, owner % 2
                mine = slice(owner * some, (owner + 1) * some)
                ff_grads[z, core, :, :up] = dwup[mine, :].astype(BF)
                ff_grads[z, core, :, up : up + proj] = dwpj[mine, :].astype(BF)
                for k in range(side):
                    first = (owner * side + k) * some
                    ff_grads[z, core, :, up + proj + k * width : up + proj + (k + 1) * width] = down[first : first + some].astype(BF)

    @pl.when(phase == 1)
    def _():
        g1 = gh1_ref[here, :]
        dwout[...] += tn(o_ref[...], g1)
        gm_ref[...] = nt(g1, wout[...]).astype(BF)
        units = [(slice(g * GROUP, (g + 1) * GROUP), p) for g in range(rows // GROUP) for p in range(width // GROUP)]

        def head_pair(at, p, i):
            return qkv_ref[at, i * width + p * GROUP : i * width + (p + 1) * GROUP]

        for at, p in units:
            dp = nt(gm_ref[at, p * GROUP : (p + 1) * GROUP], two_heads(head_pair(at, p, 2)))
            for h in range(2):
                lanes = slice((2 * p + h) * GROUP, (2 * p + h + 1) * GROUP)
                gs_ref[at, lanes] = softmax_back(p_ref[at, lanes], dp[:, h * GROUP : (h + 1) * GROUP])
        for at, p in units:
            gs = gs_ref[at, 2 * p * GROUP : 2 * (p + 1) * GROUP]
            gq_ref[at, p * GROUP : (p + 1) * GROUP] = (nn(gs, two_heads(head_pair(at, p, 1))) * HD**-0.5).astype(BF)
            gq_ref[at, width + p * GROUP : width + (p + 1) * GROUP] = one_of_two(tn(gs, head_pair(at, p, 0))).astype(BF)
            soft = p_ref[at, p * 2 * GROUP : (p + 1) * 2 * GROUP]
            gm = gm_ref[at, p * GROUP : (p + 1) * GROUP]
            gq_ref[at, 2 * width + p * GROUP : 2 * width + (p + 1) * GROUP] = one_of_two(tn(soft, gm)).astype(BF)
        for t in range(rows // chunk):
            at = slice(t * chunk, (t + 1) * chunk)
            n, r = normal_of(c_ref[at, :].astype(F32))
            u_ref[at, :] = (n * ga[...] + sa[...]).astype(BF)
            da = nt(gq_ref[at, :], win[...])
            dga[...] += column_sum(da * n)
            dsa[...] += column_sum(da)
            grad = gh1_ref[pl.ds(pl.multiple_of(step * rows + t * chunk, chunk), chunk), :].astype(F32) + norm_back(da, n, r, ga[...])
            gc_ref[at, :] = grad.astype(gc_ref.dtype)
        dwin[...] += tn(u_ref[...], gq_ref[...])

    if net_sizes:

        @pl.when(now == 2 * steps - 1)
        def _():
            some = width // n_wide
            for owner in range(n_wide):
                z, core = owner // 2, owner % 2
                mine = slice(owner * some, (owner + 1) * some)
                at_grads[z, core, :, : 3 * width] = dwin[mine, :].astype(BF)
                at_grads[z, core, :, 3 * width :] = dwout[mine, :].astype(BF)
            column, places = 0, []
            for acc in (dga, dsa, dgb, dsb, ddb, dqv, dub, dpb):
                row[:, column : column + acc.shape[1]] = acc[...]
                places.append((column, acc.shape[1]))
                column += acc.shape[1]
            row[:, column:] = word_row[...]
            for ref in word_vectors(row, *word_sizes):
                places.append((column, ref.shape[1]))
                column += ref.shape[1]
            att.start()
            rowsum.start()
            for part in words_of:
                part.finish()
            ff.finish()
            att.over_dp()
            rowsum.over_dp()
            att.over_z()
            rowsum.over_z()
            att.back_over_dp()
            rowsum.finish(outs[-1], places)
            att.finish()
            copies = [pltpu.make_async_copy(piece.done, out, keep.at[i]) for i, (piece, out) in enumerate(zip((*words_of, ff, att), outs))]
            for copy in copies:
                copy.start()
            for copy in copies:
                copy.wait()


def whole_block(shape):
    return pl.BlockSpec(shape, lambda *_: (0,) * len(shape), pipeline_mode=pl.Buffered(1))


def whole_out(shape):
    return pl.BlockSpec(shape, lambda *_: (0,) * len(shape))


def char_backward(gx, chars, counts, saved, weights, chars_per, rows, net_sizes=None, word_grads=None, word_row=None):
    total, width = chars.shape
    win, wout, wup, wdn, wpj, vec = weights
    pooled, qkv, soft, mixed, h1, h2, m, s = saved
    words, cw = total // chars_per, rows // chars_per
    ff, out = wup.shape[1], wpj.shape[1]
    steps = total // rows

    def early(count, columns):
        return pl.BlockSpec((count, columns), lambda p, i: (i + p * (steps - 1 - i), 0))

    def late(count, columns):
        return pl.BlockSpec((count, columns), lambda p, i: (i * p, 0))

    accs = [(1, width), (1, width), (width, 3 * width), (width, width), (1, width), (1, width), (width, ff), (1, ff),
            (width, ff), (1, width), (1, width), (width, out), (1, out)]
    in_specs = [early(cw, out), late(rows, width), whole_block(counts.shape), late(rows, 3 * width), late(rows, 2 * width),
                late(rows, width), early(rows, width), early(rows, width), early(rows, ff), early(rows, ff),
                whole_block(pooled.shape), whole_block(gx.shape)] + [whole_block(w.shape) for w in weights]
    operands = [gx, chars, counts, qkv, soft, mixed, h1, h2, m, s, pooled, gx, *weights]
    scratch = [pltpu.VMEM((total, width), BF), pltpu.VMEM((rows, width), BF), pltpu.VMEM((rows, width), BF),
               pltpu.VMEM((rows, ff), BF), pltpu.VMEM((rows, 3 * width), BF), pltpu.VMEM((rows, 2 * width), BF)]
    if net_sizes:
        n_dp, n_wide = net_sizes
        n_z, some = n_wide // 2, width // n_wide
        word_rows, word_width = word_grads.shape[2:]
        wide_d = n_wide * word_rows
        word_ff = word_row.shape[1] - 5 * wide_d
        operands += [word_grads, word_row]
        in_specs += [pl.BlockSpec(memory_space=pl.ANY), whole_block(word_row.shape)]
        ff_width, at_width = ff + out + ff, 4 * width
        row_width = 6 * width + ff + out + word_row.shape[1]
        word_sizes = (wide_d, word_ff)
        sums = [(n_dp, word_rows, word_width // WORD_PARTS // n_dp)] * WORD_PARTS + [(n_dp, some, ff_width // n_dp), (n_dp, some, at_width // n_dp)]
        pieces = sum(padded(n // n_wide) for n in [width] * 6 + [ff, out] + [wide_d] * 5 + [word_ff])
        out_shapes = [jax.ShapeDtypeStruct((total, width), BF)] + [jax.ShapeDtypeStruct(a, BF) for a in sums] + [jax.ShapeDtypeStruct((1, pieces), F32)]
        out_specs = [late(rows, width)] + [pl.BlockSpec(memory_space=pl.ANY)] * len(sums) + [whole_out((1, pieces))]
        scratch = (
            [pltpu.VMEM(a, F32) for a in accs]
            + scratch
            + [pltpu.VMEM((n_z, 2, some, ff_width), BF), pltpu.VMEM((n_z, 2, some, at_width), BF), pltpu.VMEM((1, row_width), F32)]
            + TwoWayReduce.scratch(n_dp, n_z, word_rows, word_width // WORD_PARTS) * WORD_PARTS
            + Reduce.scratch(n_dp, n_z, some, ff_width)
            + Reduce.scratch(n_dp, n_z, some, at_width)
            + ReduceRows.scratch(n_dp, n_z, row_width)[1:]
            + [pltpu.SemaphoreType.DMA((len(sums),))]
        )
        params = pltpu.CompilerParams(vmem_limit_bytes=VMEM_LIMIT, collective_id=3, has_side_effects=True)
    else:
        word_sizes = None
        out_shapes = [jax.ShapeDtypeStruct(a, F32) for a in [(total, width)] + accs]
        out_specs = [late(rows, width)] + [whole_out(a) for a in accs]
        params = pltpu.CompilerParams(vmem_limit_bytes=VMEM_LIMIT)
    return pl.pallas_call(
        functools.partial(char_back_kernel, chars_per, steps, net_sizes, word_sizes),
        grid=(2, steps),
        in_specs=in_specs,
        out_specs=out_specs,
        out_shape=out_shapes,
        scratch_shapes=scratch,
        compiler_params=params,
        name="char_backward",
    )(*operands)


def unpack(parts, outs, two_way):
    n_dp, rows, span = parts[0].shape
    for ref, first, columns, side in outs:
        for k in range(side):
            for at in range(0, columns, GROUP):
                column = first + k * columns + at
                part, column = column // (n_dp * span), column % (n_dp * span)
                if two_way:
                    eighth = span // 2
                    h, place, lane = column // (4 * eighth), column // eighth % 4, column % eighth
                    q = place if h else place // 2 + place % 2 * 2
                    lane += h * eighth
                else:
                    q, lane = column // span, column % span
                ref[k * rows : (k + 1) * rows, at : at + GROUP] = parts[part][q, :, lane : lane + GROUP].astype(F32)


def output_kernel(gc_low, *refs):
    word_done, (ff_done, at_done, row, gc_ref, *outs) = refs[:WORD_PARTS], refs[WORD_PARTS:]
    gc_ref[...] = gc_low[...].astype(F32)

    @pl.when(pl.program_id(0) == 0)
    def _():
        (
            oga, osa, owin, owout, ogb, osb, oup, oub, odn, odb, oqv, opj, opb,
            xga, xsa, xwin, xwout, xgb, xsb, xup, xub, xdn, xdb,
        ) = outs
        for done, across, down in ((word_done, (xwin, xwout, xup), xdn), ([ff_done], (oup, opj), odn), ([at_done], (owin, owout), None)):
            places, column = [], 0
            for ref in across:
                places.append((ref, column, ref.shape[1], 1))
                column += ref.shape[1]
            if down is not None:
                places.append((down, column, down.shape[1], down.shape[0] // done[0].shape[1]))
            unpack(done, places, len(done) > 1)
        at = 0
        for ref in (oga, osa, ogb, osb, odb, oqv, oub, opb, xga, xsa, xgb, xsb, xdb, xub):
            ref[...] = row[:, at : at + ref.shape[1]]
            at += padded(ref.shape[1])


def outputs_of(gc_low, *wholes, shapes, rows):
    total, width = gc_low.shape
    by_row = pl.BlockSpec((rows, width), lambda i: (i, 0))
    return pl.pallas_call(
        output_kernel,
        grid=(total // rows,),
        in_specs=[by_row] + [whole_block(a.shape) for a in wholes],
        out_specs=[by_row] + [whole_out(a) for a in shapes],
        out_shape=[jax.ShapeDtypeStruct(a, F32) for a in [(total, width), *shapes]],
        compiler_params=pltpu.CompilerParams(vmem_limit_bytes=VMEM_LIMIT),
        name="outputs",
    )(gc_low, *wholes)


def late_place(net_sizes, steps, step):
    if not net_sizes:
        return step
    return lax.rem((lax.axis_index("wide") + 1) * (steps // net_sizes[1]) + step, steps)


def char_forward_kernel(chars_per, steps, net_sizes, lengths, *refs):
    c_ref, cnt_ref, *refs = refs
    if net_sizes:
        net = Net(*net_sizes)
        shards, word_shards, vectors, refs = refs[:5], refs[5:9], refs[9:23], refs[23:]
        inbox, vec, *refs = refs
        char_out, word_out, refs = refs[:5], refs[5:9], refs[9:]
    else:
        win, wout, wup, wdn, wpj, vec, *refs = refs
        x_ref, *refs = refs
    pooled_ref, qkv_ref, p_ref, o_ref, h1_ref, h2_ref, m_ref, s_ref, *refs = refs
    h1_all, *refs = refs
    rows, width = c_ref.shape
    phase, step = pl.program_id(0), pl.program_id(1)
    now = phase * steps + step
    chunk = min(rows, 512)
    cw = chunk // chars_per
    words = rows // chars_per
    place = late_place(net_sizes, steps, step)

    if net_sizes:
        x_out, win, wout, wup, wdn, wpj, pieces, piece, *refs = refs
        gather = Gather(net, (shards[0], shards[1], piece), [win, wout, pieces], *refs[:3])
        shared = SharedGather(net, (*shards[2:], *word_shards), [wup, wdn, wpj, *word_out], *refs[3:10])
        exchange = Exchange(net, x_out, inbox, *refs[10:13])
        keep = refs[13]
        char_weights = (win, wout, wup, wdn, wpj)

        @pl.when(now == 0)
        def _():
            peers = [net.wide_peer(j)[1] for j in range(1, net.n_wide)] + [net.dp_peer(j)[1] for j in range(1, net.n_dp)]
            net.greet(peers)
            for ref, (at, length) in zip(vectors, lengths):
                some = length // net.n_wide
                piece[0, :, at : at + some] = ref[...].astype(F32).reshape(1, some)
            net.met(peers)
            for a in (2, 0, 1):
                gather.start(a)
            for a in (2, 0, 1):
                gather.relay(a)
            for a in range(3):
                shared.start(a)
            gather.finish(2)
            column = 0
            for at, length in lengths:
                some = length // net.n_wide
                row = jnp.concatenate([pieces[w, :, at : at + some] for w in range(net.n_wide)], 1)
                vec[:, column : column + length] = row
                column += length
            gather.finish(0)
            gather.finish(1)

        def start_words():
            for a in range(3, 7):
                shared.start(a)

        def relay_chars():
            for a in range(3):
                shared.relay(a)

        def pass_on_chars():
            for a in range(3):
                shared.pass_on(a)

        def finish_chars():
            for a in range(3):
                shared.finish(a)
            for a, weight in enumerate(char_weights):
                pltpu.make_async_copy(weight, char_out[a], keep.at[a]).start()

        schedule = [(1, start_words), (2, relay_chars), (5, pass_on_chars), (8, finish_chars)]
        schedule += [(6 + i, functools.partial(shared.relay, 3 + i)) for i in range(4)]
        schedule += [(12 + i, functools.partial(shared.pass_on, 3 + i)) for i in range(4)]
        for when, act in schedule:
            pl.when(now == when * steps // 8)(act)

    ga, sa, gb, sb, db, qv, ub, pb = char_vectors(vec, width, wup.shape[1], wpj.shape[1])

    def block(t):
        return pl.ds(pl.multiple_of(place * rows + t * chunk, chunk), chunk)

    @pl.when(phase == 0)
    def _():
        n, _ = normal_of(c_ref[...].astype(F32))
        a = (n * ga[...] + sa[...]).astype(BF)
        qkv = nn(a, win[...])
        qkv_ref[:, :width] = (qkv[:, :width] * HD**-0.5).astype(BF)
        qkv_ref[:, width:] = qkv[:, width:].astype(BF)
        ri = lax.broadcasted_iota(jnp.int32, (GROUP, GROUP), 0) // chars_per
        ci = lax.broadcasted_iota(jnp.int32, (GROUP, GROUP), 1) // chars_per
        same = ri == ci
        units = [(g, slice(g * GROUP, (g + 1) * GROUP), p) for g in range(rows // GROUP) for p in range(width // GROUP)]

        def head_pair(at, p, i):
            return qkv_ref[at, i * width + p * GROUP : i * width + (p + 1) * GROUP]

        valid = key_bias(cnt_ref[pl.ds(step, 1), :].astype(F32), chars_per)
        for g, at, p in units:
            bias = jnp.where(same, jnp.broadcast_to(valid[:1, g * GROUP : (g + 1) * GROUP], (GROUP, GROUP)), NEG)
            s = nt(head_pair(at, p, 0), two_heads(head_pair(at, p, 1)))
            for h in range(2):
                p_ref[at, (2 * p + h) * GROUP : (2 * p + h + 1) * GROUP] = softmax_low(s[:, h * GROUP : (h + 1) * GROUP] + bias)
        for _, at, p in units:
            o_ref[at, p * GROUP : (p + 1) * GROUP] = nn(p_ref[at, 2 * p * GROUP : 2 * (p + 1) * GROUP], two_heads(head_pair(at, p, 2))).astype(BF)
        for t in range(rows // chunk):
            at = slice(t * chunk, (t + 1) * chunk)
            h1 = c_ref[at, :].astype(F32) + nn(o_ref[at, :], wout[...])
            h1_ref[at, :] = h1.astype(BF)
            h1_all[pl.ds(pl.multiple_of(step * rows + t * chunk, chunk), chunk), :] = h1

    @pl.when(phase == 1)
    def _():
        counts = as_column(cnt_ref[pl.ds(place, 1), :].astype(F32))
        for t in range(rows // chunk):
            at = slice(t * chunk, (t + 1) * chunk)
            wat = slice(t * cw, (t + 1) * cw)
            h1 = h1_all[block(t), :]
            n, _ = normal_of(h1)
            u = (n * gb[...] + sb[...]).astype(BF)
            m, s = gelu_and_slope(nn(u, wup[...]) + ub[...])
            m_ref[at, :] = m.astype(BF)
            s_ref[at, :] = s.astype(BF)
            h2 = h1 + (nn(m_ref[at, :], wdn[...]) + db[...])
            h2_ref[at, :] = h2.astype(BF)
            om = pool_weights(h2, qv[...], counts[wat, :], chars_per)
            pooled_ref[wat, :] = jnp.sum(om * h2.reshape(cw, chars_per, width), 1).astype(BF)
        x = (nn(pooled_ref[...], wpj[...]) + pb[...]).astype(BF)
        if net_sizes:
            cap = x_out.shape[1]
            first_word = place * words
            target = first_word // cap
            x_out[target, pl.ds(pl.multiple_of(lax.rem(first_word, cap), words), words)] = x
            pl.when(lax.rem(first_word + words, cap) == 0)(lambda: exchange.send_block(target))
        else:
            x_ref[...] = x

    if net_sizes:

        @pl.when(now == 2 * steps - 1)
        def _():
            for a in range(3, 7):
                shared.finish(a)
            exchange.finish()
            for a, weight in enumerate(char_weights):
                pltpu.make_async_copy(weight, char_out[a], keep.at[a]).wait()


def char_forward(chars, counts, weights, chars_per, rows, net_sizes=None, word_shards=None, vectors=None, cap=None):
    total, width = chars.shape
    words, cw = total // chars_per, rows // chars_per
    ff, out = weights[2].shape[1], weights[4].shape[1]
    steps = total // rows

    def early(count, columns):
        return pl.BlockSpec((count, columns), lambda p, i: (i + p * (steps - 1 - i), 0))

    def late(count, columns):
        return pl.BlockSpec((count, columns), lambda p, i: (late_place(net_sizes, steps, i * p), 0))

    saved = [((words, width), BF, cw, late), ((total, 3 * width), BF, rows, early), ((total, 2 * width), BF, rows, early),
             ((total, width), BF, rows, early), ((total, width), BF, rows, early), ((total, width), BF, rows, late),
             ((total, ff), BF, rows, late), ((total, ff), BF, rows, late)]
    saved_specs = [where(count, s[1]) for s, _, count, where in saved]
    saved_shapes = [jax.ShapeDtypeStruct(s, d) for s, d, _, _ in saved]
    in_specs = [early(rows, width), whole_block(counts.shape)]
    operands = [chars, counts]
    scratch = [pltpu.VMEM((total, width), F32)]
    anywhere = pl.BlockSpec(memory_space=pl.ANY)
    if net_sizes:
        n_dp, n_wide = net_sizes
        n_z = n_wide // 2
        lengths, room = [], 0
        for v in vectors:
            lengths.append((room, v.shape[0] * n_wide))
            room += padded(v.shape[0])
        in_specs += [anywhere] * 9 + [whole_block(v.shape) for v in vectors]
        operands += [*weights, *word_shards, *vectors]
        vec_shape = jax.ShapeDtypeStruct((1, sum(length for _, length in lengths)), F32)
        grown = lambda a: jax.ShapeDtypeStruct((a.shape[0] * n_wide, a.shape[1]), a.dtype)
        fulls = [grown(a) for a in weights]
        out_specs = [anywhere, whole_out(vec_shape.shape)] + [anywhere] * 9 + saved_specs
        out_shapes = [jax.ShapeDtypeStruct((n_wide, cap, out), BF), vec_shape, *fulls, *(grown(a) for a in word_shards), *saved_shapes]
        scratch += (
            [pltpu.VMEM((n_wide, cap, out), BF)]
            + [pltpu.VMEM(a.shape, a.dtype) for a in fulls]
            + [pltpu.VMEM((n_wide, 1, room), F32), pltpu.VMEM((1, 1, room), F32)]
            + Gather.scratch(3, n_z)
            + SharedGather.scratch(7, n_dp, n_z)
            + Exchange.scratch(n_wide)
            + [pltpu.SemaphoreType.DMA((5,))]
        )
        params = pltpu.CompilerParams(vmem_limit_bytes=VMEM_LIMIT, collective_id=1, has_side_effects=True)
    else:
        lengths = None
        in_specs += [whole_block(w.shape) for w in weights]
        operands += [*weights]
        out_specs = [late(cw, out)] + saved_specs
        out_shapes = [jax.ShapeDtypeStruct((words, out), BF), *saved_shapes]
        params = pltpu.CompilerParams(vmem_limit_bytes=VMEM_LIMIT)
    return pl.pallas_call(
        functools.partial(char_forward_kernel, chars_per, steps, net_sizes, lengths),
        grid=(2, steps),
        in_specs=in_specs,
        out_specs=out_specs,
        out_shape=out_shapes,
        scratch_shapes=scratch,
        compiler_params=params,
        name="char_forward",
    )(*operands)


def word_kernel(slot_cap, net_sizes, *refs):
    arrived, bucket, assign, segment, grad_ref, win, wout, wup, wdn, vec, out_ref, back_out, *refs = refs
    length, width = grad_ref.shape
    ff = wup.shape[1]
    if net_sizes:
        net = Net(*net_sizes)
        grads_out, word_row, *refs = refs
        *held, word_grads, load_sem, store_sem = refs[-7:]
        refs = refs[:-7]
        loads = [pltpu.make_async_copy(src, dst, load_sem.at[i]) for i, (src, dst) in enumerate(zip((win, wout, wup, wdn), held))]
        for load in loads:
            load.start()
        win, wout, wup, wdn = held
        dga, dsa, dgb, dsb, ddb, dub = word_vectors(word_row, width, ff)
    else:
        dga, dsa, dwin, dwout, dgb, dsb, dwup, dub, dwdn, ddb, *refs = refs
    qkv_ref, p_ref, mix_ref, h_ref, s_ref, gq_ref, *refs = refs
    ga, sa, gb, sb, db, ub = word_vectors(vec, width, ff)
    owners = assign.shape[1]
    slots = owners * slot_cap
    if net_sizes:
        back_ref, *sems = refs
        exchange = Exchange(net, back_ref, back_out, *sems)
        peers = [net.wide_peer(j)[1] for j in range(1, net.n_wide)]
        net.greet(peers)
    def ready(i):
        if net_sizes:
            loads[i].wait()

    named = jnp.where(bucket[...] == lax.broadcasted_iota(jnp.int32, (owners, length), 0), 1.0, 0.0)
    ri = lax.broadcasted_iota(jnp.int32, (length, length), 0)
    ci = lax.broadcasted_iota(jnp.int32, (length, length), 1)
    earlier = nn(named.astype(BF), jnp.where(ri < ci, 1.0, 0.0).astype(BF))
    served = as_column(assign[...].astype(F32)) * slot_cap
    slot = jnp.sum(named * (served + earlier), 0, keepdims=True).astype(jnp.int32)
    hot = jnp.where(lax.broadcasted_iota(jnp.int32, (slots, length), 0) == slot, 1.0, 0.0).astype(BF)
    x = tn(hot, arrived[...].reshape(slots, width))
    n1, r1 = normal_of(x)
    a = (n1 * ga[...] + sa[...]).astype(BF)
    ready(0)
    qkv = nn(a, win[...])
    qkv_ref[:, :width] = (qkv[:, :width] * HD**-0.5).astype(BF)
    qkv_ref[:, width:] = qkv[:, width:].astype(BF)
    seg = segment[...].astype(F32)
    bias = jnp.where((seg == as_column(seg)) & (ci <= ri), 0.0, NEG)

    def pair(p):
        return [qkv_ref[:, i * width + p * GROUP : i * width + (p + 1) * GROUP] for i in range(3)]

    for p in range(width // GROUP):
        q, k, v = pair(p)
        s = nt(q, two_heads(k))
        soft = jnp.concatenate([softmax_low(s[:, h * length : (h + 1) * length] + bias) for h in range(2)], 1)
        p_ref[:, 2 * p * length : (2 * p + 2) * length] = soft
        mix_ref[:, p * GROUP : (p + 1) * GROUP] = nn(soft, two_heads(v)).astype(BF)
    ready(1)
    inner = x + nn(mix_ref[...], wout[...])
    n2, r2 = normal_of(inner)
    u = (n2 * gb[...] + sb[...]).astype(BF)
    ready(2)
    h, slope = gelu_and_slope(nn(u, wup[...]) + ub[...])
    h_ref[...] = h.astype(BF)
    s_ref[...] = slope
    ready(3)
    out_ref[...] = inner + (nn(h_ref[...], wdn[...]) + db[...])
    g = grad_ref[...]
    gz = (nt(g, wdn[...]) * s_ref[...]).astype(BF)
    du = nt(gz, wup[...])
    g1 = g.astype(F32) + norm_back(du, n2, r2, gb[...])
    g1_low = g1.astype(BF)
    gm = nt(g1_low, wout[...]).astype(BF)
    for p in range(width // GROUP):
        q, k, v = pair(p)
        gmp = gm[:, p * GROUP : (p + 1) * GROUP]
        soft = p_ref[:, 2 * p * length : (2 * p + 2) * length]
        dp = nt(gmp, two_heads(v))
        gs = jnp.concatenate([softmax_back(soft[:, h * length : (h + 1) * length], dp[:, h * length : (h + 1) * length]) for h in range(2)], 1)
        gq_ref[:, p * GROUP : (p + 1) * GROUP] = (nn(gs, two_heads(k)) * HD**-0.5).astype(BF)
        gq_ref[:, width + p * GROUP : width + (p + 1) * GROUP] = one_of_two(tn(gs, q)).astype(BF)
        gq_ref[:, 2 * width + p * GROUP : 2 * width + (p + 1) * GROUP] = one_of_two(tn(soft, gmp)).astype(BF)
    da = nt(gq_ref[...], win[...])
    gx = (g1 + norm_back(da, n1, r1, ga[...])).astype(BF)
    back = nn(hot, gx).astype(BF).reshape(owners, slot_cap, width)
    if net_sizes:
        back_ref[...] = back
        net.met(peers)
        exchange.send_all()
        some = width // net.n_wide
        side = ff // width

        def put(value, column):
            value = value.astype(BF)
            for w in range(net.n_wide):
                word_grads[w // 2, w % 2, :, column : column + value.shape[1]] = value[w * some : (w + 1) * some]

        def store(i, first, columns):
            window = pl.ds(first, columns)
            return pltpu.make_async_copy(word_grads.at[:, :, :, window], grads_out.at[:, :, :, window], store_sem.at[i])

        put(tn(a, gq_ref[...]), 0)
        put(tn(mix_ref[...], g1_low), 3 * width)
        store(0, 0, 4 * width).start()
        put(tn(u, gz), 4 * width)
        store(1, 4 * width, ff).start()
        down = tn(h_ref[...], g).astype(BF)
        for w in range(net.n_wide):
            for k in range(side):
                first = (w * side + k) * some
                column = 4 * width + ff + k * width
                word_grads[w // 2, w % 2, :, column : column + width] = down[first : first + some]
        store(2, 4 * width + ff, ff).start()
    else:
        back_out[...] = back
        dwin[...] = tn(a, gq_ref[...])
        dwout[...] = tn(mix_ref[...], g1_low)
        dwup[...] = tn(u, gz)
        dwdn[...] = tn(h_ref[...], g)
    dga[...] = column_sum(da * n1)
    dsa[...] = column_sum(da)
    dgb[...] = column_sum(du * n2)
    dsb[...] = column_sum(du)
    dub[...] = column_sum(gz.astype(F32))
    ddb[...] = column_sum(g.astype(F32))
    if net_sizes:
        exchange.finish()
        for i, (first, columns) in enumerate(((0, 4 * width), (4 * width, ff), (4 * width + ff, ff))):
            store(i, first, columns).wait()


def word_block(arrived, bucket, assign, segments, grad, weights, slot_cap, net_sizes=None):
    length, width = grad.shape
    ff = weights[2].shape[1]
    owners = assign.shape[1]
    low = lambda *s: jax.ShapeDtypeStruct(s, BF)
    full = lambda *s: jax.ShapeDtypeStruct(s, F32)
    vmem = pl.BlockSpec(memory_space=pltpu.VMEM)
    out_shapes, out_specs = [full(length, width), low(owners, slot_cap, width)], [vmem, vmem]
    scratch = [pltpu.VMEM((length, 3 * width), BF), pltpu.VMEM((length, width // HD * length), BF), pltpu.VMEM((length, width), BF),
               pltpu.VMEM((length, ff), BF), pltpu.VMEM((length, ff), F32), pltpu.VMEM((length, 3 * width), BF)]
    if net_sizes:
        n_dp, n_wide = net_sizes
        out_shapes += [low(n_wide // 2, 2, width // n_wide, 4 * width + 2 * ff), full(1, 5 * width + ff)]
        anywhere = pl.BlockSpec(memory_space=pl.ANY)
        out_specs = [vmem, anywhere, anywhere, vmem]
        in_specs = [vmem] * 5 + [anywhere] * 4 + [vmem]
        scratch += [pltpu.VMEM((owners, slot_cap, width), BF)] + Exchange.scratch(n_wide)
        scratch += [pltpu.VMEM(w.shape, BF) for w in weights[:4]] + [pltpu.VMEM(out_shapes[2].shape, BF)]
        scratch += [pltpu.SemaphoreType.DMA((4,)), pltpu.SemaphoreType.DMA((3,))]
        params = pltpu.CompilerParams(vmem_limit_bytes=VMEM_LIMIT, collective_id=2, has_side_effects=True)
    else:
        row = full(1, width)
        out_shapes += [row, row, full(width, 3 * width), full(width, width), row, row, full(width, ff), full(1, ff), full(ff, width), row]
        out_specs += [vmem] * 10
        in_specs = [vmem] * 10
        params = pltpu.CompilerParams(vmem_limit_bytes=VMEM_LIMIT)
    return pl.pallas_call(
        functools.partial(word_kernel, slot_cap, net_sizes),
        in_specs=in_specs,
        out_specs=out_specs,
        out_shape=out_shapes,
        scratch_shapes=scratch,
        compiler_params=params,
        name="word_block",
    )(arrived, bucket, assign, segments, grad, *weights)


def gathered(shard):
    return lax.all_gather(shard, "wide", axis=0, tiled=True)


def exchanged(blocks):
    return lax.all_to_all(blocks, "wide", split_axis=0, concat_axis=0, tiled=True)


def summed(grad):
    part = lax.psum_scatter(grad.astype(BF), "wide", scatter_dimension=0, tiled=True)
    return lax.psum(part, "dp").astype(F32)


def shards(
    chars, char_counts, buckets, assign, segments,
    char_gain, char_shift, char_inproj, char_outproj, char_gain_mid, char_shift_mid, char_up, char_up_bias, char_down, char_down_bias,
    pool_query, char_proj, char_proj_bias,
    word_gain, word_shift, word_inproj, word_outproj, word_gain_mid, word_shift_mid, word_up, word_up_bias, word_down, word_down_bias,
    out_grad,
):
    n_dp, n_wide = lax.axis_size("dp"), lax.axis_size("wide")
    cap, chars_per, width = chars.shape[2:]
    slots = n_wide * cap
    rows = chars.reshape(slots * chars_per, width)
    block = min(1024, rows.shape[0])
    counts = char_counts.reshape(-1, block // chars_per)
    char_shards = (char_inproj, char_outproj, char_up, char_down, char_proj)
    word_shards = (word_inproj, word_outproj, word_up, word_down)
    vectors = (char_gain, char_shift, char_gain_mid, char_shift_mid, char_down_bias, pool_query, char_up_bias, char_proj_bias,
               word_gain, word_shift, word_gain_mid, word_shift_mid, word_down_bias, word_up_bias)
    fast = (
        all(m.shape[0] % 16 == 0 for m in char_shards)
        and all(m.shape[0] % (16 * n_dp) == 0 for m in word_shards)
        and cap % (block // chars_per) == 0
        and (4 * width) % (GROUP * n_dp) == 0
        and n_wide % 2 == 0
        and n_dp == 4
        and (4 * word_up.shape[0] * n_wide + 2 * word_up.shape[1]) % (8 * GROUP * WORD_PARTS) == 0
    )
    bucket, names, upstream = buckets.reshape(1, -1), assign[None], out_grad[0]
    if fast:
        sizes = (n_dp, n_wide)
        arrived, vec, *rest = char_forward(rows, counts, char_shards, chars_per, block, sizes, word_shards, vectors, cap)
        char_full, word_full, saved = rest[:5], rest[5:9], rest[9:]
        result, returned, word_grads, word_row = word_block(arrived, bucket, names, segments, upstream, (*word_full, vec), cap, sizes)
        incoming = returned.reshape(slots, -1)
        sums = char_backward(incoming, rows, counts, saved, (*char_full, vec), chars_per, block, sizes, word_grads, word_row)
        params = (char_gain, char_shift, char_inproj, char_outproj, char_gain_mid, char_shift_mid, char_up, char_up_bias, char_down,
                  char_down_bias, pool_query, char_proj, char_proj_bias, word_gain, word_shift, word_inproj, word_outproj, word_gain_mid,
                  word_shift_mid, word_up, word_up_bias, word_down, word_down_bias)
        shapes = [p.shape if p.ndim == 2 else (1, *p.shape) for p in params]
        char_grads, *grads = outputs_of(*sums, shapes=shapes, rows=block)
        grads = [g[0] if g.shape[0] == 1 else g for g in grads]
    else:
        vec = jnp.concatenate([gathered(v) for v in vectors]).astype(F32)[None]
        char_full, word_full = [gathered(m) for m in char_shards], [gathered(m) for m in word_shards]
        outgoing, *saved = char_forward(rows, counts, (*char_full, vec), chars_per, block)
        arrived = exchanged(outgoing.reshape(n_wide, cap, -1))
        result, back, *word_grads = word_block(arrived, bucket, names, segments, upstream, (*word_full, vec), cap)
        incoming = exchanged(back).reshape(slots, -1)
        char_grads, *grads = char_backward(incoming, rows, counts, saved, (*char_full, vec), chars_per, block)
        grads[8] = grads[8].T
        grads = [summed(g[0] if g.shape[0] == 1 else g) for g in grads + word_grads]
    return (result[None], char_grads.reshape(chars.shape), *grads)


def solution(mesh):
    whole, split = ("dp", "wide"), "wide"
    row, flat = P(split, None), P(split)
    word = [flat, flat, row, row, flat, flat, row, flat, row, flat]
    char = word + [flat, row, flat]
    chars = P(whole, None, None, None, None)
    three = P(whole, None, None)
    return jax.shard_map(
        shards,
        mesh=mesh,
        in_specs=(chars, three, three, P(), P(whole, None), *char, *word, three),
        out_specs=(three, chars, *char, *word),
        check_vma=False,
    )
```

```python
import functools

import jax
import jax.numpy as jnp
from jax import lax
from jax.experimental import pallas as pl
from jax.experimental.pallas import tpu as pltpu
from jax.sharding import PartitionSpec as P

EPS = 1e-05
NEG = -1e30
ROOT_HALF = 0.7071067811865476
INV_ROOT_TWO_PI = 0.3989422804014327
LOG2_E = 1.4426950408889634
HD = 64
GROUP = 128
F32 = jnp.float32
BF = jnp.bfloat16
MESH = pl.DeviceIdType.MESH
VMEM_LIMIT = 60 << 20
WORD_PARTS = 3


def nn(a, b):
    return lax.dot_general(a, b, (((1,), (0,)), ((), ())), preferred_element_type=F32)


def nt(a, b):
    return lax.dot_general(a, b, (((1,), (1,)), ((), ())), preferred_element_type=F32)


def tn(a, b):
    return lax.dot_general(a, b, (((0,), (0,)), ((), ())), preferred_element_type=F32)


def padded(lanes):
    return -(-lanes // GROUP) * GROUP


def column_sum(x):
    return jnp.sum(x, 0, keepdims=True)


def normal_of(x):
    c = x - jnp.mean(x, -1, keepdims=True)
    r = lax.rsqrt(jnp.mean(c * c, -1, keepdims=True) + EPS)
    return c * r, r


def norm_back(d, n, r, g):
    dg = d * g
    return r * (dg - jnp.mean(dg, -1, keepdims=True) - n * jnp.mean(dg * n, -1, keepdims=True))


def gelu_and_slope(z):
    w = z * ROOT_HALF
    cdf = 0.5 + 0.5 * lax.erf(w)
    return z * cdf, cdf + (z * INV_ROOT_TWO_PI) * jnp.exp2((w * w) * -LOG2_E)


def softmax_low(s):
    ex = jnp.exp(s - jnp.max(s, -1, keepdims=True))
    return (ex * (1.0 / jnp.sum(ex, -1, keepdims=True))).astype(BF)


def softmax_back(soft, d):
    soft = soft.astype(F32)
    return (soft * (d - jnp.sum(d * soft, -1, keepdims=True))).astype(BF)


def two_heads(t):
    left = lax.broadcasted_iota(jnp.int32, t.shape, 1) < HD
    zero = jnp.zeros_like(t)
    return jnp.concatenate([jnp.where(left, t, zero), jnp.where(left, zero, t)], 0)


def one_of_two(t):
    half = t.shape[0] // 2
    left = lax.broadcasted_iota(jnp.int32, (half, t.shape[1]), 1) < HD
    return jnp.where(left, t[:half], t[half:])


def as_column(row):
    n = row.shape[1]
    same = lax.broadcasted_iota(jnp.int32, (n, n), 0) == lax.broadcasted_iota(jnp.int32, (n, n), 1)
    return jnp.sum(jnp.where(same, jnp.broadcast_to(row, (n, n)), 0.0), -1, keepdims=True)


def key_bias(row, chars_per):
    n = row.shape[1]
    lanes = n * chars_per
    of_word = lax.broadcasted_iota(jnp.int32, (n, lanes), 1) // chars_per == lax.broadcasted_iota(jnp.int32, (n, lanes), 0)
    counts = nn(jnp.broadcast_to(row, (8, n)).astype(BF), jnp.where(of_word, 1.0, 0.0).astype(BF))
    place = lax.rem(lax.broadcasted_iota(jnp.int32, (8, lanes), 1), chars_per)
    return jnp.where(place.astype(F32) < counts, 0.0, NEG)


def pool_weights(h2, query, counts, chars_per):
    rows = h2.shape[0]
    words = rows // chars_per
    e = jnp.sum(h2 * query, -1, keepdims=True) * (h2.shape[1] ** -0.5)
    e = e.reshape(words, chars_per, 1)
    place = lax.broadcasted_iota(jnp.int32, (words, chars_per, 1), 1).astype(F32)
    e = jnp.where(place < counts.reshape(words, 1, 1), e, NEG)
    ex = jnp.exp(e - jnp.max(e, 1, keepdims=True))
    return ex / jnp.sum(ex, 1, keepdims=True)


class Net:
    def __init__(self, n_dp, n_wide):
        self.n_dp, self.n_wide, self.n_z = n_dp, n_wide, n_wide // 2
        self.dp, self.wide = lax.axis_index("dp"), lax.axis_index("wide")
        self.z, self.core = self.wide // 2, lax.rem(self.wide, 2)
        self.sibling = (self.dp, self.wide + 1 - 2 * self.core)

    def z_peer(self, j):
        z = lax.rem(self.z + j, self.n_z)
        return z, (self.dp, 2 * z + self.core)

    def dp_peer(self, j):
        q = lax.rem(self.dp + j, self.n_dp)
        return q, (q, self.wide)

    def wide_peer(self, j):
        w = lax.rem(self.wide + j, self.n_wide)
        return w, (self.dp, w)

    def greet(self, peers):
        barrier = pltpu.get_barrier_semaphore()
        for peer in peers:
            pl.semaphore_signal(barrier, inc=1, device_id=peer, device_id_type=MESH)

    def met(self, peers):
        pl.semaphore_wait(pltpu.get_barrier_semaphore(), len(peers))


def remote(src, dst, send, recv, peer):
    return pltpu.make_async_remote_copy(src_ref=src, dst_ref=dst, send_sem=send, recv_sem=recv, device_id=peer, device_id_type=MESH)


class Reduce:
    def __init__(self, net, grads, first, kept, from_core, part, from_dp, from_z, done, sems):
        self.net, self.grads = net, grads
        self.columns = pl.ds(first, kept.shape[-1])
        self.kept, self.from_core, self.part = kept, from_core, part
        self.from_dp, self.from_z, self.done = from_dp, from_z, done
        self.send, self.recv = sems
        self.span = part.shape[-1]

    @staticmethod
    def scratch(n_dp, n_z, rows, width):
        span = width // n_dp
        count = 2 + 2 * n_dp + n_z
        return [
            pltpu.VMEM((n_z, rows, width), BF),
            pltpu.VMEM((n_z, rows, width), BF),
            pltpu.VMEM((n_z, rows, span), BF),
            pltpu.VMEM((n_dp - 1, n_z, rows, span), BF),
            pltpu.VMEM((n_z - 1, rows, span), BF),
            pltpu.VMEM((n_dp, rows, span), BF),
            pltpu.SemaphoreType.DMA((count,)),
            pltpu.SemaphoreType.DMA((count,)),
        ]

    def lanes(self, q):
        return pl.ds(pl.multiple_of(q * self.span, GROUP), self.span)

    def to_core(self):
        net = self.net
        return remote(self.grads.at[:, 1 - net.core, :, self.columns], self.from_core, self.send.at[0], self.recv.at[0], net.sibling)

    def own(self):
        return pltpu.make_async_copy(self.grads.at[:, self.net.core, :, self.columns], self.kept, self.recv.at[1])

    def to_dp(self, j):
        q, peer = self.net.dp_peer(j)
        return remote(self.kept.at[:, :, self.lanes(q)], self.from_dp.at[j - 1], self.send.at[1 + j], self.recv.at[1 + j], peer)

    def to_z(self, j):
        z, peer = self.net.z_peer(j)
        at = 1 + self.net.n_dp + j
        return remote(self.part.at[z], self.from_z.at[j - 1], self.send.at[at], self.recv.at[at], peer)

    def to_all(self, j):
        net = self.net
        _, peer = net.dp_peer(j)
        at = 1 + net.n_dp + net.n_z + j
        mine = self.done.at[net.dp]
        return remote(mine, mine, self.send.at[at], self.recv.at[at], peer)

    def start(self):
        self.to_core().start()
        self.own().start()

    def over_dp(self):
        net = self.net
        self.own().wait()
        self.to_core().wait()

        @pl.loop(0, net.n_z)
        def _(z):
            self.kept[z] = (self.kept[z].astype(F32) + self.from_core[z].astype(F32)).astype(BF)

        for j in range(1, net.n_dp):
            self.to_dp(j).start()

    def over_z(self):
        net = self.net
        for j in range(1, net.n_dp):
            self.to_dp(j).wait()

        @pl.loop(0, net.n_z)
        def _(z):
            total = self.kept[z, :, self.lanes(net.dp)].astype(F32)
            for j in range(net.n_dp - 1):
                total = total + self.from_dp[j, z].astype(F32)
            self.part[z] = total.astype(BF)

        for j in range(1, net.n_z):
            self.to_z(j).start()

    def back_over_dp(self):
        net = self.net
        for j in range(1, net.n_z):
            self.to_z(j).wait()
        total = self.part[net.z].astype(F32)
        for j in range(net.n_z - 1):
            total = total + self.from_z[j].astype(F32)
        self.done[net.dp] = total.astype(BF)
        for j in range(1, net.n_dp):
            self.to_all(j).start()

    def finish(self):
        for j in range(1, self.net.n_dp):
            self.to_all(j).wait()


class TwoWayReduce(Reduce):
    @staticmethod
    def scratch(n_dp, n_z, rows, width):
        count = 2 + 2 * n_dp + n_z
        return [
            pltpu.VMEM((n_z, rows, width), BF),
            pltpu.VMEM((n_z, rows, width), BF),
            pltpu.VMEM((n_z, rows, width // n_dp), BF),
            pltpu.VMEM((2, n_z, rows, width // 4), BF),
            pltpu.VMEM((2, n_z, rows, width // 8), BF),
            pltpu.VMEM((n_z - 1, rows, width // n_dp), BF),
            pltpu.VMEM((n_dp, rows, width // n_dp), BF),
            pltpu.SemaphoreType.DMA((count,)),
            pltpu.SemaphoreType.DMA((count,)),
        ]

    def __init__(self, net, grads, first, kept, from_core, part, half, quarter, from_z, done, sems):
        super().__init__(net, grads, first, kept, from_core, part, None, from_z, done, sems)
        self.half, self.quarter = half, quarter
        x, y = lax.rem(net.dp, 2), net.dp // 2
        along_x, along_y = (net.dp + 1 - 2 * x, net.wide), (lax.rem(net.dp + 2, 4), net.wide)
        self.order = ((x, y, along_x, along_y), (y, x, along_y, along_x))

    def window(self, h, a, b=None):
        eighth = self.span // 2
        at = h * 4 * eighth + a * 2 * eighth
        if b is None:
            return pl.ds(pl.multiple_of(at, GROUP), 2 * eighth)
        return pl.ds(pl.multiple_of(at + b * eighth, GROUP), eighth)

    def first_step(self, h):
        a, _, peer, _ = self.order[h]
        return remote(self.kept.at[:, :, self.window(h, 1 - a)], self.half.at[h], self.send.at[2 + h], self.recv.at[2 + h], peer)

    def second_step(self, h):
        a, b, _, peer = self.order[h]
        return remote(self.kept.at[:, :, self.window(h, a, 1 - b)], self.quarter.at[h], self.send.at[4 + h], self.recv.at[4 + h], peer)

    def over_dp(self):
        self.own().wait()
        self.to_core().wait()

        @pl.loop(0, self.net.n_z)
        def _(z):
            self.kept[z] = (self.kept[z].astype(F32) + self.from_core[z].astype(F32)).astype(BF)

        for h in range(2):
            self.first_step(h).start()

    def over_dp_again(self):
        for h in range(2):
            self.first_step(h).wait()
        for h in range(2):
            mine = self.window(h, self.order[h][0])

            @pl.loop(0, self.net.n_z)
            def _(z):
                self.kept[z, :, mine] = (self.kept[z, :, mine].astype(F32) + self.half[h, z].astype(F32)).astype(BF)

        for h in range(2):
            self.second_step(h).start()

    def over_z(self):
        net = self.net
        for h in range(2):
            self.second_step(h).wait()
        eighth = self.span // 2
        for h in range(2):
            a, b, _, _ = self.order[h]
            mine = self.window(h, a, b)

            @pl.loop(0, net.n_z)
            def _(z):
                total = self.kept[z, :, mine].astype(F32) + self.quarter[h, z].astype(F32)
                self.part[z, :, h * eighth : (h + 1) * eighth] = total.astype(BF)

        for j in range(1, net.n_z):
            self.to_z(j).start()


class ReduceRows:
    def __init__(self, net, row, from_core, of_dp, of_z, sems):
        self.net, self.row, self.from_core, self.of_dp, self.of_z = net, row, from_core, of_dp, of_z
        self.send, self.recv = sems

    @staticmethod
    def scratch(n_dp, n_z, width):
        count = 1 + n_dp + n_z
        return [
            pltpu.VMEM((1, width), F32),
            pltpu.VMEM((1, width), F32),
            pltpu.VMEM((n_dp, 1, width), F32),
            pltpu.VMEM((n_z, 1, width), F32),
            pltpu.SemaphoreType.DMA((count,)),
            pltpu.SemaphoreType.DMA((count,)),
        ]

    def to_core(self):
        return remote(self.row, self.from_core, self.send.at[0], self.recv.at[0], self.net.sibling)

    def to_dp(self, j):
        mine = self.of_dp.at[self.net.dp]
        return remote(mine, mine, self.send.at[j], self.recv.at[j], self.net.dp_peer(j)[1])

    def to_z(self, j):
        mine = self.of_z.at[self.net.z]
        at = self.net.n_dp + j
        return remote(mine, mine, self.send.at[at], self.recv.at[at], self.net.z_peer(j)[1])

    def start(self):
        self.to_core().start()

    def over_dp(self):
        self.to_core().wait()
        self.of_dp[self.net.dp] = self.row[...] + self.from_core[...]
        for j in range(1, self.net.n_dp):
            self.to_dp(j).start()

    def over_z(self):
        net = self.net
        for j in range(1, net.n_dp):
            self.to_dp(j).wait()
        total = self.of_dp[0]
        for q in range(1, net.n_dp):
            total = total + self.of_dp[q]
        self.of_z[net.z] = total
        for j in range(1, net.n_z):
            self.to_z(j).start()

    def finish(self, out, places):
        net = self.net
        for j in range(1, net.n_z):
            self.to_z(j).wait()
        total = self.of_z[0]
        for z in range(1, net.n_z):
            total = total + self.of_z[z]
        at = 0
        for first, length in places:
            piece = length // net.n_wide
            vector = jnp.broadcast_to(total[:, first : first + length], (8, length))
            turned = pltpu.roll(vector, lax.rem(length - net.wide * piece, length), 1)
            out[:, at : at + piece] = turned[:1, :piece]
            at += padded(piece)


class Gather:
    def __init__(self, net, shards, wholes, send, recv, near):
        self.net, self.shards, self.wholes = net, shards, wholes
        self.send, self.recv, self.near = send, recv, near

    @staticmethod
    def scratch(count, n_z):
        return [
            pltpu.SemaphoreType.DMA((count, 2 * n_z)),
            pltpu.SemaphoreType.DMA((count, 2 * n_z)),
            pltpu.SemaphoreType.DMA((count,)),
        ]

    def block(self, a, owner):
        rows = self.shards[a].shape[0]
        return self.wholes[a].at[pl.ds(pl.multiple_of(owner * rows, rows), rows)]

    def along_z(self, a, j):
        net = self.net
        return remote(self.shards[a], self.block(a, net.wide), self.send.at[a, j], self.recv.at[a, net.wide], net.z_peer(j)[1])

    def across(self, a):
        net = self.net
        return remote(self.shards[a], self.block(a, net.wide), self.send.at[a, 0], self.recv.at[a, net.wide], net.sibling)

    def relayed(self, a, j):
        net = self.net
        owner = 2 * net.z_peer(j)[0] + net.core
        here = self.block(a, owner)
        return remote(here, here, self.send.at[a, net.n_z + j], self.recv.at[a, owner], net.sibling)

    def own(self, a):
        return pltpu.make_async_copy(self.shards[a], self.block(a, self.net.wide), self.near.at[a])

    def arrival(self, a, owner):
        here = self.block(a, owner)
        return remote(here, here, self.send.at[a, 0], self.recv.at[a, owner], self.net.sibling)

    def start(self, a):
        for j in range(1, self.net.n_z):
            self.along_z(a, j).start()
        self.across(a).start()
        self.own(a).start()

    def relay(self, a):
        net = self.net
        for j in range(1, net.n_z):
            self.arrival(a, 2 * net.z_peer(j)[0] + net.core).wait_recv()
            self.relayed(a, j).start()

    def finish(self, a):
        net = self.net
        self.own(a).wait()
        self.across(a).wait_send()
        for j in range(1, net.n_z):
            self.along_z(a, j).wait_send()
            self.relayed(a, j).wait_send()
        for z in range(net.n_z):
            self.arrival(a, 2 * z + 1 - net.core).wait_recv()


class SharedGather:
    def __init__(self, net, shards, wholes, send_z, send_dp, send_core, recv_z, recv_dp, recv_core, near):
        self.net, self.shards, self.wholes = net, shards, wholes
        self.send_z, self.send_dp, self.send_core = send_z, send_dp, send_core
        self.recv_z, self.recv_dp, self.recv_core, self.near = recv_z, recv_dp, recv_core, near

    @staticmethod
    def scratch(count, n_dp, n_z):
        sem = pltpu.SemaphoreType.DMA
        return [
            sem((count, n_z)), sem((count, n_z, n_dp)), sem((count, n_z)),
            sem((count, n_z)), sem((count, n_z, n_dp)), sem((count, n_z)), sem((count,)),
        ]

    def block(self, a, owner):
        rows = self.shards[a].shape[0]
        return self.wholes[a].at[pl.ds(pl.multiple_of(owner * rows, rows), rows)]

    def part(self, a, q):
        rows, columns = self.shards[a].shape
        n_dp = self.net.n_dp
        if rows % (16 * n_dp) == 0:
            some = rows // n_dp
            return pl.multiple_of(q * some, some), some, 0, columns
        some = columns // n_dp
        return 0, rows, pl.multiple_of(q * some, some), some

    def piece(self, a, owner, q):
        rows = self.shards[a].shape[0]
        row, height, column, width = self.part(a, q)
        return self.wholes[a].at[pl.ds(pl.multiple_of(owner * rows + row, height), height), pl.ds(column, width)]

    def along_z(self, a, j):
        net = self.net
        row, height, column, width = self.part(a, net.dp)
        mine = self.shards[a].at[pl.ds(row, height), pl.ds(column, width)]
        return remote(mine, self.piece(a, net.wide, net.dp), self.send_z.at[a, j], self.recv_z.at[a, net.z], net.z_peer(j)[1])

    def from_z(self, a, j):
        net = self.net
        z, peer = net.z_peer(j)
        here = self.piece(a, 2 * z + net.core, net.dp)
        return remote(here, here, self.send_z.at[a, j], self.recv_z.at[a, z], peer)

    def over_dp(self, a, j, i):
        net = self.net
        z = net.z_peer(j)[0]
        here = self.piece(a, 2 * z + net.core, net.dp)
        return remote(here, here, self.send_dp.at[a, j, i], self.recv_dp.at[a, j, net.dp], net.dp_peer(i)[1])

    def from_dp(self, a, j, i):
        net = self.net
        z = net.z_peer(j)[0]
        q, peer = net.dp_peer(i)
        here = self.piece(a, 2 * z + net.core, q)
        return remote(here, here, self.send_dp.at[a, j, i], self.recv_dp.at[a, j, q], peer)

    def across(self, a, j):
        net = self.net
        z = net.z_peer(j)[0]
        here = self.block(a, 2 * z + net.core)
        source = self.shards[a] if j == 0 else here
        return remote(source, here, self.send_core.at[a, j], self.recv_core.at[a, z], net.sibling)

    def from_core(self, a, z):
        net = self.net
        here = self.block(a, 2 * z + 1 - net.core)
        return remote(here, here, self.send_core.at[a, 0], self.recv_core.at[a, z], net.sibling)

    def own(self, a):
        return pltpu.make_async_copy(self.shards[a], self.block(a, self.net.wide), self.near.at[a])

    def start(self, a):
        for j in range(1, self.net.n_z):
            self.along_z(a, j).start()
        self.across(a, 0).start()
        self.own(a).start()

    def relay(self, a):
        net = self.net
        for j in range(1, net.n_z):
            self.from_z(a, j).wait_recv()
            for i in range(1, net.n_dp):
                self.over_dp(a, j, i).start()

    def pass_on(self, a):
        net = self.net
        for j in range(1, net.n_z):
            for i in range(1, net.n_dp):
                self.from_dp(a, j, i).wait_recv()
            self.across(a, j).start()

    def finish(self, a):
        net = self.net
        self.own(a).wait()
        for j in range(1, net.n_z):
            self.along_z(a, j).wait_send()
            for i in range(1, net.n_dp):
                self.over_dp(a, j, i).wait_send()
        for j in range(net.n_z):
            self.across(a, j).wait_send()
            self.from_core(a, j).wait_recv()


class Exchange:
    def __init__(self, net, out, inbox, send, recv, near):
        self.net, self.out, self.inbox = net, out, inbox
        self.send, self.recv, self.near = send, recv, near

    @staticmethod
    def scratch(n_wide):
        return [pltpu.SemaphoreType.DMA((n_wide,)), pltpu.SemaphoreType.DMA((n_wide,)), pltpu.SemaphoreType.DMA(())]

    def to(self, w):
        net = self.net
        return remote(self.out.at[w], self.inbox.at[net.wide], self.send.at[w], self.recv.at[net.wide], (net.dp, w))

    def arrival(self, w):
        here = self.inbox.at[w]
        return remote(here, here, self.send.at[w], self.recv.at[w], (self.net.dp, w))

    def own(self):
        me = self.net.wide
        return pltpu.make_async_copy(self.out.at[me], self.inbox.at[me], self.near)

    def send_block(self, w):
        @pl.when(w != self.net.wide)
        def _():
            self.to(w).start()

        @pl.when(w == self.net.wide)
        def _():
            self.own().start()

    def send_all(self):
        for j in range(1, self.net.n_wide):
            self.to(self.net.wide_peer(j)[0]).start()
        self.own().start()

    def finish(self):
        for j in range(1, self.net.n_wide):
            w = self.net.wide_peer(j)[0]
            self.to(w).wait_send()
            self.arrival(w).wait_recv()
        self.own().wait()


def slices_of(ref, first, lengths):
    views = []
    for length in lengths:
        views.append(ref.at[:, first : first + length])
        first += length
    return views


def char_vectors(row, width, ff, out):
    return slices_of(row, 0, [width] * 6 + [ff, out])


def word_vectors(row, width, ff):
    return slices_of(row, row.shape[1] - 5 * width - ff, [width] * 5 + [ff])


def char_back_kernel(chars_per, steps, net_sizes, word_sizes, *refs):
    (
        gx_ref, c_ref, cnt_ref, qkv_ref, p_ref, o_ref, h1_ref, h2_ref, m_ref, s_ref, pooled_all, gx_all,
        win, wout, wup, wdn, wpj, vec, *refs
    ) = refs
    if net_sizes:
        word_grads, word_row, *refs = refs
    gc_ref, *refs = refs
    if net_sizes:
        outs, refs = refs[: WORD_PARTS + 3], refs[WORD_PARTS + 3 :]
    accs, refs = refs[:13], refs[13:]
    dga, dsa, dwin, dwout, dgb, dsb, dwup, dub, dwdn, ddb, dqv, dwpj, dpb = accs
    gh1_ref, gm_ref, u_ref, gz_ref, gq_ref, gs_ref, *refs = refs
    rows, width = c_ref.shape
    ga, sa, gb, sb, _, qv, _, _ = char_vectors(vec, width, wup.shape[1], wpj.shape[1])
    phase, step = pl.program_id(0), pl.program_id(1)
    now = phase * steps + step
    factor = width**-0.5
    chunk = min(rows, 512)
    cw = chunk // chars_per
    words = rows // chars_per

    if net_sizes:
        net = Net(*net_sizes)
        ff_grads, at_grads, row, *refs = refs
        each = word_grads.shape[-1] // WORD_PARTS
        words_of = []
        for part in range(WORD_PARTS):
            words_of.append(TwoWayReduce(net, word_grads, part * each, *refs[:7], refs[7:9]))
            refs = refs[9:]
        ff = Reduce(net, ff_grads, 0, *refs[:6], refs[6:8])
        att = Reduce(net, at_grads, 0, *refs[8:14], refs[14:16])
        rowsum = ReduceRows(net, row, *refs[16:19], refs[19:21])
        keep = refs[21]

        @pl.when(now == 0)
        def _():
            peers = [net.sibling] + [net.dp_peer(j)[1] for j in range(1, net.n_dp)] + [net.z_peer(j)[1] for j in range(1, net.n_z)]
            net.greet(peers)
            net.met(peers)
            for part in words_of:
                part.start()

        one, two, three = words_of
        schedule = (
            (1, one.over_dp),
            (2, two.over_dp),
            (3, one.over_dp_again),
            (4, three.over_dp),
            (5, two.over_dp_again),
            (6, one.over_z),
            (7, three.over_dp_again),
            (8, two.over_z),
            (8, ff.start),
            (9, one.back_over_dp),
            (10, three.over_z),
            (10, ff.over_dp),
            (11, two.back_over_dp),
            (13, three.back_over_dp),
            (13, ff.over_z),
            (15, ff.back_over_dp),
        )
        for when, act in schedule:
            pl.when(now == when * steps // 8)(act)

    @pl.when(now == 0)
    def _():
        for acc in accs:
            acc[...] = jnp.zeros_like(acc)
        dwpj[...] = tn(pooled_all[...], gx_all[...])
        dpb[...] = column_sum(gx_all[...].astype(F32))

    here = pl.ds(pl.multiple_of(step * rows, rows), rows)

    @pl.when(phase == 0)
    def _():
        gp = nt(gx_ref[...], wpj[...]).astype(BF).astype(F32)
        counts = as_column(cnt_ref[pl.ds(step, 1), :].astype(F32))
        for t in range(rows // chunk):
            at = slice(t * chunk, (t + 1) * chunk)
            wat = slice(t * cw, (t + 1) * cw)
            h2 = h2_ref[at, :].astype(F32)
            om = pool_weights(h2, qv[...], counts[wat, :], chars_per)
            gpb = jnp.broadcast_to(gp[wat, :].reshape(cw, 1, width), (cw, chars_per, width)).reshape(chunk, width)
            w = jnp.sum(h2 * gpb, -1, keepdims=True).reshape(cw, chars_per, 1)
            de = om * (w - jnp.sum(om * w, 1, keepdims=True))
            de = de.reshape(chunk, 1) * factor
            gh2 = om.reshape(chunk, 1) * gpb + de * qv[...]
            dqv[...] += column_sum(de * h2)
            gy = gh2.astype(BF)
            ddb[...] += column_sum(gy.astype(F32))
            gm_ref[at, :] = gy
            gz = (nt(gy, wdn[...]) * s_ref[at, :].astype(F32)).astype(BF)
            gz_ref[at, :] = gz
            dub[...] += column_sum(gz.astype(F32))
            du = nt(gz, wup[...])
            n, r = normal_of(h1_ref[at, :].astype(F32))
            dgb[...] += column_sum(du * n)
            dsb[...] += column_sum(du)
            u_ref[at, :] = (n * gb[...] + sb[...]).astype(BF)
            gh1_ref[pl.ds(pl.multiple_of(step * rows + t * chunk, chunk), chunk), :] = (gh2 + norm_back(du, n, r, gb[...])).astype(BF)
        dwup[...] += tn(u_ref[...], gz_ref[...])
        dwdn[...] += tn(gm_ref[...], m_ref[...])

    if net_sizes:
        n_z, n_wide = net.n_z, net.n_wide

        @pl.when(now == steps - 1)
        def _():
            up, proj = dwup.shape[1], dwpj.shape[1]
            down = dwdn[...].T
            some = width // n_wide
            side = down.shape[0] // n_wide // some
            for owner in range(n_wide):
                z, core = owner // 2, owner % 2
                mine = slice(owner * some, (owner + 1) * some)
                ff_grads[z, core, :, :up] = dwup[mine, :].astype(BF)
                ff_grads[z, core, :, up : up + proj] = dwpj[mine, :].astype(BF)
                for k in range(side):
                    first = (owner * side + k) * some
                    ff_grads[z, core, :, up + proj + k * width : up + proj + (k + 1) * width] = down[first : first + some].astype(BF)

    @pl.when(phase == 1)
    def _():
        g1 = gh1_ref[here, :]
        dwout[...] += tn(o_ref[...], g1)
        gm_ref[...] = nt(g1, wout[...]).astype(BF)
        units = [(slice(g * GROUP, (g + 1) * GROUP), p) for g in range(rows // GROUP) for p in range(width // GROUP)]

        def head_pair(at, p, i):
            return qkv_ref[at, i * width + p * GROUP : i * width + (p + 1) * GROUP]

        for at, p in units:
            dp = nt(gm_ref[at, p * GROUP : (p + 1) * GROUP], two_heads(head_pair(at, p, 2)))
            for h in range(2):
                lanes = slice((2 * p + h) * GROUP, (2 * p + h + 1) * GROUP)
                gs_ref[at, lanes] = softmax_back(p_ref[at, lanes], dp[:, h * GROUP : (h + 1) * GROUP])
        for at, p in units:
            gs = gs_ref[at, 2 * p * GROUP : 2 * (p + 1) * GROUP]
            gq_ref[at, p * GROUP : (p + 1) * GROUP] = (nn(gs, two_heads(head_pair(at, p, 1))) * HD**-0.5).astype(BF)
            gq_ref[at, width + p * GROUP : width + (p + 1) * GROUP] = one_of_two(tn(gs, head_pair(at, p, 0))).astype(BF)
            soft = p_ref[at, p * 2 * GROUP : (p + 1) * 2 * GROUP]
            gm = gm_ref[at, p * GROUP : (p + 1) * GROUP]
            gq_ref[at, 2 * width + p * GROUP : 2 * width + (p + 1) * GROUP] = one_of_two(tn(soft, gm)).astype(BF)
        for t in range(rows // chunk):
            at = slice(t * chunk, (t + 1) * chunk)
            n, r = normal_of(c_ref[at, :].astype(F32))
            u_ref[at, :] = (n * ga[...] + sa[...]).astype(BF)
            da = nt(gq_ref[at, :], win[...])
            dga[...] += column_sum(da * n)
            dsa[...] += column_sum(da)
            grad = gh1_ref[pl.ds(pl.multiple_of(step * rows + t * chunk, chunk), chunk), :].astype(F32) + norm_back(da, n, r, ga[...])
            gc_ref[at, :] = grad.astype(gc_ref.dtype)
        dwin[...] += tn(u_ref[...], gq_ref[...])

    if net_sizes:

        @pl.when(now == 2 * steps - 1)
        def _():
            some = width // n_wide
            for owner in range(n_wide):
                z, core = owner // 2, owner % 2
                mine = slice(owner * some, (owner + 1) * some)
                at_grads[z, core, :, : 3 * width] = dwin[mine, :].astype(BF)
                at_grads[z, core, :, 3 * width :] = dwout[mine, :].astype(BF)
            column, places = 0, []
            for acc in (dga, dsa, dgb, dsb, ddb, dqv, dub, dpb):
                row[:, column : column + acc.shape[1]] = acc[...]
                places.append((column, acc.shape[1]))
                column += acc.shape[1]
            row[:, column:] = word_row[...]
            for ref in word_vectors(row, *word_sizes):
                places.append((column, ref.shape[1]))
                column += ref.shape[1]
            att.start()
            rowsum.start()
            for part in words_of:
                part.finish()
            ff.finish()
            att.over_dp()
            rowsum.over_dp()
            att.over_z()
            rowsum.over_z()
            att.back_over_dp()
            rowsum.finish(outs[-1], places)
            att.finish()
            copies = [pltpu.make_async_copy(piece.done, out, keep.at[i]) for i, (piece, out) in enumerate(zip((*words_of, ff, att), outs))]
            for copy in copies:
                copy.start()
            for copy in copies:
                copy.wait()


def whole_block(shape):
    return pl.BlockSpec(shape, lambda *_: (0,) * len(shape), pipeline_mode=pl.Buffered(1))


def whole_out(shape):
    return pl.BlockSpec(shape, lambda *_: (0,) * len(shape))


def char_backward(gx, chars, counts, saved, weights, chars_per, rows, net_sizes=None, word_grads=None, word_row=None):
    total, width = chars.shape
    win, wout, wup, wdn, wpj, vec = weights
    pooled, qkv, soft, mixed, h1, h2, m, s = saved
    words, cw = total // chars_per, rows // chars_per
    ff, out = wup.shape[1], wpj.shape[1]
    steps = total // rows

    def early(count, columns):
        return pl.BlockSpec((count, columns), lambda p, i: (i + p * (steps - 1 - i), 0))

    def late(count, columns):
        return pl.BlockSpec((count, columns), lambda p, i: (i * p, 0))

    accs = [(1, width), (1, width), (width, 3 * width), (width, width), (1, width), (1, width), (width, ff), (1, ff),
            (width, ff), (1, width), (1, width), (width, out), (1, out)]
    in_specs = [early(cw, out), late(rows, width), whole_block(counts.shape), late(rows, 3 * width), late(rows, 2 * width),
                late(rows, width), early(rows, width), early(rows, width), early(rows, ff), early(rows, ff),
                whole_block(pooled.shape), whole_block(gx.shape)] + [whole_block(w.shape) for w in weights]
    operands = [gx, chars, counts, qkv, soft, mixed, h1, h2, m, s, pooled, gx, *weights]
    scratch = [pltpu.VMEM((total, width), BF), pltpu.VMEM((rows, width), BF), pltpu.VMEM((rows, width), BF),
               pltpu.VMEM((rows, ff), BF), pltpu.VMEM((rows, 3 * width), BF), pltpu.VMEM((rows, 2 * width), BF)]
    if net_sizes:
        n_dp, n_wide = net_sizes
        n_z, some = n_wide // 2, width // n_wide
        word_rows, word_width = word_grads.shape[2:]
        wide_d = n_wide * word_rows
        word_ff = word_row.shape[1] - 5 * wide_d
        operands += [word_grads, word_row]
        in_specs += [pl.BlockSpec(memory_space=pl.ANY), whole_block(word_row.shape)]
        ff_width, at_width = ff + out + ff, 4 * width
        row_width = 6 * width + ff + out + word_row.shape[1]
        word_sizes = (wide_d, word_ff)
        sums = [(n_dp, word_rows, word_width // WORD_PARTS // n_dp)] * WORD_PARTS + [(n_dp, some, ff_width // n_dp), (n_dp, some, at_width // n_dp)]
        pieces = sum(padded(n // n_wide) for n in [width] * 6 + [ff, out] + [wide_d] * 5 + [word_ff])
        out_shapes = [jax.ShapeDtypeStruct((total, width), BF)] + [jax.ShapeDtypeStruct(a, BF) for a in sums] + [jax.ShapeDtypeStruct((1, pieces), F32)]
        out_specs = [late(rows, width)] + [pl.BlockSpec(memory_space=pl.ANY)] * len(sums) + [whole_out((1, pieces))]
        scratch = (
            [pltpu.VMEM(a, F32) for a in accs]
            + scratch
            + [pltpu.VMEM((n_z, 2, some, ff_width), BF), pltpu.VMEM((n_z, 2, some, at_width), BF), pltpu.VMEM((1, row_width), F32)]
            + TwoWayReduce.scratch(n_dp, n_z, word_rows, word_width // WORD_PARTS) * WORD_PARTS
            + Reduce.scratch(n_dp, n_z, some, ff_width)
            + Reduce.scratch(n_dp, n_z, some, at_width)
            + ReduceRows.scratch(n_dp, n_z, row_width)[1:]
            + [pltpu.SemaphoreType.DMA((len(sums),))]
        )
        params = pltpu.CompilerParams(vmem_limit_bytes=VMEM_LIMIT, collective_id=3, has_side_effects=True)
    else:
        word_sizes = None
        out_shapes = [jax.ShapeDtypeStruct(a, F32) for a in [(total, width)] + accs]
        out_specs = [late(rows, width)] + [whole_out(a) for a in accs]
        params = pltpu.CompilerParams(vmem_limit_bytes=VMEM_LIMIT)
    return pl.pallas_call(
        functools.partial(char_back_kernel, chars_per, steps, net_sizes, word_sizes),
        grid=(2, steps),
        in_specs=in_specs,
        out_specs=out_specs,
        out_shape=out_shapes,
        scratch_shapes=scratch,
        compiler_params=params,
        name="char_backward",
    )(*operands)


def unpack(parts, outs, two_way):
    n_dp, rows, span = parts[0].shape
    for ref, first, columns, side in outs:
        for k in range(side):
            for at in range(0, columns, GROUP):
                column = first + k * columns + at
                part, column = column // (n_dp * span), column % (n_dp * span)
                if two_way:
                    eighth = span // 2
                    h, place, lane = column // (4 * eighth), column // eighth % 4, column % eighth
                    q = place if h else place // 2 + place % 2 * 2
                    lane += h * eighth
                else:
                    q, lane = column // span, column % span
                ref[k * rows : (k + 1) * rows, at : at + GROUP] = parts[part][q, :, lane : lane + GROUP].astype(F32)


def output_kernel(gc_low, *refs):
    word_done, (ff_done, at_done, row, gc_ref, *outs) = refs[:WORD_PARTS], refs[WORD_PARTS:]
    gc_ref[...] = gc_low[...].astype(F32)

    @pl.when(pl.program_id(0) == 0)
    def _():
        (
            oga, osa, owin, owout, ogb, osb, oup, oub, odn, odb, oqv, opj, opb,
            xga, xsa, xwin, xwout, xgb, xsb, xup, xub, xdn, xdb,
        ) = outs
        for done, across, down in ((word_done, (xwin, xwout, xup), xdn), ([ff_done], (oup, opj), odn), ([at_done], (owin, owout), None)):
            places, column = [], 0
            for ref in across:
                places.append((ref, column, ref.shape[1], 1))
                column += ref.shape[1]
            if down is not None:
                places.append((down, column, down.shape[1], down.shape[0] // done[0].shape[1]))
            unpack(done, places, len(done) > 1)
        at = 0
        for ref in (oga, osa, ogb, osb, odb, oqv, oub, opb, xga, xsa, xgb, xsb, xdb, xub):
            ref[...] = row[:, at : at + ref.shape[1]]
            at += padded(ref.shape[1])


def outputs_of(gc_low, *wholes, shapes, rows):
    total, width = gc_low.shape
    by_row = pl.BlockSpec((rows, width), lambda i: (i, 0))
    return pl.pallas_call(
        output_kernel,
        grid=(total // rows,),
        in_specs=[by_row] + [whole_block(a.shape) for a in wholes],
        out_specs=[by_row] + [whole_out(a) for a in shapes],
        out_shape=[jax.ShapeDtypeStruct(a, F32) for a in [(total, width), *shapes]],
        compiler_params=pltpu.CompilerParams(vmem_limit_bytes=VMEM_LIMIT),
        name="outputs",
    )(gc_low, *wholes)


def late_place(net_sizes, steps, step):
    if not net_sizes:
        return step
    return lax.rem((lax.axis_index("wide") + 1) * (steps // net_sizes[1]) + step, steps)


def char_forward_kernel(chars_per, steps, net_sizes, lengths, *refs):
    c_ref, cnt_ref, *refs = refs
    if net_sizes:
        net = Net(*net_sizes)
        shards, word_shards, vectors, refs = refs[:5], refs[5:9], refs[9:23], refs[23:]
        inbox, vec, *refs = refs
        char_out, word_out, refs = refs[:5], refs[5:9], refs[9:]
    else:
        win, wout, wup, wdn, wpj, vec, *refs = refs
        x_ref, *refs = refs
    pooled_ref, qkv_ref, p_ref, o_ref, h1_ref, h2_ref, m_ref, s_ref, *refs = refs
    h1_all, *refs = refs
    rows, width = c_ref.shape
    phase, step = pl.program_id(0), pl.program_id(1)
    now = phase * steps + step
    chunk = min(rows, 512)
    cw = chunk // chars_per
    words = rows // chars_per
    place = late_place(net_sizes, steps, step)

    if net_sizes:
        x_out, win, wout, wup, wdn, wpj, pieces, piece, *refs = refs
        gather = Gather(net, (shards[0], shards[1], piece), [win, wout, pieces], *refs[:3])
        shared = SharedGather(net, (*shards[2:], *word_shards), [wup, wdn, wpj, *word_out], *refs[3:10])
        exchange = Exchange(net, x_out, inbox, *refs[10:13])
        keep = refs[13]
        char_weights = (win, wout, wup, wdn, wpj)

        @pl.when(now == 0)
        def _():
            peers = [net.wide_peer(j)[1] for j in range(1, net.n_wide)] + [net.dp_peer(j)[1] for j in range(1, net.n_dp)]
            net.greet(peers)
            for ref, (at, length) in zip(vectors, lengths):
                some = length // net.n_wide
                piece[0, :, at : at + some] = ref[...].astype(F32).reshape(1, some)
            net.met(peers)
            for a in (2, 0, 1):
                gather.start(a)
            for a in (2, 0, 1):
                gather.relay(a)
            for a in range(3):
                shared.start(a)
            gather.finish(2)
            column = 0
            for at, length in lengths:
                some = length // net.n_wide
                row = jnp.concatenate([pieces[w, :, at : at + some] for w in range(net.n_wide)], 1)
                vec[:, column : column + length] = row
                column += length
            gather.finish(0)
            gather.finish(1)

        def start_words():
            for a in range(3, 7):
                shared.start(a)

        def relay_chars():
            for a in range(3):
                shared.relay(a)

        def pass_on_chars():
            for a in range(3):
                shared.pass_on(a)

        def finish_chars():
            for a in range(3):
                shared.finish(a)
            for a, weight in enumerate(char_weights):
                pltpu.make_async_copy(weight, char_out[a], keep.at[a]).start()

        schedule = [(1, start_words), (2, relay_chars), (5, pass_on_chars), (8, finish_chars)]
        schedule += [(6 + i, functools.partial(shared.relay, 3 + i)) for i in range(4)]
        schedule += [(12 + i, functools.partial(shared.pass_on, 3 + i)) for i in range(4)]
        for when, act in schedule:
            pl.when(now == when * steps // 8)(act)

    ga, sa, gb, sb, db, qv, ub, pb = char_vectors(vec, width, wup.shape[1], wpj.shape[1])

    def block(t):
        return pl.ds(pl.multiple_of(place * rows + t * chunk, chunk), chunk)

    @pl.when(phase == 0)
    def _():
        n, _ = normal_of(c_ref[...].astype(F32))
        a = (n * ga[...] + sa[...]).astype(BF)
        qkv = nn(a, win[...])
        qkv_ref[:, :width] = (qkv[:, :width] * HD**-0.5).astype(BF)
        qkv_ref[:, width:] = qkv[:, width:].astype(BF)
        ri = lax.broadcasted_iota(jnp.int32, (GROUP, GROUP), 0) // chars_per
        ci = lax.broadcasted_iota(jnp.int32, (GROUP, GROUP), 1) // chars_per
        same = ri == ci
        units = [(g, slice(g * GROUP, (g + 1) * GROUP), p) for g in range(rows // GROUP) for p in range(width // GROUP)]

        def head_pair(at, p, i):
            return qkv_ref[at, i * width + p * GROUP : i * width + (p + 1) * GROUP]

        valid = key_bias(cnt_ref[pl.ds(step, 1), :].astype(F32), chars_per)
        for g, at, p in units:
            bias = jnp.where(same, jnp.broadcast_to(valid[:1, g * GROUP : (g + 1) * GROUP], (GROUP, GROUP)), NEG)
            s = nt(head_pair(at, p, 0), two_heads(head_pair(at, p, 1)))
            for h in range(2):
                p_ref[at, (2 * p + h) * GROUP : (2 * p + h + 1) * GROUP] = softmax_low(s[:, h * GROUP : (h + 1) * GROUP] + bias)
        for _, at, p in units:
            o_ref[at, p * GROUP : (p + 1) * GROUP] = nn(p_ref[at, 2 * p * GROUP : 2 * (p + 1) * GROUP], two_heads(head_pair(at, p, 2))).astype(BF)
        for t in range(rows // chunk):
            at = slice(t * chunk, (t + 1) * chunk)
            h1 = c_ref[at, :].astype(F32) + nn(o_ref[at, :], wout[...])
            h1_ref[at, :] = h1.astype(BF)
            h1_all[pl.ds(pl.multiple_of(step * rows + t * chunk, chunk), chunk), :] = h1

    @pl.when(phase == 1)
    def _():
        counts = as_column(cnt_ref[pl.ds(place, 1), :].astype(F32))
        for t in range(rows // chunk):
            at = slice(t * chunk, (t + 1) * chunk)
            wat = slice(t * cw, (t + 1) * cw)
            h1 = h1_all[block(t), :]
            n, _ = normal_of(h1)
            u = (n * gb[...] + sb[...]).astype(BF)
            m, s = gelu_and_slope(nn(u, wup[...]) + ub[...])
            m_ref[at, :] = m.astype(BF)
            s_ref[at, :] = s.astype(BF)
            h2 = h1 + (nn(m_ref[at, :], wdn[...]) + db[...])
            h2_ref[at, :] = h2.astype(BF)
            om = pool_weights(h2, qv[...], counts[wat, :], chars_per)
            pooled_ref[wat, :] = jnp.sum(om * h2.reshape(cw, chars_per, width), 1).astype(BF)
        x = (nn(pooled_ref[...], wpj[...]) + pb[...]).astype(BF)
        if net_sizes:
            cap = x_out.shape[1]
            first_word = place * words
            target = first_word // cap
            x_out[target, pl.ds(pl.multiple_of(lax.rem(first_word, cap), words), words)] = x
            pl.when(lax.rem(first_word + words, cap) == 0)(lambda: exchange.send_block(target))
        else:
            x_ref[...] = x

    if net_sizes:

        @pl.when(now == 2 * steps - 1)
        def _():
            for a in range(3, 7):
                shared.finish(a)
            exchange.finish()
            for a, weight in enumerate(char_weights):
                pltpu.make_async_copy(weight, char_out[a], keep.at[a]).wait()


def char_forward(chars, counts, weights, chars_per, rows, net_sizes=None, word_shards=None, vectors=None, cap=None):
    total, width = chars.shape
    words, cw = total // chars_per, rows // chars_per
    ff, out = weights[2].shape[1], weights[4].shape[1]
    steps = total // rows

    def early(count, columns):
        return pl.BlockSpec((count, columns), lambda p, i: (i + p * (steps - 1 - i), 0))

    def late(count, columns):
        return pl.BlockSpec((count, columns), lambda p, i: (late_place(net_sizes, steps, i * p), 0))

    saved = [((words, width), BF, cw, late), ((total, 3 * width), BF, rows, early), ((total, 2 * width), BF, rows, early),
             ((total, width), BF, rows, early), ((total, width), BF, rows, early), ((total, width), BF, rows, late),
             ((total, ff), BF, rows, late), ((total, ff), BF, rows, late)]
    saved_specs = [where(count, s[1]) for s, _, count, where in saved]
    saved_shapes = [jax.ShapeDtypeStruct(s, d) for s, d, _, _ in saved]
    in_specs = [early(rows, width), whole_block(counts.shape)]
    operands = [chars, counts]
    scratch = [pltpu.VMEM((total, width), F32)]
    anywhere = pl.BlockSpec(memory_space=pl.ANY)
    if net_sizes:
        n_dp, n_wide = net_sizes
        n_z = n_wide // 2
        lengths, room = [], 0
        for v in vectors:
            lengths.append((room, v.shape[0] * n_wide))
            room += padded(v.shape[0])
        in_specs += [anywhere] * 9 + [whole_block(v.shape) for v in vectors]
        operands += [*weights, *word_shards, *vectors]
        vec_shape = jax.ShapeDtypeStruct((1, sum(length for _, length in lengths)), F32)
        grown = lambda a: jax.ShapeDtypeStruct((a.shape[0] * n_wide, a.shape[1]), a.dtype)
        fulls = [grown(a) for a in weights]
        out_specs = [anywhere, whole_out(vec_shape.shape)] + [anywhere] * 9 + saved_specs
        out_shapes = [jax.ShapeDtypeStruct((n_wide, cap, out), BF), vec_shape, *fulls, *(grown(a) for a in word_shards), *saved_shapes]
        scratch += (
            [pltpu.VMEM((n_wide, cap, out), BF)]
            + [pltpu.VMEM(a.shape, a.dtype) for a in fulls]
            + [pltpu.VMEM((n_wide, 1, room), F32), pltpu.VMEM((1, 1, room), F32)]
            + Gather.scratch(3, n_z)
            + SharedGather.scratch(7, n_dp, n_z)
            + Exchange.scratch(n_wide)
            + [pltpu.SemaphoreType.DMA((5,))]
        )
        params = pltpu.CompilerParams(vmem_limit_bytes=VMEM_LIMIT, collective_id=1, has_side_effects=True)
    else:
        lengths = None
        in_specs += [whole_block(w.shape) for w in weights]
        operands += [*weights]
        out_specs = [late(cw, out)] + saved_specs
        out_shapes = [jax.ShapeDtypeStruct((words, out), BF), *saved_shapes]
        params = pltpu.CompilerParams(vmem_limit_bytes=VMEM_LIMIT)
    return pl.pallas_call(
        functools.partial(char_forward_kernel, chars_per, steps, net_sizes, lengths),
        grid=(2, steps),
        in_specs=in_specs,
        out_specs=out_specs,
        out_shape=out_shapes,
        scratch_shapes=scratch,
        compiler_params=params,
        name="char_forward",
    )(*operands)


def word_kernel(slot_cap, net_sizes, *refs):
    arrived, bucket, assign, segment, grad_ref, win, wout, wup, wdn, vec, out_ref, back_out, *refs = refs
    length, width = grad_ref.shape
    ff = wup.shape[1]
    if net_sizes:
        net = Net(*net_sizes)
        grads_out, word_row, *refs = refs
        *held, word_grads, load_sem, store_sem = refs[-7:]
        refs = refs[:-7]
        loads = [pltpu.make_async_copy(src, dst, load_sem.at[i]) for i, (src, dst) in enumerate(zip((win, wout, wup, wdn), held))]
        for load in loads:
            load.start()
        win, wout, wup, wdn = held
        dga, dsa, dgb, dsb, ddb, dub = word_vectors(word_row, width, ff)
    else:
        dga, dsa, dwin, dwout, dgb, dsb, dwup, dub, dwdn, ddb, *refs = refs
    qkv_ref, p_ref, mix_ref, h_ref, s_ref, gq_ref, gs_ref, *refs = refs
    ga, sa, gb, sb, db, ub = word_vectors(vec, width, ff)
    owners = assign.shape[1]
    slots = owners * slot_cap
    if net_sizes:
        back_ref, *sems = refs
        exchange = Exchange(net, back_ref, back_out, *sems)
        peers = [net.wide_peer(j)[1] for j in range(1, net.n_wide)]
        net.greet(peers)
    def ready(i):
        if net_sizes:
            loads[i].wait()

    named = jnp.where(bucket[...] == lax.broadcasted_iota(jnp.int32, (owners, length), 0), 1.0, 0.0)
    ri = lax.broadcasted_iota(jnp.int32, (length, length), 0)
    ci = lax.broadcasted_iota(jnp.int32, (length, length), 1)
    earlier = nn(named.astype(BF), jnp.where(ri < ci, 1.0, 0.0).astype(BF))
    served = as_column(assign[...].astype(F32)) * slot_cap
    slot = jnp.sum(named * (served + earlier), 0, keepdims=True).astype(jnp.int32)
    hot = jnp.where(lax.broadcasted_iota(jnp.int32, (slots, length), 0) == slot, 1.0, 0.0).astype(BF)
    x = tn(hot, arrived[...].reshape(slots, width))
    n1, r1 = normal_of(x)
    a = (n1 * ga[...] + sa[...]).astype(BF)
    ready(0)
    qkv = nn(a, win[...])
    qkv_ref[:, :width] = (qkv[:, :width] * HD**-0.5).astype(BF)
    qkv_ref[:, width:] = qkv[:, width:].astype(BF)
    seg = segment[...].astype(F32)
    bias = jnp.where((seg == as_column(seg)) & (ci <= ri), 0.0, NEG)

    def pair(p):
        return [qkv_ref[:, i * width + p * GROUP : i * width + (p + 1) * GROUP] for i in range(3)]

    pairs = range(width // GROUP)

    def both(p):
        return slice(2 * p * length, (2 * p + 2) * length)

    for p in pairs:
        q, k, _ = pair(p)
        s = nt(q, two_heads(k))
        for h in range(2):
            p_ref[:, (2 * p + h) * length : (2 * p + h + 1) * length] = softmax_low(s[:, h * length : (h + 1) * length] + bias)
    for p in pairs:
        mix_ref[:, p * GROUP : (p + 1) * GROUP] = nn(p_ref[:, both(p)], two_heads(pair(p)[2])).astype(BF)
    ready(1)
    inner = x + nn(mix_ref[...], wout[...])
    n2, r2 = normal_of(inner)
    u = (n2 * gb[...] + sb[...]).astype(BF)
    ready(2)
    h, slope = gelu_and_slope(nn(u, wup[...]) + ub[...])
    h_ref[...] = h.astype(BF)
    s_ref[...] = slope
    ready(3)
    out_ref[...] = inner + (nn(h_ref[...], wdn[...]) + db[...])
    g = grad_ref[...]
    gz = (nt(g, wdn[...]) * s_ref[...]).astype(BF)
    du = nt(gz, wup[...])
    g1 = g.astype(F32) + norm_back(du, n2, r2, gb[...])
    g1_low = g1.astype(BF)
    gm = nt(g1_low, wout[...]).astype(BF)
    for p in pairs:
        dp = nt(gm[:, p * GROUP : (p + 1) * GROUP], two_heads(pair(p)[2]))
        for h in range(2):
            lanes = slice((2 * p + h) * length, (2 * p + h + 1) * length)
            gs_ref[:, lanes] = softmax_back(p_ref[:, lanes], dp[:, h * length : (h + 1) * length])
    for p in pairs:
        q, k, _ = pair(p)
        gs = gs_ref[:, both(p)]
        gq_ref[:, p * GROUP : (p + 1) * GROUP] = (nn(gs, two_heads(k)) * HD**-0.5).astype(BF)
        gq_ref[:, width + p * GROUP : width + (p + 1) * GROUP] = one_of_two(tn(gs, q)).astype(BF)
        gmp = gm[:, p * GROUP : (p + 1) * GROUP]
        gq_ref[:, 2 * width + p * GROUP : 2 * width + (p + 1) * GROUP] = one_of_two(tn(p_ref[:, both(p)], gmp)).astype(BF)
    da = nt(gq_ref[...], win[...])
    gx = (g1 + norm_back(da, n1, r1, ga[...])).astype(BF)
    back = nn(hot, gx).astype(BF).reshape(owners, slot_cap, width)
    if net_sizes:
        back_ref[...] = back
        net.met(peers)
        exchange.send_all()
        some = width // net.n_wide
        side = ff // width

        def put(value, column):
            value = value.astype(BF)
            for w in range(net.n_wide):
                word_grads[w // 2, w % 2, :, column : column + value.shape[1]] = value[w * some : (w + 1) * some]

        def store(i, first, columns):
            window = pl.ds(first, columns)
            return pltpu.make_async_copy(word_grads.at[:, :, :, window], grads_out.at[:, :, :, window], store_sem.at[i])

        put(tn(a, gq_ref[...]), 0)
        put(tn(mix_ref[...], g1_low), 3 * width)
        store(0, 0, 4 * width).start()
        put(tn(u, gz), 4 * width)
        store(1, 4 * width, ff).start()
        down = tn(h_ref[...], g).astype(BF)
        for w in range(net.n_wide):
            for k in range(side):
                first = (w * side + k) * some
                column = 4 * width + ff + k * width
                word_grads[w // 2, w % 2, :, column : column + width] = down[first : first + some]
        store(2, 4 * width + ff, ff).start()
    else:
        back_out[...] = back
        dwin[...] = tn(a, gq_ref[...])
        dwout[...] = tn(mix_ref[...], g1_low)
        dwup[...] = tn(u, gz)
        dwdn[...] = tn(h_ref[...], g)
    dga[...] = column_sum(da * n1)
    dsa[...] = column_sum(da)
    dgb[...] = column_sum(du * n2)
    dsb[...] = column_sum(du)
    dub[...] = column_sum(gz.astype(F32))
    ddb[...] = column_sum(g.astype(F32))
    if net_sizes:
        exchange.finish()
        for i, (first, columns) in enumerate(((0, 4 * width), (4 * width, ff), (4 * width + ff, ff))):
            store(i, first, columns).wait()


def word_block(arrived, bucket, assign, segments, grad, weights, slot_cap, net_sizes=None):
    length, width = grad.shape
    ff = weights[2].shape[1]
    owners = assign.shape[1]
    low = lambda *s: jax.ShapeDtypeStruct(s, BF)
    full = lambda *s: jax.ShapeDtypeStruct(s, F32)
    vmem = pl.BlockSpec(memory_space=pltpu.VMEM)
    out_shapes, out_specs = [full(length, width), low(owners, slot_cap, width)], [vmem, vmem]
    scratch = [pltpu.VMEM((length, 3 * width), BF), pltpu.VMEM((length, width // HD * length), BF), pltpu.VMEM((length, width), BF),
               pltpu.VMEM((length, ff), BF), pltpu.VMEM((length, ff), F32), pltpu.VMEM((length, 3 * width), BF),
               pltpu.VMEM((length, width // HD * length), BF)]
    if net_sizes:
        n_dp, n_wide = net_sizes
        out_shapes += [low(n_wide // 2, 2, width // n_wide, 4 * width + 2 * ff), full(1, 5 * width + ff)]
        anywhere = pl.BlockSpec(memory_space=pl.ANY)
        out_specs = [vmem, anywhere, anywhere, vmem]
        in_specs = [vmem] * 5 + [anywhere] * 4 + [vmem]
        scratch += [pltpu.VMEM((owners, slot_cap, width), BF)] + Exchange.scratch(n_wide)
        scratch += [pltpu.VMEM(w.shape, BF) for w in weights[:4]] + [pltpu.VMEM(out_shapes[2].shape, BF)]
        scratch += [pltpu.SemaphoreType.DMA((4,)), pltpu.SemaphoreType.DMA((3,))]
        params = pltpu.CompilerParams(vmem_limit_bytes=VMEM_LIMIT, collective_id=2, has_side_effects=True)
    else:
        row = full(1, width)
        out_shapes += [row, row, full(width, 3 * width), full(width, width), row, row, full(width, ff), full(1, ff), full(ff, width), row]
        out_specs += [vmem] * 10
        in_specs = [vmem] * 10
        params = pltpu.CompilerParams(vmem_limit_bytes=VMEM_LIMIT)
    return pl.pallas_call(
        functools.partial(word_kernel, slot_cap, net_sizes),
        in_specs=in_specs,
        out_specs=out_specs,
        out_shape=out_shapes,
        scratch_shapes=scratch,
        compiler_params=params,
        name="word_block",
    )(arrived, bucket, assign, segments, grad, *weights)


def gathered(shard):
    return lax.all_gather(shard, "wide", axis=0, tiled=True)


def exchanged(blocks):
    return lax.all_to_all(blocks, "wide", split_axis=0, concat_axis=0, tiled=True)


def summed(grad):
    part = lax.psum_scatter(grad.astype(BF), "wide", scatter_dimension=0, tiled=True)
    return lax.psum(part, "dp").astype(F32)


def shards(
    chars, char_counts, buckets, assign, segments,
    char_gain, char_shift, char_inproj, char_outproj, char_gain_mid, char_shift_mid, char_up, char_up_bias, char_down, char_down_bias,
    pool_query, char_proj, char_proj_bias,
    word_gain, word_shift, word_inproj, word_outproj, word_gain_mid, word_shift_mid, word_up, word_up_bias, word_down, word_down_bias,
    out_grad,
):
    n_dp, n_wide = lax.axis_size("dp"), lax.axis_size("wide")
    cap, chars_per, width = chars.shape[2:]
    slots = n_wide * cap
    rows = chars.reshape(slots * chars_per, width)
    block = min(1024, rows.shape[0])
    counts = char_counts.reshape(-1, block // chars_per)
    char_shards = (char_inproj, char_outproj, char_up, char_down, char_proj)
    word_shards = (word_inproj, word_outproj, word_up, word_down)
    vectors = (char_gain, char_shift, char_gain_mid, char_shift_mid, char_down_bias, pool_query, char_up_bias, char_proj_bias,
               word_gain, word_shift, word_gain_mid, word_shift_mid, word_down_bias, word_up_bias)
    fast = (
        all(m.shape[0] % 16 == 0 for m in char_shards)
        and all(m.shape[0] % (16 * n_dp) == 0 for m in word_shards)
        and cap % (block // chars_per) == 0
        and (4 * width) % (GROUP * n_dp) == 0
        and n_wide % 2 == 0
        and n_dp == 4
        and (4 * word_up.shape[0] * n_wide + 2 * word_up.shape[1]) % (8 * GROUP * WORD_PARTS) == 0
    )
    bucket, names, upstream = buckets.reshape(1, -1), assign[None], out_grad[0]
    if fast:
        sizes = (n_dp, n_wide)
        arrived, vec, *rest = char_forward(rows, counts, char_shards, chars_per, block, sizes, word_shards, vectors, cap)
        char_full, word_full, saved = rest[:5], rest[5:9], rest[9:]
        result, returned, word_grads, word_row = word_block(arrived, bucket, names, segments, upstream, (*word_full, vec), cap, sizes)
        incoming = returned.reshape(slots, -1)
        sums = char_backward(incoming, rows, counts, saved, (*char_full, vec), chars_per, block, sizes, word_grads, word_row)
        params = (char_gain, char_shift, char_inproj, char_outproj, char_gain_mid, char_shift_mid, char_up, char_up_bias, char_down,
                  char_down_bias, pool_query, char_proj, char_proj_bias, word_gain, word_shift, word_inproj, word_outproj, word_gain_mid,
                  word_shift_mid, word_up, word_up_bias, word_down, word_down_bias)
        shapes = [p.shape if p.ndim == 2 else (1, *p.shape) for p in params]
        char_grads, *grads = outputs_of(*sums, shapes=shapes, rows=min(2048, rows.shape[0]))
        grads = [g[0] if g.shape[0] == 1 else g for g in grads]
    else:
        vec = jnp.concatenate([gathered(v) for v in vectors]).astype(F32)[None]
        char_full, word_full = [gathered(m) for m in char_shards], [gathered(m) for m in word_shards]
        outgoing, *saved = char_forward(rows, counts, (*char_full, vec), chars_per, block)
        arrived = exchanged(outgoing.reshape(n_wide, cap, -1))
        result, back, *word_grads = word_block(arrived, bucket, names, segments, upstream, (*word_full, vec), cap)
        incoming = exchanged(back).reshape(slots, -1)
        char_grads, *grads = char_backward(incoming, rows, counts, saved, (*char_full, vec), chars_per, block)
        grads[8] = grads[8].T
        grads = [summed(g[0] if g.shape[0] == 1 else g) for g in grads + word_grads]
    return (result[None], char_grads.reshape(chars.shape), *grads)


def solution(mesh):
    whole, split = ("dp", "wide"), "wide"
    row, flat = P(split, None), P(split)
    word = [flat, flat, row, row, flat, flat, row, flat, row, flat]
    char = word + [flat, row, flat]
    chars = P(whole, None, None, None, None)
    three = P(whole, None, None)
    return jax.shard_map(
        shards,
        mesh=mesh,
        in_specs=(chars, three, three, P(), P(whole, None), *char, *word, three),
        out_specs=(three, chars, *char, *word),
        check_vma=False,
    )
```

```python
import functools

import jax
import jax.numpy as jnp
from jax import lax
from jax.experimental import pallas as pl
from jax.experimental.pallas import tpu as pltpu
from jax.sharding import PartitionSpec as P

EPS = 1e-05
NEG = -1e30
ROOT_HALF = 0.7071067811865476
INV_ROOT_TWO_PI = 0.3989422804014327
LOG2_E = 1.4426950408889634
HD = 64
GROUP = 128
F32 = jnp.float32
BF = jnp.bfloat16
MESH = pl.DeviceIdType.MESH
VMEM_LIMIT = 60 << 20
WORD_PARTS = 3


def nn(a, b):
    return lax.dot_general(a, b, (((1,), (0,)), ((), ())), preferred_element_type=F32)


def nt(a, b):
    return lax.dot_general(a, b, (((1,), (1,)), ((), ())), preferred_element_type=F32)


def tn(a, b):
    return lax.dot_general(a, b, (((0,), (0,)), ((), ())), preferred_element_type=F32)


def padded(lanes):
    return -(-lanes // GROUP) * GROUP


def column_sum(x):
    return jnp.sum(x, 0, keepdims=True)


def normal_of(x):
    c = x - jnp.mean(x, -1, keepdims=True)
    r = lax.rsqrt(jnp.mean(c * c, -1, keepdims=True) + EPS)
    return c * r, r


def norm_back(d, n, r, g):
    dg = d * g
    return r * (dg - jnp.mean(dg, -1, keepdims=True) - n * jnp.mean(dg * n, -1, keepdims=True))


def gelu_and_slope(z):
    w = z * ROOT_HALF
    cdf = 0.5 + 0.5 * lax.erf(w)
    return z * cdf, cdf + (z * INV_ROOT_TWO_PI) * jnp.exp2((w * w) * -LOG2_E)


def softmax_low(s):
    ex = jnp.exp(s - jnp.max(s, -1, keepdims=True))
    return (ex * (1.0 / jnp.sum(ex, -1, keepdims=True))).astype(BF)


def softmax_back(soft, d):
    soft = soft.astype(F32)
    return (soft * (d - jnp.sum(d * soft, -1, keepdims=True))).astype(BF)


def two_heads(t):
    left = lax.broadcasted_iota(jnp.int32, t.shape, 1) < HD
    zero = jnp.zeros_like(t)
    return jnp.concatenate([jnp.where(left, t, zero), jnp.where(left, zero, t)], 0)


def one_of_two(t):
    half = t.shape[0] // 2
    left = lax.broadcasted_iota(jnp.int32, (half, t.shape[1]), 1) < HD
    return jnp.where(left, t[:half], t[half:])


def as_column(row):
    n = row.shape[1]
    same = lax.broadcasted_iota(jnp.int32, (n, n), 0) == lax.broadcasted_iota(jnp.int32, (n, n), 1)
    return jnp.sum(jnp.where(same, jnp.broadcast_to(row, (n, n)), 0.0), -1, keepdims=True)


def key_bias(row, chars_per):
    n = row.shape[1]
    lanes = n * chars_per
    of_word = lax.broadcasted_iota(jnp.int32, (n, lanes), 1) // chars_per == lax.broadcasted_iota(jnp.int32, (n, lanes), 0)
    counts = nn(jnp.broadcast_to(row, (8, n)).astype(BF), jnp.where(of_word, 1.0, 0.0).astype(BF))
    place = lax.rem(lax.broadcasted_iota(jnp.int32, (8, lanes), 1), chars_per)
    return jnp.where(place.astype(F32) < counts, 0.0, NEG)


def pool_weights(h2, query, counts, chars_per):
    rows = h2.shape[0]
    words = rows // chars_per
    e = jnp.sum(h2 * query, -1, keepdims=True) * (h2.shape[1] ** -0.5)
    e = e.reshape(words, chars_per, 1)
    place = lax.broadcasted_iota(jnp.int32, (words, chars_per, 1), 1).astype(F32)
    e = jnp.where(place < counts.reshape(words, 1, 1), e, NEG)
    ex = jnp.exp(e - jnp.max(e, 1, keepdims=True))
    return ex / jnp.sum(ex, 1, keepdims=True)


class Net:
    def __init__(self, n_dp, n_wide):
        self.n_dp, self.n_wide, self.n_z = n_dp, n_wide, n_wide // 2
        self.dp, self.wide = lax.axis_index("dp"), lax.axis_index("wide")
        self.z, self.core = self.wide // 2, lax.rem(self.wide, 2)
        self.sibling = (self.dp, self.wide + 1 - 2 * self.core)

    def z_peer(self, j):
        z = lax.rem(self.z + j, self.n_z)
        return z, (self.dp, 2 * z + self.core)

    def dp_peer(self, j):
        q = lax.rem(self.dp + j, self.n_dp)
        return q, (q, self.wide)

    def wide_peer(self, j):
        w = lax.rem(self.wide + j, self.n_wide)
        return w, (self.dp, w)

    def greet(self, peers):
        barrier = pltpu.get_barrier_semaphore()
        for peer in peers:
            pl.semaphore_signal(barrier, inc=1, device_id=peer, device_id_type=MESH)

    def met(self, peers):
        pl.semaphore_wait(pltpu.get_barrier_semaphore(), len(peers))


def remote(src, dst, send, recv, peer):
    return pltpu.make_async_remote_copy(src_ref=src, dst_ref=dst, send_sem=send, recv_sem=recv, device_id=peer, device_id_type=MESH)


class Reduce:
    def __init__(self, net, grads, first, kept, from_core, part, from_dp, from_z, done, sems):
        self.net, self.grads = net, grads
        self.columns = pl.ds(first, kept.shape[-1])
        self.kept, self.from_core, self.part = kept, from_core, part
        self.from_dp, self.from_z, self.done = from_dp, from_z, done
        self.send, self.recv = sems
        self.span = part.shape[-1]

    @staticmethod
    def scratch(n_dp, n_z, rows, width):
        span = width // n_dp
        count = 2 + 2 * n_dp + n_z
        return [
            pltpu.VMEM((n_z, rows, width), BF),
            pltpu.VMEM((n_z, rows, width), BF),
            pltpu.VMEM((n_z, rows, span), BF),
            pltpu.VMEM((n_dp - 1, n_z, rows, span), BF),
            pltpu.VMEM((n_z - 1, rows, span), BF),
            pltpu.VMEM((n_dp, rows, span), BF),
            pltpu.SemaphoreType.DMA((count,)),
            pltpu.SemaphoreType.DMA((count,)),
        ]

    def lanes(self, q):
        return pl.ds(pl.multiple_of(q * self.span, GROUP), self.span)

    def to_core(self):
        net = self.net
        return remote(self.grads.at[:, 1 - net.core, :, self.columns], self.from_core, self.send.at[0], self.recv.at[0], net.sibling)

    def own(self):
        return pltpu.make_async_copy(self.grads.at[:, self.net.core, :, self.columns], self.kept, self.recv.at[1])

    def to_dp(self, j):
        q, peer = self.net.dp_peer(j)
        return remote(self.kept.at[:, :, self.lanes(q)], self.from_dp.at[j - 1], self.send.at[1 + j], self.recv.at[1 + j], peer)

    def to_z(self, j):
        z, peer = self.net.z_peer(j)
        at = 1 + self.net.n_dp + j
        return remote(self.part.at[z], self.from_z.at[j - 1], self.send.at[at], self.recv.at[at], peer)

    def to_all(self, j):
        net = self.net
        _, peer = net.dp_peer(j)
        at = 1 + net.n_dp + net.n_z + j
        mine = self.done.at[net.dp]
        return remote(mine, mine, self.send.at[at], self.recv.at[at], peer)

    def start(self):
        self.to_core().start()
        self.own().start()

    def over_dp(self):
        net = self.net
        self.own().wait()
        self.to_core().wait()

        @pl.loop(0, net.n_z)
        def _(z):
            self.kept[z] = (self.kept[z].astype(F32) + self.from_core[z].astype(F32)).astype(BF)

        for j in range(1, net.n_dp):
            self.to_dp(j).start()

    def over_z(self):
        net = self.net
        for j in range(1, net.n_dp):
            self.to_dp(j).wait()

        @pl.loop(0, net.n_z)
        def _(z):
            total = self.kept[z, :, self.lanes(net.dp)].astype(F32)
            for j in range(net.n_dp - 1):
                total = total + self.from_dp[j, z].astype(F32)
            self.part[z] = total.astype(BF)

        for j in range(1, net.n_z):
            self.to_z(j).start()

    def back_over_dp(self):
        net = self.net
        for j in range(1, net.n_z):
            self.to_z(j).wait()
        total = self.part[net.z].astype(F32)
        for j in range(net.n_z - 1):
            total = total + self.from_z[j].astype(F32)
        self.done[net.dp] = total.astype(BF)
        for j in range(1, net.n_dp):
            self.to_all(j).start()

    def finish(self):
        for j in range(1, self.net.n_dp):
            self.to_all(j).wait()


class TwoWayReduce(Reduce):
    @staticmethod
    def scratch(n_dp, n_z, rows, width):
        count = 2 + 2 * n_dp + n_z
        return [
            pltpu.VMEM((n_z, rows, width), BF),
            pltpu.VMEM((n_z, rows, width), BF),
            pltpu.VMEM((n_z, rows, width // n_dp), BF),
            pltpu.VMEM((2, n_z, rows, width // 4), BF),
            pltpu.VMEM((2, n_z, rows, width // 8), BF),
            pltpu.VMEM((n_z - 1, rows, width // n_dp), BF),
            pltpu.VMEM((n_dp, rows, width // n_dp), BF),
            pltpu.SemaphoreType.DMA((count,)),
            pltpu.SemaphoreType.DMA((count,)),
        ]

    def __init__(self, net, grads, first, kept, from_core, part, half, quarter, from_z, done, sems):
        super().__init__(net, grads, first, kept, from_core, part, None, from_z, done, sems)
        self.half, self.quarter = half, quarter
        x, y = lax.rem(net.dp, 2), net.dp // 2
        along_x, along_y = (net.dp + 1 - 2 * x, net.wide), (lax.rem(net.dp + 2, 4), net.wide)
        self.order = ((x, y, along_x, along_y), (y, x, along_y, along_x))

    def window(self, h, a, b=None):
        eighth = self.span // 2
        at = h * 4 * eighth + a * 2 * eighth
        if b is None:
            return pl.ds(pl.multiple_of(at, GROUP), 2 * eighth)
        return pl.ds(pl.multiple_of(at + b * eighth, GROUP), eighth)

    def first_step(self, h):
        a, _, peer, _ = self.order[h]
        return remote(self.kept.at[:, :, self.window(h, 1 - a)], self.half.at[h], self.send.at[2 + h], self.recv.at[2 + h], peer)

    def second_step(self, h):
        a, b, _, peer = self.order[h]
        return remote(self.kept.at[:, :, self.window(h, a, 1 - b)], self.quarter.at[h], self.send.at[4 + h], self.recv.at[4 + h], peer)

    def over_dp(self):
        self.own().wait()
        self.to_core().wait()

        @pl.loop(0, self.net.n_z)
        def _(z):
            self.kept[z] = (self.kept[z].astype(F32) + self.from_core[z].astype(F32)).astype(BF)

        for h in range(2):
            self.first_step(h).start()

    def over_dp_again(self):
        for h in range(2):
            self.first_step(h).wait()
        for h in range(2):
            mine = self.window(h, self.order[h][0])

            @pl.loop(0, self.net.n_z)
            def _(z):
                self.kept[z, :, mine] = (self.kept[z, :, mine].astype(F32) + self.half[h, z].astype(F32)).astype(BF)

        for h in range(2):
            self.second_step(h).start()

    def over_z(self):
        net = self.net
        for h in range(2):
            self.second_step(h).wait()
        eighth = self.span // 2
        for h in range(2):
            a, b, _, _ = self.order[h]
            mine = self.window(h, a, b)

            @pl.loop(0, net.n_z)
            def _(z):
                total = self.kept[z, :, mine].astype(F32) + self.quarter[h, z].astype(F32)
                self.part[z, :, h * eighth : (h + 1) * eighth] = total.astype(BF)

        for j in range(1, net.n_z):
            self.to_z(j).start()


class ReduceRows:
    def __init__(self, net, row, from_core, of_dp, of_z, sems):
        self.net, self.row, self.from_core, self.of_dp, self.of_z = net, row, from_core, of_dp, of_z
        self.send, self.recv = sems

    @staticmethod
    def scratch(n_dp, n_z, width):
        count = 1 + n_dp + n_z
        return [
            pltpu.VMEM((1, width), F32),
            pltpu.VMEM((1, width), F32),
            pltpu.VMEM((n_dp, 1, width), F32),
            pltpu.VMEM((n_z, 1, width), F32),
            pltpu.SemaphoreType.DMA((count,)),
            pltpu.SemaphoreType.DMA((count,)),
        ]

    def to_core(self):
        return remote(self.row, self.from_core, self.send.at[0], self.recv.at[0], self.net.sibling)

    def to_dp(self, j):
        mine = self.of_dp.at[self.net.dp]
        return remote(mine, mine, self.send.at[j], self.recv.at[j], self.net.dp_peer(j)[1])

    def to_z(self, j):
        mine = self.of_z.at[self.net.z]
        at = self.net.n_dp + j
        return remote(mine, mine, self.send.at[at], self.recv.at[at], self.net.z_peer(j)[1])

    def start(self):
        self.to_core().start()

    def over_dp(self):
        self.to_core().wait()
        self.of_dp[self.net.dp] = self.row[...] + self.from_core[...]
        for j in range(1, self.net.n_dp):
            self.to_dp(j).start()

    def over_z(self):
        net = self.net
        for j in range(1, net.n_dp):
            self.to_dp(j).wait()
        total = self.of_dp[0]
        for q in range(1, net.n_dp):
            total = total + self.of_dp[q]
        self.of_z[net.z] = total
        for j in range(1, net.n_z):
            self.to_z(j).start()

    def finish(self, out, places):
        net = self.net
        for j in range(1, net.n_z):
            self.to_z(j).wait()
        total = self.of_z[0]
        for z in range(1, net.n_z):
            total = total + self.of_z[z]
        at = 0
        for first, length in places:
            piece = length // net.n_wide
            vector = jnp.broadcast_to(total[:, first : first + length], (8, length))
            turned = pltpu.roll(vector, lax.rem(length - net.wide * piece, length), 1)
            out[:, at : at + piece] = turned[:1, :piece]
            at += padded(piece)


class Gather:
    def __init__(self, net, shards, wholes, send, recv, near):
        self.net, self.shards, self.wholes = net, shards, wholes
        self.send, self.recv, self.near = send, recv, near

    @staticmethod
    def scratch(count, n_z):
        return [
            pltpu.SemaphoreType.DMA((count, 2 * n_z)),
            pltpu.SemaphoreType.DMA((count, 2 * n_z)),
            pltpu.SemaphoreType.DMA((count,)),
        ]

    def block(self, a, owner):
        rows = self.shards[a].shape[0]
        return self.wholes[a].at[pl.ds(pl.multiple_of(owner * rows, rows), rows)]

    def along_z(self, a, j):
        net = self.net
        return remote(self.shards[a], self.block(a, net.wide), self.send.at[a, j], self.recv.at[a, net.wide], net.z_peer(j)[1])

    def across(self, a):
        net = self.net
        return remote(self.shards[a], self.block(a, net.wide), self.send.at[a, 0], self.recv.at[a, net.wide], net.sibling)

    def relayed(self, a, j):
        net = self.net
        owner = 2 * net.z_peer(j)[0] + net.core
        here = self.block(a, owner)
        return remote(here, here, self.send.at[a, net.n_z + j], self.recv.at[a, owner], net.sibling)

    def own(self, a):
        return pltpu.make_async_copy(self.shards[a], self.block(a, self.net.wide), self.near.at[a])

    def arrival(self, a, owner):
        here = self.block(a, owner)
        return remote(here, here, self.send.at[a, 0], self.recv.at[a, owner], self.net.sibling)

    def start(self, a):
        for j in range(1, self.net.n_z):
            self.along_z(a, j).start()
        self.across(a).start()
        self.own(a).start()

    def relay(self, a):
        net = self.net
        for j in range(1, net.n_z):
            self.arrival(a, 2 * net.z_peer(j)[0] + net.core).wait_recv()
            self.relayed(a, j).start()

    def finish(self, a):
        net = self.net
        self.own(a).wait()
        self.across(a).wait_send()
        for j in range(1, net.n_z):
            self.along_z(a, j).wait_send()
            self.relayed(a, j).wait_send()
        for z in range(net.n_z):
            self.arrival(a, 2 * z + 1 - net.core).wait_recv()


class SharedGather:
    def __init__(self, net, shards, wholes, send_z, send_dp, send_core, recv_z, recv_dp, recv_core, near):
        self.net, self.shards, self.wholes = net, shards, wholes
        self.send_z, self.send_dp, self.send_core = send_z, send_dp, send_core
        self.recv_z, self.recv_dp, self.recv_core, self.near = recv_z, recv_dp, recv_core, near

    @staticmethod
    def scratch(count, n_dp, n_z):
        sem = pltpu.SemaphoreType.DMA
        return [
            sem((count, n_z)), sem((count, n_z, n_dp)), sem((count, n_z)),
            sem((count, n_z)), sem((count, n_z, n_dp)), sem((count, n_z)), sem((count,)),
        ]

    def block(self, a, owner):
        rows = self.shards[a].shape[0]
        return self.wholes[a].at[pl.ds(pl.multiple_of(owner * rows, rows), rows)]

    def part(self, a, q):
        rows, columns = self.shards[a].shape
        n_dp = self.net.n_dp
        if rows % (16 * n_dp) == 0:
            some = rows // n_dp
            return pl.multiple_of(q * some, some), some, 0, columns
        some = columns // n_dp
        return 0, rows, pl.multiple_of(q * some, some), some

    def piece(self, a, owner, q):
        rows = self.shards[a].shape[0]
        row, height, column, width = self.part(a, q)
        return self.wholes[a].at[pl.ds(pl.multiple_of(owner * rows + row, height), height), pl.ds(column, width)]

    def along_z(self, a, j):
        net = self.net
        row, height, column, width = self.part(a, net.dp)
        mine = self.shards[a].at[pl.ds(row, height), pl.ds(column, width)]
        return remote(mine, self.piece(a, net.wide, net.dp), self.send_z.at[a, j], self.recv_z.at[a, net.z], net.z_peer(j)[1])

    def from_z(self, a, j):
        net = self.net
        z, peer = net.z_peer(j)
        here = self.piece(a, 2 * z + net.core, net.dp)
        return remote(here, here, self.send_z.at[a, j], self.recv_z.at[a, z], peer)

    def over_dp(self, a, j, i):
        net = self.net
        z = net.z_peer(j)[0]
        here = self.piece(a, 2 * z + net.core, net.dp)
        return remote(here, here, self.send_dp.at[a, j, i], self.recv_dp.at[a, j, net.dp], net.dp_peer(i)[1])

    def from_dp(self, a, j, i):
        net = self.net
        z = net.z_peer(j)[0]
        q, peer = net.dp_peer(i)
        here = self.piece(a, 2 * z + net.core, q)
        return remote(here, here, self.send_dp.at[a, j, i], self.recv_dp.at[a, j, q], peer)

    def across(self, a, j):
        net = self.net
        z = net.z_peer(j)[0]
        here = self.block(a, 2 * z + net.core)
        source = self.shards[a] if j == 0 else here
        return remote(source, here, self.send_core.at[a, j], self.recv_core.at[a, z], net.sibling)

    def from_core(self, a, z):
        net = self.net
        here = self.block(a, 2 * z + 1 - net.core)
        return remote(here, here, self.send_core.at[a, 0], self.recv_core.at[a, z], net.sibling)

    def own(self, a):
        return pltpu.make_async_copy(self.shards[a], self.block(a, self.net.wide), self.near.at[a])

    def start(self, a):
        for j in range(1, self.net.n_z):
            self.along_z(a, j).start()
        self.across(a, 0).start()
        self.own(a).start()

    def relay(self, a):
        net = self.net
        for j in range(1, net.n_z):
            self.from_z(a, j).wait_recv()
            for i in range(1, net.n_dp):
                self.over_dp(a, j, i).start()

    def pass_on(self, a):
        net = self.net
        for j in range(1, net.n_z):
            for i in range(1, net.n_dp):
                self.from_dp(a, j, i).wait_recv()
            self.across(a, j).start()

    def finish(self, a):
        net = self.net
        self.own(a).wait()
        for j in range(1, net.n_z):
            self.along_z(a, j).wait_send()
            for i in range(1, net.n_dp):
                self.over_dp(a, j, i).wait_send()
        for j in range(net.n_z):
            self.across(a, j).wait_send()
            self.from_core(a, j).wait_recv()


class Exchange:
    def __init__(self, net, out, inbox, send, recv, near):
        self.net, self.out, self.inbox = net, out, inbox
        self.send, self.recv, self.near = send, recv, near

    @staticmethod
    def scratch(n_wide):
        return [pltpu.SemaphoreType.DMA((n_wide,)), pltpu.SemaphoreType.DMA((n_wide,)), pltpu.SemaphoreType.DMA(())]

    def to(self, w):
        net = self.net
        return remote(self.out.at[w], self.inbox.at[net.wide], self.send.at[w], self.recv.at[net.wide], (net.dp, w))

    def arrival(self, w):
        here = self.inbox.at[w]
        return remote(here, here, self.send.at[w], self.recv.at[w], (self.net.dp, w))

    def own(self):
        me = self.net.wide
        return pltpu.make_async_copy(self.out.at[me], self.inbox.at[me], self.near)

    def send_block(self, w):
        @pl.when(w != self.net.wide)
        def _():
            self.to(w).start()

        @pl.when(w == self.net.wide)
        def _():
            self.own().start()

    def send_all(self):
        for j in range(1, self.net.n_wide):
            self.to(self.net.wide_peer(j)[0]).start()
        self.own().start()

    def finish(self):
        for j in range(1, self.net.n_wide):
            w = self.net.wide_peer(j)[0]
            self.to(w).wait_send()
            self.arrival(w).wait_recv()
        self.own().wait()


def slices_of(ref, first, lengths):
    views = []
    for length in lengths:
        views.append(ref.at[:, first : first + length])
        first += length
    return views


def char_vectors(row, width, ff, out):
    return slices_of(row, 0, [width] * 6 + [ff, out])


def word_vectors(row, width, ff):
    return slices_of(row, row.shape[1] - 5 * width - ff, [width] * 5 + [ff])


def char_back_kernel(chars_per, steps, net_sizes, word_sizes, *refs):
    (
        gx_ref, c_ref, cnt_ref, qkv_ref, p_ref, o_ref, h1_ref, h2_ref, m_ref, s_ref, pooled_all, gx_all,
        win, wout, wup, wdn, wpj, vec, *refs
    ) = refs
    if net_sizes:
        word_grads, word_row, *refs = refs
    gc_ref, *refs = refs
    if net_sizes:
        outs, refs = refs[: WORD_PARTS + 3], refs[WORD_PARTS + 3 :]
    accs, refs = refs[:13], refs[13:]
    dga, dsa, dwin, dwout, dgb, dsb, dwup, dub, dwdn, ddb, dqv, dwpj, dpb = accs
    gh1_ref, gm_ref, u_ref, gz_ref, gq_ref, gs_ref, *refs = refs
    rows, width = c_ref.shape
    ga, sa, gb, sb, _, qv, _, _ = char_vectors(vec, width, wup.shape[1], wpj.shape[1])
    phase, step = pl.program_id(0), pl.program_id(1)
    now = phase * steps + step
    factor = width**-0.5
    chunk = min(rows, 512)
    cw = chunk // chars_per
    words = rows // chars_per

    if net_sizes:
        net = Net(*net_sizes)
        ff_grads, at_grads, row, *refs = refs
        each = word_grads.shape[-1] // WORD_PARTS
        words_of = []
        for part in range(WORD_PARTS):
            words_of.append(TwoWayReduce(net, word_grads, part * each, *refs[:7], refs[7:9]))
            refs = refs[9:]
        ff = Reduce(net, ff_grads, 0, *refs[:6], refs[6:8])
        att = Reduce(net, at_grads, 0, *refs[8:14], refs[14:16])
        rowsum = ReduceRows(net, row, *refs[16:19], refs[19:21])
        keep = refs[21]

        @pl.when(now == 0)
        def _():
            peers = [net.sibling] + [net.dp_peer(j)[1] for j in range(1, net.n_dp)] + [net.z_peer(j)[1] for j in range(1, net.n_z)]
            net.greet(peers)
            net.met(peers)
            for part in words_of:
                part.start()

        one, two, three = words_of
        schedule = (
            (1, one.over_dp),
            (2, two.over_dp),
            (3, one.over_dp_again),
            (4, three.over_dp),
            (5, two.over_dp_again),
            (6, one.over_z),
            (7, three.over_dp_again),
            (8, two.over_z),
            (8, ff.start),
            (9, one.back_over_dp),
            (10, three.over_z),
            (10, ff.over_dp),
            (11, two.back_over_dp),
            (13, three.back_over_dp),
            (13, ff.over_z),
            (15, ff.back_over_dp),
        )
        for when, act in schedule:
            pl.when(now == when * steps // 8)(act)

    @pl.when(now == 0)
    def _():
        for acc in accs:
            acc[...] = jnp.zeros_like(acc)
        dwpj[...] = tn(pooled_all[...], gx_all[...])
        dpb[...] = column_sum(gx_all[...].astype(F32))

    here = pl.ds(pl.multiple_of(step * rows, rows), rows)

    @pl.when(phase == 0)
    def _():
        gp = nt(gx_ref[...], wpj[...]).astype(BF).astype(F32)
        counts = as_column(cnt_ref[pl.ds(step, 1), :].astype(F32))
        for t in range(rows // chunk):
            at = slice(t * chunk, (t + 1) * chunk)
            wat = slice(t * cw, (t + 1) * cw)
            h2 = h2_ref[at, :].astype(F32)
            om = pool_weights(h2, qv[...], counts[wat, :], chars_per)
            gpb = jnp.broadcast_to(gp[wat, :].reshape(cw, 1, width), (cw, chars_per, width)).reshape(chunk, width)
            w = jnp.sum(h2 * gpb, -1, keepdims=True).reshape(cw, chars_per, 1)
            de = om * (w - jnp.sum(om * w, 1, keepdims=True))
            de = de.reshape(chunk, 1) * factor
            gh2 = om.reshape(chunk, 1) * gpb + de * qv[...]
            dqv[...] += column_sum(de * h2)
            gy = gh2.astype(BF)
            ddb[...] += column_sum(gy.astype(F32))
            gm_ref[at, :] = gy
            gz = nt(gy, wdn[...]).astype(BF) * s_ref[at, :]
            gz_ref[at, :] = gz
            dub[...] += column_sum(gz.astype(F32))
            du = nt(gz, wup[...])
            n, r = normal_of(h1_ref[at, :].astype(F32))
            dgb[...] += column_sum(du * n)
            dsb[...] += column_sum(du)
            u_ref[at, :] = (n * gb[...] + sb[...]).astype(BF)
            gh1_ref[pl.ds(pl.multiple_of(step * rows + t * chunk, chunk), chunk), :] = (gh2 + norm_back(du, n, r, gb[...])).astype(BF)
        dwup[...] += tn(u_ref[...], gz_ref[...])
        dwdn[...] += tn(gm_ref[...], m_ref[...])

    if net_sizes:
        n_z, n_wide = net.n_z, net.n_wide

        @pl.when(now == steps - 1)
        def _():
            up, proj = dwup.shape[1], dwpj.shape[1]
            down = dwdn[...].T
            some = width // n_wide
            side = down.shape[0] // n_wide // some
            for owner in range(n_wide):
                z, core = owner // 2, owner % 2
                mine = slice(owner * some, (owner + 1) * some)
                ff_grads[z, core, :, :up] = dwup[mine, :].astype(BF)
                ff_grads[z, core, :, up : up + proj] = dwpj[mine, :].astype(BF)
                for k in range(side):
                    first = (owner * side + k) * some
                    ff_grads[z, core, :, up + proj + k * width : up + proj + (k + 1) * width] = down[first : first + some].astype(BF)

    @pl.when(phase == 1)
    def _():
        g1 = gh1_ref[here, :]
        dwout[...] += tn(o_ref[...], g1)
        gm_ref[...] = nt(g1, wout[...]).astype(BF)
        units = [(slice(g * GROUP, (g + 1) * GROUP), p) for g in range(rows // GROUP) for p in range(width // GROUP)]

        def head_pair(at, p, i):
            return qkv_ref[at, i * width + p * GROUP : i * width + (p + 1) * GROUP]

        for at, p in units:
            dp = nt(gm_ref[at, p * GROUP : (p + 1) * GROUP], two_heads(head_pair(at, p, 2)))
            for h in range(2):
                lanes = slice((2 * p + h) * GROUP, (2 * p + h + 1) * GROUP)
                gs_ref[at, lanes] = softmax_back(p_ref[at, lanes], dp[:, h * GROUP : (h + 1) * GROUP])
        for at, p in units:
            gs = gs_ref[at, 2 * p * GROUP : 2 * (p + 1) * GROUP]
            gq_ref[at, p * GROUP : (p + 1) * GROUP] = (nn(gs, two_heads(head_pair(at, p, 1))) * HD**-0.5).astype(BF)
            gq_ref[at, width + p * GROUP : width + (p + 1) * GROUP] = one_of_two(tn(gs, head_pair(at, p, 0))).astype(BF)
            soft = p_ref[at, p * 2 * GROUP : (p + 1) * 2 * GROUP]
            gm = gm_ref[at, p * GROUP : (p + 1) * GROUP]
            gq_ref[at, 2 * width + p * GROUP : 2 * width + (p + 1) * GROUP] = one_of_two(tn(soft, gm)).astype(BF)
        for t in range(rows // chunk):
            at = slice(t * chunk, (t + 1) * chunk)
            n, r = normal_of(c_ref[at, :].astype(F32))
            u_ref[at, :] = (n * ga[...] + sa[...]).astype(BF)
            da = nt(gq_ref[at, :], win[...])
            dga[...] += column_sum(da * n)
            dsa[...] += column_sum(da)
            grad = gh1_ref[pl.ds(pl.multiple_of(step * rows + t * chunk, chunk), chunk), :].astype(F32) + norm_back(da, n, r, ga[...])
            gc_ref[at, :] = grad.astype(gc_ref.dtype)
        dwin[...] += tn(u_ref[...], gq_ref[...])

    if net_sizes:

        @pl.when(now == 2 * steps - 1)
        def _():
            some = width // n_wide
            for owner in range(n_wide):
                z, core = owner // 2, owner % 2
                mine = slice(owner * some, (owner + 1) * some)
                at_grads[z, core, :, : 3 * width] = dwin[mine, :].astype(BF)
                at_grads[z, core, :, 3 * width :] = dwout[mine, :].astype(BF)
            column, places = 0, []
            for acc in (dga, dsa, dgb, dsb, ddb, dqv, dub, dpb):
                row[:, column : column + acc.shape[1]] = acc[...]
                places.append((column, acc.shape[1]))
                column += acc.shape[1]
            row[:, column:] = word_row[...]
            for ref in word_vectors(row, *word_sizes):
                places.append((column, ref.shape[1]))
                column += ref.shape[1]
            att.start()
            rowsum.start()
            for part in words_of:
                part.finish()
            ff.finish()
            att.over_dp()
            rowsum.over_dp()
            att.over_z()
            rowsum.over_z()
            att.back_over_dp()
            rowsum.finish(outs[-1], places)
            att.finish()
            copies = [pltpu.make_async_copy(piece.done, out, keep.at[i]) for i, (piece, out) in enumerate(zip((*words_of, ff, att), outs))]
            for copy in copies:
                copy.start()
            for copy in copies:
                copy.wait()


def whole_block(shape):
    return pl.BlockSpec(shape, lambda *_: (0,) * len(shape), pipeline_mode=pl.Buffered(1))


def whole_out(shape):
    return pl.BlockSpec(shape, lambda *_: (0,) * len(shape))


def char_backward(gx, chars, counts, saved, weights, chars_per, rows, net_sizes=None, word_grads=None, word_row=None):
    total, width = chars.shape
    win, wout, wup, wdn, wpj, vec = weights
    pooled, qkv, soft, mixed, h1, h2, m, s = saved
    words, cw = total // chars_per, rows // chars_per
    ff, out = wup.shape[1], wpj.shape[1]
    steps = total // rows

    def early(count, columns):
        return pl.BlockSpec((count, columns), lambda p, i: (i + p * (steps - 1 - i), 0))

    def late(count, columns):
        return pl.BlockSpec((count, columns), lambda p, i: (i * p, 0))

    accs = [(1, width), (1, width), (width, 3 * width), (width, width), (1, width), (1, width), (width, ff), (1, ff),
            (width, ff), (1, width), (1, width), (width, out), (1, out)]
    in_specs = [early(cw, out), late(rows, width), whole_block(counts.shape), late(rows, 3 * width), late(rows, 2 * width),
                late(rows, width), early(rows, width), early(rows, width), early(rows, ff), early(rows, ff),
                whole_block(pooled.shape), whole_block(gx.shape)] + [whole_block(w.shape) for w in weights]
    operands = [gx, chars, counts, qkv, soft, mixed, h1, h2, m, s, pooled, gx, *weights]
    scratch = [pltpu.VMEM((total, width), BF), pltpu.VMEM((rows, width), BF), pltpu.VMEM((rows, width), BF),
               pltpu.VMEM((rows, ff), BF), pltpu.VMEM((rows, 3 * width), BF), pltpu.VMEM((rows, 2 * width), BF)]
    if net_sizes:
        n_dp, n_wide = net_sizes
        n_z, some = n_wide // 2, width // n_wide
        word_rows, word_width = word_grads.shape[2:]
        wide_d = n_wide * word_rows
        word_ff = word_row.shape[1] - 5 * wide_d
        operands += [word_grads, word_row]
        in_specs += [pl.BlockSpec(memory_space=pl.ANY), whole_block(word_row.shape)]
        ff_width, at_width = ff + out + ff, 4 * width
        row_width = 6 * width + ff + out + word_row.shape[1]
        word_sizes = (wide_d, word_ff)
        sums = [(n_dp, word_rows, word_width // WORD_PARTS // n_dp)] * WORD_PARTS + [(n_dp, some, ff_width // n_dp), (n_dp, some, at_width // n_dp)]
        pieces = sum(padded(n // n_wide) for n in [width] * 6 + [ff, out] + [wide_d] * 5 + [word_ff])
        out_shapes = [jax.ShapeDtypeStruct((total, width), BF)] + [jax.ShapeDtypeStruct(a, BF) for a in sums] + [jax.ShapeDtypeStruct((1, pieces), F32)]
        out_specs = [late(rows, width)] + [pl.BlockSpec(memory_space=pl.ANY)] * len(sums) + [whole_out((1, pieces))]
        scratch = (
            [pltpu.VMEM(a, F32) for a in accs]
            + scratch
            + [pltpu.VMEM((n_z, 2, some, ff_width), BF), pltpu.VMEM((n_z, 2, some, at_width), BF), pltpu.VMEM((1, row_width), F32)]
            + TwoWayReduce.scratch(n_dp, n_z, word_rows, word_width // WORD_PARTS) * WORD_PARTS
            + Reduce.scratch(n_dp, n_z, some, ff_width)
            + Reduce.scratch(n_dp, n_z, some, at_width)
            + ReduceRows.scratch(n_dp, n_z, row_width)[1:]
            + [pltpu.SemaphoreType.DMA((len(sums),))]
        )
        params = pltpu.CompilerParams(vmem_limit_bytes=VMEM_LIMIT, collective_id=3, has_side_effects=True)
    else:
        word_sizes = None
        out_shapes = [jax.ShapeDtypeStruct(a, F32) for a in [(total, width)] + accs]
        out_specs = [late(rows, width)] + [whole_out(a) for a in accs]
        params = pltpu.CompilerParams(vmem_limit_bytes=VMEM_LIMIT)
    return pl.pallas_call(
        functools.partial(char_back_kernel, chars_per, steps, net_sizes, word_sizes),
        grid=(2, steps),
        in_specs=in_specs,
        out_specs=out_specs,
        out_shape=out_shapes,
        scratch_shapes=scratch,
        compiler_params=params,
        name="char_backward",
    )(*operands)


def unpack(parts, outs, two_way):
    n_dp, rows, span = parts[0].shape
    for ref, first, columns, side in outs:
        for k in range(side):
            for at in range(0, columns, GROUP):
                column = first + k * columns + at
                part, column = column // (n_dp * span), column % (n_dp * span)
                if two_way:
                    eighth = span // 2
                    h, place, lane = column // (4 * eighth), column // eighth % 4, column % eighth
                    q = place if h else place // 2 + place % 2 * 2
                    lane += h * eighth
                else:
                    q, lane = column // span, column % span
                ref[k * rows : (k + 1) * rows, at : at + GROUP] = parts[part][q, :, lane : lane + GROUP].astype(F32)


def output_kernel(gc_low, *refs):
    word_done, (ff_done, at_done, row, gc_ref, *outs) = refs[:WORD_PARTS], refs[WORD_PARTS:]
    gc_ref[...] = gc_low[...].astype(F32)

    @pl.when(pl.program_id(0) == 0)
    def _():
        (
            oga, osa, owin, owout, ogb, osb, oup, oub, odn, odb, oqv, opj, opb,
            xga, xsa, xwin, xwout, xgb, xsb, xup, xub, xdn, xdb,
        ) = outs
        for done, across, down in ((word_done, (xwin, xwout, xup), xdn), ([ff_done], (oup, opj), odn), ([at_done], (owin, owout), None)):
            places, column = [], 0
            for ref in across:
                places.append((ref, column, ref.shape[1], 1))
                column += ref.shape[1]
            if down is not None:
                places.append((down, column, down.shape[1], down.shape[0] // done[0].shape[1]))
            unpack(done, places, len(done) > 1)
        at = 0
        for ref in (oga, osa, ogb, osb, odb, oqv, oub, opb, xga, xsa, xgb, xsb, xdb, xub):
            ref[...] = row[:, at : at + ref.shape[1]]
            at += padded(ref.shape[1])


def outputs_of(gc_low, *wholes, shapes, rows):
    total, width = gc_low.shape
    by_row = pl.BlockSpec((rows, width), lambda i: (i, 0))
    return pl.pallas_call(
        output_kernel,
        grid=(total // rows,),
        in_specs=[by_row] + [whole_block(a.shape) for a in wholes],
        out_specs=[by_row] + [whole_out(a) for a in shapes],
        out_shape=[jax.ShapeDtypeStruct(a, F32) for a in [(total, width), *shapes]],
        compiler_params=pltpu.CompilerParams(vmem_limit_bytes=VMEM_LIMIT),
        name="outputs",
    )(gc_low, *wholes)


def late_place(net_sizes, steps, step):
    if not net_sizes:
        return step
    return lax.rem((lax.axis_index("wide") + 1) * (steps // net_sizes[1]) + step, steps)


def char_forward_kernel(chars_per, steps, net_sizes, lengths, *refs):
    c_ref, cnt_ref, *refs = refs
    if net_sizes:
        net = Net(*net_sizes)
        shards, word_shards, vectors, refs = refs[:5], refs[5:9], refs[9:23], refs[23:]
        inbox, vec, *refs = refs
        char_out, word_out, refs = refs[:5], refs[5:9], refs[9:]
    else:
        win, wout, wup, wdn, wpj, vec, *refs = refs
        x_ref, *refs = refs
    pooled_ref, qkv_ref, p_ref, o_ref, h1_ref, h2_ref, m_ref, s_ref, *refs = refs
    h1_all, c_all, n_all, c_sem, *refs = refs
    rows, width = c_ref.shape[0] // steps, c_ref.shape[1]
    phase, step = pl.program_id(0), pl.program_id(1)
    now = phase * steps + step
    chunk = min(rows, 512)
    cw = chunk // chars_per
    words = rows // chars_per
    place = late_place(net_sizes, steps, step)
    load = pltpu.make_async_copy(c_ref, c_all, c_sem)

    def normalize():
        load.wait()

        @pl.loop(0, steps * rows // chunk)
        def _(t):
            at = pl.ds(pl.multiple_of(t * chunk, chunk), chunk)
            n_all[at, :], _ = normal_of(c_all[at, :].astype(F32))

    pl.when(now == 0)(load.start)

    if net_sizes:
        x_out, win, wout, wup, wdn, wpj, pieces, piece, *refs = refs
        gather = Gather(net, (shards[0], shards[1], piece), [win, wout, pieces], *refs[:3])
        shared = SharedGather(net, (*shards[2:], *word_shards), [wup, wdn, wpj, *word_out], *refs[3:10])
        exchange = Exchange(net, x_out, inbox, *refs[10:13])
        keep = refs[13]
        char_weights = (win, wout, wup, wdn, wpj)

        @pl.when(now == 0)
        def _():
            peers = [net.wide_peer(j)[1] for j in range(1, net.n_wide)] + [net.dp_peer(j)[1] for j in range(1, net.n_dp)]
            net.greet(peers)
            for ref, (at, length) in zip(vectors, lengths):
                some = length // net.n_wide
                piece[0, :, at : at + some] = ref[...].astype(F32).reshape(1, some)
            net.met(peers)
            for a in (2, 0, 1):
                gather.start(a)
            normalize()
            for a in (2, 0, 1):
                gather.relay(a)
            for a in range(3):
                shared.start(a)
            gather.finish(2)
            column = 0
            for at, length in lengths:
                some = length // net.n_wide
                row = jnp.concatenate([pieces[w, :, at : at + some] for w in range(net.n_wide)], 1)
                vec[:, column : column + length] = row
                column += length
            gather.finish(0)
            gather.finish(1)

        def start_words():
            for a in range(3, 7):
                shared.start(a)

        def relay_chars():
            for a in range(3):
                shared.relay(a)

        def pass_on_chars():
            for a in range(3):
                shared.pass_on(a)

        def finish_chars():
            for a in range(3):
                shared.finish(a)
            for a, weight in enumerate(char_weights):
                pltpu.make_async_copy(weight, char_out[a], keep.at[a]).start()

        schedule = [(1, start_words), (2, relay_chars), (5, pass_on_chars), (8, finish_chars)]
        schedule += [(6 + i, functools.partial(shared.relay, 3 + i)) for i in range(4)]
        schedule += [(12 + i, functools.partial(shared.pass_on, 3 + i)) for i in range(4)]
        for when, act in schedule:
            pl.when(now == when * steps // 8)(act)

    else:
        pl.when(now == 0)(normalize)

    ga, sa, gb, sb, db, qv, ub, pb = char_vectors(vec, width, wup.shape[1], wpj.shape[1])

    def block(t):
        return pl.ds(pl.multiple_of(place * rows + t * chunk, chunk), chunk)

    @pl.when(phase == 0)
    def _():
        a = (n_all[pl.ds(pl.multiple_of(step * rows, rows), rows), :] * ga[...] + sa[...]).astype(BF)
        qkv = nn(a, win[...])
        qkv_ref[:, :width] = (qkv[:, :width] * HD**-0.5).astype(BF)
        qkv_ref[:, width:] = qkv[:, width:].astype(BF)
        ri = lax.broadcasted_iota(jnp.int32, (GROUP, GROUP), 0) // chars_per
        ci = lax.broadcasted_iota(jnp.int32, (GROUP, GROUP), 1) // chars_per
        same = ri == ci
        units = [(g, slice(g * GROUP, (g + 1) * GROUP), p) for g in range(rows // GROUP) for p in range(width // GROUP)]

        def head_pair(at, p, i):
            return qkv_ref[at, i * width + p * GROUP : i * width + (p + 1) * GROUP]

        valid = key_bias(cnt_ref[pl.ds(step, 1), :].astype(F32), chars_per)
        for g, at, p in units:
            bias = jnp.where(same, jnp.broadcast_to(valid[:1, g * GROUP : (g + 1) * GROUP], (GROUP, GROUP)), NEG)
            s = nt(head_pair(at, p, 0), two_heads(head_pair(at, p, 1)))
            for h in range(2):
                p_ref[at, (2 * p + h) * GROUP : (2 * p + h + 1) * GROUP] = softmax_low(s[:, h * GROUP : (h + 1) * GROUP] + bias)
        for _, at, p in units:
            o_ref[at, p * GROUP : (p + 1) * GROUP] = nn(p_ref[at, 2 * p * GROUP : 2 * (p + 1) * GROUP], two_heads(head_pair(at, p, 2))).astype(BF)
        for t in range(rows // chunk):
            at = slice(t * chunk, (t + 1) * chunk)
            here = pl.ds(pl.multiple_of(step * rows + t * chunk, chunk), chunk)
            h1 = c_all[here, :].astype(F32) + nn(o_ref[at, :], wout[...])
            h1_ref[at, :] = h1.astype(BF)
            h1_all[here, :] = h1

    @pl.when(phase == 1)
    def _():
        counts = as_column(cnt_ref[pl.ds(place, 1), :].astype(F32))
        for t in range(rows // chunk):
            at = slice(t * chunk, (t + 1) * chunk)
            wat = slice(t * cw, (t + 1) * cw)
            h1 = h1_all[block(t), :]
            n, _ = normal_of(h1)
            u = (n * gb[...] + sb[...]).astype(BF)
            m, s = gelu_and_slope(nn(u, wup[...]) + ub[...])
            m_ref[at, :] = m.astype(BF)
            s_ref[at, :] = s.astype(BF)
            h2 = h1 + (nn(m_ref[at, :], wdn[...]) + db[...])
            h2_ref[at, :] = h2.astype(BF)
            om = pool_weights(h2, qv[...], counts[wat, :], chars_per)
            pooled_ref[wat, :] = jnp.sum(om * h2.reshape(cw, chars_per, width), 1).astype(BF)
        x = (nn(pooled_ref[...], wpj[...]) + pb[...]).astype(BF)
        if net_sizes:
            cap = x_out.shape[1]
            first_word = place * words
            target = first_word // cap
            x_out[target, pl.ds(pl.multiple_of(lax.rem(first_word, cap), words), words)] = x
            pl.when(lax.rem(first_word + words, cap) == 0)(lambda: exchange.send_block(target))
        else:
            x_ref[...] = x

    if net_sizes:

        @pl.when(now == 2 * steps - 1)
        def _():
            for a in range(3, 7):
                shared.finish(a)
            exchange.finish()
            for a, weight in enumerate(char_weights):
                pltpu.make_async_copy(weight, char_out[a], keep.at[a]).wait()


def char_forward(chars, counts, weights, chars_per, rows, net_sizes=None, word_shards=None, vectors=None, cap=None):
    total, width = chars.shape
    words, cw = total // chars_per, rows // chars_per
    ff, out = weights[2].shape[1], weights[4].shape[1]
    steps = total // rows

    def early(count, columns):
        return pl.BlockSpec((count, columns), lambda p, i: (i + p * (steps - 1 - i), 0))

    def late(count, columns):
        return pl.BlockSpec((count, columns), lambda p, i: (late_place(net_sizes, steps, i * p), 0))

    saved = [((words, width), BF, cw, late), ((total, 3 * width), BF, rows, early), ((total, 2 * width), BF, rows, early),
             ((total, width), BF, rows, early), ((total, width), BF, rows, early), ((total, width), BF, rows, late),
             ((total, ff), BF, rows, late), ((total, ff), BF, rows, late)]
    saved_specs = [where(count, s[1]) for s, _, count, where in saved]
    saved_shapes = [jax.ShapeDtypeStruct(s, d) for s, d, _, _ in saved]
    anywhere = pl.BlockSpec(memory_space=pl.ANY)
    in_specs = [anywhere, whole_block(counts.shape)]
    operands = [chars, counts]
    scratch = [pltpu.VMEM((total, width), F32), pltpu.VMEM((total, width), BF), pltpu.VMEM((total, width), F32), pltpu.SemaphoreType.DMA(())]
    if net_sizes:
        n_dp, n_wide = net_sizes
        n_z = n_wide // 2
        lengths, room = [], 0
        for v in vectors:
            lengths.append((room, v.shape[0] * n_wide))
            room += padded(v.shape[0])
        in_specs += [anywhere] * 9 + [whole_block(v.shape) for v in vectors]
        operands += [*weights, *word_shards, *vectors]
        vec_shape = jax.ShapeDtypeStruct((1, sum(length for _, length in lengths)), F32)
        grown = lambda a: jax.ShapeDtypeStruct((a.shape[0] * n_wide, a.shape[1]), a.dtype)
        fulls = [grown(a) for a in weights]
        out_specs = [anywhere, whole_out(vec_shape.shape)] + [anywhere] * 9 + saved_specs
        out_shapes = [jax.ShapeDtypeStruct((n_wide, cap, out), BF), vec_shape, *fulls, *(grown(a) for a in word_shards), *saved_shapes]
        scratch += (
            [pltpu.VMEM((n_wide, cap, out), BF)]
            + [pltpu.VMEM(a.shape, a.dtype) for a in fulls]
            + [pltpu.VMEM((n_wide, 1, room), F32), pltpu.VMEM((1, 1, room), F32)]
            + Gather.scratch(3, n_z)
            + SharedGather.scratch(7, n_dp, n_z)
            + Exchange.scratch(n_wide)
            + [pltpu.SemaphoreType.DMA((5,))]
        )
        params = pltpu.CompilerParams(vmem_limit_bytes=VMEM_LIMIT, collective_id=1, has_side_effects=True)
    else:
        lengths = None
        in_specs += [whole_block(w.shape) for w in weights]
        operands += [*weights]
        out_specs = [late(cw, out)] + saved_specs
        out_shapes = [jax.ShapeDtypeStruct((words, out), BF), *saved_shapes]
        params = pltpu.CompilerParams(vmem_limit_bytes=VMEM_LIMIT)
    return pl.pallas_call(
        functools.partial(char_forward_kernel, chars_per, steps, net_sizes, lengths),
        grid=(2, steps),
        in_specs=in_specs,
        out_specs=out_specs,
        out_shape=out_shapes,
        scratch_shapes=scratch,
        compiler_params=params,
        name="char_forward",
    )(*operands)


def word_kernel(slot_cap, net_sizes, *refs):
    arrived, bucket, assign, segment, grad_ref, win, wout, wup, wdn, vec, out_ref, back_out, *refs = refs
    length, width = grad_ref.shape
    ff = wup.shape[1]
    if net_sizes:
        net = Net(*net_sizes)
        grads_out, word_row, *refs = refs
        *held, word_grads, load_sem, store_sem = refs[-7:]
        refs = refs[:-7]
        loads = [pltpu.make_async_copy(src, dst, load_sem.at[i]) for i, (src, dst) in enumerate(zip((win, wout, wup, wdn), held))]
        for load in loads:
            load.start()
        win, wout, wup, wdn = held
        dga, dsa, dgb, dsb, ddb, dub = word_vectors(word_row, width, ff)
    else:
        dga, dsa, dwin, dwout, dgb, dsb, dwup, dub, dwdn, ddb, *refs = refs
    qkv_ref, p_ref, mix_ref, h_ref, s_ref, gq_ref, gs_ref, *refs = refs
    ga, sa, gb, sb, db, ub = word_vectors(vec, width, ff)
    owners = assign.shape[1]
    slots = owners * slot_cap
    if net_sizes:
        back_ref, *sems = refs
        exchange = Exchange(net, back_ref, back_out, *sems)
        peers = [net.wide_peer(j)[1] for j in range(1, net.n_wide)]
        net.greet(peers)
    def ready(i):
        if net_sizes:
            loads[i].wait()

    named = jnp.where(bucket[...] == lax.broadcasted_iota(jnp.int32, (owners, length), 0), 1.0, 0.0)
    ri = lax.broadcasted_iota(jnp.int32, (length, length), 0)
    ci = lax.broadcasted_iota(jnp.int32, (length, length), 1)
    earlier = nn(named.astype(BF), jnp.where(ri < ci, 1.0, 0.0).astype(BF))
    served = as_column(assign[...].astype(F32)) * slot_cap
    slot = jnp.sum(named * (served + earlier), 0, keepdims=True).astype(jnp.int32)
    hot = jnp.where(lax.broadcasted_iota(jnp.int32, (slots, length), 0) == slot, 1.0, 0.0).astype(BF)
    x = tn(hot, arrived[...].reshape(slots, width))
    n1, r1 = normal_of(x)
    a = (n1 * ga[...] + sa[...]).astype(BF)
    ready(0)
    qkv = nn(a, win[...])
    qkv_ref[:, :width] = (qkv[:, :width] * HD**-0.5).astype(BF)
    qkv_ref[:, width:] = qkv[:, width:].astype(BF)
    seg = segment[...].astype(F32)
    bias = jnp.where((seg == as_column(seg)) & (ci <= ri), 0.0, NEG)

    def pair(p):
        return [qkv_ref[:, i * width + p * GROUP : i * width + (p + 1) * GROUP] for i in range(3)]

    pairs = range(width // GROUP)

    def both(p):
        return slice(2 * p * length, (2 * p + 2) * length)

    for p in pairs:
        q, k, _ = pair(p)
        s = nt(q, two_heads(k))
        for h in range(2):
            p_ref[:, (2 * p + h) * length : (2 * p + h + 1) * length] = softmax_low(s[:, h * length : (h + 1) * length] + bias)
    for p in pairs:
        mix_ref[:, p * GROUP : (p + 1) * GROUP] = nn(p_ref[:, both(p)], two_heads(pair(p)[2])).astype(BF)
    ready(1)
    inner = x + nn(mix_ref[...], wout[...])
    n2, r2 = normal_of(inner)
    u = (n2 * gb[...] + sb[...]).astype(BF)
    ready(2)
    h, slope = gelu_and_slope(nn(u, wup[...]) + ub[...])
    h_ref[...] = h.astype(BF)
    s_ref[...] = slope
    ready(3)
    out_ref[...] = inner + (nn(h_ref[...], wdn[...]) + db[...])
    g = grad_ref[...]
    gz = (nt(g, wdn[...]) * s_ref[...]).astype(BF)
    du = nt(gz, wup[...])
    g1 = g.astype(F32) + norm_back(du, n2, r2, gb[...])
    g1_low = g1.astype(BF)
    gm = nt(g1_low, wout[...]).astype(BF)
    for p in pairs:
        dp = nt(gm[:, p * GROUP : (p + 1) * GROUP], two_heads(pair(p)[2]))
        for h in range(2):
            lanes = slice((2 * p + h) * length, (2 * p + h + 1) * length)
            gs_ref[:, lanes] = softmax_back(p_ref[:, lanes], dp[:, h * length : (h + 1) * length])
    for p in pairs:
        q, k, _ = pair(p)
        gs = gs_ref[:, both(p)]
        gq_ref[:, p * GROUP : (p + 1) * GROUP] = (nn(gs, two_heads(k)) * HD**-0.5).astype(BF)
        gq_ref[:, width + p * GROUP : width + (p + 1) * GROUP] = one_of_two(tn(gs, q)).astype(BF)
        gmp = gm[:, p * GROUP : (p + 1) * GROUP]
        gq_ref[:, 2 * width + p * GROUP : 2 * width + (p + 1) * GROUP] = one_of_two(tn(p_ref[:, both(p)], gmp)).astype(BF)
    da = nt(gq_ref[...], win[...])
    gx = (g1 + norm_back(da, n1, r1, ga[...])).astype(BF)
    back = nn(hot, gx).astype(BF).reshape(owners, slot_cap, width)
    if net_sizes:
        back_ref[...] = back
        net.met(peers)
        exchange.send_all()
        some = width // net.n_wide
        side = ff // width

        def put(value, column):
            value = value.astype(BF)
            for w in range(net.n_wide):
                word_grads[w // 2, w % 2, :, column : column + value.shape[1]] = value[w * some : (w + 1) * some]

        def store(i, first, columns):
            window = pl.ds(first, columns)
            return pltpu.make_async_copy(word_grads.at[:, :, :, window], grads_out.at[:, :, :, window], store_sem.at[i])

        put(tn(a, gq_ref[...]), 0)
        put(tn(mix_ref[...], g1_low), 3 * width)
        store(0, 0, 4 * width).start()
        put(tn(u, gz), 4 * width)
        store(1, 4 * width, ff).start()
        down = tn(h_ref[...], g).astype(BF)
        for w in range(net.n_wide):
            for k in range(side):
                first = (w * side + k) * some
                column = 4 * width + ff + k * width
                word_grads[w // 2, w % 2, :, column : column + width] = down[first : first + some]
        store(2, 4 * width + ff, ff).start()
    else:
        back_out[...] = back
        dwin[...] = tn(a, gq_ref[...])
        dwout[...] = tn(mix_ref[...], g1_low)
        dwup[...] = tn(u, gz)
        dwdn[...] = tn(h_ref[...], g)
    dga[...] = column_sum(da * n1)
    dsa[...] = column_sum(da)
    dgb[...] = column_sum(du * n2)
    dsb[...] = column_sum(du)
    dub[...] = column_sum(gz.astype(F32))
    ddb[...] = column_sum(g.astype(F32))
    if net_sizes:
        exchange.finish()
        for i, (first, columns) in enumerate(((0, 4 * width), (4 * width, ff), (4 * width + ff, ff))):
            store(i, first, columns).wait()


def word_block(arrived, bucket, assign, segments, grad, weights, slot_cap, net_sizes=None):
    length, width = grad.shape
    ff = weights[2].shape[1]
    owners = assign.shape[1]
    low = lambda *s: jax.ShapeDtypeStruct(s, BF)
    full = lambda *s: jax.ShapeDtypeStruct(s, F32)
    vmem = pl.BlockSpec(memory_space=pltpu.VMEM)
    out_shapes, out_specs = [full(length, width), low(owners, slot_cap, width)], [vmem, vmem]
    scratch = [pltpu.VMEM((length, 3 * width), BF), pltpu.VMEM((length, width // HD * length), BF), pltpu.VMEM((length, width), BF),
               pltpu.VMEM((length, ff), BF), pltpu.VMEM((length, ff), F32), pltpu.VMEM((length, 3 * width), BF),
               pltpu.VMEM((length, width // HD * length), BF)]
    if net_sizes:
        n_dp, n_wide = net_sizes
        out_shapes += [low(n_wide // 2, 2, width // n_wide, 4 * width + 2 * ff), full(1, 5 * width + ff)]
        anywhere = pl.BlockSpec(memory_space=pl.ANY)
        out_specs = [vmem, anywhere, anywhere, vmem]
        in_specs = [vmem] * 5 + [anywhere] * 4 + [vmem]
        scratch += [pltpu.VMEM((owners, slot_cap, width), BF)] + Exchange.scratch(n_wide)
        scratch += [pltpu.VMEM(w.shape, BF) for w in weights[:4]] + [pltpu.VMEM(out_shapes[2].shape, BF)]
        scratch += [pltpu.SemaphoreType.DMA((4,)), pltpu.SemaphoreType.DMA((3,))]
        params = pltpu.CompilerParams(vmem_limit_bytes=VMEM_LIMIT, collective_id=2, has_side_effects=True)
    else:
        row = full(1, width)
        out_shapes += [row, row, full(width, 3 * width), full(width, width), row, row, full(width, ff), full(1, ff), full(ff, width), row]
        out_specs += [vmem] * 10
        in_specs = [vmem] * 10
        params = pltpu.CompilerParams(vmem_limit_bytes=VMEM_LIMIT)
    return pl.pallas_call(
        functools.partial(word_kernel, slot_cap, net_sizes),
        in_specs=in_specs,
        out_specs=out_specs,
        out_shape=out_shapes,
        scratch_shapes=scratch,
        compiler_params=params,
        name="word_block",
    )(arrived, bucket, assign, segments, grad, *weights)


def gathered(shard):
    return lax.all_gather(shard, "wide", axis=0, tiled=True)


def exchanged(blocks):
    return lax.all_to_all(blocks, "wide", split_axis=0, concat_axis=0, tiled=True)


def summed(grad):
    part = lax.psum_scatter(grad.astype(BF), "wide", scatter_dimension=0, tiled=True)
    return lax.psum(part, "dp").astype(F32)


def shards(
    chars, char_counts, buckets, assign, segments,
    char_gain, char_shift, char_inproj, char_outproj, char_gain_mid, char_shift_mid, char_up, char_up_bias, char_down, char_down_bias,
    pool_query, char_proj, char_proj_bias,
    word_gain, word_shift, word_inproj, word_outproj, word_gain_mid, word_shift_mid, word_up, word_up_bias, word_down, word_down_bias,
    out_grad,
):
    n_dp, n_wide = lax.axis_size("dp"), lax.axis_size("wide")
    cap, chars_per, width = chars.shape[2:]
    slots = n_wide * cap
    rows = chars.reshape(slots * chars_per, width)
    block = min(1024, rows.shape[0])
    counts = char_counts.reshape(-1, block // chars_per)
    char_shards = (char_inproj, char_outproj, char_up, char_down, char_proj)
    word_shards = (word_inproj, word_outproj, word_up, word_down)
    vectors = (char_gain, char_shift, char_gain_mid, char_shift_mid, char_down_bias, pool_query, char_up_bias, char_proj_bias,
               word_gain, word_shift, word_gain_mid, word_shift_mid, word_down_bias, word_up_bias)
    fast = (
        all(m.shape[0] % 16 == 0 for m in char_shards)
        and all(m.shape[0] % (16 * n_dp) == 0 for m in word_shards)
        and cap % (block // chars_per) == 0
        and (4 * width) % (GROUP * n_dp) == 0
        and n_wide % 2 == 0
        and n_dp == 4
        and (4 * word_up.shape[0] * n_wide + 2 * word_up.shape[1]) % (8 * GROUP * WORD_PARTS) == 0
    )
    bucket, names, upstream = buckets.reshape(1, -1), assign[None], out_grad[0]
    if fast:
        sizes = (n_dp, n_wide)
        arrived, vec, *rest = char_forward(rows, counts, char_shards, chars_per, block, sizes, word_shards, vectors, cap)
        char_full, word_full, saved = rest[:5], rest[5:9], rest[9:]
        result, returned, word_grads, word_row = word_block(arrived, bucket, names, segments, upstream, (*word_full, vec), cap, sizes)
        incoming = returned.reshape(slots, -1)
        sums = char_backward(incoming, rows, counts, saved, (*char_full, vec), chars_per, block, sizes, word_grads, word_row)
        params = (char_gain, char_shift, char_inproj, char_outproj, char_gain_mid, char_shift_mid, char_up, char_up_bias, char_down,
                  char_down_bias, pool_query, char_proj, char_proj_bias, word_gain, word_shift, word_inproj, word_outproj, word_gain_mid,
                  word_shift_mid, word_up, word_up_bias, word_down, word_down_bias)
        shapes = [p.shape if p.ndim == 2 else (1, *p.shape) for p in params]
        char_grads, *grads = outputs_of(*sums, shapes=shapes, rows=min(2048, rows.shape[0]))
        grads = [g[0] if g.shape[0] == 1 else g for g in grads]
    else:
        vec = jnp.concatenate([gathered(v) for v in vectors]).astype(F32)[None]
        char_full, word_full = [gathered(m) for m in char_shards], [gathered(m) for m in word_shards]
        outgoing, *saved = char_forward(rows, counts, (*char_full, vec), chars_per, block)
        arrived = exchanged(outgoing.reshape(n_wide, cap, -1))
        result, back, *word_grads = word_block(arrived, bucket, names, segments, upstream, (*word_full, vec), cap)
        incoming = exchanged(back).reshape(slots, -1)
        char_grads, *grads = char_backward(incoming, rows, counts, saved, (*char_full, vec), chars_per, block)
        grads[8] = grads[8].T
        grads = [summed(g[0] if g.shape[0] == 1 else g) for g in grads + word_grads]
    return (result[None], char_grads.reshape(chars.shape), *grads)


def solution(mesh):
    whole, split = ("dp", "wide"), "wide"
    row, flat = P(split, None), P(split)
    word = [flat, flat, row, row, flat, flat, row, flat, row, flat]
    char = word + [flat, row, flat]
    chars = P(whole, None, None, None, None)
    three = P(whole, None, None)
    return jax.shard_map(
        shards,
        mesh=mesh,
        in_specs=(chars, three, three, P(), P(whole, None), *char, *word, three),
        out_specs=(three, chars, *char, *word),
        check_vma=False,
    )
```

```python
import functools

import jax
import jax.numpy as jnp
from jax import lax
from jax.experimental import pallas as pl
from jax.experimental.pallas import tpu as pltpu
from jax.sharding import PartitionSpec as P

EPS = 1e-05
NEG = -1e30
ROOT_HALF = 0.7071067811865476
INV_ROOT_TWO_PI = 0.3989422804014327
LOG2_E = 1.4426950408889634
HD = 64
GROUP = 128
F32 = jnp.float32
BF = jnp.bfloat16
MESH = pl.DeviceIdType.MESH
VMEM_LIMIT = 60 << 20
WORD_PARTS = 3


def nn(a, b):
    return lax.dot_general(a, b, (((1,), (0,)), ((), ())), preferred_element_type=F32)


def nt(a, b):
    return lax.dot_general(a, b, (((1,), (1,)), ((), ())), preferred_element_type=F32)


def tn(a, b):
    return lax.dot_general(a, b, (((0,), (0,)), ((), ())), preferred_element_type=F32)


def padded(lanes):
    return -(-lanes // GROUP) * GROUP


def column_sum(x):
    return jnp.sum(x, 0, keepdims=True)


def normal_of(x):
    c = x - jnp.mean(x, -1, keepdims=True)
    r = lax.rsqrt(jnp.mean(c * c, -1, keepdims=True) + EPS)
    return c * r, r


def norm_back(d, n, r, g):
    dg = d * g
    return r * (dg - jnp.mean(dg, -1, keepdims=True) - n * jnp.mean(dg * n, -1, keepdims=True))


def gelu_and_slope(z):
    w = z * ROOT_HALF
    cdf = 0.5 + 0.5 * lax.erf(w)
    return z * cdf, cdf + (z * INV_ROOT_TWO_PI) * jnp.exp2((w * w) * -LOG2_E)


def two_terms(x):
    high = x.astype(BF)
    return high, (x - high.astype(F32)).astype(BF)


def norm_vector_grads(weight, weight_grad, upstream_sum, gain, shift):
    shift_grad = sum(nt(jnp.broadcast_to(part, (8, part.shape[1])), weight) for part in two_terms(upstream_sum))[:1]
    product = weight.astype(F32) * weight_grad
    ones = jnp.ones((8, weight.shape[1]), BF)
    both = sum(nt(ones, part) for part in two_terms(product))[:1]
    return (both - shift * shift_grad) / gain, shift_grad


def softmax_low(s):
    ex = jnp.exp(s - jnp.max(s, -1, keepdims=True))
    return (ex * (1.0 / jnp.sum(ex, -1, keepdims=True))).astype(BF)


def softmax_back(soft, d):
    soft = soft.astype(F32)
    return (soft * (d - jnp.sum(d * soft, -1, keepdims=True))).astype(BF)


def two_heads(t):
    left = lax.broadcasted_iota(jnp.int32, t.shape, 1) < HD
    zero = jnp.zeros_like(t)
    return jnp.concatenate([jnp.where(left, t, zero), jnp.where(left, zero, t)], 0)


def one_of_two(t):
    half = t.shape[0] // 2
    left = lax.broadcasted_iota(jnp.int32, (half, t.shape[1]), 1) < HD
    return jnp.where(left, t[:half], t[half:])


def as_column(row):
    n = row.shape[1]
    same = lax.broadcasted_iota(jnp.int32, (n, n), 0) == lax.broadcasted_iota(jnp.int32, (n, n), 1)
    return jnp.sum(jnp.where(same, jnp.broadcast_to(row, (n, n)), 0.0), -1, keepdims=True)


def key_bias(row, chars_per):
    n = row.shape[1]
    lanes = n * chars_per
    of_word = lax.broadcasted_iota(jnp.int32, (n, lanes), 1) // chars_per == lax.broadcasted_iota(jnp.int32, (n, lanes), 0)
    counts = nn(jnp.broadcast_to(row, (8, n)).astype(BF), jnp.where(of_word, 1.0, 0.0).astype(BF))
    place = lax.rem(lax.broadcasted_iota(jnp.int32, (8, lanes), 1), chars_per)
    return jnp.where(place.astype(F32) < counts, 0.0, NEG)


def pool_weights(h2, query, counts, chars_per):
    rows = h2.shape[0]
    words = rows // chars_per
    e = jnp.sum(h2 * query, -1, keepdims=True) * (h2.shape[1] ** -0.5)
    e = e.reshape(words, chars_per, 1)
    place = lax.broadcasted_iota(jnp.int32, (words, chars_per, 1), 1).astype(F32)
    e = jnp.where(place < counts.reshape(words, 1, 1), e, NEG)
    ex = jnp.exp(e - jnp.max(e, 1, keepdims=True))
    return ex / jnp.sum(ex, 1, keepdims=True)


class Net:
    def __init__(self, n_dp, n_wide):
        self.n_dp, self.n_wide, self.n_z = n_dp, n_wide, n_wide // 2
        self.dp, self.wide = lax.axis_index("dp"), lax.axis_index("wide")
        self.z, self.core = self.wide // 2, lax.rem(self.wide, 2)
        self.sibling = (self.dp, self.wide + 1 - 2 * self.core)

    def z_peer(self, j):
        z = lax.rem(self.z + j, self.n_z)
        return z, (self.dp, 2 * z + self.core)

    def dp_peer(self, j):
        q = lax.rem(self.dp + j, self.n_dp)
        return q, (q, self.wide)

    def wide_peer(self, j):
        w = lax.rem(self.wide + j, self.n_wide)
        return w, (self.dp, w)

    def greet(self, peers):
        barrier = pltpu.get_barrier_semaphore()
        for peer in peers:
            pl.semaphore_signal(barrier, inc=1, device_id=peer, device_id_type=MESH)

    def met(self, peers):
        pl.semaphore_wait(pltpu.get_barrier_semaphore(), len(peers))


def remote(src, dst, send, recv, peer):
    return pltpu.make_async_remote_copy(src_ref=src, dst_ref=dst, send_sem=send, recv_sem=recv, device_id=peer, device_id_type=MESH)


class Reduce:
    def __init__(self, net, grads, first, kept, from_core, part, from_dp, from_z, done, sems):
        self.net, self.grads = net, grads
        self.columns = pl.ds(first, kept.shape[-1])
        self.kept, self.from_core, self.part = kept, from_core, part
        self.from_dp, self.from_z, self.done = from_dp, from_z, done
        self.send, self.recv = sems
        self.span = part.shape[-1]

    @staticmethod
    def scratch(n_dp, n_z, rows, width):
        span = width // n_dp
        count = 2 + 2 * n_dp + n_z
        return [
            pltpu.VMEM((n_z, rows, width), BF),
            pltpu.VMEM((n_z, rows, width), BF),
            pltpu.VMEM((n_z, rows, span), BF),
            pltpu.VMEM((n_dp - 1, n_z, rows, span), BF),
            pltpu.VMEM((n_z - 1, rows, span), BF),
            pltpu.VMEM((n_dp, rows, span), BF),
            pltpu.SemaphoreType.DMA((count,)),
            pltpu.SemaphoreType.DMA((count,)),
        ]

    def lanes(self, q):
        return pl.ds(pl.multiple_of(q * self.span, GROUP), self.span)

    def to_core(self):
        net = self.net
        return remote(self.grads.at[:, 1 - net.core, :, self.columns], self.from_core, self.send.at[0], self.recv.at[0], net.sibling)

    def own(self):
        return pltpu.make_async_copy(self.grads.at[:, self.net.core, :, self.columns], self.kept, self.recv.at[1])

    def to_dp(self, j):
        q, peer = self.net.dp_peer(j)
        return remote(self.kept.at[:, :, self.lanes(q)], self.from_dp.at[j - 1], self.send.at[1 + j], self.recv.at[1 + j], peer)

    def to_z(self, j):
        z, peer = self.net.z_peer(j)
        at = 1 + self.net.n_dp + j
        return remote(self.part.at[z], self.from_z.at[j - 1], self.send.at[at], self.recv.at[at], peer)

    def to_all(self, j):
        net = self.net
        _, peer = net.dp_peer(j)
        at = 1 + net.n_dp + net.n_z + j
        mine = self.done.at[net.dp]
        return remote(mine, mine, self.send.at[at], self.recv.at[at], peer)

    def start(self):
        self.to_core().start()
        self.own().start()

    def over_dp(self):
        net = self.net
        self.own().wait()
        self.to_core().wait()

        @pl.loop(0, net.n_z)
        def _(z):
            self.kept[z] = (self.kept[z].astype(F32) + self.from_core[z].astype(F32)).astype(BF)

        for j in range(1, net.n_dp):
            self.to_dp(j).start()

    def over_z(self):
        net = self.net
        for j in range(1, net.n_dp):
            self.to_dp(j).wait()

        @pl.loop(0, net.n_z)
        def _(z):
            total = self.kept[z, :, self.lanes(net.dp)].astype(F32)
            for j in range(net.n_dp - 1):
                total = total + self.from_dp[j, z].astype(F32)
            self.part[z] = total.astype(BF)

        for j in range(1, net.n_z):
            self.to_z(j).start()

    def back_over_dp(self):
        net = self.net
        for j in range(1, net.n_z):
            self.to_z(j).wait()
        total = self.part[net.z].astype(F32)
        for j in range(net.n_z - 1):
            total = total + self.from_z[j].astype(F32)
        self.done[net.dp] = total.astype(BF)
        for j in range(1, net.n_dp):
            self.to_all(j).start()

    def finish(self):
        for j in range(1, self.net.n_dp):
            self.to_all(j).wait()


class TwoWayReduce(Reduce):
    @staticmethod
    def scratch(n_dp, n_z, rows, width):
        count = 2 + 2 * n_dp + n_z
        return [
            pltpu.VMEM((n_z, rows, width), BF),
            pltpu.VMEM((n_z, rows, width), BF),
            pltpu.VMEM((n_z, rows, width // n_dp), BF),
            pltpu.VMEM((2, n_z, rows, width // 4), BF),
            pltpu.VMEM((2, n_z, rows, width // 8), BF),
            pltpu.VMEM((n_z - 1, rows, width // n_dp), BF),
            pltpu.VMEM((n_dp, rows, width // n_dp), BF),
            pltpu.SemaphoreType.DMA((count,)),
            pltpu.SemaphoreType.DMA((count,)),
        ]

    def __init__(self, net, grads, first, kept, from_core, part, half, quarter, from_z, done, sems):
        super().__init__(net, grads, first, kept, from_core, part, None, from_z, done, sems)
        self.half, self.quarter = half, quarter
        x, y = lax.rem(net.dp, 2), net.dp // 2
        along_x, along_y = (net.dp + 1 - 2 * x, net.wide), (lax.rem(net.dp + 2, 4), net.wide)
        self.order = ((x, y, along_x, along_y), (y, x, along_y, along_x))

    def window(self, h, a, b=None):
        eighth = self.span // 2
        at = h * 4 * eighth + a * 2 * eighth
        if b is None:
            return pl.ds(pl.multiple_of(at, GROUP), 2 * eighth)
        return pl.ds(pl.multiple_of(at + b * eighth, GROUP), eighth)

    def first_step(self, h):
        a, _, peer, _ = self.order[h]
        return remote(self.kept.at[:, :, self.window(h, 1 - a)], self.half.at[h], self.send.at[2 + h], self.recv.at[2 + h], peer)

    def second_step(self, h):
        a, b, _, peer = self.order[h]
        return remote(self.kept.at[:, :, self.window(h, a, 1 - b)], self.quarter.at[h], self.send.at[4 + h], self.recv.at[4 + h], peer)

    def over_dp(self):
        self.own().wait()
        self.to_core().wait()

        @pl.loop(0, self.net.n_z)
        def _(z):
            self.kept[z] = (self.kept[z].astype(F32) + self.from_core[z].astype(F32)).astype(BF)

        for h in range(2):
            self.first_step(h).start()

    def over_dp_again(self):
        for h in range(2):
            self.first_step(h).wait()
        for h in range(2):
            mine = self.window(h, self.order[h][0])

            @pl.loop(0, self.net.n_z)
            def _(z):
                self.kept[z, :, mine] = (self.kept[z, :, mine].astype(F32) + self.half[h, z].astype(F32)).astype(BF)

        for h in range(2):
            self.second_step(h).start()

    def over_z(self):
        net = self.net
        for h in range(2):
            self.second_step(h).wait()
        eighth = self.span // 2
        for h in range(2):
            a, b, _, _ = self.order[h]
            mine = self.window(h, a, b)

            @pl.loop(0, net.n_z)
            def _(z):
                total = self.kept[z, :, mine].astype(F32) + self.quarter[h, z].astype(F32)
                self.part[z, :, h * eighth : (h + 1) * eighth] = total.astype(BF)

        for j in range(1, net.n_z):
            self.to_z(j).start()


class ReduceRows:
    def __init__(self, net, row, from_core, of_dp, of_z, sems):
        self.net, self.row, self.from_core, self.of_dp, self.of_z = net, row, from_core, of_dp, of_z
        self.send, self.recv = sems

    @staticmethod
    def scratch(n_dp, n_z, width):
        count = 1 + n_dp + n_z
        return [
            pltpu.VMEM((1, width), F32),
            pltpu.VMEM((1, width), F32),
            pltpu.VMEM((n_dp, 1, width), F32),
            pltpu.VMEM((n_z, 1, width), F32),
            pltpu.SemaphoreType.DMA((count,)),
            pltpu.SemaphoreType.DMA((count,)),
        ]

    def to_core(self):
        return remote(self.row, self.from_core, self.send.at[0], self.recv.at[0], self.net.sibling)

    def to_dp(self, j):
        mine = self.of_dp.at[self.net.dp]
        return remote(mine, mine, self.send.at[j], self.recv.at[j], self.net.dp_peer(j)[1])

    def to_z(self, j):
        mine = self.of_z.at[self.net.z]
        at = self.net.n_dp + j
        return remote(mine, mine, self.send.at[at], self.recv.at[at], self.net.z_peer(j)[1])

    def start(self):
        self.to_core().start()

    def over_dp(self):
        self.to_core().wait()
        self.of_dp[self.net.dp] = self.row[...] + self.from_core[...]
        for j in range(1, self.net.n_dp):
            self.to_dp(j).start()

    def over_z(self):
        net = self.net
        for j in range(1, net.n_dp):
            self.to_dp(j).wait()
        total = self.of_dp[0]
        for q in range(1, net.n_dp):
            total = total + self.of_dp[q]
        self.of_z[net.z] = total
        for j in range(1, net.n_z):
            self.to_z(j).start()

    def finish(self, out, places):
        net = self.net
        for j in range(1, net.n_z):
            self.to_z(j).wait()
        total = self.of_z[0]
        for z in range(1, net.n_z):
            total = total + self.of_z[z]
        at = 0
        for first, length in places:
            piece = length // net.n_wide
            vector = jnp.broadcast_to(total[:, first : first + length], (8, length))
            turned = pltpu.roll(vector, lax.rem(length - net.wide * piece, length), 1)
            out[:, at : at + piece] = turned[:1, :piece]
            at += padded(piece)


class Gather:
    def __init__(self, net, shards, wholes, send, recv, near):
        self.net, self.shards, self.wholes = net, shards, wholes
        self.send, self.recv, self.near = send, recv, near

    @staticmethod
    def scratch(count, n_z):
        return [
            pltpu.SemaphoreType.DMA((count, 2 * n_z)),
            pltpu.SemaphoreType.DMA((count, 2 * n_z)),
            pltpu.SemaphoreType.DMA((count,)),
        ]

    def block(self, a, owner):
        rows = self.shards[a].shape[0]
        return self.wholes[a].at[pl.ds(pl.multiple_of(owner * rows, rows), rows)]

    def along_z(self, a, j):
        net = self.net
        return remote(self.shards[a], self.block(a, net.wide), self.send.at[a, j], self.recv.at[a, net.wide], net.z_peer(j)[1])

    def across(self, a):
        net = self.net
        return remote(self.shards[a], self.block(a, net.wide), self.send.at[a, 0], self.recv.at[a, net.wide], net.sibling)

    def relayed(self, a, j):
        net = self.net
        owner = 2 * net.z_peer(j)[0] + net.core
        here = self.block(a, owner)
        return remote(here, here, self.send.at[a, net.n_z + j], self.recv.at[a, owner], net.sibling)

    def own(self, a):
        return pltpu.make_async_copy(self.shards[a], self.block(a, self.net.wide), self.near.at[a])

    def arrival(self, a, owner):
        here = self.block(a, owner)
        return remote(here, here, self.send.at[a, 0], self.recv.at[a, owner], self.net.sibling)

    def start(self, a):
        for j in range(1, self.net.n_z):
            self.along_z(a, j).start()
        self.across(a).start()
        self.own(a).start()

    def relay(self, a):
        net = self.net
        for j in range(1, net.n_z):
            self.arrival(a, 2 * net.z_peer(j)[0] + net.core).wait_recv()
            self.relayed(a, j).start()

    def finish(self, a):
        net = self.net
        self.own(a).wait()
        self.across(a).wait_send()
        for j in range(1, net.n_z):
            self.along_z(a, j).wait_send()
            self.relayed(a, j).wait_send()
        for z in range(net.n_z):
            self.arrival(a, 2 * z + 1 - net.core).wait_recv()


class SharedGather:
    def __init__(self, net, shards, wholes, send_z, send_dp, send_core, recv_z, recv_dp, recv_core, near):
        self.net, self.shards, self.wholes = net, shards, wholes
        self.send_z, self.send_dp, self.send_core = send_z, send_dp, send_core
        self.recv_z, self.recv_dp, self.recv_core, self.near = recv_z, recv_dp, recv_core, near

    @staticmethod
    def scratch(count, n_dp, n_z):
        sem = pltpu.SemaphoreType.DMA
        return [
            sem((count, n_z)), sem((count, n_z, n_dp)), sem((count, n_z)),
            sem((count, n_z)), sem((count, n_z, n_dp)), sem((count, n_z)), sem((count,)),
        ]

    def block(self, a, owner):
        rows = self.shards[a].shape[0]
        return self.wholes[a].at[pl.ds(pl.multiple_of(owner * rows, rows), rows)]

    def part(self, a, q):
        rows, columns = self.shards[a].shape
        n_dp = self.net.n_dp
        if rows % (16 * n_dp) == 0:
            some = rows // n_dp
            return pl.multiple_of(q * some, some), some, 0, columns
        some = columns // n_dp
        return 0, rows, pl.multiple_of(q * some, some), some

    def piece(self, a, owner, q):
        rows = self.shards[a].shape[0]
        row, height, column, width = self.part(a, q)
        return self.wholes[a].at[pl.ds(pl.multiple_of(owner * rows + row, height), height), pl.ds(column, width)]

    def along_z(self, a, j):
        net = self.net
        row, height, column, width = self.part(a, net.dp)
        mine = self.shards[a].at[pl.ds(row, height), pl.ds(column, width)]
        return remote(mine, self.piece(a, net.wide, net.dp), self.send_z.at[a, j], self.recv_z.at[a, net.z], net.z_peer(j)[1])

    def from_z(self, a, j):
        net = self.net
        z, peer = net.z_peer(j)
        here = self.piece(a, 2 * z + net.core, net.dp)
        return remote(here, here, self.send_z.at[a, j], self.recv_z.at[a, z], peer)

    def over_dp(self, a, j, i):
        net = self.net
        z = net.z_peer(j)[0]
        here = self.piece(a, 2 * z + net.core, net.dp)
        return remote(here, here, self.send_dp.at[a, j, i], self.recv_dp.at[a, j, net.dp], net.dp_peer(i)[1])

    def from_dp(self, a, j, i):
        net = self.net
        z = net.z_peer(j)[0]
        q, peer = net.dp_peer(i)
        here = self.piece(a, 2 * z + net.core, q)
        return remote(here, here, self.send_dp.at[a, j, i], self.recv_dp.at[a, j, q], peer)

    def across(self, a, j):
        net = self.net
        z = net.z_peer(j)[0]
        here = self.block(a, 2 * z + net.core)
        source = self.shards[a] if j == 0 else here
        return remote(source, here, self.send_core.at[a, j], self.recv_core.at[a, z], net.sibling)

    def from_core(self, a, z):
        net = self.net
        here = self.block(a, 2 * z + 1 - net.core)
        return remote(here, here, self.send_core.at[a, 0], self.recv_core.at[a, z], net.sibling)

    def own(self, a):
        return pltpu.make_async_copy(self.shards[a], self.block(a, self.net.wide), self.near.at[a])

    def start(self, a):
        for j in range(1, self.net.n_z):
            self.along_z(a, j).start()
        self.across(a, 0).start()
        self.own(a).start()

    def relay(self, a):
        net = self.net
        for j in range(1, net.n_z):
            self.from_z(a, j).wait_recv()
            for i in range(1, net.n_dp):
                self.over_dp(a, j, i).start()

    def pass_on(self, a):
        net = self.net
        for j in range(1, net.n_z):
            for i in range(1, net.n_dp):
                self.from_dp(a, j, i).wait_recv()
            self.across(a, j).start()

    def finish(self, a):
        net = self.net
        self.own(a).wait()
        for j in range(1, net.n_z):
            self.along_z(a, j).wait_send()
            for i in range(1, net.n_dp):
                self.over_dp(a, j, i).wait_send()
        for j in range(net.n_z):
            self.across(a, j).wait_send()
            self.from_core(a, j).wait_recv()


class Exchange:
    def __init__(self, net, out, inbox, send, recv, near):
        self.net, self.out, self.inbox = net, out, inbox
        self.send, self.recv, self.near = send, recv, near

    @staticmethod
    def scratch(n_wide):
        return [pltpu.SemaphoreType.DMA((n_wide,)), pltpu.SemaphoreType.DMA((n_wide,)), pltpu.SemaphoreType.DMA(())]

    def to(self, w):
        net = self.net
        return remote(self.out.at[w], self.inbox.at[net.wide], self.send.at[w], self.recv.at[net.wide], (net.dp, w))

    def arrival(self, w):
        here = self.inbox.at[w]
        return remote(here, here, self.send.at[w], self.recv.at[w], (self.net.dp, w))

    def own(self):
        me = self.net.wide
        return pltpu.make_async_copy(self.out.at[me], self.inbox.at[me], self.near)

    def send_block(self, w):
        @pl.when(w != self.net.wide)
        def _():
            self.to(w).start()

        @pl.when(w == self.net.wide)
        def _():
            self.own().start()

    def send_all(self):
        for j in range(1, self.net.n_wide):
            self.to(self.net.wide_peer(j)[0]).start()
        self.own().start()

    def finish(self):
        for j in range(1, self.net.n_wide):
            w = self.net.wide_peer(j)[0]
            self.to(w).wait_send()
            self.arrival(w).wait_recv()
        self.own().wait()


def slices_of(ref, first, lengths):
    views = []
    for length in lengths:
        views.append(ref.at[:, first : first + length])
        first += length
    return views


def char_vectors(row, width, ff, out):
    return slices_of(row, 0, [width] * 6 + [ff, out])


def word_vectors(row, width, ff):
    return slices_of(row, row.shape[1] - 5 * width - ff, [width] * 5 + [ff])


def char_back_kernel(chars_per, steps, net_sizes, word_sizes, *refs):
    (
        gx_ref, c_ref, cnt_ref, qkv_ref, p_ref, o_ref, h1_ref, h2_ref, m_ref, s_ref, pooled_all, gx_all,
        win, wout, wup, wdn, wpj, vec, *refs
    ) = refs
    if net_sizes:
        word_grads, word_row, *refs = refs
    gc_ref, *refs = refs
    if net_sizes:
        outs, refs = refs[: WORD_PARTS + 3], refs[WORD_PARTS + 3 :]
    accs, refs = refs[:13], refs[13:]
    dga, dsa, dwin, dwout, dgb, dsb, dwup, dub, dwdn, ddb, dqv, dwpj, dpb = accs
    gh1_ref, gm_ref, u_ref, gz_ref, gq_ref, gs_ref, *refs = refs
    rows, width = c_ref.shape
    ga, sa, gb, sb, _, qv, _, _ = char_vectors(vec, width, wup.shape[1], wpj.shape[1])
    phase, step = pl.program_id(0), pl.program_id(1)
    now = phase * steps + step
    factor = width**-0.5
    chunk = min(rows, 512)
    cw = chunk // chars_per
    words = rows // chars_per

    if net_sizes:
        net = Net(*net_sizes)
        ff_grads, at_grads, row, *refs = refs
        each = word_grads.shape[-1] // WORD_PARTS
        words_of = []
        for part in range(WORD_PARTS):
            words_of.append(TwoWayReduce(net, word_grads, part * each, *refs[:7], refs[7:9]))
            refs = refs[9:]
        ff = Reduce(net, ff_grads, 0, *refs[:6], refs[6:8])
        att = Reduce(net, at_grads, 0, *refs[8:14], refs[14:16])
        rowsum = ReduceRows(net, row, *refs[16:19], refs[19:21])
        keep = refs[21]

        @pl.when(now == 0)
        def _():
            peers = [net.sibling] + [net.dp_peer(j)[1] for j in range(1, net.n_dp)] + [net.z_peer(j)[1] for j in range(1, net.n_z)]
            net.greet(peers)
            net.met(peers)
            for part in words_of:
                part.start()

        one, two, three = words_of
        schedule = (
            (1, one.over_dp),
            (2, two.over_dp),
            (3, one.over_dp_again),
            (4, three.over_dp),
            (5, two.over_dp_again),
            (6, one.over_z),
            (7, three.over_dp_again),
            (8, two.over_z),
            (8, ff.start),
            (9, one.back_over_dp),
            (10, three.over_z),
            (10, ff.over_dp),
            (11, two.back_over_dp),
            (13, three.back_over_dp),
            (13, ff.over_z),
            (15, ff.back_over_dp),
        )
        for when, act in schedule:
            pl.when(now == when * steps // 8)(act)

    @pl.when(now == 0)
    def _():
        for acc in accs:
            acc[...] = jnp.zeros_like(acc)
        dwpj[...] = tn(pooled_all[...], gx_all[...])
        dpb[...] = column_sum(gx_all[...].astype(F32))

    here = pl.ds(pl.multiple_of(step * rows, rows), rows)

    @pl.when(phase == 0)
    def _():
        gp = nt(gx_ref[...], wpj[...]).astype(BF).astype(F32)
        counts = as_column(cnt_ref[pl.ds(step, 1), :].astype(F32))
        for t in range(rows // chunk):
            at = slice(t * chunk, (t + 1) * chunk)
            wat = slice(t * cw, (t + 1) * cw)
            h2 = h2_ref[at, :].astype(F32)
            om = pool_weights(h2, qv[...], counts[wat, :], chars_per)
            gpb = jnp.broadcast_to(gp[wat, :].reshape(cw, 1, width), (cw, chars_per, width)).reshape(chunk, width)
            w = jnp.sum(h2 * gpb, -1, keepdims=True).reshape(cw, chars_per, 1)
            de = om * (w - jnp.sum(om * w, 1, keepdims=True))
            de = de.reshape(chunk, 1) * factor
            gh2 = om.reshape(chunk, 1) * gpb + de * qv[...]
            dqv[...] += column_sum(de * h2)
            gy = gh2.astype(BF)
            ddb[...] += column_sum(gy.astype(F32))
            gm_ref[at, :] = gy
            gz = nt(gy, wdn[...]).astype(BF) * s_ref[at, :]
            gz_ref[at, :] = gz
            dub[...] += column_sum(gz.astype(F32))
            du = nt(gz, wup[...])
            n, r = normal_of(h1_ref[at, :].astype(F32))
            u_ref[at, :] = (n * gb[...] + sb[...]).astype(BF)
            gh1_ref[pl.ds(pl.multiple_of(step * rows + t * chunk, chunk), chunk), :] = (gh2 + norm_back(du, n, r, gb[...])).astype(BF)
        dwup[...] += tn(u_ref[...], gz_ref[...])
        dwdn[...] += tn(gm_ref[...], m_ref[...])

    @pl.when(now == steps - 1)
    def _():
        dgb[...], dsb[...] = norm_vector_grads(wup[...], dwup[...], dub[...], gb[...], sb[...])

    if net_sizes:
        n_z, n_wide = net.n_z, net.n_wide

        @pl.when(now == steps - 1)
        def _():
            up, proj = dwup.shape[1], dwpj.shape[1]
            down = dwdn[...].T
            some = width // n_wide
            side = down.shape[0] // n_wide // some
            for owner in range(n_wide):
                z, core = owner // 2, owner % 2
                mine = slice(owner * some, (owner + 1) * some)
                ff_grads[z, core, :, :up] = dwup[mine, :].astype(BF)
                ff_grads[z, core, :, up : up + proj] = dwpj[mine, :].astype(BF)
                for k in range(side):
                    first = (owner * side + k) * some
                    ff_grads[z, core, :, up + proj + k * width : up + proj + (k + 1) * width] = down[first : first + some].astype(BF)

    @pl.when(phase == 1)
    def _():
        g1 = gh1_ref[here, :]
        dwout[...] += tn(o_ref[...], g1)
        gm_ref[...] = nt(g1, wout[...]).astype(BF)
        units = [(slice(g * GROUP, (g + 1) * GROUP), p) for g in range(rows // GROUP) for p in range(width // GROUP)]

        def head_pair(at, p, i):
            return qkv_ref[at, i * width + p * GROUP : i * width + (p + 1) * GROUP]

        for at, p in units:
            dp = nt(gm_ref[at, p * GROUP : (p + 1) * GROUP], two_heads(head_pair(at, p, 2)))
            for h in range(2):
                lanes = slice((2 * p + h) * GROUP, (2 * p + h + 1) * GROUP)
                gs_ref[at, lanes] = softmax_back(p_ref[at, lanes], dp[:, h * GROUP : (h + 1) * GROUP])
        for at, p in units:
            gs = gs_ref[at, 2 * p * GROUP : 2 * (p + 1) * GROUP]
            gq_ref[at, p * GROUP : (p + 1) * GROUP] = (nn(gs, two_heads(head_pair(at, p, 1))) * HD**-0.5).astype(BF)
            gq_ref[at, width + p * GROUP : width + (p + 1) * GROUP] = one_of_two(tn(gs, head_pair(at, p, 0))).astype(BF)
            soft = p_ref[at, p * 2 * GROUP : (p + 1) * 2 * GROUP]
            gm = gm_ref[at, p * GROUP : (p + 1) * GROUP]
            gq_ref[at, 2 * width + p * GROUP : 2 * width + (p + 1) * GROUP] = one_of_two(tn(soft, gm)).astype(BF)
        for t in range(rows // chunk):
            at = slice(t * chunk, (t + 1) * chunk)
            n, r = normal_of(c_ref[at, :].astype(F32))
            u_ref[at, :] = (n * ga[...] + sa[...]).astype(BF)
            da = nt(gq_ref[at, :], win[...])
            dga[...] += column_sum(da * n)
            dsa[...] += column_sum(da)
            grad = gh1_ref[pl.ds(pl.multiple_of(step * rows + t * chunk, chunk), chunk), :].astype(F32) + norm_back(da, n, r, ga[...])
            gc_ref[at, :] = grad.astype(gc_ref.dtype)
        dwin[...] += tn(u_ref[...], gq_ref[...])

    if net_sizes:

        @pl.when(now == 2 * steps - 1)
        def _():
            some = width // n_wide
            for owner in range(n_wide):
                z, core = owner // 2, owner % 2
                mine = slice(owner * some, (owner + 1) * some)
                at_grads[z, core, :, : 3 * width] = dwin[mine, :].astype(BF)
                at_grads[z, core, :, 3 * width :] = dwout[mine, :].astype(BF)
            column, places = 0, []
            for acc in (dga, dsa, dgb, dsb, ddb, dqv, dub, dpb):
                row[:, column : column + acc.shape[1]] = acc[...]
                places.append((column, acc.shape[1]))
                column += acc.shape[1]
            row[:, column:] = word_row[...]
            for ref in word_vectors(row, *word_sizes):
                places.append((column, ref.shape[1]))
                column += ref.shape[1]
            att.start()
            rowsum.start()
            att.over_dp()
            rowsum.over_dp()
            copies = [pltpu.make_async_copy(piece.done, out, keep.at[i]) for i, (piece, out) in enumerate(zip((*words_of, ff, att), outs))]
            for piece, copy in zip((*words_of, ff), copies):
                piece.finish()
                copy.start()
            att.over_z()
            rowsum.over_z()
            att.back_over_dp()
            rowsum.finish(outs[-1], places)
            att.finish()
            copies[-1].start()
            for copy in copies:
                copy.wait()


def whole_block(shape):
    return pl.BlockSpec(shape, lambda *_: (0,) * len(shape), pipeline_mode=pl.Buffered(1))


def whole_out(shape):
    return pl.BlockSpec(shape, lambda *_: (0,) * len(shape))


def char_backward(gx, chars, counts, saved, weights, chars_per, rows, net_sizes=None, word_grads=None, word_row=None):
    total, width = chars.shape
    win, wout, wup, wdn, wpj, vec = weights
    pooled, qkv, soft, mixed, h1, h2, m, s = saved
    words, cw = total // chars_per, rows // chars_per
    ff, out = wup.shape[1], wpj.shape[1]
    steps = total // rows

    def early(count, columns):
        return pl.BlockSpec((count, columns), lambda p, i: (i + p * (steps - 1 - i), 0))

    def late(count, columns):
        return pl.BlockSpec((count, columns), lambda p, i: (i * p, 0))

    accs = [(1, width), (1, width), (width, 3 * width), (width, width), (1, width), (1, width), (width, ff), (1, ff),
            (width, ff), (1, width), (1, width), (width, out), (1, out)]
    in_specs = [early(cw, out), late(rows, width), whole_block(counts.shape), late(rows, 3 * width), late(rows, 2 * width),
                late(rows, width), early(rows, width), early(rows, width), early(rows, ff), early(rows, ff),
                whole_block(pooled.shape), whole_block(gx.shape)] + [whole_block(w.shape) for w in weights]
    operands = [gx, chars, counts, qkv, soft, mixed, h1, h2, m, s, pooled, gx, *weights]
    scratch = [pltpu.VMEM((total, width), BF), pltpu.VMEM((rows, width), BF), pltpu.VMEM((rows, width), BF),
               pltpu.VMEM((rows, ff), BF), pltpu.VMEM((rows, 3 * width), BF), pltpu.VMEM((rows, 2 * width), BF)]
    if net_sizes:
        n_dp, n_wide = net_sizes
        n_z, some = n_wide // 2, width // n_wide
        word_rows, word_width = word_grads.shape[2:]
        wide_d = n_wide * word_rows
        word_ff = word_row.shape[1] - 5 * wide_d
        operands += [word_grads, word_row]
        in_specs += [pl.BlockSpec(memory_space=pl.ANY), whole_block(word_row.shape)]
        ff_width, at_width = ff + out + ff, 4 * width
        row_width = 6 * width + ff + out + word_row.shape[1]
        word_sizes = (wide_d, word_ff)
        sums = [(n_dp, word_rows, word_width // WORD_PARTS // n_dp)] * WORD_PARTS + [(n_dp, some, ff_width // n_dp), (n_dp, some, at_width // n_dp)]
        pieces = sum(padded(n // n_wide) for n in [width] * 6 + [ff, out] + [wide_d] * 5 + [word_ff])
        out_shapes = [jax.ShapeDtypeStruct((total, width), BF)] + [jax.ShapeDtypeStruct(a, BF) for a in sums] + [jax.ShapeDtypeStruct((1, pieces), F32)]
        out_specs = [late(rows, width)] + [pl.BlockSpec(memory_space=pl.ANY)] * len(sums) + [whole_out((1, pieces))]
        scratch = (
            [pltpu.VMEM(a, F32) for a in accs]
            + scratch
            + [pltpu.VMEM((n_z, 2, some, ff_width), BF), pltpu.VMEM((n_z, 2, some, at_width), BF), pltpu.VMEM((1, row_width), F32)]
            + TwoWayReduce.scratch(n_dp, n_z, word_rows, word_width // WORD_PARTS) * WORD_PARTS
            + Reduce.scratch(n_dp, n_z, some, ff_width)
            + Reduce.scratch(n_dp, n_z, some, at_width)
            + ReduceRows.scratch(n_dp, n_z, row_width)[1:]
            + [pltpu.SemaphoreType.DMA((len(sums),))]
        )
        params = pltpu.CompilerParams(vmem_limit_bytes=VMEM_LIMIT, collective_id=3, has_side_effects=True)
    else:
        word_sizes = None
        out_shapes = [jax.ShapeDtypeStruct(a, F32) for a in [(total, width)] + accs]
        out_specs = [late(rows, width)] + [whole_out(a) for a in accs]
        params = pltpu.CompilerParams(vmem_limit_bytes=VMEM_LIMIT)
    return pl.pallas_call(
        functools.partial(char_back_kernel, chars_per, steps, net_sizes, word_sizes),
        grid=(2, steps),
        in_specs=in_specs,
        out_specs=out_specs,
        out_shape=out_shapes,
        scratch_shapes=scratch,
        compiler_params=params,
        name="char_backward",
    )(*operands)


def unpack(parts, outs, two_way):
    n_dp, rows, span = parts[0].shape
    for ref, first, columns, side in outs:
        for k in range(side):
            for at in range(0, columns, GROUP):
                column = first + k * columns + at
                part, column = column // (n_dp * span), column % (n_dp * span)
                if two_way:
                    eighth = span // 2
                    h, place, lane = column // (4 * eighth), column // eighth % 4, column % eighth
                    q = place if h else place // 2 + place % 2 * 2
                    lane += h * eighth
                else:
                    q, lane = column // span, column % span
                ref[k * rows : (k + 1) * rows, at : at + GROUP] = parts[part][q, :, lane : lane + GROUP].astype(F32)


def output_kernel(gc_low, *refs):
    word_done, (ff_done, at_done, row, gc_ref, *outs) = refs[:WORD_PARTS], refs[WORD_PARTS:]
    gc_ref[...] = gc_low[...].astype(F32)

    @pl.when(pl.program_id(0) == 0)
    def _():
        (
            oga, osa, owin, owout, ogb, osb, oup, oub, odn, odb, oqv, opj, opb,
            xga, xsa, xwin, xwout, xgb, xsb, xup, xub, xdn, xdb,
        ) = outs
        for done, across, down in ((word_done, (xwin, xwout, xup), xdn), ([ff_done], (oup, opj), odn), ([at_done], (owin, owout), None)):
            places, column = [], 0
            for ref in across:
                places.append((ref, column, ref.shape[1], 1))
                column += ref.shape[1]
            if down is not None:
                places.append((down, column, down.shape[1], down.shape[0] // done[0].shape[1]))
            unpack(done, places, len(done) > 1)
        at = 0
        for ref in (oga, osa, ogb, osb, odb, oqv, oub, opb, xga, xsa, xgb, xsb, xdb, xub):
            ref[...] = row[:, at : at + ref.shape[1]]
            at += padded(ref.shape[1])


def outputs_of(gc_low, *wholes, shapes, rows):
    total, width = gc_low.shape
    by_row = pl.BlockSpec((rows, width), lambda i: (i, 0))
    return pl.pallas_call(
        output_kernel,
        grid=(total // rows,),
        in_specs=[by_row] + [whole_block(a.shape) for a in wholes],
        out_specs=[by_row] + [whole_out(a) for a in shapes],
        out_shape=[jax.ShapeDtypeStruct(a, F32) for a in [(total, width), *shapes]],
        compiler_params=pltpu.CompilerParams(vmem_limit_bytes=VMEM_LIMIT),
        name="outputs",
    )(gc_low, *wholes)


def late_place(net_sizes, steps, step):
    if not net_sizes:
        return step
    return lax.rem((lax.axis_index("wide") + 1) * (steps // net_sizes[1]) + step, steps)


def char_forward_kernel(chars_per, steps, net_sizes, lengths, *refs):
    c_ref, cnt_ref, *refs = refs
    if net_sizes:
        net = Net(*net_sizes)
        shards, word_shards, vectors, refs = refs[:5], refs[5:9], refs[9:23], refs[23:]
        inbox, vec, *refs = refs
        char_out, word_out, refs = refs[:5], refs[5:9], refs[9:]
    else:
        win, wout, wup, wdn, wpj, vec, *refs = refs
        x_ref, *refs = refs
    pooled_ref, qkv_ref, p_ref, o_ref, h1_ref, h2_ref, m_ref, s_ref, *refs = refs
    h1_all, c_all, n_all, c_sem, *refs = refs
    rows, width = c_ref.shape[0] // steps, c_ref.shape[1]
    phase, step = pl.program_id(0), pl.program_id(1)
    now = phase * steps + step
    chunk = min(rows, 512)
    cw = chunk // chars_per
    words = rows // chars_per
    place = late_place(net_sizes, steps, step)
    load = pltpu.make_async_copy(c_ref, c_all, c_sem)

    def normalize():
        load.wait()

        @pl.loop(0, steps * rows // chunk)
        def _(t):
            at = pl.ds(pl.multiple_of(t * chunk, chunk), chunk)
            n_all[at, :], _ = normal_of(c_all[at, :].astype(F32))

    pl.when(now == 0)(load.start)

    if net_sizes:
        x_out, win, wout, wup, wdn, wpj, pieces, piece, *refs = refs
        gather = Gather(net, (shards[0], shards[1], piece), [win, wout, pieces], *refs[:3])
        shared = SharedGather(net, (*shards[2:], *word_shards), [wup, wdn, wpj, *word_out], *refs[3:10])
        exchange = Exchange(net, x_out, inbox, *refs[10:13])
        keep = refs[13]
        char_weights = (win, wout, wup, wdn, wpj)

        @pl.when(now == 0)
        def _():
            peers = [net.wide_peer(j)[1] for j in range(1, net.n_wide)] + [net.dp_peer(j)[1] for j in range(1, net.n_dp)]
            net.greet(peers)
            for ref, (at, length) in zip(vectors, lengths):
                some = length // net.n_wide
                piece[0, :, at : at + some] = ref[...].astype(F32).reshape(1, some)
            net.met(peers)
            for a in (2, 0, 1):
                gather.start(a)
            normalize()
            for a in (2, 0, 1):
                gather.relay(a)
            for a in range(3):
                shared.start(a)
            gather.finish(2)
            column = 0
            for at, length in lengths:
                some = length // net.n_wide
                row = jnp.concatenate([pieces[w, :, at : at + some] for w in range(net.n_wide)], 1)
                vec[:, column : column + length] = row
                column += length
            gather.finish(0)
            gather.finish(1)

        def start_words():
            for a in range(3, 7):
                shared.start(a)

        def relay_chars():
            for a in range(3):
                shared.relay(a)

        def pass_on_chars():
            for a in range(3):
                shared.pass_on(a)

        def finish_chars():
            for a in range(3):
                shared.finish(a)
            for a, weight in enumerate(char_weights):
                pltpu.make_async_copy(weight, char_out[a], keep.at[a]).start()

        schedule = [(1, start_words), (2, relay_chars), (5, pass_on_chars), (8, finish_chars)]
        schedule += [(6 + i, functools.partial(shared.relay, 3 + i)) for i in range(4)]
        schedule += [(12 + i, functools.partial(shared.pass_on, 3 + i)) for i in range(4)]
        for when, act in schedule:
            pl.when(now == when * steps // 8)(act)

    else:
        pl.when(now == 0)(normalize)

    ga, sa, gb, sb, db, qv, ub, pb = char_vectors(vec, width, wup.shape[1], wpj.shape[1])

    def block(t):
        return pl.ds(pl.multiple_of(place * rows + t * chunk, chunk), chunk)

    @pl.when(phase == 0)
    def _():
        a = (n_all[pl.ds(pl.multiple_of(step * rows, rows), rows), :] * ga[...] + sa[...]).astype(BF)
        qkv = nn(a, win[...])
        qkv_ref[:, :width] = (qkv[:, :width] * HD**-0.5).astype(BF)
        qkv_ref[:, width:] = qkv[:, width:].astype(BF)
        ri = lax.broadcasted_iota(jnp.int32, (GROUP, GROUP), 0) // chars_per
        ci = lax.broadcasted_iota(jnp.int32, (GROUP, GROUP), 1) // chars_per
        same = ri == ci
        units = [(g, slice(g * GROUP, (g + 1) * GROUP), p) for g in range(rows // GROUP) for p in range(width // GROUP)]

        def head_pair(at, p, i):
            return qkv_ref[at, i * width + p * GROUP : i * width + (p + 1) * GROUP]

        valid = key_bias(cnt_ref[pl.ds(step, 1), :].astype(F32), chars_per)
        for g, at, p in units:
            bias = jnp.where(same, jnp.broadcast_to(valid[:1, g * GROUP : (g + 1) * GROUP], (GROUP, GROUP)), NEG)
            s = nt(head_pair(at, p, 0), two_heads(head_pair(at, p, 1)))
            for h in range(2):
                p_ref[at, (2 * p + h) * GROUP : (2 * p + h + 1) * GROUP] = softmax_low(s[:, h * GROUP : (h + 1) * GROUP] + bias)
        for _, at, p in units:
            o_ref[at, p * GROUP : (p + 1) * GROUP] = nn(p_ref[at, 2 * p * GROUP : 2 * (p + 1) * GROUP], two_heads(head_pair(at, p, 2))).astype(BF)
        for t in range(rows // chunk):
            at = slice(t * chunk, (t + 1) * chunk)
            here = pl.ds(pl.multiple_of(step * rows + t * chunk, chunk), chunk)
            h1 = c_all[here, :].astype(F32) + nn(o_ref[at, :], wout[...])
            h1_ref[at, :] = h1.astype(BF)
            h1_all[here, :] = h1

    @pl.when(phase == 1)
    def _():
        counts = as_column(cnt_ref[pl.ds(place, 1), :].astype(F32))
        for t in range(rows // chunk):
            at = slice(t * chunk, (t + 1) * chunk)
            wat = slice(t * cw, (t + 1) * cw)
            h1 = h1_all[block(t), :]
            n, _ = normal_of(h1)
            u = (n * gb[...] + sb[...]).astype(BF)
            m, s = gelu_and_slope(nn(u, wup[...]) + ub[...])
            m_ref[at, :] = m.astype(BF)
            s_ref[at, :] = s.astype(BF)
            h2 = h1 + (nn(m_ref[at, :], wdn[...]) + db[...])
            h2_ref[at, :] = h2.astype(BF)
            om = pool_weights(h2, qv[...], counts[wat, :], chars_per)
            pooled_ref[wat, :] = jnp.sum(om * h2.reshape(cw, chars_per, width), 1).astype(BF)
        x = (nn(pooled_ref[...], wpj[...]) + pb[...]).astype(BF)
        if net_sizes:
            cap = x_out.shape[1]
            first_word = place * words
            target = first_word // cap
            x_out[target, pl.ds(pl.multiple_of(lax.rem(first_word, cap), words), words)] = x
            pl.when(lax.rem(first_word + words, cap) == 0)(lambda: exchange.send_block(target))
        else:
            x_ref[...] = x

    if net_sizes:

        @pl.when(now == 2 * steps - 1)
        def _():
            for a in range(3, 7):
                shared.finish(a)
            exchange.finish()
            for a, weight in enumerate(char_weights):
                pltpu.make_async_copy(weight, char_out[a], keep.at[a]).wait()


def char_forward(chars, counts, weights, chars_per, rows, net_sizes=None, word_shards=None, vectors=None, cap=None):
    total, width = chars.shape
    words, cw = total // chars_per, rows // chars_per
    ff, out = weights[2].shape[1], weights[4].shape[1]
    steps = total // rows

    def early(count, columns):
        return pl.BlockSpec((count, columns), lambda p, i: (i + p * (steps - 1 - i), 0))

    def late(count, columns):
        return pl.BlockSpec((count, columns), lambda p, i: (late_place(net_sizes, steps, i * p), 0))

    saved = [((words, width), BF, cw, late), ((total, 3 * width), BF, rows, early), ((total, 2 * width), BF, rows, early),
             ((total, width), BF, rows, early), ((total, width), BF, rows, early), ((total, width), BF, rows, late),
             ((total, ff), BF, rows, late), ((total, ff), BF, rows, late)]
    saved_specs = [where(count, s[1]) for s, _, count, where in saved]
    saved_shapes = [jax.ShapeDtypeStruct(s, d) for s, d, _, _ in saved]
    anywhere = pl.BlockSpec(memory_space=pl.ANY)
    in_specs = [anywhere, whole_block(counts.shape)]
    operands = [chars, counts]
    scratch = [pltpu.VMEM((total, width), F32), pltpu.VMEM((total, width), BF), pltpu.VMEM((total, width), F32), pltpu.SemaphoreType.DMA(())]
    if net_sizes:
        n_dp, n_wide = net_sizes
        n_z = n_wide // 2
        lengths, room = [], 0
        for v in vectors:
            lengths.append((room, v.shape[0] * n_wide))
            room += padded(v.shape[0])
        in_specs += [anywhere] * 9 + [whole_block(v.shape) for v in vectors]
        operands += [*weights, *word_shards, *vectors]
        vec_shape = jax.ShapeDtypeStruct((1, sum(length for _, length in lengths)), F32)
        grown = lambda a: jax.ShapeDtypeStruct((a.shape[0] * n_wide, a.shape[1]), a.dtype)
        fulls = [grown(a) for a in weights]
        out_specs = [anywhere, whole_out(vec_shape.shape)] + [anywhere] * 9 + saved_specs
        out_shapes = [jax.ShapeDtypeStruct((n_wide, cap, out), BF), vec_shape, *fulls, *(grown(a) for a in word_shards), *saved_shapes]
        scratch += (
            [pltpu.VMEM((n_wide, cap, out), BF)]
            + [pltpu.VMEM(a.shape, a.dtype) for a in fulls]
            + [pltpu.VMEM((n_wide, 1, room), F32), pltpu.VMEM((1, 1, room), F32)]
            + Gather.scratch(3, n_z)
            + SharedGather.scratch(7, n_dp, n_z)
            + Exchange.scratch(n_wide)
            + [pltpu.SemaphoreType.DMA((5,))]
        )
        params = pltpu.CompilerParams(vmem_limit_bytes=VMEM_LIMIT, collective_id=1, has_side_effects=True)
    else:
        lengths = None
        in_specs += [whole_block(w.shape) for w in weights]
        operands += [*weights]
        out_specs = [late(cw, out)] + saved_specs
        out_shapes = [jax.ShapeDtypeStruct((words, out), BF), *saved_shapes]
        params = pltpu.CompilerParams(vmem_limit_bytes=VMEM_LIMIT)
    return pl.pallas_call(
        functools.partial(char_forward_kernel, chars_per, steps, net_sizes, lengths),
        grid=(2, steps),
        in_specs=in_specs,
        out_specs=out_specs,
        out_shape=out_shapes,
        scratch_shapes=scratch,
        compiler_params=params,
        name="char_forward",
    )(*operands)


def word_kernel(slot_cap, net_sizes, *refs):
    arrived, bucket, assign, segment, grad_ref, win, wout, wup, wdn, vec, out_ref, back_out, *refs = refs
    length, width = grad_ref.shape
    ff = wup.shape[1]
    if net_sizes:
        net = Net(*net_sizes)
        grads_out, word_row, *refs = refs
        *held, word_grads, load_sem, store_sem = refs[-7:]
        refs = refs[:-7]
        loads = [pltpu.make_async_copy(src, dst, load_sem.at[i]) for i, (src, dst) in enumerate(zip((win, wout, wup, wdn), held))]
        for load in loads:
            load.start()
        win, wout, wup, wdn = held
        dga, dsa, dgb, dsb, ddb, dub = word_vectors(word_row, width, ff)
    else:
        dga, dsa, dwin, dwout, dgb, dsb, dwup, dub, dwdn, ddb, *refs = refs
    qkv_ref, p_ref, mix_ref, h_ref, s_ref, gq_ref, gs_ref, *refs = refs
    ga, sa, gb, sb, db, ub = word_vectors(vec, width, ff)
    owners = assign.shape[1]
    slots = owners * slot_cap
    if net_sizes:
        back_ref, *sems = refs
        exchange = Exchange(net, back_ref, back_out, *sems)
        peers = [net.wide_peer(j)[1] for j in range(1, net.n_wide)]
        net.greet(peers)
    def ready(i):
        if net_sizes:
            loads[i].wait()

    named = jnp.where(bucket[...] == lax.broadcasted_iota(jnp.int32, (owners, length), 0), 1.0, 0.0)
    ri = lax.broadcasted_iota(jnp.int32, (length, length), 0)
    ci = lax.broadcasted_iota(jnp.int32, (length, length), 1)
    earlier = nn(named.astype(BF), jnp.where(ri < ci, 1.0, 0.0).astype(BF))
    served = as_column(assign[...].astype(F32)) * slot_cap
    slot = jnp.sum(named * (served + earlier), 0, keepdims=True).astype(jnp.int32)
    hot = jnp.where(lax.broadcasted_iota(jnp.int32, (slots, length), 0) == slot, 1.0, 0.0).astype(BF)
    x = tn(hot, arrived[...].reshape(slots, width))
    n1, r1 = normal_of(x)
    a = (n1 * ga[...] + sa[...]).astype(BF)
    ready(0)
    qkv = nn(a, win[...])
    qkv_ref[:, :width] = (qkv[:, :width] * HD**-0.5).astype(BF)
    qkv_ref[:, width:] = qkv[:, width:].astype(BF)
    seg = segment[...].astype(F32)
    bias = jnp.where((seg == as_column(seg)) & (ci <= ri), 0.0, NEG)

    def pair(p):
        return [qkv_ref[:, i * width + p * GROUP : i * width + (p + 1) * GROUP] for i in range(3)]

    pairs = range(width // GROUP)

    def both(p):
        return slice(2 * p * length, (2 * p + 2) * length)

    for p in pairs:
        q, k, _ = pair(p)
        s = nt(q, two_heads(k))
        for h in range(2):
            p_ref[:, (2 * p + h) * length : (2 * p + h + 1) * length] = softmax_low(s[:, h * length : (h + 1) * length] + bias)
    for p in pairs:
        mix_ref[:, p * GROUP : (p + 1) * GROUP] = nn(p_ref[:, both(p)], two_heads(pair(p)[2])).astype(BF)
    ready(1)
    inner = x + nn(mix_ref[...], wout[...])
    n2, r2 = normal_of(inner)
    u = (n2 * gb[...] + sb[...]).astype(BF)
    ready(2)
    h, slope = gelu_and_slope(nn(u, wup[...]) + ub[...])
    h_ref[...] = h.astype(BF)
    s_ref[...] = slope
    ready(3)
    out_ref[...] = inner + (nn(h_ref[...], wdn[...]) + db[...])
    g = grad_ref[...]
    gz = (nt(g, wdn[...]) * s_ref[...]).astype(BF)
    du = nt(gz, wup[...])
    g1 = g.astype(F32) + norm_back(du, n2, r2, gb[...])
    g1_low = g1.astype(BF)
    gm = nt(g1_low, wout[...]).astype(BF)
    for p in pairs:
        dp = nt(gm[:, p * GROUP : (p + 1) * GROUP], two_heads(pair(p)[2]))
        for h in range(2):
            lanes = slice((2 * p + h) * length, (2 * p + h + 1) * length)
            gs_ref[:, lanes] = softmax_back(p_ref[:, lanes], dp[:, h * length : (h + 1) * length])
    for p in pairs:
        q, k, _ = pair(p)
        gs = gs_ref[:, both(p)]
        gq_ref[:, p * GROUP : (p + 1) * GROUP] = (nn(gs, two_heads(k)) * HD**-0.5).astype(BF)
        gq_ref[:, width + p * GROUP : width + (p + 1) * GROUP] = one_of_two(tn(gs, q)).astype(BF)
        gmp = gm[:, p * GROUP : (p + 1) * GROUP]
        gq_ref[:, 2 * width + p * GROUP : 2 * width + (p + 1) * GROUP] = one_of_two(tn(p_ref[:, both(p)], gmp)).astype(BF)
    da = nt(gq_ref[...], win[...])
    gx = (g1 + norm_back(da, n1, r1, ga[...])).astype(BF)
    back = nn(hot, gx).astype(BF).reshape(owners, slot_cap, width)
    if net_sizes:
        back_ref[...] = back
        net.met(peers)
        exchange.send_all()
        some = width // net.n_wide
        side = ff // width

        def put(value, column):
            value = value.astype(BF)
            for w in range(net.n_wide):
                word_grads[w // 2, w % 2, :, column : column + value.shape[1]] = value[w * some : (w + 1) * some]

        def store(i, first, columns):
            window = pl.ds(first, columns)
            return pltpu.make_async_copy(word_grads.at[:, :, :, window], grads_out.at[:, :, :, window], store_sem.at[i])

        put(tn(a, gq_ref[...]), 0)
        put(tn(mix_ref[...], g1_low), 3 * width)
        store(0, 0, 4 * width).start()
        put(tn(u, gz), 4 * width)
        store(1, 4 * width, ff).start()
        down = tn(h_ref[...], g).astype(BF)
        for w in range(net.n_wide):
            for k in range(side):
                first = (w * side + k) * some
                column = 4 * width + ff + k * width
                word_grads[w // 2, w % 2, :, column : column + width] = down[first : first + some]
        store(2, 4 * width + ff, ff).start()
    else:
        back_out[...] = back
        dwin[...] = tn(a, gq_ref[...])
        dwout[...] = tn(mix_ref[...], g1_low)
        dwup[...] = tn(u, gz)
        dwdn[...] = tn(h_ref[...], g)
    dga[...] = column_sum(da * n1)
    dsa[...] = column_sum(da)
    dgb[...] = column_sum(du * n2)
    dsb[...] = column_sum(du)
    dub[...] = column_sum(gz.astype(F32))
    ddb[...] = column_sum(g.astype(F32))
    if net_sizes:
        exchange.finish()
        for i, (first, columns) in enumerate(((0, 4 * width), (4 * width, ff), (4 * width + ff, ff))):
            store(i, first, columns).wait()


def word_block(arrived, bucket, assign, segments, grad, weights, slot_cap, net_sizes=None):
    length, width = grad.shape
    ff = weights[2].shape[1]
    owners = assign.shape[1]
    low = lambda *s: jax.ShapeDtypeStruct(s, BF)
    full = lambda *s: jax.ShapeDtypeStruct(s, F32)
    vmem = pl.BlockSpec(memory_space=pltpu.VMEM)
    out_shapes, out_specs = [full(length, width), low(owners, slot_cap, width)], [vmem, vmem]
    scratch = [pltpu.VMEM((length, 3 * width), BF), pltpu.VMEM((length, width // HD * length), BF), pltpu.VMEM((length, width), BF),
               pltpu.VMEM((length, ff), BF), pltpu.VMEM((length, ff), F32), pltpu.VMEM((length, 3 * width), BF),
               pltpu.VMEM((length, width // HD * length), BF)]
    if net_sizes:
        n_dp, n_wide = net_sizes
        out_shapes += [low(n_wide // 2, 2, width // n_wide, 4 * width + 2 * ff), full(1, 5 * width + ff)]
        anywhere = pl.BlockSpec(memory_space=pl.ANY)
        out_specs = [vmem, anywhere, anywhere, vmem]
        in_specs = [vmem] * 5 + [anywhere] * 4 + [vmem]
        scratch += [pltpu.VMEM((owners, slot_cap, width), BF)] + Exchange.scratch(n_wide)
        scratch += [pltpu.VMEM(w.shape, BF) for w in weights[:4]] + [pltpu.VMEM(out_shapes[2].shape, BF)]
        scratch += [pltpu.SemaphoreType.DMA((4,)), pltpu.SemaphoreType.DMA((3,))]
        params = pltpu.CompilerParams(vmem_limit_bytes=VMEM_LIMIT, collective_id=2, has_side_effects=True)
    else:
        row = full(1, width)
        out_shapes += [row, row, full(width, 3 * width), full(width, width), row, row, full(width, ff), full(1, ff), full(ff, width), row]
        out_specs += [vmem] * 10
        in_specs = [vmem] * 10
        params = pltpu.CompilerParams(vmem_limit_bytes=VMEM_LIMIT)
    return pl.pallas_call(
        functools.partial(word_kernel, slot_cap, net_sizes),
        in_specs=in_specs,
        out_specs=out_specs,
        out_shape=out_shapes,
        scratch_shapes=scratch,
        compiler_params=params,
        name="word_block",
    )(arrived, bucket, assign, segments, grad, *weights)


def gathered(shard):
    return lax.all_gather(shard, "wide", axis=0, tiled=True)


def exchanged(blocks):
    return lax.all_to_all(blocks, "wide", split_axis=0, concat_axis=0, tiled=True)


def summed(grad):
    part = lax.psum_scatter(grad.astype(BF), "wide", scatter_dimension=0, tiled=True)
    return lax.psum(part, "dp").astype(F32)


def shards(
    chars, char_counts, buckets, assign, segments,
    char_gain, char_shift, char_inproj, char_outproj, char_gain_mid, char_shift_mid, char_up, char_up_bias, char_down, char_down_bias,
    pool_query, char_proj, char_proj_bias,
    word_gain, word_shift, word_inproj, word_outproj, word_gain_mid, word_shift_mid, word_up, word_up_bias, word_down, word_down_bias,
    out_grad,
):
    n_dp, n_wide = lax.axis_size("dp"), lax.axis_size("wide")
    cap, chars_per, width = chars.shape[2:]
    slots = n_wide * cap
    rows = chars.reshape(slots * chars_per, width)
    block = min(1024, rows.shape[0])
    counts = char_counts.reshape(-1, block // chars_per)
    char_shards = (char_inproj, char_outproj, char_up, char_down, char_proj)
    word_shards = (word_inproj, word_outproj, word_up, word_down)
    vectors = (char_gain, char_shift, char_gain_mid, char_shift_mid, char_down_bias, pool_query, char_up_bias, char_proj_bias,
               word_gain, word_shift, word_gain_mid, word_shift_mid, word_down_bias, word_up_bias)
    fast = (
        all(m.shape[0] % 16 == 0 for m in char_shards)
        and all(m.shape[0] % (16 * n_dp) == 0 for m in word_shards)
        and cap % (block // chars_per) == 0
        and (4 * width) % (GROUP * n_dp) == 0
        and n_wide % 2 == 0
        and n_dp == 4
        and (4 * word_up.shape[0] * n_wide + 2 * word_up.shape[1]) % (8 * GROUP * WORD_PARTS) == 0
    )
    bucket, names, upstream = buckets.reshape(1, -1), assign[None], out_grad[0]
    if fast:
        sizes = (n_dp, n_wide)
        arrived, vec, *rest = char_forward(rows, counts, char_shards, chars_per, block, sizes, word_shards, vectors, cap)
        char_full, word_full, saved = rest[:5], rest[5:9], rest[9:]
        result, returned, word_grads, word_row = word_block(arrived, bucket, names, segments, upstream, (*word_full, vec), cap, sizes)
        incoming = returned.reshape(slots, -1)
        sums = char_backward(incoming, rows, counts, saved, (*char_full, vec), chars_per, block, sizes, word_grads, word_row)
        params = (char_gain, char_shift, char_inproj, char_outproj, char_gain_mid, char_shift_mid, char_up, char_up_bias, char_down,
                  char_down_bias, pool_query, char_proj, char_proj_bias, word_gain, word_shift, word_inproj, word_outproj, word_gain_mid,
                  word_shift_mid, word_up, word_up_bias, word_down, word_down_bias)
        shapes = [p.shape if p.ndim == 2 else (1, *p.shape) for p in params]
        char_grads, *grads = outputs_of(*sums, shapes=shapes, rows=min(2048, rows.shape[0]))
        grads = [g[0] if g.shape[0] == 1 else g for g in grads]
    else:
        vec = jnp.concatenate([gathered(v) for v in vectors]).astype(F32)[None]
        char_full, word_full = [gathered(m) for m in char_shards], [gathered(m) for m in word_shards]
        outgoing, *saved = char_forward(rows, counts, (*char_full, vec), chars_per, block)
        arrived = exchanged(outgoing.reshape(n_wide, cap, -1))
        result, back, *word_grads = word_block(arrived, bucket, names, segments, upstream, (*word_full, vec), cap)
        incoming = exchanged(back).reshape(slots, -1)
        char_grads, *grads = char_backward(incoming, rows, counts, saved, (*char_full, vec), chars_per, block)
        grads[8] = grads[8].T
        grads = [summed(g[0] if g.shape[0] == 1 else g) for g in grads + word_grads]
    return (result[None], char_grads.reshape(chars.shape), *grads)


def solution(mesh):
    whole, split = ("dp", "wide"), "wide"
    row, flat = P(split, None), P(split)
    word = [flat, flat, row, row, flat, flat, row, flat, row, flat]
    char = word + [flat, row, flat]
    chars = P(whole, None, None, None, None)
    three = P(whole, None, None)
    return jax.shard_map(
        shards,
        mesh=mesh,
        in_specs=(chars, three, three, P(), P(whole, None), *char, *word, three),
        out_specs=(three, chars, *char, *word),
        check_vma=False,
    )
```
